128 devices in a mesh: ctx: 8 (over z, y_lo), fsdp: 16 (over y_hi, x, core).
Axes of the slice: x: 4, y: 4 (y_hi: 2, y_lo: 2; y = y_hi * 2 + y_lo), z: 4, core: 2. Of those that a mesh axis runs over, the one named last changes fastest.
Arguments:
- tokens: bfloat16 [2, 16, 1024, 1024], P(None, 'fsdp', 'ctx'), may hold values from -6 to 6
- segments: int32 [2, 16, 1024], P(None, 'fsdp'), may hold values from 0 to 1, as said below
- routes: int32 [2, 16, 1024, 8], P(None, 'fsdp', 'ctx'), may hold values from 0 to 31, all different within a row; in each aligned block of 128 rows (0 to 127, 128 to 255, ..., all dimensions but the last counted through in order) at most 48 rows name the same one
- w_query: bfloat16 [1024, 1024], P(('ctx', 'fsdp')), may hold values from -0.1875 to 0.1875
- w_key: bfloat16 [1024, 512], P(('ctx', 'fsdp')), may hold values from -0.1875 to 0.1875
- w_value: bfloat16 [1024, 512], P(('ctx', 'fsdp')), may hold values from -0.1875 to 0.1875
- w_out: bfloat16 [1024, 1024], P(('ctx', 'fsdp')), may hold values from -3 to 3
- w_router: bfloat16 [1024, 32], P(('ctx', 'fsdp')), may hold values from -0.09375 to 0.09375
- attn_gain: bfloat16 [1024], P(('ctx', 'fsdp')), may hold values from 0.5 to 1.5
- mlp_gain: bfloat16 [1024], P(('ctx', 'fsdp')), may hold values from 0.5 to 1.5
- qk_gain: bfloat16 [128], P(('ctx', 'fsdp')), may hold values from 0.5 to 1.5
- w_gate: bfloat16 [32, 1024, 512], P('fsdp', 'ctx'), may hold values from -0.1875 to 0.1875
- w_up: bfloat16 [32, 1024, 512], P('fsdp', 'ctx'), may hold values from -0.1875 to 0.1875
- w_down: bfloat16 [32, 1024, 512], P('fsdp', 'ctx'), may hold values from -1 to 1
- cotangent: bfloat16 [2, 16, 1024, 1024], P(None, 'fsdp', 'ctx'), may hold values from -6 to 6
Outputs:
- out: bfloat16 [2, 16, 1024, 1024], P(None, 'fsdp', 'ctx')
- d_tokens: float32 [2, 16, 1024, 1024], P(None, 'fsdp', 'ctx')
- grad_query: float32 [1024, 1024], P(('ctx', 'fsdp'))
- grad_key: float32 [1024, 512], P(('ctx', 'fsdp'))
- grad_value: float32 [1024, 512], P(('ctx', 'fsdp'))
- grad_out: float32 [1024, 1024], P(('ctx', 'fsdp'))
- grad_router: float32 [1024, 32], P(('ctx', 'fsdp'))
- grad_attn_gain: float32 [1024], P(('ctx', 'fsdp'))
- grad_mlp_gain: float32 [1024], P(('ctx', 'fsdp'))
- grad_qk_gain: float32 [128], P(('ctx', 'fsdp'))
- grad_gate: float32 [32, 1024, 512], P('fsdp', 'ctx')
- grad_up: float32 [32, 1024, 512], P('fsdp', 'ctx')
- grad_down: float32 [32, 1024, 512], P('fsdp', 'ctx')
The draws below stay inside these ranges and needn't reach their ends.
Inputs may be any that keep to these rules, and one draw needn't show every extreme that they name: `segments`: segment ids never fall along a sequence; a sequence holds one or two documents; for each of the 16 sequence slots, one of the 2 micro-batches, drawn from the seed, holds a single document of all 1024 tokens. `routes`: A token's 8 experts differ; among the 128 tokens of one device in one micro-batch no expert is named more than 48 times.
All inputs are finite; a program needn't handle non-finite values.
Results may differ from the reference program's by a relative error of at most 0.03.
Values may be sent and summed in bfloat16 or wider, within the bound.
No kernel may reach another device: no remote copies, remote signals or barrier semaphores. Data moves between devices by JAX's collectives and lax.ppermute only.
A program may use at most 192 MiB of HBM per device.

```python
import math
import jax
import jax.numpy as jnp
import numpy as np
from jax import lax

D = 1024
H = 16
KV = 8
DH = 64
FF = 512
TOPK = 8
WINDOW = 1024
MICRO = 2
LEN = 1024
EXPERTS = 32
SEQS = 16
TOK = 128
CAP = 48


def draw_segments(key, part):
    key = jax.random.fold_in(key, 7)
    pick_key, cut_key = jax.random.split(key)
    whole = jax.random.randint(pick_key, (SEQS,), 0, MICRO)
    cuts = jax.random.randint(cut_key, (MICRO, SEQS), LEN // 8, LEN - LEN // 8 + 1)
    cuts = jnp.where(jnp.arange(MICRO)[:, None] == whole[None, :], LEN, cuts)
    return (jnp.arange(LEN)[None, None, :] >= cuts[:, :, None]).astype(jnp.int32)


def shard_levels(key, extent, pieces, smallest, top_value):
    loudness = 1.0
    for dim, parts in pieces:
        steps = jax.random.uniform(jax.random.fold_in(jax.random.fold_in(key, 6), dim), (parts,), jnp.float32, smallest / len(pieces), top_value / len(pieces))
        loudness = loudness * jnp.repeat(jnp.exp(steps), extent[dim] // parts).reshape((-1,) + (1,) * (len(extent) - 1 - dim))
    return loudness


def routed_block(stream_key, own, number, rows, number_of, top, reach, lean):
    order = jax.random.permutation(stream_key, number_of)
    crowded, usual = shares(number_of, rows * top, reach, lean, True), shares(number_of, rows * top, reach, lean, False)
    places = jnp.arange(number_of)

    def named(lengths, offset_by):
        used = int((lengths > 0).sum())
        fixed = max(1, used // 4)
        moved = fixed + (places - fixed + offset_by * (used - fixed)) % max(1, number_of - fixed)
        return jnp.zeros((number_of,), jnp.int32).at[order[jnp.where(places < fixed, places, moved)]].set(jnp.asarray(lengths, jnp.int32))

    lengths = jnp.where(number % 4 == 0, named(crowded, number // 4), named(usual, number - number // 4 - 1))
    mixed = jax.random.permutation(jax.random.fold_in(own, 3), number_of)
    giver, sink = mixed[0:number_of // 2 * 2:2], mixed[1:number_of // 2 * 2:2]
    room = jnp.minimum(lengths[giver] - 1, reach - lengths[sink]) // 2
    room = jnp.where((giver == order[0]) | (sink == order[0]) | (lengths[sink] == 0), 0, jnp.maximum(room, 0))
    moved = jax.random.randint(jax.random.fold_in(own, 4), (number_of // 2,), 0, 1 << 20) % (room + 1)
    lengths = lengths.at[giver].add(-moved).at[sink].add(moved)
    labels = jnp.searchsorted(jnp.cumsum(lengths), jnp.arange(rows * top), side="right").astype(jnp.int32)
    grid = labels.reshape(top, rows).T
    grid = grid[jax.random.permutation(jax.random.fold_in(own, 1), rows)]
    offset_by = jax.random.randint(jax.random.fold_in(own, 2), (rows, 1), 0, top)
    return jnp.take_along_axis(grid, (jnp.arange(top)[None, :] + offset_by) % top, axis=1)


def shares(number_of, total, most, skew, full):
    weights = [(1 << 20) // math.isqrt(standing ** skew) + 1 for standing in range(1, number_of + 1)]
    largest = most if full else min(most, max(-(-total // number_of), total * weights[0] // sum(weights)))
    least = 1 if total - largest >= number_of - 1 else 0
    holding, spare = [largest] + [least] * (number_of - 1), total - largest - least * (number_of - 1)
    while spare > 0:
        movable = [i for i in range(1, number_of) if holding[i] < largest] or [i for i in range(1, number_of) if holding[i] < most]
        pool, budget = sum([weights[i] for i in movable]), spare
        for i in movable:
            more = min(most - holding[i], max(1, budget * weights[i] // pool), spare)
            holding[i] = holding[i] + more
            spare = spare - more
    return np.array(holding)


def centred(key, dims, spread, most, cuts=(), kind=jnp.bfloat16):
    drawn = jax.random.normal(key, dims, jnp.float32) * spread
    if len(cuts) > 0:
        drawn = shard_levels(key, dims, cuts, -0.22, 0.18) * drawn
    return jnp.clip(drawn, min=-most, max=most).astype(kind)


def setup_inputs(seed: int = 0) -> dict:
    splits = jax.random.split(jax.random.key(seed), 16)
    tokens = centred(splits[0], (MICRO, SEQS, LEN, D), 1.0, 6.0, ((1, 16), (2, 8)))
    segments = draw_segments(jax.random.fold_in(splits[15], 71), 0)
    routes_keys = jax.random.split(jax.random.fold_in(splits[2], 1), MICRO * SEQS * LEN // TOK)
    routes_turns = jax.random.permutation(jax.random.fold_in(splits[2], 3), MICRO * SEQS * LEN // TOK)
    routes = jax.vmap(lambda own, number: routed_block(jax.random.fold_in(splits[2], 2), own, number, TOK, EXPERTS, TOPK, CAP, 2))(routes_keys, routes_turns).reshape((MICRO, SEQS, LEN, TOPK))
    w_query = centred(splits[3], (D, H * DH), D ** -0.5, 0.1875, ((0, 128),))
    w_key = centred(splits[4], (D, KV * DH), D ** -0.5, 0.1875, ((0, 128),))
    w_value = centred(splits[5], (D, KV * DH), D ** -0.5, 0.1875, ((0, 128),))
    w_out = centred(splits[6], (H * DH, D), (max(1, H * DH // 256)) ** -0.5, 3.0, ((0, 128),))
    w_router = centred(splits[7], (D, EXPERTS), (4 * D) ** -0.5, 0.09375, ((0, 128),))
    attn_gain = jnp.clip(1.0 + 0.1 * jax.random.normal(splits[8], (D,), jnp.float32), 0.5, 1.5).astype(jnp.bfloat16)
    mlp_gain = jnp.clip(1.0 + 0.1 * jax.random.normal(splits[9], (D,), jnp.float32), 0.5, 1.5).astype(jnp.bfloat16)
    qk_gain = jnp.clip(1.0 + 0.1 * jax.random.normal(splits[10], (2 * DH,), jnp.float32), 0.5, 1.5).astype(jnp.bfloat16)
    w_gate = centred(splits[11], (EXPERTS, D, FF), D ** -0.5, 0.1875, ((0, 16), (1, 8)))
    w_up = centred(splits[12], (EXPERTS, D, FF), D ** -0.5, 0.1875, ((0, 16), (1, 8)))
    w_down = centred(splits[13], (EXPERTS, D, FF), (max(1, FF // 16)) ** -0.5, 1.0, ((0, 16), (1, 8)))
    cotangent = centred(splits[14], (MICRO, SEQS, LEN, D), 1.0, 6.0, ((1, 16), (2, 8)))
    return {"tokens": tokens, "segments": segments, "routes": routes, "w_query": w_query, "w_key": w_key, "w_value": w_value, "w_out": w_out, "w_router": w_router, "attn_gain": attn_gain, "mlp_gain": mlp_gain, "qk_gain": qk_gain, "w_gate": w_gate, "w_up": w_up, "w_down": w_down, "cotangent": cotangent}


EPS = 1e-06
THETA = 10000.0
HIGH = lax.Precision.HIGHEST

@jax.custom_vjp
def low(v):
    return lax.optimization_barrier(v.astype(jnp.bfloat16)).astype(jnp.float32)

@jax.custom_vjp
def low_back(v):
    return v

def low_keep(v):
    return (low(v), None)

def low_pass(kept, grad):
    return (grad,)

def back_keep(v):
    return (v, None)

def back_low(kept, grad):
    return (low(grad),)
low.defvjp(low_keep, low_pass)
low_back.defvjp(back_keep, back_low)

def rms_scale(values, gain):
    return values * lax.rsqrt(lax.optimization_barrier(jnp.mean(values * values, axis=-1, keepdims=True)) + EPS) * gain

def rope_tables(positions):
    half = DH // 2
    inverse = THETA ** (-(jnp.arange(half, dtype=jnp.float32) * 2.0) / DH)
    angles = positions.astype(jnp.float32)[:, None] * inverse[None, :]
    return (jnp.cos(angles), jnp.sin(angles))

def head_post(raw, gain, cosine, sine, heads):
    shaped = raw.reshape(raw.shape[:-1] + (heads, DH))
    normed = rms_scale(shaped, gain)
    half = DH // 2
    first_half = normed[..., :half]
    second_half = normed[..., half:]
    cos_grid = cosine[:, None, :]
    sin_grid = sine[:, None, :]
    return jnp.concatenate([first_half * cos_grid - second_half * sin_grid, second_half * cos_grid + first_half * sin_grid], axis=-1)

def reference(tokens, segments, routes, w_query, w_key, w_value, w_out, w_router, attn_gain, mlp_gain, qk_gain, w_gate, w_up, w_down, cotangent):
    seq_count = MICRO * SEQS
    group = math.gcd(seq_count, max(1, 4096 // LEN))
    groups = seq_count // group
    per_seq = LEN // TOK
    radius = WINDOW // 2
    scale = DH ** (-0.5)
    flat_routes = routes.reshape(seq_count * per_seq, TOK * TOPK)
    one_hot = (flat_routes[:, :, None] == jnp.arange(EXPERTS, dtype=jnp.int32)[None, None, :]).astype(jnp.int32)
    slots = lax.optimization_barrier(jnp.sum(jnp.cumsum(one_hot, axis=1) * one_hot, axis=2)) - 1
    slots = slots.reshape(groups, group, LEN, TOPK).astype(jnp.int32)
    route_groups = routes.reshape(groups, group, LEN, TOPK)
    seg_groups = segments.reshape(groups, group, LEN)
    x_groups = tokens.astype(jnp.float32).reshape(groups, group, LEN, D)
    position = jnp.arange(LEN, dtype=jnp.int32)
    cosine, sine = rope_tables(position)
    window_mask = jnp.abs(position[:, None] - position[None, :]) < radius
    seq_grid = jnp.arange(group, dtype=jnp.int32)[:, None, None]
    pos_grid = jnp.arange(LEN, dtype=jnp.int32)[None, :, None]
    pick_grid = jnp.arange(TOPK, dtype=jnp.int32)[None, None, :]
    row_ids = jnp.broadcast_to((seq_grid * LEN + pos_grid) * TOPK + pick_grid, (group, LEN, TOPK)).astype(jnp.int32)
    block_ids = jnp.broadcast_to(seq_grid * per_seq + pos_grid // TOK, (group, LEN, TOPK)).astype(jnp.int32)
    sentinel = group * LEN * TOPK
    buffer_rows = group * per_seq * CAP

    def attend(inputs):
        queries, keys, values, seg_row = inputs
        grouped = queries.reshape(LEN, KV, H // KV, DH)
        scores = low_back(jnp.einsum('qgrd,kgd->grqk', grouped, keys, precision=HIGH) * scale)
        allowed = (seg_row[:, None] == seg_row[None, :]) & window_mask
        scores = jnp.where(allowed, scores, -1e+30)
        weights = low(jax.nn.softmax(scores, axis=-1))
        mixed = jnp.einsum('grqk,kgd->qgrd', weights, values, precision=HIGH)
        return mixed.reshape(LEN, H * DH)
    attend_saved = jax.checkpoint(attend)

    def layer(params, x_group, seg_group, route_group, slot_group):
        weight_query, weight_key, weight_value, weight_out, weight_router, gain_attn, gain_mlp, gain_heads, weight_gate, weight_up, weight_down = params
        hidden = low(rms_scale(x_group, gain_attn))
        query_raw = low_back(jnp.einsum('gld,de->gle', hidden, weight_query, precision=HIGH))
        key_raw = low_back(jnp.einsum('gld,de->gle', hidden, weight_key, precision=HIGH))
        value_raw = low(low_back(jnp.einsum('gld,de->gle', hidden, weight_value, precision=HIGH)))
        queries = low(head_post(query_raw, gain_heads[:DH], cosine, sine, H))
        keys = low(head_post(key_raw, gain_heads[DH:], cosine, sine, KV))
        values = value_raw.reshape(group, LEN, KV, DH)
        mixed = lax.map(attend_saved, (queries, keys, values, seg_group))
        mixed = low(low_back(mixed))
        branch = low_back(jnp.einsum('gle,ed->gld', mixed, weight_out, precision=HIGH))
        middle = x_group + branch
        hidden_two = low(rms_scale(middle, gain_mlp))
        logits = low_back(jnp.einsum('gld,de->gle', hidden_two, weight_router, precision=HIGH))
        chosen = jnp.take_along_axis(logits, route_group, axis=-1)
        gates = jax.nn.softmax(chosen, axis=-1)
        buffer_pos = (block_ids * CAP + slot_group).astype(jnp.int32)
        table = jnp.full((EXPERTS, buffer_rows), sentinel, jnp.int32)
        table = table.at[route_group.reshape(-1), buffer_pos.reshape(-1)].set(row_ids.reshape(-1))
        token_index = jnp.where(table == sentinel, group * LEN, table // TOPK).astype(jnp.int32)
        padded = jnp.concatenate([hidden_two.reshape(group * LEN, D), jnp.zeros((1, D), hidden_two.dtype)], axis=0)
        expert_in = padded[token_index]
        gate_proj = low_back(jnp.einsum('erd,edf->erf', expert_in, weight_gate, precision=HIGH))
        up_proj = low_back(jnp.einsum('erd,edf->erf', expert_in, weight_up, precision=HIGH))
        active = low(jax.nn.silu(gate_proj) * up_proj)
        expert_out = low(low_back(jnp.einsum('erf,edf->erd', active, weight_down, precision=HIGH)))
        picked = expert_out[route_group, buffer_pos]
        return middle + jnp.einsum('glk,glkd->gld', gates, picked, precision=HIGH)
    layer_saved = jax.checkpoint(layer)

    def forward(params, inputs):

        def run_group(package):
            return layer_saved(params, package[0], package[1], package[2], package[3])
        return lax.map(run_group, (inputs, seg_groups, route_groups, slots))
    params = (w_query.astype(jnp.float32), w_key.astype(jnp.float32), w_value.astype(jnp.float32), w_out.astype(jnp.float32), w_router.astype(jnp.float32), attn_gain.astype(jnp.float32), mlp_gain.astype(jnp.float32), qk_gain.astype(jnp.float32), w_gate.astype(jnp.float32), w_up.astype(jnp.float32), w_down.astype(jnp.float32))
    result, pullback = jax.vjp(forward, params, x_groups)
    param_grads, input_grad = pullback(cotangent.astype(jnp.float32).reshape(groups, group, LEN, D))
    return (result.reshape(MICRO, SEQS, LEN, D).astype(jnp.bfloat16), input_grad.reshape(MICRO, SEQS, LEN, D), param_grads[0], param_grads[1], param_grads[2], param_grads[3], param_grads[4], param_grads[5], param_grads[6], param_grads[7], param_grads[8], param_grads[9], param_grads[10])
```

```python
import jax
import jax.numpy as jnp
from jax import lax
from jax.sharding import PartitionSpec as P

H = 16
KV = 8
DH = 64
TOPK = 8
WINDOW = 1024
EPS = 1e-06
THETA = 10000.0

BF = jnp.bfloat16
F32 = jnp.float32


def ctx_perm(dz, dyl):
    return [(z * 2 + y, ((z + dz) % 4) * 2 + (y + dyl) % 2) for z in range(4) for y in range(2)]


def fsdp_perm(dyh, dx, dcore):
    return [
        ((y * 4 + x) * 2 + c, (((y + dyh) % 2) * 4 + (x + dx) % 4) * 2 + (c + dcore) % 2)
        for y in range(2)
        for x in range(4)
        for c in range(2)
    ]


RING = {
    "z": ("ctx", ctx_perm(1, 0), ctx_perm(-1, 0)),
    "x": ("fsdp", fsdp_perm(0, 1, 0), fsdp_perm(0, -1, 0)),
}
PAIR = {
    "yl": ("ctx", ctx_perm(0, 1)),
    "yh": ("fsdp", fsdp_perm(1, 0, 0)),
    "core": ("fsdp", fsdp_perm(0, 0, 1)),
}


def gather_stage(block, name):
    if name in PAIR:
        axis, swap = PAIR[name]
        return jnp.concatenate([block, lax.ppermute(block, axis, swap)], axis=0)
    axis, up, down = RING[name]
    half = block.shape[0] // 2
    before = lax.ppermute(block, axis, up)
    after = lax.ppermute(block, axis, down)
    far_low = lax.ppermute(before[:half], axis, up)
    far_high = lax.ppermute(after[half:], axis, down)
    return jnp.concatenate([block, after, far_low, far_high, before], axis=0)


def gather_all(block, names):
    for name in names:
        block = gather_stage(block, name)
    return block


def add(a, b):
    return (a.astype(F32) + b.astype(F32)).astype(BF)


def scatter_stage(parts, name):
    if name in PAIR:
        axis, swap = PAIR[name]
        half = parts.shape[0] // 2
        return add(parts[:half], lax.ppermute(parts[half:], axis, swap))
    axis, up, down = RING[name]
    size = parts.shape[0] // 4
    half = size // 2
    own, after, far, before = (parts[k * size : (k + 1) * size] for k in range(4))
    low = lax.ppermute(far[:half], axis, up)
    high = lax.ppermute(far[half:], axis, down)
    after = jnp.concatenate([add(after[:half], low), after[half:]], axis=0)
    before = jnp.concatenate([before[:half], add(before[half:], high)], axis=0)
    from_before = lax.ppermute(after, axis, up)
    from_after = lax.ppermute(before, axis, down)
    return (own.astype(F32) + from_before.astype(F32) + from_after.astype(F32)).astype(BF)


def scatter_all(parts, names):
    for name in reversed(names):
        parts = scatter_stage(parts, name)
    return parts


SIZES = {"z": 4, "x": 4, "yl": 2, "yh": 2, "core": 2}


def coordinates():
    c = lax.axis_index("ctx")
    f = lax.axis_index("fsdp")
    return {"z": c // 2, "yl": c % 2, "yh": f // 8, "x": (f // 2) % 4, "core": f % 2}


def owner_order(names, rows):
    place = jnp.arange(128 * rows, dtype=jnp.int32)
    inner = place % rows
    rest = place // rows
    here = coordinates()
    digit = {}
    for name in names:
        digit[name] = (rest % SIZES[name] + here[name]) % SIZES[name]
        rest = rest // SIZES[name]
    block = (((digit["z"] * 2 + digit["yl"]) * 2 + digit["yh"]) * 4 + digit["x"]) * 2 + digit["core"]
    return block * rows + inner


def order_matrix(order):
    return (jnp.arange(order.shape[0], dtype=jnp.int32)[:, None] == order[None, :]).astype(BF)


PATH_A = ("yl", "z", "yh", "x", "core")
PATH_B = ("x", "yh", "yl", "z", "core")
PATH_E = ("yh", "x", "core")


def rms_scale(values, gain):
    return values * lax.rsqrt(jnp.mean(values * values, axis=-1, keepdims=True) + EPS) * gain


def rope_tables(positions):
    half = DH // 2
    inverse = THETA ** (-(jnp.arange(half, dtype=F32) * 2.0) / DH)
    angles = positions.astype(F32)[:, None] * inverse[None, :]
    return (jnp.cos(angles), jnp.sin(angles))


def head_post(raw, gain, cosine, sine, heads):
    shaped = raw.reshape(raw.shape[:-1] + (heads, DH))
    normed = rms_scale(shaped, gain)
    half = DH // 2
    first_half = normed[..., :half]
    second_half = normed[..., half:]
    cos_grid = cosine[:, None, :]
    sin_grid = sine[:, None, :]
    return jnp.concatenate(
        [
            first_half * cos_grid - second_half * sin_grid,
            second_half * cos_grid + first_half * sin_grid,
        ],
        axis=-1,
    )


def mm(a, b):
    return jnp.dot(a, b, preferred_element_type=F32)


def mm_t(a, b):
    return lax.dot_general(a, b, (((1,), (1,)), ((), ())), preferred_element_type=F32)


def t_mm(a, b):
    return lax.dot_general(a, b, (((0,), (0,)), ((), ())), preferred_element_type=F32)


def ein(spec, a, b):
    return jnp.einsum(spec, a, b, preferred_element_type=F32)


def split(v):
    high = v.astype(BF)
    return high, (v - high.astype(F32)).astype(BF)


def body(
    tokens,
    segments,
    routes,
    w_query,
    w_key,
    w_value,
    w_out,
    w_router,
    attn_gain,
    mlp_gain,
    qk_gain,
    w_gate,
    w_up,
    w_down,
    cotangent,
):
    micro = tokens.shape[0]
    tok = tokens.shape[2]
    width = tokens.shape[3]
    length = segments.shape[2]
    rows = w_query.shape[0]
    n_ctx = lax.axis_size("ctx")
    n_fsdp = lax.axis_size("fsdp")
    place = lax.axis_index("ctx")
    shard = lax.axis_index("fsdp")
    local = w_gate.shape[0]
    experts = local * n_fsdp
    cap = (3 * tok * TOPK + 2 * experts - 1) // (2 * experts)
    all_tok = micro * tok
    scale = DH ** (-0.5)

    small = jnp.concatenate(
        [
            w_router,
            attn_gain[:, None],
            mlp_gain[:, None],
            jnp.pad(qk_gain[:, None], ((0, rows - 1), (0, 0))),
        ],
        axis=1,
    )
    small = jnp.pad(small, ((0, 0), (0, 128 - small.shape[1])))
    rel_a = gather_all(jnp.concatenate([small, w_query], axis=1), PATH_A)
    rel_b = gather_all(jnp.concatenate([w_key, w_value], axis=1), PATH_B)
    out_rel = gather_all(w_out, PATH_A)
    order_a = order_matrix(owner_order(PATH_A, rows))
    order_b = order_matrix(owner_order(PATH_B, rows))
    query_rel = rel_a[:, 128:]
    small_all = mm(order_a, rel_a[:, :128])
    router = small_all[:, :experts].astype(BF)
    gain_attn = small_all[:, experts]
    gain_mlp = small_all[:, experts + 1]
    gain_heads = small_all[:, experts + 2].reshape(-1, rows)[:, 0]

    weight_gate = lax.all_gather(w_gate, "ctx", axis=1, tiled=True)
    weight_up = lax.all_gather(w_up, "ctx", axis=1, tiled=True)
    weight_down = lax.all_gather(w_down, "ctx", axis=1, tiled=True)

    cot = cotangent.reshape(all_tok, width)
    route_rows = routes.reshape(all_tok, TOPK)
    routes_low = route_rows.astype(BF).reshape(-1, width)
    pack = jnp.concatenate([cot, routes_low], axis=0)
    pack_all = gather_all(pack[None], PATH_E)
    cot_all = pack_all[:, :all_tok].reshape(n_fsdp, micro, tok, width)
    routes_all = (
        pack_all[:, all_tok:].reshape(n_fsdp, micro, tok, TOPK).astype(jnp.int32)
    )

    start = tokens.reshape(all_tok, width).astype(F32)
    normed_one, norm_one_back = jax.vjp(rms_scale, start, gain_attn)
    hidden = normed_one.astype(BF)
    hidden_a = mm(hidden, order_a).astype(BF)
    hidden_b = mm(hidden, order_b).astype(BF)
    query_raw = mm(hidden_a, query_rel)
    kv_raw = mm(hidden_b, rel_b)
    positions = place * tok + jnp.arange(tok, dtype=jnp.int32)
    cosine, sine = rope_tables(positions)
    cosine = jnp.tile(cosine, (micro, 1))
    sine = jnp.tile(sine, (micro, 1))

    def query_post(raw, gain):
        return head_post(raw, gain, cosine, sine, H)

    def key_post(raw, gain):
        return head_post(raw, gain, cosine, sine, KV)

    query_rot, query_back = jax.vjp(query_post, query_raw, gain_heads[:DH])
    key_rot, key_back = jax.vjp(key_post, kv_raw[:, : KV * DH], gain_heads[DH:])
    ratio = H // KV
    query_low = query_rot.astype(BF).reshape(all_tok, KV, ratio * DH)
    key_low = key_rot.astype(BF)
    value_low = kv_raw[:, KV * DH :].astype(BF).reshape(all_tok, KV, DH)
    qkv = jnp.concatenate([query_low, key_low, value_low], axis=2)
    qkv = qkv.transpose(1, 0, 2)
    qkv_heads = lax.all_to_all(qkv, "ctx", split_axis=0, concat_axis=0, tiled=True)
    qkv_heads = (
        qkv_heads.reshape(n_ctx, micro, tok, -1).transpose(1, 0, 2, 3).reshape(micro, length, -1)
    )
    q_h = qkv_heads[:, :, : ratio * DH].reshape(micro, length, ratio, DH)
    k_h = qkv_heads[:, :, ratio * DH : (ratio + 1) * DH]
    v_h = qkv_heads[:, :, (ratio + 1) * DH :]
    spots = jnp.arange(length, dtype=jnp.int32)
    near = jnp.abs(spots[:, None] - spots[None, :]) < WINDOW // 2
    seg = segments[:, 0]
    allowed = (seg[:, :, None] == seg[:, None, :]) & near[None]

    def scores_of():
        return jnp.where(allowed[:, None], ein("mqrd,mkd->mrqk", q_h, k_h) * scale, -1e30)

    scores = scores_of()
    highest = jnp.max(scores, axis=-1, keepdims=True)
    shifted = jnp.exp(scores - highest)
    total = jnp.sum(shifted, axis=-1, keepdims=True)
    log_total = highest + jnp.log(total)
    probs_low = (shifted / total).astype(BF)
    mixed_h = ein("mrqk,mkd->mqrd", probs_low, v_h).astype(BF).reshape(micro, length, ratio * DH)

    def to_tokens(v):
        v = v.reshape(micro, n_ctx, tok, -1).transpose(1, 0, 2, 3).reshape(n_ctx, all_tok, -1)
        v = lax.all_to_all(v, "ctx", split_axis=0, concat_axis=0, tiled=True)
        return v.transpose(1, 0, 2)

    mixed = to_tokens(mixed_h).reshape(all_tok, width)
    mixed_a = mm(mixed, order_a).astype(BF)
    middle = start + mm(mixed_a, out_rel)
    normed_two, norm_two_back = jax.vjp(rms_scale, middle, gain_mlp)
    hidden_two = normed_two.astype(BF)

    expert_ids = jnp.arange(experts, dtype=jnp.int32)

    def gates_of(rows_low, row_routes):
        logits = mm(rows_low, router)
        chosen = jnp.any(row_routes[:, :, None] == expert_ids, axis=1)
        logits = jnp.where(chosen, logits, -1e30)
        return jnp.where(chosen, jax.nn.softmax(logits, axis=-1), 0.0)

    gates_own = gates_of(hidden_two, route_rows)
    own_ids = shard * local + jnp.arange(local, dtype=jnp.int32)
    own_column = (expert_ids[:, None] == own_ids[None, :]).astype(F32)
    before = jnp.arange(tok, dtype=jnp.int32)
    lower = (before[:, None] >= before[None, :]).astype(BF)
    slot_ids = jnp.arange(cap, dtype=jnp.int32)

    moe_rows = []
    grad_two_rows = []
    grad_gate_rows = []
    expert_grads = None
    for m in range(micro):
        x_all = gather_all(hidden_two[m * tok : (m + 1) * tok][None], PATH_E)
        g_all = cot_all[:, m]
        r_all = routes_all[:, m]
        gates = gates_of(x_all.reshape(-1, width), r_all.reshape(-1, TOPK))
        gates = jnp.sum(gates[:, :, None] * own_column[None], axis=1).reshape(n_fsdp, tok, local)
        mask = jnp.any(r_all[..., None] == own_ids, axis=2)
        count = ein("ut,ste->sue", lower, mask.astype(BF)).astype(jnp.int32)
        slot = jnp.where(mask, count - 1, -1)
        pick = slot[..., None] == slot_ids
        pick_low = pick.astype(BF)
        gate_slots = jnp.sum(jnp.where(pick, gates[..., None], 0.0), axis=1)
        x_e = ein("stej,std->sejd", pick_low, x_all).astype(BF)
        g_e = ein("stej,std->sejd", pick_low, g_all).astype(BF)
        a = ein("sejd,edf->sejf", x_e, weight_gate)
        b = ein("sejd,edf->sejf", x_e, weight_up)
        sig = jax.nn.sigmoid(a)
        silu = a * sig
        active = (silu * b).astype(BF)
        expert_out = ein("sejf,edf->sejd", active, weight_down).astype(BF).astype(F32)
        g_wide = g_e.astype(F32)
        d_gate_slots = jnp.sum(expert_out * g_wide, axis=-1)
        d_gates = jnp.sum(jnp.where(pick, d_gate_slots[:, None], 0.0), axis=-1)
        d_expert = (gate_slots[..., None] * g_wide).astype(BF)
        moe_part = ein(
            "stej,sejd->std", pick_low, (gate_slots[..., None] * expert_out).astype(BF)
        ).astype(BF)
        d_active = ein("sejd,edf->sejf", d_expert, weight_down)
        da = (d_active * b * (sig * (1.0 + a * (1.0 - sig)))).astype(BF)
        db = (d_active * silu).astype(BF)
        grads = (
            ein("sejd,sejf->edf", x_e, da),
            ein("sejd,sejf->edf", x_e, db),
            ein("sejd,sejf->edf", d_expert, active),
        )
        expert_grads = (
            grads if expert_grads is None else jax.tree.map(jnp.add, expert_grads, grads)
        )
        d_route = ein("sejf,edf->sejd", da, weight_gate) + ein("sejf,edf->sejd", db, weight_up)
        d_two_part = ein("stej,sejd->std", pick_low, d_route.astype(BF)).astype(BF)
        d_gates_wide = jnp.sum(d_gates[:, :, None, :] * own_column, axis=-1)
        gate_pack = jnp.stack(split(d_gates_wide), axis=1).reshape(n_fsdp, -1, width)
        back = scatter_all(jnp.concatenate([d_two_part, gate_pack], axis=1), PATH_E)[0]
        grad_two_rows.append(back[:tok].astype(F32))
        gate_back = back[tok:].astype(F32).reshape(2, tok, experts)
        grad_gate_rows.append(gate_back[0] + gate_back[1])
        moe_rows.append(scatter_all(moe_part, PATH_E)[0])

    out = (middle + jnp.concatenate(moe_rows, axis=0).astype(F32)).astype(BF)
    grad_top = cot.astype(F32)
    d_gates = jnp.concatenate(grad_gate_rows, axis=0)
    d_select = gates_own * (d_gates - jnp.sum(gates_own * d_gates, axis=-1, keepdims=True))
    d_logits = d_select.astype(BF)
    grad_router = t_mm(hidden_two, d_logits)
    d_hidden_two = jnp.concatenate(grad_two_rows, axis=0) + mm_t(d_logits, router)
    d_middle, grad_mlp = norm_two_back(d_hidden_two)
    d_middle = d_middle + grad_top
    d_branch = d_middle.astype(BF)
    grad_out_rel = t_mm(mixed_a, d_branch)
    d_mixed = mm_t(mm_t(d_branch, out_rel).astype(BF), order_a).astype(BF)

    d_mixed = d_mixed.reshape(all_tok, KV, ratio * DH).transpose(1, 0, 2)
    d_mixed_h = lax.all_to_all(d_mixed, "ctx", split_axis=0, concat_axis=0, tiled=True)
    d_mixed_h = (
        d_mixed_h.reshape(n_ctx, micro, tok, -1)
        .transpose(1, 0, 2, 3)
        .reshape(micro, length, ratio, DH)
    )
    probs = jnp.exp(scores_of() - log_total)
    probs_again = probs.astype(BF)
    d_probs = ein("mqrd,mkd->mrqk", d_mixed_h, v_h)
    d_scores = (probs * (d_probs - jnp.sum(probs * d_probs, axis=-1, keepdims=True))).astype(BF)
    d_q = ein("mrqk,mkd->mqrd", d_scores, k_h) * scale
    d_k = ein("mrqk,mqrd->mkd", d_scores, q_h) * scale
    d_v = ein("mrqk,mqrd->mkd", probs_again, d_mixed_h)
    d_qkv = jnp.concatenate(
        [
            d_q.astype(BF).reshape(micro, length, ratio * DH),
            d_k.astype(BF),
            d_v.astype(BF),
        ],
        axis=2,
    )
    d_qkv = to_tokens(d_qkv)
    d_query_rot = d_qkv[:, :, : ratio * DH].reshape(all_tok, H, DH).astype(F32)
    d_key_rot = d_qkv[:, :, ratio * DH : (ratio + 1) * DH].astype(F32)
    d_value = d_qkv[:, :, (ratio + 1) * DH :].reshape(all_tok, KV * DH)
    d_query_raw, d_query_gain = query_back(d_query_rot)
    d_key_raw, d_key_gain = key_back(d_key_rot)
    dq = d_query_raw.reshape(all_tok, H * DH).astype(BF)
    dkv = jnp.concatenate([d_key_raw.reshape(all_tok, KV * DH).astype(BF), d_value], axis=1)
    grad_query_rel = t_mm(hidden_a, dq)
    grad_kv_rel = t_mm(hidden_b, dkv)
    d_hidden = 0.0
    for part, order in ((mm_t(dq, query_rel), order_a), (mm_t(dkv, rel_b), order_b)):
        for piece in split(part):
            d_hidden = d_hidden + mm_t(piece, order)
    d_start, grad_attn = norm_one_back(d_hidden)
    d_tokens = d_middle + d_start

    grad_heads = jnp.pad(
        jnp.concatenate([d_query_gain, d_key_gain])[:, None], ((0, 0), (0, rows - 1))
    ).reshape(-1)
    grad_small = jnp.concatenate(
        [grad_router, grad_attn[:, None], grad_mlp[:, None], grad_heads[:, None]], axis=1
    )
    grad_small = jnp.pad(grad_small, ((0, 0), (0, 128 - grad_small.shape[1]))).astype(BF)
    grad_small_rel = t_mm(order_a, grad_small)
    own_a = scatter_all(
        jnp.concatenate([grad_small_rel, grad_query_rel], axis=1).astype(BF), PATH_A
    ).astype(F32)
    own_b = scatter_all(grad_kv_rel.astype(BF), PATH_B).astype(F32)
    own_out = scatter_all(grad_out_rel.astype(BF), PATH_A).astype(F32)
    expert_own = tuple(
        lax.psum_scatter(g.astype(BF), "ctx", scatter_dimension=1, tiled=True).astype(F32)
        for g in expert_grads
    )
    return (
        out.reshape(micro, 1, tok, width),
        d_tokens.reshape(micro, 1, tok, width),
        own_a[:, 128:],
        own_b[:, : KV * DH],
        own_b[:, KV * DH :],
        own_out,
        own_a[:, :experts],
        own_a[:, experts],
        own_a[:, experts + 1],
        own_a[:1, experts + 2],
    ) + expert_own


def solution(mesh):
    weight = P(("ctx", "fsdp"), None)
    gain = P(("ctx", "fsdp"))
    rows = P(None, "fsdp", "ctx", None)
    expert = P("fsdp", "ctx", None)
    return jax.shard_map(
        body,
        mesh=mesh,
        in_specs=(rows, P(None, "fsdp", None), rows)
        + (weight,) * 5
        + (gain,) * 3
        + (expert,) * 3
        + (rows,),
        out_specs=(rows, rows) + (weight,) * 5 + (gain,) * 3 + (expert,) * 3,
        check_vma=False,
    )
```

```python
import jax
import jax.numpy as jnp
from jax import lax
from jax.experimental import pallas as pl
from jax.experimental.pallas import tpu as pltpu
from jax.sharding import PartitionSpec as P

BF = jnp.bfloat16
F32 = jnp.float32


H = 16
KV = 8
DH = 64
TOPK = 8
WINDOW = 1024
EPS = 1e-06
THETA = 10000.0
PATH_E = ("yh", "x", "core")
ALL = ("ctx", "fsdp")


def ctx_perm(dz, dyl):
    return [(z * 2 + y, ((z + dz) % 4) * 2 + (y + dyl) % 2) for z in range(4) for y in range(2)]


def fsdp_perm(dyh, dx, dcore):
    return [
        ((y * 4 + x) * 2 + c, (((y + dyh) % 2) * 4 + (x + dx) % 4) * 2 + (c + dcore) % 2)
        for y in range(2)
        for x in range(4)
        for c in range(2)
    ]


RING = {
    "z": ("ctx", ctx_perm(1, 0), ctx_perm(-1, 0)),
    "x": ("fsdp", fsdp_perm(0, 1, 0), fsdp_perm(0, -1, 0)),
}
PAIR = {
    "yl": ("ctx", ctx_perm(0, 1)),
    "yh": ("fsdp", fsdp_perm(1, 0, 0)),
    "core": ("fsdp", fsdp_perm(0, 0, 1)),
}


def gather_stage(block, name):
    if name in PAIR:
        axis, swap = PAIR[name]
        return jnp.concatenate([block, lax.ppermute(block, axis, swap)], axis=0)
    axis, up, down = RING[name]
    half = block.shape[0] // 2
    before = lax.ppermute(block, axis, up)
    after = lax.ppermute(block, axis, down)
    far_low = lax.ppermute(before[:half], axis, up)
    far_high = lax.ppermute(after[half:], axis, down)
    return jnp.concatenate([block, after, far_low, far_high, before], axis=0)


def gather_all(block, names):
    for name in names:
        block = gather_stage(block, name)
    return block


def add(a, b):
    return (a.astype(F32) + b.astype(F32)).astype(BF)


def scatter_stage(parts, name):
    if name in PAIR:
        axis, swap = PAIR[name]
        half = parts.shape[0] // 2
        return add(parts[:half], lax.ppermute(parts[half:], axis, swap))
    axis, up, down = RING[name]
    size = parts.shape[0] // 4
    half = size // 2
    own, after, far, before = (parts[k * size : (k + 1) * size] for k in range(4))
    low = lax.ppermute(far[:half], axis, up)
    high = lax.ppermute(far[half:], axis, down)
    after = jnp.concatenate([add(after[:half], low), after[half:]], axis=0)
    before = jnp.concatenate([before[:half], add(before[half:], high)], axis=0)
    from_before = lax.ppermute(after, axis, up)
    from_after = lax.ppermute(before, axis, down)
    return (own.astype(F32) + from_before.astype(F32) + from_after.astype(F32)).astype(BF)


def scatter_all(parts, names):
    for name in reversed(names):
        parts = scatter_stage(parts, name)
    return parts


SIZES = {"z": 4, "x": 4, "yl": 2, "yh": 2, "core": 2}


def coordinates():
    c = lax.axis_index("ctx")
    f = lax.axis_index("fsdp")
    return {"z": c // 2, "yl": c % 2, "yh": f // 8, "x": (f // 2) % 4, "core": f % 2}


def rms_scale(values, gain):
    return values * lax.rsqrt(jnp.mean(values * values, axis=-1, keepdims=True) + EPS) * gain


def rope_tables(positions):
    half = DH // 2
    inverse = THETA ** (-(jnp.arange(half, dtype=F32) * 2.0) / DH)
    angles = positions.astype(F32)[:, None] * inverse[None, :]
    return (jnp.cos(angles), jnp.sin(angles))


def head_post(raw, gain, cosine, sine, heads):
    shaped = raw.reshape(raw.shape[:-1] + (heads, DH))
    normed = rms_scale(shaped, gain)
    half = DH // 2
    first_half = normed[..., :half]
    second_half = normed[..., half:]
    cos_grid = cosine[:, None, :]
    sin_grid = sine[:, None, :]
    return jnp.concatenate(
        [
            first_half * cos_grid - second_half * sin_grid,
            second_half * cos_grid + first_half * sin_grid,
        ],
        axis=-1,
    )


def dot(a, b, ca, cb):
    return lax.dot_general(a, b, (((ca,), (cb,)), ((), ())), preferred_element_type=F32)


def halves(v):
    high = v.astype(BF)
    return high, (v - high.astype(F32)).astype(BF)


def expert_kernel(
    scalar_ref,
    x_ref,
    g_ref,
    router_ref,
    gate_ref,
    up_ref,
    down_ref,
    out_ref,
    back_ref,
    xe_ref,
    de_ref,
    act_ref,
    da_ref,
    db_ref,
    pick_ref,
    weight_ref,
    dgate_ref,
    eo_ref,
    dr_ref,
):
    sources, tok, width = x_ref.shape
    local, slots, hidden = act_ref.shape
    cap = slots // sources
    first = scalar_ref[0]
    lane = lax.broadcasted_iota(jnp.int32, (tok, 128), 1)
    place = lax.broadcasted_iota(jnp.int32, (tok, local * cap), 1)
    row_expert = lax.broadcasted_iota(jnp.int32, (local * cap, 128), 0) // cap
    slot_lane = lax.broadcasted_iota(jnp.int32, (local * cap, 128), 1)
    own_lane = slot_lane == first + row_expert

    def fetch(s, carry):
        x = x_ref[s]
        held = g_ref[s, :, width:].astype(F32)
        chosen = held >= 0.0
        logits = jnp.where(chosen, dot(x, router_ref[...], 1, 0), -1e30)
        top = jnp.max(logits, axis=1, keepdims=True)
        raised = jnp.where(chosen, jnp.exp(logits - top), 0.0)
        gates = raised / jnp.sum(raised, axis=1, keepdims=True)
        pick = jnp.zeros((tok, local * cap), F32)
        for e in range(local):
            mine = jnp.max(jnp.where(lane == first + e, held, -1.0), axis=1, keepdims=True)
            goal = jnp.where(mine >= 0.0, mine + e * cap, -1.0).astype(jnp.int32)
            pick = jnp.where(place == goal, 1.0, pick)
        pick = pick.astype(BF)
        pick_ref[s] = pick
        rows = pl.ds(pl.multiple_of(s * cap, 16), cap)
        x_slots = dot(pick, x, 0, 0).astype(BF)
        g_slots = dot(pick, g_ref[s, :, :width], 0, 0).astype(BF)
        high, low = halves(gates)
        weight = dot(pick, high, 0, 0) + dot(pick, low, 0, 0)
        weight = jnp.sum(jnp.where(own_lane, weight, 0.0), axis=1, keepdims=True)
        for e in range(local):
            part = slice(e * cap, (e + 1) * cap)
            xe_ref[e, rows] = x_slots[part]
            de_ref[e, rows] = g_slots[part]
            weight_ref[e, rows] = weight[part]
        return carry

    lax.fori_loop(0, sources, fetch, 0)
    chunk = 256

    def work(i, carry):
        e = i // (slots // chunk)
        rows = pl.ds(pl.multiple_of((i % (slots // chunk)) * chunk, chunk), chunk)
        w_gate = gate_ref[:, e].reshape(width, hidden)
        w_up = up_ref[:, e].reshape(width, hidden)
        w_down = down_ref[:, e].reshape(width, hidden)
        x = xe_ref[e, rows]
        a = dot(x, w_gate, 1, 0)
        b = dot(x, w_up, 1, 0)
        sig = 1.0 / (1.0 + jnp.exp(-a))
        silu = a * sig
        active = (silu * b).astype(BF)
        act_ref[e, rows] = active
        slope = b * (sig * (1.0 + a * (1.0 - sig)))
        weight = weight_ref[e, rows]
        g = de_ref[e, rows].astype(F32)
        result = dot(active, w_down, 1, 1).astype(BF).astype(F32)
        dgate_ref[e, rows] = jnp.sum(result * g, axis=1, keepdims=True)
        eo_ref[e, rows] = (weight * result).astype(BF)
        d_expert = (weight * g).astype(BF)
        de_ref[e, rows] = d_expert
        d_active = dot(d_expert, w_down, 1, 0)
        da = (d_active * slope).astype(BF)
        db = (d_active * silu).astype(BF)
        da_ref[e, rows] = da
        db_ref[e, rows] = db
        dr_ref[e, rows] = (dot(da, w_gate, 1, 1) + dot(db, w_up, 1, 1)).astype(BF)
        return carry

    lax.fori_loop(0, local * (slots // chunk), work, 0)

    def give(s, carry):
        rows = pl.ds(pl.multiple_of(s * cap, 16), cap)
        pick = pick_ref[s]
        eo = jnp.concatenate([eo_ref[e, rows] for e in range(local)], axis=0)
        dr = jnp.concatenate([dr_ref[e, rows] for e in range(local)], axis=0)
        dgate = jnp.concatenate([dgate_ref[e, rows] for e in range(local)], axis=0)
        high, low = halves(dgate)
        spread = jnp.where(own_lane, high.astype(F32), 0.0) + jnp.where(
            slot_lane == first + row_expert + 64, low.astype(F32), 0.0
        )
        out_ref[scalar_ref[s + 1]] = dot(pick, eo, 1, 0).astype(BF)
        back_ref[s, :, :width] = dot(pick, dr, 1, 0).astype(BF)
        back_ref[s, :, width:] = dot(pick, spread.astype(BF), 1, 0).astype(BF)
        return carry

    lax.fori_loop(0, sources, give, 0)


def run_experts(scalars, x_all, g_all, micro, router, w_gate, w_up, w_down, cap):
    sources, tok, width = x_all.shape
    local, hidden = w_gate.shape[1], w_gate.shape[3]
    slots = sources * cap
    wide = g_all.shape[2]
    shape = jax.ShapeDtypeStruct
    outs = [
        shape((sources, tok, width), BF),
        shape((sources, tok, wide), BF),
        shape((local, slots, width), BF),
        shape((local, slots, width), BF),
        shape((local, slots, hidden), BF),
        shape((local, slots, hidden), BF),
        shape((local, slots, hidden), BF),
    ]
    one = lambda s: pl.BlockSpec(s.shape, lambda i: (0,) * len(s.shape), pipeline_mode=pl.Buffered(1))
    flops = 2 * local * slots * width * hidden * 6
    return pl.pallas_call(
        expert_kernel,
        out_shape=outs,
        grid=(1,),
        in_specs=[
            pl.BlockSpec(memory_space=pltpu.SMEM),
            one(x_all),
            pl.BlockSpec((sources, tok, wide), lambda i: (0, micro, 0), pipeline_mode=pl.Buffered(1)),
            one(router),
            one(w_gate),
            one(w_up),
            one(w_down),
        ],
        out_specs=[one(o) for o in outs],
        scratch_shapes=[
            pltpu.VMEM((sources, tok, local * cap), BF),
            pltpu.VMEM((local, slots, 1), F32),
            pltpu.VMEM((local, slots, 1), F32),
            pltpu.VMEM((local, slots, width), BF),
            pltpu.VMEM((local, slots, width), BF),
        ],
        compiler_params=pltpu.CompilerParams(vmem_limit_bytes=56 * 1024 * 1024),
        cost_estimate=pl.CostEstimate(flops=flops, bytes_accessed=40 << 20, transcendentals=0),
    )(scalars, x_all, g_all, router, w_gate, w_up, w_down)


def mm(a, b):
    return jnp.dot(a, b, preferred_element_type=F32)


def mm_t(a, b):
    return lax.dot_general(a, b, (((1,), (1,)), ((), ())), preferred_element_type=F32)


def t_mm(a, b):
    return lax.dot_general(a, b, (((0,), (0,)), ((), ())), preferred_element_type=F32)


def ein(spec, a, b):
    return jnp.einsum(spec, a, b, preferred_element_type=F32)


def spread(block, axis, copies):
    wide = jnp.broadcast_to(block[None], (copies,) + block.shape)
    return lax.all_to_all(wide, axis, split_axis=0, concat_axis=0, tiled=True)


def swap(parts, axis):
    return lax.all_to_all(parts, axis, split_axis=0, concat_axis=0, tiled=True)


def body(
    tokens,
    segments,
    routes,
    w_query,
    w_key,
    w_value,
    w_out,
    w_router,
    attn_gain,
    mlp_gain,
    qk_gain,
    w_gate,
    w_up,
    w_down,
    cotangent,
):
    micro = tokens.shape[0]
    tok = tokens.shape[2]
    width = tokens.shape[3]
    length = segments.shape[2]
    rows = w_query.shape[0]
    n_ctx = lax.axis_size("ctx")
    n_fsdp = lax.axis_size("fsdp")
    n_all = n_ctx * n_fsdp
    shard = lax.axis_index("fsdp")
    local = w_gate.shape[0]
    experts = local * n_fsdp
    cap = (3 * tok * TOPK + 2 * experts - 1) // (2 * experts)
    all_tok = micro * tok
    scale = DH ** (-0.5)
    ratio = H // KV
    heads = ratio * DH

    small = jnp.concatenate(
        [
            w_router,
            attn_gain[:, None],
            mlp_gain[:, None],
            jnp.pad(qk_gain[:, None], ((0, rows - 1), (0, 0))),
        ],
        axis=1,
    )
    small = jnp.pad(small, ((0, 0), (0, 128 - small.shape[1])))
    pieces = jnp.concatenate(
        [
            w_query.reshape(rows, n_ctx, heads),
            w_key.reshape(rows, n_ctx, DH),
            w_value.reshape(rows, n_ctx, DH),
            jnp.broadcast_to(small[:, None], (rows, n_ctx, 128)),
        ],
        axis=2,
    ).transpose(1, 0, 2)
    pieces = jnp.broadcast_to(pieces[:, None], (n_ctx, n_fsdp) + pieces.shape[1:])
    head_all = swap(pieces.reshape((n_all,) + pieces.shape[2:]), ALL).reshape(width, -1)
    w_heads = head_all[:, : heads + 2 * DH]
    small_all = head_all[:, heads + 2 * DH :]
    router = small_all[:, :experts]
    small_wide = small_all.astype(F32)
    gain_attn = small_wide[:, experts]
    gain_mlp = small_wide[:, experts + 1]
    gain_heads = small_wide[:, experts + 2].reshape(-1, rows)[:, 0]

    seq_rows = [
        spread(tokens[m, 0], "ctx", n_ctx).reshape(length, width) for m in range(micro)
    ]
    out_full = spread(w_out, ALL, n_all).reshape(width, width)

    weight_gate = lax.all_gather(w_gate, "ctx", axis=0)
    weight_up = lax.all_gather(w_up, "ctx", axis=0)
    weight_down = lax.all_gather(w_down, "ctx", axis=0)

    expert_ids = jnp.arange(experts, dtype=jnp.int32)
    cot = cotangent.reshape(all_tok, width)
    chosen = jnp.any(routes.reshape(all_tok, TOPK)[:, :, None] == expert_ids, axis=1)
    before = jnp.arange(tok, dtype=jnp.int32)
    lower = (before[:, None] >= before[None, :]).astype(BF)
    counts = ein("ut,mte->mue", lower, chosen.reshape(micro, tok, experts).astype(BF))
    held = jnp.where(chosen, counts.reshape(all_tok, experts) - 1.0, -1.0)
    held = jnp.pad(held, ((0, 0), (0, 128 - experts)), constant_values=-1.0).astype(BF)
    pack_all = gather_all(jnp.concatenate([cot, held], axis=1)[None], PATH_E)

    positions = jnp.arange(length, dtype=jnp.int32)
    cosine, sine = rope_tables(positions)
    near = jnp.abs(positions[:, None] - positions[None, :]) < WINDOW // 2

    def attend(m):
        normed, back = jax.vjp(rms_scale, seq_rows[m].astype(F32), gain_attn)
        hidden = normed.astype(BF)
        raw = mm(hidden, w_heads)
        query_rot, query_back = jax.vjp(
            lambda r, g: head_post(r, g, cosine, sine, ratio), raw[:, :heads], gain_heads[:DH]
        )
        key_rot, key_back = jax.vjp(
            lambda r, g: head_post(r, g, cosine, sine, 1),
            raw[:, heads : heads + DH],
            gain_heads[DH:],
        )
        q = query_rot.astype(BF)
        k = key_rot.astype(BF)[:, 0]
        v = raw[:, heads + DH :].astype(BF)
        seg = segments[m, 0]
        allowed = (seg[:, None] == seg[None, :]) & near

        def scores_of():
            return jnp.where(allowed[None], ein("qrd,kd->rqk", q, k) * scale, -1e30)

        scores = scores_of()
        highest = jnp.max(scores, axis=-1, keepdims=True)
        shifted = jnp.exp(scores - highest)
        total = jnp.sum(shifted, axis=-1, keepdims=True)
        log_total = highest + jnp.log(total)
        probs_low = (shifted / total).astype(BF)
        mixed = ein("rqk,kd->qrd", probs_low, v).astype(BF).reshape(length, heads)

        def backward(d_mixed):
            d_mixed = d_mixed.reshape(length, ratio, DH)
            probs = jnp.exp(scores_of() - log_total)
            d_probs = ein("qrd,kd->rqk", d_mixed, v)
            d_scores = (
                probs * (d_probs - jnp.sum(probs * d_probs, axis=-1, keepdims=True))
            ).astype(BF)
            d_q = ein("rqk,kd->qrd", d_scores, k) * scale
            d_k = ein("rqk,qrd->kd", d_scores, q) * scale
            d_v = ein("rqk,qrd->kd", probs.astype(BF), d_mixed)
            d_q_raw, d_q_gain = query_back(d_q)
            d_k_raw, d_k_gain = key_back(d_k[:, None])
            d_raw = jnp.concatenate([d_q_raw, d_k_raw, d_v], axis=1).astype(BF)
            grad_heads = t_mm(hidden, d_raw)
            d_hidden = mm_t(d_raw, w_heads)
            wide = seq_rows[m].astype(F32)
            inverse = lax.rsqrt(jnp.mean(wide * wide, axis=-1, keepdims=True) + EPS)
            grad_gain = jnp.sum(d_hidden * wide * inverse, axis=0)
            return (
                d_hidden.astype(BF),
                grad_heads,
                grad_gain,
                jnp.concatenate([d_q_gain, d_k_gain]),
            )

        return mixed, backward

    def to_owner(v):
        return swap(v.reshape(n_ctx, tok, -1), "ctx")

    router_pad = jnp.pad(router, ((0, 0), (0, 128 - experts)))
    first = jnp.full((1,), shard * local, jnp.int32)
    here = coordinates()
    rel = jnp.arange(n_fsdp, dtype=jnp.int32)
    digits = {}
    rest = rel
    for name in PATH_E:
        digits[name] = (rest % SIZES[name] + here[name]) % SIZES[name]
        rest = rest // SIZES[name]
    whole = (digits["yh"] * 4 + digits["x"]) * 2 + digits["core"]
    scalars = jnp.concatenate([first, whole])

    outs, d_inputs = [], []
    backs, kept, grads = [], [], []
    forward = []
    for m in range(micro):
        mixed_h, backward = attend(m)
        backs.append(backward)
        mixed = to_owner(mixed_h).transpose(1, 0, 2).reshape(tok, width)
        start = tokens[m, 0].astype(F32)
        middle = start + mm(mixed, out_full)
        normed, norm_back = jax.vjp(rms_scale, middle, gain_mlp)
        hidden_two = normed.astype(BF)
        chosen_m = chosen[m * tok : (m + 1) * tok]
        logits = jnp.where(chosen_m, mm(hidden_two, router), -1e30)
        gates = jnp.where(chosen_m, jax.nn.softmax(logits, axis=-1), 0.0)
        x_all = gather_all(hidden_two[None], PATH_E)
        forward.append((mixed, middle, norm_back, hidden_two, gates, x_all))
    expert_parts = []
    for m in range(micro):
        mixed, middle, norm_back, hidden_two, gates, x_all = forward[m]
        moe_part, back_part, *saved = run_experts(
            scalars, x_all, pack_all, m, router_pad, weight_gate, weight_up, weight_down, cap
        )
        kept.append(saved)
        back = scatter_all(back_part, PATH_E)[0]
        moe = lax.psum_scatter(moe_part, "fsdp", scatter_dimension=0, tiled=True)[0]
        outs.append((middle + moe.astype(F32)).astype(BF))
        grad_top = cot[m * tok : (m + 1) * tok].astype(F32)
        tail = back[:, width:].astype(F32)
        d_gates = tail[:, :experts] + tail[:, 64 : 64 + experts]
        d_select = gates * (d_gates - jnp.sum(gates * d_gates, axis=-1, keepdims=True))
        d_logits = d_select.astype(BF)
        grad_router = t_mm(hidden_two, d_logits)
        d_two = back[:, :width].astype(F32) + mm_t(d_logits, router)
        d_middle, grad_mlp = norm_back(d_two)
        d_middle = d_middle + grad_top
        d_branch = d_middle.astype(BF)
        grad_out = t_mm(mixed, d_branch)
        d_mixed = mm_t(d_branch, out_full).astype(BF)
        d_mixed = d_mixed.reshape(tok, n_ctx, heads).transpose(1, 0, 2)
        d_mixed = swap(d_mixed, "ctx").reshape(length, heads)
        d_hidden, grad_heads, grad_attn, grad_qk = backs[m](d_mixed)
        d_hidden = jnp.sum(to_owner(d_hidden).astype(F32), axis=0)
        start = tokens[m, 0].astype(F32)
        inverse = lax.rsqrt(jnp.mean(start * start, axis=-1, keepdims=True) + EPS)
        u = d_hidden * gain_attn
        d_inputs.append(
            d_middle
            + inverse * u
            - start * (inverse**3 * jnp.mean(u * start, axis=-1, keepdims=True))
        )
        grads.append((grad_out, grad_heads, grad_router, grad_attn, grad_mlp, grad_qk))
    grad_out, grad_heads, grad_router, grad_attn, grad_mlp, grad_qk = jax.tree.map(
        jnp.add, grads[0], grads[1]
    )

    grad_out = swap(grad_out.astype(BF).reshape(n_all, rows, width), ALL)
    own_out = jnp.sum(grad_out.astype(F32), axis=0)
    grad_qk = jnp.pad(grad_qk[:, None], ((0, 0), (0, rows - 1))).reshape(-1)
    grad_small = jnp.concatenate(
        [grad_router, grad_attn[:, None], grad_mlp[:, None], grad_qk[:, None]], axis=1
    )
    grad_small = jnp.pad(grad_small, ((0, 0), (0, 128 - grad_small.shape[1])))
    grad_pack = jnp.concatenate([grad_heads, grad_small], axis=1).astype(BF)
    grad_pack = swap(grad_pack.reshape(n_all, rows, -1), ALL).astype(F32)
    own_heads = jnp.sum(grad_pack[:, :, : heads + 2 * DH].reshape(n_ctx, n_fsdp, rows, -1), axis=1)
    own_heads = own_heads.transpose(1, 0, 2)
    own_small = jnp.sum(grad_pack[:, :, heads + 2 * DH :], axis=0)

    def expert_grad(left, right):
        total = None
        for m in range(micro):
            part = ein("ejd,ejf->edf", kept[m][left], kept[m][right])
            total = part if total is None else total + part
        parts = total.astype(BF).reshape(local, n_ctx, -1, total.shape[2]).transpose(1, 0, 2, 3)
        return jnp.sum(swap(parts, "ctx").astype(F32), axis=0)

    return (
        jnp.stack(outs)[:, None],
        jnp.stack(d_inputs)[:, None],
        own_heads[:, :, :heads].reshape(rows, -1),
        own_heads[:, :, heads : heads + DH].reshape(rows, -1),
        own_heads[:, :, heads + DH :].reshape(rows, -1),
        own_out,
        own_small[:, :experts],
        own_small[:, experts],
        own_small[:, experts + 1],
        own_small[:1, experts + 2],
        expert_grad(0, 3),
        expert_grad(0, 4),
        expert_grad(1, 2),
    )


def solution(mesh):
    weight = P(("ctx", "fsdp"), None)
    gain = P(("ctx", "fsdp"))
    rows = P(None, "fsdp", "ctx", None)
    expert = P("fsdp", "ctx", None)
    return jax.shard_map(
        body,
        mesh=mesh,
        in_specs=(rows, P(None, "fsdp", None), rows)
        + (weight,) * 5
        + (gain,) * 3
        + (expert,) * 3
        + (rows,),
        out_specs=(rows, rows) + (weight,) * 5 + (gain,) * 3 + (expert,) * 3,
        check_vma=False,
    )
```

```python
import functools

import jax
import jax.numpy as jnp
from jax import lax
from jax.experimental import pallas as pl
from jax.experimental.pallas import tpu as pltpu
from jax.sharding import Mesh
from jax.sharding import PartitionSpec as P

BF = jnp.bfloat16
F32 = jnp.float32
H = 16
KV = 8
DH = 64
TOPK = 8
WINDOW = 1024
EPS = 1e-06
THETA = 10000.0


def dot(a, b, ca, cb):
    return lax.dot_general(a, b, (((ca,), (cb,)), ((), ())), preferred_element_type=F32)


def lanes_of(v):
    return lax.broadcasted_iota(jnp.int32, v.shape, v.ndim - 1)


def head_sums(v):
    low = lanes_of(v) < DH
    first = jnp.sum(jnp.where(low, v, 0.0), axis=1, keepdims=True)
    second = jnp.sum(jnp.where(low, 0.0, v), axis=1, keepdims=True)
    return jnp.where(low, first, second)


def trade(v):
    return jnp.where(
        lanes_of(v) % DH < DH // 2, pltpu.roll(v, 128 - DH // 2, 1), pltpu.roll(v, DH // 2, 1)
    )


def both_halves(v, second):
    low = lanes_of(v) < DH
    other = pltpu.roll(v, DH, 1)
    return jnp.where(low, other, v) if second else jnp.where(low, v, other)


def stack_heads(v):
    low = lanes_of(v) < DH
    zero = jnp.zeros_like(v)
    return jnp.concatenate([jnp.where(low, v, zero), jnp.where(low, zero, v)], axis=0)


def key_span(start, block, length):
    reach = WINDOW // 2 - 1
    low = max(0, start - reach) // 128 * 128
    high = min(length, -(-(start + block + reach) // 128) * 128)
    return low, high


def masked_probs(q_two, keys, seg_col, seg_row, start, low):
    block = q_two.shape[0] // 2
    scores = dot(q_two, keys, 1, 1)
    shape = (block, keys.shape[0])
    gap = (
        lax.broadcasted_iota(jnp.int32, shape, 0)
        - lax.broadcasted_iota(jnp.int32, shape, 1)
        + (start - low)
    )
    allowed = (seg_col == seg_row) & (jnp.abs(gap) < WINDOW // 2)
    bias = jnp.where(allowed, 0.0, -1e30)
    scores = scores + jnp.concatenate([bias, bias], axis=0)
    raised = jnp.exp(scores - jnp.max(scores, axis=1, keepdims=True))
    return raised * (1.0 / jnp.sum(raised, axis=1, keepdims=True))


def attend_kernel(
    order_ref,
    own_ref,
    after_ref,
    far_low_ref,
    far_high_ref,
    before_ref,
    gain_ref,
    w_ref,
    head_gain_ref,
    cos_ref,
    sin_ref,
    seg_col_ref,
    seg_row_ref,
    mixed_ref,
    hidden_ref,
    q_ref,
    kv_ref,
    keys_ref,
    values_ref,
):
    tok, width = own_ref.shape[1:]
    length = hidden_ref.shape[0]
    pieces = [
        (own_ref, 0),
        (own_ref, 1),
        (after_ref, 0),
        (after_ref, 1),
        (far_low_ref, 0),
        (far_high_ref, 0),
        (before_ref, 0),
        (before_ref, 1),
    ]
    for r, (ref, i) in enumerate(pieces):
        x = ref[i].astype(F32)
        x = x * lax.rsqrt(jnp.mean(x * x, axis=1, keepdims=True) + EPS) * gain_ref[...]
        rows = pl.ds(pl.multiple_of(order_ref[r] * tok, tok), tok)
        hidden_ref[rows] = x.astype(BF)
    raw = dot(hidden_ref[...], w_ref[...], 1, 0)
    for half in range(2):
        u = raw[:, half * 128 : half * 128 + 128]
        gain = head_gain_ref[:, half * 128 : half * 128 + 128]
        n = u * lax.rsqrt(head_sums(u * u) * (1.0 / DH) + EPS) * gain
        turned = n * cos_ref[...] + trade(n) * sin_ref[...]
        if half == 0:
            q_ref[...] = turned.astype(BF)
        else:
            kv = jnp.where(lanes_of(u) < DH, turned, u)
            kv_ref[...] = kv.astype(BF)
            keys_ref[...] = both_halves(kv, False).astype(BF)
            values_ref[...] = both_halves(kv, True).astype(BF)
    block = 256
    for start in range(0, length, block):
        low, high = key_span(start, block, length)
        q_two = stack_heads(q_ref[start : start + block].astype(F32) * DH**-0.5).astype(BF)
        probs = masked_probs(
            q_two,
            keys_ref[low:high],
            seg_col_ref[start : start + block],
            seg_row_ref[:, low:high],
            start,
            low,
        )
        result = dot(probs.astype(BF), values_ref[low:high], 1, 0)
        first = lanes_of(result[:block]) < DH
        mixed_ref[start : start + block] = jnp.where(first, result[:block], result[block:]).astype(
            BF
        )


def attend_back_kernel(
    hidden_ref,
    q_ref,
    kv_ref,
    d_mixed_ref,
    gain_ref,
    w_ref,
    head_gain_ref,
    cos_ref,
    sin_ref,
    seg_col_ref,
    seg_row_ref,
    d_hidden_ref,
    grad_w_ref,
    grad_gain_ref,
    grad_heads_ref,
    keys_ref,
    values_ref,
    d_q_ref,
    d_k_ref,
    d_v_ref,
    d_raw_ref,
):
    length = hidden_ref.shape[0]
    kv = kv_ref[...].astype(F32)
    keys_ref[...] = both_halves(kv, False).astype(BF)
    values_ref[...] = both_halves(kv, True).astype(BF)
    d_k_ref[...] = jnp.zeros_like(d_k_ref)
    d_v_ref[...] = jnp.zeros_like(d_v_ref)
    block = 256
    for start in range(0, length, block):
        low, high = key_span(start, block, length)
        q_two = stack_heads(q_ref[start : start + block].astype(F32) * DH**-0.5).astype(BF)
        m_two = stack_heads(d_mixed_ref[start : start + block].astype(F32)).astype(BF)
        probs = masked_probs(
            q_two,
            keys_ref[low:high],
            seg_col_ref[start : start + block],
            seg_row_ref[:, low:high],
            start,
            low,
        )
        d_probs = dot(m_two, values_ref[low:high], 1, 1)
        inner = jnp.sum(probs * d_probs, axis=1, keepdims=True)
        d_scores = (probs * (d_probs - inner)).astype(BF)
        result = dot(d_scores, keys_ref[low:high], 1, 0)
        first = lanes_of(result[:block]) < DH
        d_q_ref[start : start + block] = jnp.where(first, result[:block], result[block:]) * (
            DH**-0.5
        )
        d_k_ref[low:high] += dot(d_scores, q_two, 0, 0)
        d_v_ref[low:high] += dot(probs.astype(BF), m_two, 0, 0)
    raw = dot(hidden_ref[...], w_ref[...], 1, 0)
    d_k = d_k_ref[...]
    d_k = d_k + pltpu.roll(d_k, DH, 1)
    d_v = d_v_ref[...]
    d_v = d_v + pltpu.roll(d_v, DH, 1)
    for half in range(2):
        lanes = slice(half * 128, half * 128 + 128)
        u = raw[:, lanes]
        gain = head_gain_ref[:, lanes]
        d = d_q_ref[...] if half == 0 else d_k
        d = d * cos_ref[...] + trade(d * sin_ref[...])
        r = lax.rsqrt(head_sums(u * u) * (1.0 / DH) + EPS)
        grad_heads_ref[:, lanes] = jnp.sum(d * u * r, axis=0, keepdims=True)
        d = d * gain
        d = d * r - u * (r * r * r * (head_sums(d * u) * (1.0 / DH)))
        if half == 1:
            d = jnp.where(lanes_of(d) < DH, d, d_v)
        d_raw_ref[:, lanes] = d.astype(BF)
    grad_w_ref[...] = dot(hidden_ref[...], d_raw_ref[...], 0, 0)
    total = jnp.zeros(grad_gain_ref.shape, F32)
    for start in range(0, length, block):
        rows = slice(start, start + block)
        d_hidden = dot(d_raw_ref[rows], w_ref[...], 1, 1)
        d_hidden_ref[rows] = d_hidden.astype(BF)
        total = total + jnp.sum(d_hidden * hidden_ref[rows].astype(F32), axis=0, keepdims=True)
    grad_gain_ref[...] = total / gain_ref[...]


def whole(a):
    return pl.BlockSpec(a.shape, lambda i: (0,) * len(a.shape), pipeline_mode=pl.Buffered(1))


def attend_forward(order, pieces, gain, w_heads, head_gain, cosine, sine, seg_col, seg_row):
    length = cosine.shape[0]
    width = w_heads.shape[0]
    shape = jax.ShapeDtypeStruct
    outs = [
        shape((length, 128), BF),
        shape((length, width), BF),
        shape((length, 128), BF),
        shape((length, 128), BF),
    ]
    args = list(pieces) + [gain, w_heads, head_gain, cosine, sine, seg_col, seg_row]
    return pl.pallas_call(
        attend_kernel,
        out_shape=outs,
        grid=(1,),
        in_specs=[pl.BlockSpec(memory_space=pltpu.SMEM)] + [whole(a) for a in args],
        out_specs=[whole(o) for o in outs],
        scratch_shapes=[pltpu.VMEM((length, 128), BF), pltpu.VMEM((length, 128), BF)],
        compiler_params=pltpu.CompilerParams(vmem_limit_bytes=40 * 1024 * 1024),
        cost_estimate=pl.CostEstimate(flops=12 * 10**9, bytes_accessed=8 << 20, transcendentals=0),
    )(order, *args)


def attend_backward(
    hidden, q, kv, d_mixed, gain, w_heads, head_gain, cosine, sine, seg_col, seg_row
):
    length, width = hidden.shape
    shape = jax.ShapeDtypeStruct
    outs = [
        shape((length, width), BF),
        shape((width, 256), F32),
        shape((1, width), F32),
        shape((1, 256), F32),
    ]
    args = [hidden, q, kv, d_mixed, gain, w_heads, head_gain, cosine, sine, seg_col, seg_row]
    return pl.pallas_call(
        attend_back_kernel,
        out_shape=outs,
        grid=(1,),
        in_specs=[whole(a) for a in args],
        out_specs=[whole(o) for o in outs],
        scratch_shapes=[pltpu.VMEM((length, 128), BF)] * 2
        + [pltpu.VMEM((length, 128), F32)] * 3
        + [pltpu.VMEM((length, 256), BF)],
        compiler_params=pltpu.CompilerParams(vmem_limit_bytes=40 * 1024 * 1024),
        cost_estimate=pl.CostEstimate(flops=25 * 10**9, bytes_accessed=8 << 20, transcendentals=0),
    )(*args)


def halves(v):
    high = v.astype(BF)
    return high, (v - high.astype(F32)).astype(BF)


def expert_kernel(
    scalar_ref,
    x_own_ref,
    x_other_ref,
    g_own_ref,
    g_other_ref,
    router_ref,
    w_ref,
    out_ref,
    back_own_ref,
    back_other_ref,
    xe_ref,
    de_ref,
    act_ref,
    da_ref,
    db_ref,
    pick_ref,
    weight_ref,
    dgate_ref,
    eo_ref,
    dr_ref,
):
    half, tok, width = x_own_ref.shape
    sources = 2 * half
    core = scalar_ref[1]
    local, slots, hidden = act_ref.shape
    cap = slots // sources
    first = scalar_ref[0]
    lane = lax.broadcasted_iota(jnp.int32, (tok, 128), 1)
    place = lax.broadcasted_iota(jnp.int32, (tok, local * cap), 1)
    row_expert = lax.broadcasted_iota(jnp.int32, (local * cap, 128), 0) // cap
    slot_lane = lax.broadcasted_iota(jnp.int32, (local * cap, 128), 1)
    own_lane = slot_lane == first + row_expert

    def fetch(i, carry, x_ref, g_ref, offset):
        s = i + offset
        x = x_ref[i]
        from_g = scalar_ref[i + 2]
        held = g_ref[from_g, :, width:].astype(F32)
        chosen = held >= 0.0
        logits = jnp.where(chosen, dot(x, router_ref[...], 1, 0), -1e30)
        top = jnp.max(logits, axis=1, keepdims=True)
        raised = jnp.where(chosen, jnp.exp(logits - top), 0.0)
        gates = raised / jnp.sum(raised, axis=1, keepdims=True)
        pick = jnp.zeros((tok, local * cap), F32)
        for e in range(local):
            mine = jnp.max(jnp.where(lane == first + e, held, -1.0), axis=1, keepdims=True)
            goal = jnp.where(mine >= 0.0, mine + e * cap, -1.0).astype(jnp.int32)
            pick = jnp.where(place == goal, 1.0, pick)
        pick = pick.astype(BF)
        pick_ref[s] = pick
        rows = pl.ds(pl.multiple_of(s * cap, 16), cap)
        x_slots = dot(pick, x, 0, 0).astype(BF)
        g_slots = dot(pick, g_ref[from_g, :, :width], 0, 0).astype(BF)
        high, low = halves(gates)
        weight = dot(pick, high, 0, 0) + dot(pick, low, 0, 0)
        weight = jnp.sum(jnp.where(own_lane, weight, 0.0), axis=1, keepdims=True)
        for e in range(local):
            part = slice(e * cap, (e + 1) * cap)
            xe_ref[e, rows] = x_slots[part]
            de_ref[e, rows] = g_slots[part]
            weight_ref[e, rows] = weight[part]
        return carry

    for x_ref, g_ref, offset in ((x_own_ref, g_own_ref, 0), (x_other_ref, g_other_ref, half)):
        lax.fori_loop(
            0, half, functools.partial(fetch, x_ref=x_ref, g_ref=g_ref, offset=offset), 0
        )
    chunk = 256

    def work(i, carry):
        e = i // (slots // chunk)
        rows = pl.ds(pl.multiple_of((i % (slots // chunk)) * chunk, chunk), chunk)
        w_gate = w_ref[:, 0, e].reshape(width, hidden)
        w_up = w_ref[:, 1, e].reshape(width, hidden)
        w_down = w_ref[:, 2, e].reshape(width, hidden)
        x = xe_ref[e, rows]
        a = dot(x, w_gate, 1, 0)
        b = dot(x, w_up, 1, 0)
        sig = 1.0 / (1.0 + jnp.exp(-a))
        silu = a * sig
        active = (silu * b).astype(BF)
        act_ref[e, rows] = active
        slope = b * (sig * (1.0 + a * (1.0 - sig)))
        weight = weight_ref[e, rows]
        g = de_ref[e, rows].astype(F32)
        result = dot(active, w_down, 1, 1).astype(BF).astype(F32)
        dgate_ref[e, rows] = jnp.sum(result * g, axis=1, keepdims=True)
        eo_ref[e, rows] = (weight * result).astype(BF)
        d_expert = (weight * g).astype(BF)
        de_ref[e, rows] = d_expert
        d_active = dot(d_expert, w_down, 1, 0)
        da = (d_active * slope).astype(BF)
        db = (d_active * silu).astype(BF)
        da_ref[e, rows] = da
        db_ref[e, rows] = db
        dr_ref[e, rows] = (dot(da, w_gate, 1, 1) + dot(db, w_up, 1, 1)).astype(BF)
        return carry

    lax.fori_loop(0, local * (slots // chunk), work, 0)

    def give(i, carry, back_ref, offset, column):
        s = i + offset
        rows = pl.ds(pl.multiple_of(s * cap, 16), cap)
        pick = pick_ref[s]
        eo = jnp.concatenate([eo_ref[e, rows] for e in range(local)], axis=0)
        dr = jnp.concatenate([dr_ref[e, rows] for e in range(local)], axis=0)
        dgate = jnp.concatenate([dgate_ref[e, rows] for e in range(local)], axis=0)
        high, low = halves(dgate)
        spread = jnp.where(own_lane, high.astype(F32), 0.0) + jnp.where(
            slot_lane == first + row_expert + 64, low.astype(F32), 0.0
        )
        out_ref[2 * i + column] = dot(pick, eo, 1, 0).astype(BF)
        back_ref[i, :, :width] = dot(pick, dr, 1, 0).astype(BF)
        back_ref[i, :, width:] = dot(pick, spread.astype(BF), 1, 0).astype(BF)
        return carry

    for back_ref, offset, column in ((back_own_ref, 0, core), (back_other_ref, half, 1 - core)):
        lax.fori_loop(
            0, half, functools.partial(give, back_ref=back_ref, offset=offset, column=column), 0
        )


def run_experts(scalars, x_own, x_other, g_own, g_other, micro, router, weights, cap):
    half, tok, width = x_own.shape
    sources = 2 * half
    local, hidden = weights.shape[2], weights.shape[4]
    slots = sources * cap
    wide = g_own.shape[2]
    shape = jax.ShapeDtypeStruct
    outs = [
        shape((sources, tok, width), BF),
        shape((half, tok, wide), BF),
        shape((half, tok, wide), BF),
        shape((local, slots, width), BF),
        shape((local, slots, width), BF),
        shape((local, slots, hidden), BF),
        shape((local, slots, hidden), BF),
        shape((local, slots, hidden), BF),
    ]
    g_spec = pl.BlockSpec(
        (half, tok, wide), lambda i: (0, micro, 0), pipeline_mode=pl.Buffered(1)
    )
    args = [router, weights]
    return pl.pallas_call(
        expert_kernel,
        out_shape=outs,
        grid=(1,),
        in_specs=[pl.BlockSpec(memory_space=pltpu.SMEM), whole(x_own), whole(x_other)]
        + [g_spec, g_spec]
        + [whole(a) for a in args],
        out_specs=[whole(o) for o in outs],
        scratch_shapes=[
            pltpu.VMEM((sources, tok, local * cap), BF),
            pltpu.VMEM((local, slots, 1), F32),
            pltpu.VMEM((local, slots, 1), F32),
            pltpu.VMEM((local, slots, width), BF),
            pltpu.VMEM((local, slots, width), BF),
        ],
        compiler_params=pltpu.CompilerParams(vmem_limit_bytes=56 * 1024 * 1024),
        cost_estimate=pl.CostEstimate(flops=40 * 10**9, bytes_accessed=40 << 20, transcendentals=0),
    )(scalars, x_own, x_other, g_own, g_other, *args)


def expert_grad_kernel(xe0, xe1, de0, de1, act0, act1, da0, da1, db0, db1, out_ref):
    left = {0: (xe0, xe1), 1: (xe0, xe1), 2: (de0, de1)}
    right = {0: (da0, da1), 1: (db0, db1), 2: (act0, act1)}
    step = pl.program_id(0)
    pieces, depth = out_ref.shape[0], out_ref.shape[2]
    for kind in range(3):

        @pl.when(step % 3 == kind)
        def _(kind=kind):
            total = dot(left[kind][0][0], right[kind][0][0], 0, 0)
            total = total + dot(left[kind][1][0], right[kind][1][0], 0, 0)
            out_ref[:, 0] = total.reshape(pieces, depth, -1).astype(BF)


def expert_grads(kept, pieces):
    local, slots, width = kept[0][0].shape
    hidden = kept[0][2].shape[2]
    args = [kept[m][i] for i in range(5) for m in range(2)]
    spec = lambda a: pl.BlockSpec((1,) + a.shape[1:], lambda i: (i // 3, 0, 0))
    depth = width // pieces
    return pl.pallas_call(
        expert_grad_kernel,
        out_shape=jax.ShapeDtypeStruct((pieces, 3 * local, depth, hidden), BF),
        grid=(3 * local,),
        in_specs=[spec(a) for a in args],
        out_specs=pl.BlockSpec((pieces, 1, depth, hidden), lambda i: (0, i, 0, 0)),
        compiler_params=pltpu.CompilerParams(vmem_limit_bytes=48 * 1024 * 1024),
        cost_estimate=pl.CostEstimate(flops=14 * 10**9, bytes_accessed=28 << 20, transcendentals=0),
    )(*args)


CTX = ("z", "yl")
GROUP = ("yh", "x")
FSDP = ("yh", "x", "core")
ALL = CTX + FSDP
UP = [(i, (i + 1) % 4) for i in range(4)]
DOWN = [(i, (i - 1) % 4) for i in range(4)]
FLIP = [(0, 1), (1, 0)]


def mm(a, b):
    return jnp.dot(a, b, preferred_element_type=F32)


def mm_t(a, b):
    return lax.dot_general(a, b, (((1,), (1,)), ((), ())), preferred_element_type=F32)


def t_mm(a, b):
    return lax.dot_general(a, b, (((0,), (0,)), ((), ())), preferred_element_type=F32)


def ein(spec, a, b):
    return jnp.einsum(spec, a, b, preferred_element_type=F32)


def swap(parts, axis):
    return lax.all_to_all(parts, axis, split_axis=0, concat_axis=0, tiled=True)


def spread(block, axis, copies):
    return swap(jnp.broadcast_to(block[None], (copies,) + block.shape), axis)


def flip(block, axis):
    return lax.ppermute(block, axis, FLIP)


def pair_and_ring(block, pair, ring):
    both = jnp.concatenate([block, flip(block, pair)], axis=0)
    before = lax.ppermute(both, ring, UP)
    after = lax.ppermute(both, ring, DOWN)
    far_low = lax.ppermute(before[:1], ring, UP)
    far_high = lax.ppermute(after[1:], ring, DOWN)
    return [both, after, far_low, far_high, before]


def after_all(value, *others):
    return lax.optimization_barrier((value,) + others)[0]


def rope_tables(positions):
    half = DH // 2
    inverse = THETA ** (-(jnp.arange(half, dtype=F32) * 2.0) / DH)
    angles = positions.astype(F32)[:, None] * inverse[None, :]
    return (jnp.cos(angles), jnp.sin(angles))


def rms_scale(values, gain):
    return values * lax.rsqrt(jnp.mean(values * values, axis=-1, keepdims=True) + EPS) * gain


def body(
    tokens,
    segments,
    routes,
    w_query,
    w_key,
    w_value,
    w_out,
    w_router,
    attn_gain,
    mlp_gain,
    qk_gain,
    w_gate,
    w_up,
    w_down,
    cotangent,
):
    micro = tokens.shape[0]
    tok = tokens.shape[2]
    width = tokens.shape[3]
    length = segments.shape[2]
    rows = w_query.shape[0]
    n_ctx, n_fsdp = 8, 16
    n_all = n_ctx * n_fsdp
    z, yl, yh, x, core = (lax.axis_index(name) for name in ALL)
    shard = (yh * 4 + x) * 2 + core
    local = w_gate.shape[0]
    experts = local * n_fsdp
    cap = (3 * tok * TOPK + 2 * experts - 1) // (2 * experts)
    all_tok = micro * tok
    ratio = H // KV
    heads = ratio * DH
    span = heads + 2 * DH

    small = jnp.concatenate(
        [
            w_router,
            attn_gain[:, None],
            mlp_gain[:, None],
            jnp.pad(qk_gain[:, None], ((0, rows - 1), (0, 0))),
        ],
        axis=1,
    )
    small = jnp.pad(small, ((0, 0), (0, 128 - small.shape[1])))
    pieces = jnp.concatenate(
        [
            w_query.reshape(rows, n_ctx, heads),
            w_key.reshape(rows, n_ctx, DH),
            w_value.reshape(rows, n_ctx, DH),
            jnp.broadcast_to(small[:, None], (rows, n_ctx, 128)),
        ],
        axis=2,
    ).transpose(1, 0, 2)
    pieces = jnp.broadcast_to(pieces[:, None], (n_ctx, n_fsdp) + pieces.shape[1:])
    head_all = swap(pieces.reshape((n_all,) + pieces.shape[2:]), ALL).reshape(width, -1)
    w_heads = head_all[:, :span]
    small_all = head_all[:, span:]
    router = small_all[:, :experts]
    small_wide = small_all.astype(F32)
    gain_attn = small_wide[:, experts]
    gain_mlp = small_wide[:, experts + 1]
    gain_heads = small_wide[:, experts + 2].reshape(-1, rows)[:, 0]
    gain_row = gain_attn[None]
    head_row = jnp.concatenate(
        [gain_heads[:DH]] * ratio + [gain_heads[DH:], jnp.ones((DH,), F32)]
    )[None]
    router_pad = jnp.pad(router, ((0, 0), (0, 128 - experts)))

    seq_rows = [pair_and_ring(tokens[m], "yl", "z") for m in range(micro)]
    w_out = after_all(w_out, head_all)
    out_full = spread(w_out, ALL, n_all).reshape(width, width)

    expert_all = lax.all_gather(jnp.stack([w_gate, w_up, w_down]), CTX, axis=0)

    expert_ids = jnp.arange(experts, dtype=jnp.int32)
    cot = cotangent.reshape(all_tok, width)
    chosen = jnp.any(routes.reshape(all_tok, TOPK)[:, :, None] == expert_ids, axis=1)
    before = jnp.arange(tok, dtype=jnp.int32)
    lower = (before[:, None] >= before[None, :]).astype(BF)
    counts = ein("ut,mte->mue", lower, chosen.reshape(micro, tok, experts).astype(BF))
    held = jnp.where(chosen, counts.reshape(all_tok, experts) - 1.0, -1.0)
    held = jnp.pad(held, ((0, 0), (0, 128 - experts)), constant_values=-1.0).astype(BF)
    g_own = jnp.concatenate(
        pair_and_ring(jnp.concatenate([cot, held], axis=1)[None], "yh", "x"), axis=0
    )
    g_other = flip(g_own, "core")

    cosine, sine = rope_tables(jnp.arange(length, dtype=jnp.int32))
    cosine = jnp.tile(cosine, (1, 4))
    sine = jnp.tile(jnp.concatenate([-sine, sine], axis=1), (1, 2))
    rel = jnp.arange(n_ctx, dtype=jnp.int32)
    order = ((z + rel // 2) % 4) * 2 + (yl + rel % 2) % 2
    g_place = ((rel % 4 - x) % 4) * 2 + (rel // 4 - yh) % 2
    scalars = jnp.concatenate([jnp.stack([shard * local, core]), g_place]).astype(jnp.int32)

    def to_owner(v):
        return swap(v.reshape(n_ctx, tok, -1), CTX)

    def attention_args(m):
        seg = segments[m, 0]
        return gain_row, w_heads, head_row, cosine, sine, seg[:, None], seg[None, :]

    forward, saved = [], []
    for m in range(micro):
        mixed_h, *keep = attend_forward(order, seq_rows[m], *attention_args(m))
        saved.append(keep)
        mixed = to_owner(mixed_h).transpose(1, 0, 2).reshape(tok, width)
        start = tokens[m, 0].astype(F32)
        middle = start + mm(mixed, out_full)
        normed, norm_back = jax.vjp(rms_scale, middle, gain_mlp)
        hidden_two = normed.astype(BF)
        chosen_m = chosen[m * tok : (m + 1) * tok]
        logits = jnp.where(chosen_m, mm(hidden_two, router), -1e30)
        gates = jnp.where(chosen_m, jax.nn.softmax(logits, axis=-1), 0.0)
        x_own = spread(hidden_two, GROUP, n_ctx).reshape(n_ctx, tok, width)
        x_other = flip(x_own, "core")
        forward.append((mixed, middle, norm_back, hidden_two, gates, x_own, x_other))

    outs, d_inputs, kept, grads = [], [], [], []
    backs = []
    for m in range(micro):
        x_own, x_other = forward[m][5:]
        if m:
            x_other = after_all(x_other, *backs[-1][:1])
        moe_part, back_own, back_other, *keep = run_experts(
            scalars,
            x_own,
            x_other,
            g_own,
            g_other,
            m,
            router_pad,
            expert_all,
            cap,
        )
        kept.append(keep)
        back = (back_own.astype(F32) + flip(back_other, "core").astype(F32)).astype(BF)
        backs.append((back, moe_part))
    for m in range(micro):
        mixed, middle, norm_back, hidden_two, gates = forward[m][:5]
        back, moe_part = backs[m]
        back = jnp.sum(swap(back, GROUP).astype(F32), axis=0)
        moe = lax.psum_scatter(moe_part, FSDP, scatter_dimension=0, tiled=True)[0]
        outs.append((middle + moe.astype(F32)).astype(BF))
        grad_top = cot[m * tok : (m + 1) * tok].astype(F32)
        tail = back[:, width:]
        d_gates = tail[:, :experts] + tail[:, 64 : 64 + experts]
        d_select = gates * (d_gates - jnp.sum(gates * d_gates, axis=-1, keepdims=True))
        d_logits = d_select.astype(BF)
        grad_router = t_mm(hidden_two, d_logits)
        d_two = back[:, :width] + mm_t(d_logits, router)
        d_middle, grad_mlp = norm_back(d_two)
        d_middle = d_middle + grad_top
        d_branch = d_middle.astype(BF)
        grad_out = t_mm(mixed, d_branch)
        d_mixed = mm_t(d_branch, out_full).astype(BF)
        d_mixed = swap(d_mixed.reshape(tok, n_ctx, heads).transpose(1, 0, 2), CTX)
        d_hidden, grad_heads, grad_attn, grad_qk = attend_backward(
            *saved[m], d_mixed.reshape(length, heads), *attention_args(m)
        )
        d_hidden = jnp.sum(to_owner(d_hidden).astype(F32), axis=0)
        start = tokens[m, 0].astype(F32)
        inverse = lax.rsqrt(jnp.mean(start * start, axis=-1, keepdims=True) + EPS)
        u = d_hidden * gain_attn
        d_inputs.append(
            d_middle
            + inverse * u
            - start * (inverse**3 * jnp.mean(u * start, axis=-1, keepdims=True))
        )
        grad_qk = jnp.concatenate(
            [grad_qk[0, :DH] + grad_qk[0, DH : 2 * DH], grad_qk[0, 2 * DH : 3 * DH]]
        )
        grads.append((grad_out, grad_heads, grad_router, grad_attn[0], grad_mlp, grad_qk))
    grad_out, grad_heads, grad_router, grad_attn, grad_mlp, grad_qk = jax.tree.map(
        jnp.add, grads[0], grads[1]
    )

    grad_out = swap(grad_out.astype(BF).reshape(n_all, rows, width), ALL)
    own_out = jnp.sum(grad_out.astype(F32), axis=0)
    grad_qk = jnp.pad(grad_qk[:, None], ((0, 0), (0, rows - 1))).reshape(-1)
    grad_small = jnp.concatenate(
        [grad_router, grad_attn[:, None], grad_mlp[:, None], grad_qk[:, None]], axis=1
    )
    grad_small = jnp.pad(grad_small, ((0, 0), (0, 128 - grad_small.shape[1])))
    grad_pack = jnp.concatenate([grad_heads, grad_small], axis=1).astype(BF)
    grad_pack = swap(grad_pack.reshape(n_all, rows, -1), ALL).astype(F32)
    own_heads = jnp.sum(grad_pack[:, :, :span].reshape(n_ctx, n_fsdp, rows, -1), axis=1)
    own_heads = own_heads.transpose(1, 0, 2)
    own_small = jnp.sum(grad_pack[:, :, span:], axis=0)
    kept[1][0] = after_all(kept[1][0], backs[1][0])
    expert_own = lax.psum_scatter(
        expert_grads(kept, n_ctx), CTX, scatter_dimension=0, tiled=True
    )[0].astype(F32)
    expert_own = expert_own.reshape((local, 3) + expert_own.shape[1:])

    return (
        jnp.stack(outs)[:, None],
        jnp.stack(d_inputs)[:, None],
        own_heads[:, :, :heads].reshape(rows, -1),
        own_heads[:, :, heads : heads + DH].reshape(rows, -1),
        own_heads[:, :, heads + DH :].reshape(rows, -1),
        own_out,
        own_small[:, :experts],
        own_small[:, experts],
        own_small[:, experts + 1],
        own_small[:1, experts + 2],
        expert_own[:, 0],
        expert_own[:, 1],
        expert_own[:, 2],
    )


def solution(mesh):
    mesh = Mesh(mesh.devices.reshape(4, 2, 2, 4, 2), ALL)
    weight = P(ALL, None)
    gain = P(ALL)
    rows = P(None, FSDP, CTX, None)
    expert = P(FSDP, CTX, None)
    return jax.shard_map(
        body,
        mesh=mesh,
        in_specs=(rows, P(None, FSDP, None), rows)
        + (weight,) * 5
        + (gain,) * 3
        + (expert,) * 3
        + (rows,),
        out_specs=(rows, rows) + (weight,) * 5 + (gain,) * 3 + (expert,) * 3,
        check_vma=False,
    )
```

```python
import functools

import jax
import jax.numpy as jnp
from jax import lax
from jax.experimental import pallas as pl
from jax.experimental.pallas import tpu as pltpu
from jax.sharding import Mesh
from jax.sharding import PartitionSpec as P

BF = jnp.bfloat16
F32 = jnp.float32
H = 16
KV = 8
DH = 64
TOPK = 8
WINDOW = 1024
EPS = 1e-06
THETA = 10000.0


def dot(a, b, ca, cb):
    return lax.dot_general(a, b, (((ca,), (cb,)), ((), ())), preferred_element_type=F32)


def lanes_of(v):
    return lax.broadcasted_iota(jnp.int32, v.shape, v.ndim - 1)


def head_sums(v):
    low = lanes_of(v) < DH
    first = jnp.sum(jnp.where(low, v, 0.0), axis=1, keepdims=True)
    second = jnp.sum(jnp.where(low, 0.0, v), axis=1, keepdims=True)
    return jnp.where(low, first, second)


def trade(v):
    return jnp.where(
        lanes_of(v) % DH < DH // 2, pltpu.roll(v, 128 - DH // 2, 1), pltpu.roll(v, DH // 2, 1)
    )


def both_halves(v, second):
    low = lanes_of(v) < DH
    other = pltpu.roll(v, DH, 1)
    return jnp.where(low, other, v) if second else jnp.where(low, v, other)


def stack_heads(v):
    low = lanes_of(v) < DH
    zero = jnp.zeros_like(v)
    return jnp.concatenate([jnp.where(low, v, zero), jnp.where(low, zero, v)], axis=0)


def key_span(start, block, length):
    reach = WINDOW // 2 - 1
    low = max(0, start - reach) // 128 * 128
    high = min(length, -(-(start + block + reach) // 128) * 128)
    return low, high


def masked_probs(q_two, keys, seg_col, seg_row, start, low):
    block = q_two.shape[0] // 2
    scores = dot(q_two, keys, 1, 1)
    shape = (block, keys.shape[0])
    gap = (
        lax.broadcasted_iota(jnp.int32, shape, 0)
        - lax.broadcasted_iota(jnp.int32, shape, 1)
        + (start - low)
    )
    allowed = (seg_col == seg_row) & (jnp.abs(gap) < WINDOW // 2)
    bias = jnp.where(allowed, 0.0, -1e30)
    scores = scores + jnp.concatenate([bias, bias], axis=0)
    raised = jnp.exp(scores - jnp.max(scores, axis=1, keepdims=True))
    return raised * (1.0 / jnp.sum(raised, axis=1, keepdims=True))


def attend_kernel(
    order_ref,
    own_ref,
    after_ref,
    far_low_ref,
    far_high_ref,
    before_ref,
    gain_ref,
    w_ref,
    head_gain_ref,
    cos_ref,
    sin_ref,
    seg_col_ref,
    seg_row_ref,
    mixed_ref,
    hidden_ref,
    q_ref,
    kv_ref,
    keys_ref,
    values_ref,
):
    tok, width = own_ref.shape[1:]
    length = hidden_ref.shape[0]
    pieces = [
        (own_ref, 0),
        (own_ref, 1),
        (after_ref, 0),
        (after_ref, 1),
        (far_low_ref, 0),
        (far_high_ref, 0),
        (before_ref, 0),
        (before_ref, 1),
    ]
    for r, (ref, i) in enumerate(pieces):
        x = ref[i].astype(F32)
        x = x * lax.rsqrt(jnp.mean(x * x, axis=1, keepdims=True) + EPS) * gain_ref[...]
        rows = pl.ds(pl.multiple_of(order_ref[r] * tok, tok), tok)
        hidden_ref[rows] = x.astype(BF)
    raw = dot(hidden_ref[...], w_ref[...], 1, 0)
    for half in range(2):
        u = raw[:, half * 128 : half * 128 + 128]
        gain = head_gain_ref[:, half * 128 : half * 128 + 128]
        n = u * lax.rsqrt(head_sums(u * u) * (1.0 / DH) + EPS) * gain
        turned = n * cos_ref[...] + trade(n) * sin_ref[...]
        if half == 0:
            q_ref[...] = turned.astype(BF)
        else:
            kv = jnp.where(lanes_of(u) < DH, turned, u)
            kv_ref[...] = kv.astype(BF)
            keys_ref[...] = both_halves(kv, False).astype(BF)
            values_ref[...] = both_halves(kv, True).astype(BF)
    block = 256
    for start in range(0, length, block):
        low, high = key_span(start, block, length)
        q_two = stack_heads(q_ref[start : start + block].astype(F32) * DH**-0.5).astype(BF)
        probs = masked_probs(
            q_two,
            keys_ref[low:high],
            seg_col_ref[start : start + block],
            seg_row_ref[:, low:high],
            start,
            low,
        )
        result = dot(probs.astype(BF), values_ref[low:high], 1, 0)
        first = lanes_of(result[:block]) < DH
        mixed_ref[start : start + block] = jnp.where(first, result[:block], result[block:]).astype(
            BF
        )


def attend_back_kernel(
    hidden_ref,
    q_ref,
    kv_ref,
    d_mixed_ref,
    gain_ref,
    w_ref,
    head_gain_ref,
    cos_ref,
    sin_ref,
    seg_col_ref,
    seg_row_ref,
    d_hidden_ref,
    grad_w_ref,
    grad_gain_ref,
    grad_heads_ref,
    keys_ref,
    values_ref,
    d_q_ref,
    d_k_ref,
    d_v_ref,
    d_raw_ref,
):
    length = hidden_ref.shape[0]
    kv = kv_ref[...].astype(F32)
    keys_ref[...] = both_halves(kv, False).astype(BF)
    values_ref[...] = both_halves(kv, True).astype(BF)
    d_k_ref[...] = jnp.zeros_like(d_k_ref)
    d_v_ref[...] = jnp.zeros_like(d_v_ref)
    block = 256
    for start in range(0, length, block):
        low, high = key_span(start, block, length)
        q_two = stack_heads(q_ref[start : start + block].astype(F32) * DH**-0.5).astype(BF)
        m_two = stack_heads(d_mixed_ref[start : start + block].astype(F32)).astype(BF)
        probs = masked_probs(
            q_two,
            keys_ref[low:high],
            seg_col_ref[start : start + block],
            seg_row_ref[:, low:high],
            start,
            low,
        )
        d_probs = dot(m_two, values_ref[low:high], 1, 1)
        inner = jnp.sum(probs * d_probs, axis=1, keepdims=True)
        d_scores = (probs * (d_probs - inner)).astype(BF)
        result = dot(d_scores, keys_ref[low:high], 1, 0)
        first = lanes_of(result[:block]) < DH
        d_q_ref[start : start + block] = jnp.where(first, result[:block], result[block:]) * (
            DH**-0.5
        )
        d_k_ref[low:high] += dot(d_scores, q_two, 0, 0)
        d_v_ref[low:high] += dot(probs.astype(BF), m_two, 0, 0)
    raw = dot(hidden_ref[...], w_ref[...], 1, 0)
    d_k = d_k_ref[...]
    d_k = d_k + pltpu.roll(d_k, DH, 1)
    d_v = d_v_ref[...]
    d_v = d_v + pltpu.roll(d_v, DH, 1)
    for half in range(2):
        lanes = slice(half * 128, half * 128 + 128)
        u = raw[:, lanes]
        gain = head_gain_ref[:, lanes]
        d = d_q_ref[...] if half == 0 else d_k
        d = d * cos_ref[...] + trade(d * sin_ref[...])
        r = lax.rsqrt(head_sums(u * u) * (1.0 / DH) + EPS)
        grad_heads_ref[:, lanes] = jnp.sum(d * u * r, axis=0, keepdims=True)
        d = d * gain
        d = d * r - u * (r * r * r * (head_sums(d * u) * (1.0 / DH)))
        if half == 1:
            d = jnp.where(lanes_of(d) < DH, d, d_v)
        d_raw_ref[:, lanes] = d.astype(BF)
    grad_w_ref[...] = dot(hidden_ref[...], d_raw_ref[...], 0, 0)
    total = jnp.zeros(grad_gain_ref.shape, F32)
    for start in range(0, length, block):
        rows = slice(start, start + block)
        d_hidden = dot(d_raw_ref[rows], w_ref[...], 1, 1)
        d_hidden_ref[rows] = d_hidden.astype(BF)
        total = total + jnp.sum(d_hidden * hidden_ref[rows].astype(F32), axis=0, keepdims=True)
    grad_gain_ref[...] = total / gain_ref[...]


def whole(a):
    return pl.BlockSpec(a.shape, lambda i: (0,) * len(a.shape), pipeline_mode=pl.Buffered(1))


def attend_forward(order, pieces, gain, w_heads, head_gain, cosine, sine, seg_col, seg_row):
    length = cosine.shape[0]
    width = w_heads.shape[0]
    shape = jax.ShapeDtypeStruct
    outs = [
        shape((length, 128), BF),
        shape((length, width), BF),
        shape((length, 128), BF),
        shape((length, 128), BF),
    ]
    args = list(pieces) + [gain, w_heads, head_gain, cosine, sine, seg_col, seg_row]
    return pl.pallas_call(
        attend_kernel,
        out_shape=outs,
        grid=(1,),
        in_specs=[pl.BlockSpec(memory_space=pltpu.SMEM)] + [whole(a) for a in args],
        out_specs=[whole(o) for o in outs],
        scratch_shapes=[pltpu.VMEM((length, 128), BF), pltpu.VMEM((length, 128), BF)],
        compiler_params=pltpu.CompilerParams(vmem_limit_bytes=40 * 1024 * 1024),
        cost_estimate=pl.CostEstimate(flops=12 * 10**9, bytes_accessed=8 << 20, transcendentals=0),
    )(order, *args)


def attend_backward(
    hidden, q, kv, d_mixed, gain, w_heads, head_gain, cosine, sine, seg_col, seg_row
):
    length, width = hidden.shape
    shape = jax.ShapeDtypeStruct
    outs = [
        shape((length, width), BF),
        shape((width, 256), F32),
        shape((1, width), F32),
        shape((1, 256), F32),
    ]
    args = [hidden, q, kv, d_mixed, gain, w_heads, head_gain, cosine, sine, seg_col, seg_row]
    return pl.pallas_call(
        attend_back_kernel,
        out_shape=outs,
        grid=(1,),
        in_specs=[whole(a) for a in args],
        out_specs=[whole(o) for o in outs],
        scratch_shapes=[pltpu.VMEM((length, 128), BF)] * 2
        + [pltpu.VMEM((length, 128), F32)] * 3
        + [pltpu.VMEM((length, 256), BF)],
        compiler_params=pltpu.CompilerParams(vmem_limit_bytes=40 * 1024 * 1024),
        cost_estimate=pl.CostEstimate(flops=25 * 10**9, bytes_accessed=8 << 20, transcendentals=0),
    )(*args)


def halves(v):
    high = v.astype(BF)
    return high, (v - high.astype(F32)).astype(BF)


def expert_kernel(scalar_ref, *refs, joined):
    x_own_ref, x_other_ref, g_ref, router_ref = refs[:4]
    first_pieces, second_pieces = refs[4:9], refs[9:11]
    refs = refs[11:]
    if joined:
        out_ref, refs = refs[0], refs[1:]
    else:
        (out_own_ref, out_other_ref), refs = refs[:2], refs[2:]
    back_own_ref, back_other_ref, xe_ref, de_ref, act_ref, da_ref, db_ref = refs[:7]
    pick_ref, weight_ref, dgate_ref, eo_ref, dr_ref, w_ref = refs[7:]
    half, tok, width = x_own_ref.shape
    sources = 2 * half
    core = scalar_ref[1]
    depth = w_ref.shape[2] // 8

    def place(expert, r, ref, i):
        rows = pl.ds(pl.multiple_of(scalar_ref[2 + r] * depth, depth), depth)
        w_ref[expert, :, rows] = ref[i]

    both_ref, after_ref, far_low_ref, far_high_ref, before_ref = first_pieces
    for r, (ref, i) in enumerate(
        [
            (both_ref, 0),
            (both_ref, 1),
            (after_ref, 0),
            (after_ref, 1),
            (far_low_ref, 0),
            (far_high_ref, 0),
            (before_ref, 0),
            (before_ref, 1),
        ]
    ):
        place(0, r, ref, i)
    for r in range(8):
        place(1, r, second_pieces[r % 2], r // 2)
    local, slots, hidden = act_ref.shape
    cap = slots // sources
    first = scalar_ref[0]
    lane = lax.broadcasted_iota(jnp.int32, (tok, 128), 1)
    spot = lax.broadcasted_iota(jnp.int32, (tok, local * cap), 1)
    row_expert = lax.broadcasted_iota(jnp.int32, (local * cap, 128), 0) // cap
    slot_lane = lax.broadcasted_iota(jnp.int32, (local * cap, 128), 1)
    own_lane = slot_lane == first + row_expert

    def fetch(i, carry, x_ref, offset, column):
        s = i + offset
        x = x_ref[i]
        from_g = 2 * i + column
        held = g_ref[from_g, :, width:].astype(F32)
        chosen = held >= 0.0
        logits = jnp.where(chosen, dot(x, router_ref[...], 1, 0), -1e30)
        top = jnp.max(logits, axis=1, keepdims=True)
        raised = jnp.where(chosen, jnp.exp(logits - top), 0.0)
        gates = raised / jnp.sum(raised, axis=1, keepdims=True)
        pick = jnp.zeros((tok, local * cap), F32)
        for e in range(local):
            mine = jnp.max(jnp.where(lane == first + e, held, -1.0), axis=1, keepdims=True)
            goal = jnp.where(mine >= 0.0, mine + e * cap, -1.0).astype(jnp.int32)
            pick = jnp.where(spot == goal, 1.0, pick)
        pick = pick.astype(BF)
        pick_ref[s] = pick
        rows = pl.ds(pl.multiple_of(s * cap, 16), cap)
        x_slots = dot(pick, x, 0, 0).astype(BF)
        g_slots = dot(pick, g_ref[from_g, :, :width], 0, 0).astype(BF)
        high, low = halves(gates)
        weight = dot(pick, high, 0, 0) + dot(pick, low, 0, 0)
        weight = jnp.sum(jnp.where(own_lane, weight, 0.0), axis=1, keepdims=True)
        for e in range(local):
            part = slice(e * cap, (e + 1) * cap)
            xe_ref[e, rows] = x_slots[part]
            de_ref[e, rows] = g_slots[part]
            weight_ref[e, rows] = weight[part]
        return carry

    for x_ref, offset, column in ((x_own_ref, 0, core), (x_other_ref, half, 1 - core)):
        lax.fori_loop(
            0, half, functools.partial(fetch, x_ref=x_ref, offset=offset, column=column), 0
        )
    chunk = 256

    def work(i, carry):
        e = i // (slots // chunk)
        rows = pl.ds(pl.multiple_of((i % (slots // chunk)) * chunk, chunk), chunk)
        w_gate = w_ref[e, 0]
        w_up = w_ref[e, 1]
        w_down = w_ref[e, 2]
        x = xe_ref[e, rows]
        a = dot(x, w_gate, 1, 0)
        b = dot(x, w_up, 1, 0)
        sig = 1.0 / (1.0 + jnp.exp(-a))
        silu = a * sig
        active = (silu * b).astype(BF)
        act_ref[e, rows] = active
        slope = b * (sig * (1.0 + a * (1.0 - sig)))
        weight = weight_ref[e, rows]
        g = de_ref[e, rows].astype(F32)
        result = dot(active, w_down, 1, 1).astype(BF).astype(F32)
        dgate_ref[e, rows] = jnp.sum(result * g, axis=1, keepdims=True)
        eo_ref[e, rows] = (weight * result).astype(BF)
        d_expert = (weight * g).astype(BF)
        de_ref[e, rows] = d_expert
        d_active = dot(d_expert, w_down, 1, 0)
        da = (d_active * slope).astype(BF)
        db = (d_active * silu).astype(BF)
        da_ref[e, rows] = da
        db_ref[e, rows] = db
        dr_ref[e, rows] = (dot(da, w_gate, 1, 1) + dot(db, w_up, 1, 1)).astype(BF)
        return carry

    lax.fori_loop(0, local * (slots // chunk), work, 0)

    def give(i, carry, back_ref, part_ref, offset, column):
        s = i + offset
        rows = pl.ds(pl.multiple_of(s * cap, 16), cap)
        pick = pick_ref[s]
        eo = jnp.concatenate([eo_ref[e, rows] for e in range(local)], axis=0)
        dr = jnp.concatenate([dr_ref[e, rows] for e in range(local)], axis=0)
        dgate = jnp.concatenate([dgate_ref[e, rows] for e in range(local)], axis=0)
        high, low = halves(dgate)
        spread = jnp.where(own_lane, high.astype(F32), 0.0) + jnp.where(
            slot_lane == first + row_expert + 64, low.astype(F32), 0.0
        )
        part_ref[2 * i + column if joined else i] = dot(pick, eo, 1, 0).astype(BF)
        back_ref[i, :, :width] = dot(pick, dr, 1, 0).astype(BF)
        back_ref[i, :, width:] = dot(pick, spread.astype(BF), 1, 0).astype(BF)
        return carry

    parts = (out_ref, out_ref) if joined else (out_own_ref, out_other_ref)
    for back_ref, part_ref, offset, column in (
        (back_own_ref, parts[0], 0, core),
        (back_other_ref, parts[1], half, 1 - core),
    ):
        step = functools.partial(
            give, back_ref=back_ref, part_ref=part_ref, offset=offset, column=column
        )
        lax.fori_loop(0, half, step, 0)


def run_experts(scalars, x_own, x_other, g_all, micro, router, first, second, cap, joined):
    half, tok, width = x_own.shape
    sources = 2 * half
    local = 2
    hidden = second[0].shape[3]
    slots = sources * cap
    wide = g_all.shape[2]
    shape = jax.ShapeDtypeStruct
    outs = [shape((sources, tok, width), BF)] if joined else [shape((half, tok, width), BF)] * 2
    outs = outs + [
        shape((half, tok, wide), BF),
        shape((half, tok, wide), BF),
        shape((local, slots, width), BF),
        shape((local, slots, width), BF),
        shape((local, slots, hidden), BF),
        shape((local, slots, hidden), BF),
        shape((local, slots, hidden), BF),
    ]
    g_spec = pl.BlockSpec(
        (sources, tok, wide), lambda i: (0, micro, 0), pipeline_mode=pl.Buffered(1)
    )
    args = [router, *first, *second]
    return pl.pallas_call(
        functools.partial(expert_kernel, joined=joined),
        out_shape=outs,
        grid=(1,),
        in_specs=[pl.BlockSpec(memory_space=pltpu.SMEM), whole(x_own), whole(x_other), g_spec]
        + [whole(a) for a in args],
        out_specs=[whole(o) for o in outs],
        scratch_shapes=[
            pltpu.VMEM((sources, tok, local * cap), BF),
            pltpu.VMEM((local, slots, 1), F32),
            pltpu.VMEM((local, slots, 1), F32),
            pltpu.VMEM((local, slots, width), BF),
            pltpu.VMEM((local, slots, width), BF),
            pltpu.VMEM((local, 3, width, hidden), BF),
        ],
        compiler_params=pltpu.CompilerParams(vmem_limit_bytes=60 * 1024 * 1024),
        cost_estimate=pl.CostEstimate(flops=40 * 10**9, bytes_accessed=40 << 20, transcendentals=0),
    )(scalars, x_own, x_other, g_all, *args)


def expert_grad_kernel(xe0, xe1, de0, de1, act0, act1, da0, da1, db0, db1, out_ref):
    left = {0: (xe0, xe1), 1: (xe0, xe1), 2: (de0, de1)}
    right = {0: (da0, da1), 1: (db0, db1), 2: (act0, act1)}
    step = pl.program_id(0)
    pieces, depth = out_ref.shape[0], out_ref.shape[2]
    for kind in range(3):

        @pl.when(step % 3 == kind)
        def _(kind=kind):
            total = dot(left[kind][0][0], right[kind][0][0], 0, 0)
            total = total + dot(left[kind][1][0], right[kind][1][0], 0, 0)
            out_ref[:, 0] = total.reshape(pieces, depth, -1).astype(BF)


def expert_grads(kept, pieces):
    local, slots, width = kept[0][0].shape
    hidden = kept[0][2].shape[2]
    args = [kept[m][i] for i in range(5) for m in range(2)]
    spec = lambda a: pl.BlockSpec((1,) + a.shape[1:], lambda i: (i // 3, 0, 0))
    depth = width // pieces
    return pl.pallas_call(
        expert_grad_kernel,
        out_shape=jax.ShapeDtypeStruct((pieces, 3 * local, depth, hidden), BF),
        grid=(3 * local,),
        in_specs=[spec(a) for a in args],
        out_specs=pl.BlockSpec((pieces, 1, depth, hidden), lambda i: (0, i, 0, 0)),
        compiler_params=pltpu.CompilerParams(vmem_limit_bytes=48 * 1024 * 1024),
        cost_estimate=pl.CostEstimate(flops=14 * 10**9, bytes_accessed=28 << 20, transcendentals=0),
    )(*args)


CTX = ("z", "yl")
GROUP = ("yh", "x")
FSDP = ("yh", "x", "core")
ALL = CTX + FSDP
UP = [(i, (i + 1) % 4) for i in range(4)]
DOWN = [(i, (i - 1) % 4) for i in range(4)]
FLIP = [(0, 1), (1, 0)]


def mm(a, b):
    return jnp.dot(a, b, preferred_element_type=F32)


def mm_t(a, b):
    return lax.dot_general(a, b, (((1,), (1,)), ((), ())), preferred_element_type=F32)


def t_mm(a, b):
    return lax.dot_general(a, b, (((0,), (0,)), ((), ())), preferred_element_type=F32)


def ein(spec, a, b):
    return jnp.einsum(spec, a, b, preferred_element_type=F32)


def swap(parts, axis):
    return lax.all_to_all(parts, axis, split_axis=0, concat_axis=0, tiled=True)


def flip(block, axis):
    return lax.ppermute(block, axis, FLIP)


def ring_of(both):
    before = lax.ppermute(both, "z", UP)
    after = lax.ppermute(both, "z", DOWN)
    far_low = lax.ppermute(before[:1], "z", UP)
    far_high = lax.ppermute(after[1:], "z", DOWN)
    return [both, after, far_low, far_high, before]


class Exchange:
    def __init__(self):
        self.last = None

    def __call__(self, parts, axis):
        if self.last is not None:
            parts = after_all(parts, self.last)
        self.last = swap(parts, axis)
        return self.last

    def copies(self, block, axis, count):
        return self(jnp.broadcast_to(block[None], (count,) + block.shape), axis)


def sum_parts(parts):
    return jnp.sum(parts.astype(F32), axis=0)


def after_all(value, *others):
    return lax.optimization_barrier((value,) + others)[0]


def rope_tables(positions):
    half = DH // 2
    inverse = THETA ** (-(jnp.arange(half, dtype=F32) * 2.0) / DH)
    angles = positions.astype(F32)[:, None] * inverse[None, :]
    return (jnp.cos(angles), jnp.sin(angles))


def rms_scale(values, gain):
    return values * lax.rsqrt(jnp.mean(values * values, axis=-1, keepdims=True) + EPS) * gain


def body(
    tokens,
    segments,
    routes,
    w_query,
    w_key,
    w_value,
    w_out,
    w_router,
    attn_gain,
    mlp_gain,
    qk_gain,
    w_gate,
    w_up,
    w_down,
    cotangent,
):
    micro = tokens.shape[0]
    tok = tokens.shape[2]
    width = tokens.shape[3]
    length = segments.shape[2]
    rows = w_query.shape[0]
    n_ctx, n_fsdp = 8, 16
    n_all = n_ctx * n_fsdp
    z, yl, yh, x, core = (lax.axis_index(name) for name in ALL)
    shard = (yh * 4 + x) * 2 + core
    local = w_gate.shape[0]
    experts = local * n_fsdp
    cap = (3 * tok * TOPK + 2 * experts - 1) // (2 * experts)
    all_tok = micro * tok
    ratio = H // KV
    heads = ratio * DH
    span = heads + 2 * DH

    exchange = Exchange()
    small = jnp.concatenate(
        [
            w_router,
            attn_gain[:, None],
            mlp_gain[:, None],
            jnp.pad(qk_gain[:, None], ((0, rows - 1), (0, 0))),
        ],
        axis=1,
    )
    small = jnp.pad(small, ((0, 0), (0, 128 - small.shape[1])))
    pieces = jnp.concatenate(
        [
            w_query.reshape(rows, n_ctx, heads),
            w_key.reshape(rows, n_ctx, DH),
            w_value.reshape(rows, n_ctx, DH),
            jnp.broadcast_to(small[:, None], (rows, n_ctx, 128)),
        ],
        axis=2,
    ).transpose(1, 0, 2)
    pieces = jnp.broadcast_to(pieces[:, None], (n_ctx, n_fsdp) + pieces.shape[1:])
    head_all = exchange(pieces.reshape((n_all,) + pieces.shape[2:]), ALL).reshape(width, -1)
    w_heads = head_all[:, :span]
    small_all = head_all[:, span:]
    router = small_all[:, :experts]
    small_wide = small_all.astype(F32)
    gain_attn = small_wide[:, experts]
    gain_mlp = small_wide[:, experts + 1]
    gain_heads = small_wide[:, experts + 2].reshape(-1, rows)[:, 0]
    gain_row = gain_attn[None]
    head_row = jnp.concatenate(
        [gain_heads[:DH]] * ratio + [gain_heads[DH:], jnp.ones((DH,), F32)]
    )[None]
    router_pad = jnp.pad(router, ((0, 0), (0, 128 - experts)))

    own = exchange.copies(w_out, CTX + GROUP, n_all // 2)
    other = flip(own, "core")
    out_full = jnp.where(
        core == 0, jnp.stack([own, other], axis=1), jnp.stack([other, own], axis=1)
    ).reshape(width, width)

    both = [jnp.concatenate([tokens[m], flip(tokens[m], "yl")], axis=0) for m in range(micro)]
    seq_rows = [ring_of(both[0])]
    seq_rows.append(ring_of(after_all(both[1], seq_rows[0][1], seq_rows[0][4])))

    stack = jnp.stack([w_gate, w_up, w_down], axis=1)
    second_own = after_all(stack[1:], seq_rows[1][1], seq_rows[1][4])
    second_before = lax.ppermute(second_own, "z", UP)
    second_after = lax.ppermute(second_own, "z", DOWN)
    half = stack.shape[2] // 2
    second_far = jnp.concatenate(
        [
            lax.ppermute(second_before[:, :, :half], "z", UP),
            lax.ppermute(second_after[:, :, half:], "z", DOWN),
        ],
        axis=2,
    )
    second_near = jnp.concatenate([second_own, second_after, second_far, second_before], axis=0)
    second = [second_near, flip(second_near, "yl")]
    first_own = jnp.concatenate([stack[:1], flip(stack[:1], "yl")], axis=0)
    first = ring_of(after_all(first_own, second_before, second_after))

    expert_ids = jnp.arange(experts, dtype=jnp.int32)
    cot = cotangent.reshape(all_tok, width)
    chosen = jnp.any(routes.reshape(all_tok, TOPK)[:, :, None] == expert_ids, axis=1)
    before = jnp.arange(tok, dtype=jnp.int32)
    lower = (before[:, None] >= before[None, :]).astype(BF)
    counts = ein("ut,mte->mue", lower, chosen.reshape(micro, tok, experts).astype(BF))
    held = jnp.where(chosen, counts.reshape(all_tok, experts) - 1.0, -1.0)
    held = jnp.pad(held, ((0, 0), (0, 128 - experts)), constant_values=-1.0).astype(BF)
    g_all = lax.all_gather(jnp.concatenate([cot, held], axis=1), FSDP, axis=0)

    cosine, sine = rope_tables(jnp.arange(length, dtype=jnp.int32))
    cosine = jnp.tile(cosine, (1, 4))
    sine = jnp.tile(jnp.concatenate([-sine, sine], axis=1), (1, 2))
    rel = jnp.arange(n_ctx, dtype=jnp.int32)
    order = ((z + rel // 2) % 4) * 2 + (yl + rel % 2) % 2
    scalars = jnp.concatenate([jnp.stack([shard * local, core]), order]).astype(jnp.int32)

    def to_owner(v):
        return exchange(v.reshape(n_ctx, tok, -1), CTX)

    def attention_args(m):
        seg = segments[m, 0]
        return gain_row, w_heads, head_row, cosine, sine, seg[:, None], seg[None, :]

    forward, saved = [], []
    for m in range(micro):
        mixed_h, *keep = attend_forward(order, seq_rows[m], *attention_args(m))
        saved.append(keep)
        if m == 0:
            mixed_h = after_all(mixed_h, seq_rows[1][1], seq_rows[1][4])
        mixed = to_owner(mixed_h).transpose(1, 0, 2).reshape(tok, width)
        start = tokens[m, 0].astype(F32)
        middle = start + mm(mixed, out_full)
        normed, norm_back = jax.vjp(rms_scale, middle, gain_mlp)
        hidden_two = normed.astype(BF)
        chosen_m = chosen[m * tok : (m + 1) * tok]
        logits = jnp.where(chosen_m, mm(hidden_two, router), -1e30)
        gates = jnp.where(chosen_m, jax.nn.softmax(logits, axis=-1), 0.0)
        x_own = exchange.copies(hidden_two, GROUP, n_ctx)
        forward.append((mixed, middle, norm_back, hidden_two, gates, x_own))

    def experts_of(m, x_own):
        return run_experts(
            scalars,
            x_own,
            flip(x_own, "core"),
            g_all,
            m,
            router_pad,
            first,
            second,
            cap,
            m == 0,
        )

    def back_sum(own, other):
        return (own.astype(F32) + flip(other, "core").astype(F32)).astype(BF)

    def middle_back(m, back):
        mixed, middle, norm_back, hidden_two, gates = forward[m][:5]
        grad_top = cot[m * tok : (m + 1) * tok].astype(F32)
        tail = back[:, width:]
        d_gates = tail[:, :experts] + tail[:, 64 : 64 + experts]
        d_select = gates * (d_gates - jnp.sum(gates * d_gates, axis=-1, keepdims=True))
        d_logits = d_select.astype(BF)
        grad_router = t_mm(hidden_two, d_logits)
        d_two = back[:, :width] + mm_t(d_logits, router)
        d_middle, grad_mlp = norm_back(d_two)
        d_middle = d_middle + grad_top
        d_branch = d_middle.astype(BF)
        grad_out = t_mm(mixed, d_branch)
        d_mixed = mm_t(d_branch, out_full).astype(BF)
        d_mixed = d_mixed.reshape(tok, n_ctx, heads).transpose(1, 0, 2)
        return d_middle, d_mixed, (grad_out, grad_router, grad_mlp)

    def attention_back(m, d_mixed):
        d_hidden, grad_heads, grad_attn, grad_qk = attend_backward(
            *saved[m], d_mixed.reshape(length, heads), *attention_args(m)
        )
        grad_qk = jnp.concatenate(
            [grad_qk[0, :DH] + grad_qk[0, DH : 2 * DH], grad_qk[0, 2 * DH : 3 * DH]]
        )
        return d_hidden, (grad_heads, grad_attn[0], grad_qk)

    def input_grad(m, d_hidden, d_middle):
        start = tokens[m, 0].astype(F32)
        inverse = lax.rsqrt(jnp.mean(start * start, axis=-1, keepdims=True) + EPS)
        u = d_hidden * gain_attn
        return (
            d_middle
            + inverse * u
            - start * (inverse**3 * jnp.mean(u * start, axis=-1, keepdims=True))
        )

    moe_0, back_own, back_other, *kept_0 = experts_of(0, forward[0][5])
    x_1, back_own, back_other, moe_0 = lax.optimization_barrier(
        (forward[1][5], back_own, back_other, moe_0)
    )
    back_0 = back_sum(back_own, back_other)
    moe_0 = lax.psum_scatter(moe_0, FSDP, scatter_dimension=0, tiled=True)[0]
    x_1 = after_all(x_1, back_0)
    back_0 = exchange(back_0, GROUP)
    moe_own, moe_other, back_own, back_other, *kept_1 = experts_of(1, x_1)
    back_0, back_own, back_other, moe_own, moe_other = lax.optimization_barrier(
        (back_0, back_own, back_other, moe_own, moe_other)
    )
    back_1 = back_sum(back_own, back_other)
    d_middle_0, d_mixed_0, grads_0 = middle_back(0, sum_parts(back_0))
    d_mixed_0 = exchange(d_mixed_0, CTX)
    expert_sums = expert_grads((kept_0, kept_1), n_ctx)
    back_1 = exchange(back_1, GROUP)
    d_hidden_0, head_grads_0 = attention_back(0, d_mixed_0)
    back_1, d_hidden_0, expert_sums, moe_0 = lax.optimization_barrier(
        (back_1, d_hidden_0, expert_sums, moe_0)
    )
    expert_own = lax.psum_scatter(expert_sums, CTX, scatter_dimension=0, tiled=True)[0]
    d_middle_1, d_mixed_1, grads_1 = middle_back(1, sum_parts(back_1))
    d_mixed_1 = exchange(d_mixed_1, CTX)
    moe_1 = back_sum(moe_own, moe_other)
    d_hidden_0 = to_owner(d_hidden_0)
    d_hidden_1, head_grads_1 = attention_back(1, d_mixed_1)
    d_hidden_0, d_hidden_1 = lax.optimization_barrier((d_hidden_0, d_hidden_1))
    d_hidden_1 = to_owner(d_hidden_1)
    grad_out, grad_router, grad_mlp = jax.tree.map(jnp.add, grads_0, grads_1)
    grad_heads, grad_attn, grad_qk = jax.tree.map(jnp.add, head_grads_0, head_grads_1)

    grad_qk = jnp.pad(grad_qk[:, None], ((0, 0), (0, rows - 1))).reshape(-1)
    grad_small = jnp.concatenate(
        [grad_router, grad_attn[:, None], grad_mlp[:, None], grad_qk[:, None]], axis=1
    )
    grad_small = jnp.pad(grad_small, ((0, 0), (0, 128 - grad_small.shape[1])))
    grad_pack = jnp.concatenate([grad_heads, grad_small], axis=1).astype(BF)
    grad_pack = exchange(grad_pack.reshape(n_all, rows, -1), ALL).astype(F32)
    own_heads = jnp.sum(grad_pack[:, :, :span].reshape(n_ctx, n_fsdp, rows, -1), axis=1)
    own_heads = own_heads.transpose(1, 0, 2)
    own_small = jnp.sum(grad_pack[:, :, span:], axis=0)
    grad_out = grad_out.astype(BF).reshape(n_all // 2, 2, rows, width)
    grad_own = lax.dynamic_index_in_dim(grad_out, core, axis=1, keepdims=False)
    grad_other = lax.dynamic_index_in_dim(grad_out, 1 - core, axis=1, keepdims=False)
    own_out = sum_parts(exchange(back_sum(grad_own, grad_other), CTX + GROUP))
    moe_1 = sum_parts(exchange(moe_1, GROUP))
    expert_own = expert_own.astype(F32).reshape((local, 3) + expert_own.shape[1:])
    outs = [
        (forward[0][1] + moe_0.astype(F32)).astype(BF),
        (forward[1][1] + moe_1).astype(BF),
    ]
    d_inputs = [
        input_grad(0, sum_parts(d_hidden_0), d_middle_0),
        input_grad(1, sum_parts(d_hidden_1), d_middle_1),
    ]

    return (
        jnp.stack(outs)[:, None],
        jnp.stack(d_inputs)[:, None],
        own_heads[:, :, :heads].reshape(rows, -1),
        own_heads[:, :, heads : heads + DH].reshape(rows, -1),
        own_heads[:, :, heads + DH :].reshape(rows, -1),
        own_out,
        own_small[:, :experts],
        own_small[:, experts],
        own_small[:, experts + 1],
        own_small[:1, experts + 2],
        expert_own[:, 0],
        expert_own[:, 1],
        expert_own[:, 2],
    )


def solution(mesh):
    mesh = Mesh(mesh.devices.reshape(4, 2, 2, 4, 2), ALL)
    weight = P(ALL, None)
    gain = P(ALL)
    rows = P(None, FSDP, CTX, None)
    expert = P(FSDP, CTX, None)
    return jax.shard_map(
        body,
        mesh=mesh,
        in_specs=(rows, P(None, FSDP, None), rows)
        + (weight,) * 5
        + (gain,) * 3
        + (expert,) * 3
        + (rows,),
        out_specs=(rows, rows) + (weight,) * 5 + (gain,) * 3 + (expert,) * 3,
        check_vma=False,
    )
```

```python
import functools

import jax
import jax.numpy as jnp
from jax import lax
from jax.experimental import pallas as pl
from jax.experimental.pallas import tpu as pltpu
from jax.sharding import Mesh
from jax.sharding import PartitionSpec as P

BF = jnp.bfloat16
F32 = jnp.float32
H = 16
KV = 8
DH = 64
TOPK = 8
WINDOW = 1024
EPS = 1e-06
THETA = 10000.0


def dot(a, b, ca, cb):
    return lax.dot_general(a, b, (((ca,), (cb,)), ((), ())), preferred_element_type=F32)


def lanes_of(v):
    return lax.broadcasted_iota(jnp.int32, v.shape, v.ndim - 1)


def head_sums(v):
    low = lanes_of(v) < DH
    first = jnp.sum(jnp.where(low, v, 0.0), axis=1, keepdims=True)
    second = jnp.sum(jnp.where(low, 0.0, v), axis=1, keepdims=True)
    return jnp.where(low, first, second)


def trade(v):
    return jnp.where(
        lanes_of(v) % DH < DH // 2, pltpu.roll(v, 128 - DH // 2, 1), pltpu.roll(v, DH // 2, 1)
    )


def both_halves(v, second):
    low = lanes_of(v) < DH
    other = pltpu.roll(v, DH, 1)
    return jnp.where(low, other, v) if second else jnp.where(low, v, other)


def stack_heads(v):
    low = lanes_of(v) < DH
    zero = jnp.zeros_like(v)
    return jnp.concatenate([jnp.where(low, v, zero), jnp.where(low, zero, v)], axis=0)


def key_span(start, block, length):
    reach = WINDOW // 2 - 1
    low = max(0, start - reach) // 128 * 128
    high = min(length, -(-(start + block + reach) // 128) * 128)
    return low, high


def masked_probs(q_two, keys, seg_col, seg_row, start, low):
    block = q_two.shape[0] // 2
    scores = dot(q_two, keys, 1, 1)
    shape = (block, keys.shape[0])
    gap = (
        lax.broadcasted_iota(jnp.int32, shape, 0)
        - lax.broadcasted_iota(jnp.int32, shape, 1)
        + (start - low)
    )
    allowed = (seg_col == seg_row) & (jnp.abs(gap) < WINDOW // 2)
    bias = jnp.where(allowed, 0.0, -1e30)
    scores = scores + jnp.concatenate([bias, bias], axis=0)
    raised = jnp.exp(scores - jnp.max(scores, axis=1, keepdims=True))
    return raised * (1.0 / jnp.sum(raised, axis=1, keepdims=True))


def attend_kernel(
    order_ref,
    own_ref,
    after_ref,
    far_low_ref,
    far_high_ref,
    before_ref,
    gain_ref,
    w_ref,
    head_gain_ref,
    cos_ref,
    sin_ref,
    seg_col_ref,
    seg_row_ref,
    mixed_ref,
    hidden_ref,
    q_ref,
    kv_ref,
    keys_ref,
    values_ref,
):
    tok, width = own_ref.shape[1:]
    length = hidden_ref.shape[0]
    pieces = [
        (own_ref, 0),
        (own_ref, 1),
        (after_ref, 0),
        (after_ref, 1),
        (far_low_ref, 0),
        (far_high_ref, 0),
        (before_ref, 0),
        (before_ref, 1),
    ]
    for r, (ref, i) in enumerate(pieces):
        x = ref[i].astype(F32)
        x = x * lax.rsqrt(jnp.mean(x * x, axis=1, keepdims=True) + EPS) * gain_ref[...]
        rows = pl.ds(pl.multiple_of(order_ref[r] * tok, tok), tok)
        hidden_ref[rows] = x.astype(BF)
    raw = dot(hidden_ref[...], w_ref[...], 1, 0)
    for half in range(2):
        u = raw[:, half * 128 : half * 128 + 128]
        gain = head_gain_ref[:, half * 128 : half * 128 + 128]
        n = u * lax.rsqrt(head_sums(u * u) * (1.0 / DH) + EPS) * gain
        turned = n * cos_ref[...] + trade(n) * sin_ref[...]
        if half == 0:
            q_ref[...] = turned.astype(BF)
        else:
            kv = jnp.where(lanes_of(u) < DH, turned, u)
            kv_ref[...] = kv.astype(BF)
            keys_ref[...] = both_halves(kv, False).astype(BF)
            values_ref[...] = both_halves(kv, True).astype(BF)
    block = 256
    for start in range(0, length, block):
        low, high = key_span(start, block, length)
        q_two = stack_heads(q_ref[start : start + block].astype(F32) * DH**-0.5).astype(BF)
        probs = masked_probs(
            q_two,
            keys_ref[low:high],
            seg_col_ref[start : start + block],
            seg_row_ref[:, low:high],
            start,
            low,
        )
        result = dot(probs.astype(BF), values_ref[low:high], 1, 0)
        first = lanes_of(result[:block]) < DH
        mixed_ref[start : start + block] = jnp.where(first, result[:block], result[block:]).astype(
            BF
        )


def attend_back_kernel(
    hidden_ref,
    q_ref,
    kv_ref,
    d_mixed_ref,
    gain_ref,
    w_ref,
    head_gain_ref,
    cos_ref,
    sin_ref,
    seg_col_ref,
    seg_row_ref,
    d_hidden_ref,
    grad_w_ref,
    grad_gain_ref,
    grad_heads_ref,
    keys_ref,
    values_ref,
    d_q_ref,
    d_k_ref,
    d_v_ref,
    d_raw_ref,
):
    length = hidden_ref.shape[0]
    kv = kv_ref[...].astype(F32)
    keys_ref[...] = both_halves(kv, False).astype(BF)
    values_ref[...] = both_halves(kv, True).astype(BF)
    d_k_ref[...] = jnp.zeros_like(d_k_ref)
    d_v_ref[...] = jnp.zeros_like(d_v_ref)
    block = 256
    for start in range(0, length, block):
        low, high = key_span(start, block, length)
        q_two = stack_heads(q_ref[start : start + block].astype(F32) * DH**-0.5).astype(BF)
        m_two = stack_heads(d_mixed_ref[start : start + block].astype(F32)).astype(BF)
        probs = masked_probs(
            q_two,
            keys_ref[low:high],
            seg_col_ref[start : start + block],
            seg_row_ref[:, low:high],
            start,
            low,
        )
        d_probs = dot(m_two, values_ref[low:high], 1, 1)
        inner = jnp.sum(probs * d_probs, axis=1, keepdims=True)
        d_scores = (probs * (d_probs - inner)).astype(BF)
        result = dot(d_scores, keys_ref[low:high], 1, 0)
        first = lanes_of(result[:block]) < DH
        d_q_ref[start : start + block] = jnp.where(first, result[:block], result[block:]) * (
            DH**-0.5
        )
        d_k_ref[low:high] += dot(d_scores, q_two, 0, 0)
        d_v_ref[low:high] += dot(probs.astype(BF), m_two, 0, 0)
    raw = dot(hidden_ref[...], w_ref[...], 1, 0)
    d_k = d_k_ref[...]
    d_k = d_k + pltpu.roll(d_k, DH, 1)
    d_v = d_v_ref[...]
    d_v = d_v + pltpu.roll(d_v, DH, 1)
    for half in range(2):
        lanes = slice(half * 128, half * 128 + 128)
        u = raw[:, lanes]
        gain = head_gain_ref[:, lanes]
        d = d_q_ref[...] if half == 0 else d_k
        d = d * cos_ref[...] + trade(d * sin_ref[...])
        r = lax.rsqrt(head_sums(u * u) * (1.0 / DH) + EPS)
        grad_heads_ref[:, lanes] = jnp.sum(d * u * r, axis=0, keepdims=True)
        d = d * gain
        d = d * r - u * (r * r * r * (head_sums(d * u) * (1.0 / DH)))
        if half == 1:
            d = jnp.where(lanes_of(d) < DH, d, d_v)
        d_raw_ref[:, lanes] = d.astype(BF)
    grad_w_ref[...] = dot(hidden_ref[...], d_raw_ref[...], 0, 0)
    total = jnp.zeros(grad_gain_ref.shape, F32)
    for start in range(0, length, block):
        rows = slice(start, start + block)
        d_hidden = dot(d_raw_ref[rows], w_ref[...], 1, 1)
        d_hidden_ref[rows] = d_hidden.astype(BF)
        total = total + jnp.sum(d_hidden * hidden_ref[rows].astype(F32), axis=0, keepdims=True)
    grad_gain_ref[...] = total / gain_ref[...]


def whole(a):
    return pl.BlockSpec(a.shape, lambda i: (0,) * len(a.shape), pipeline_mode=pl.Buffered(1))


def attend_forward(order, pieces, gain, w_heads, head_gain, cosine, sine, seg_col, seg_row):
    length = cosine.shape[0]
    width = w_heads.shape[0]
    shape = jax.ShapeDtypeStruct
    outs = [
        shape((length, 128), BF),
        shape((length, width), BF),
        shape((length, 128), BF),
        shape((length, 128), BF),
    ]
    args = list(pieces) + [gain, w_heads, head_gain, cosine, sine, seg_col, seg_row]
    return pl.pallas_call(
        attend_kernel,
        out_shape=outs,
        grid=(1,),
        in_specs=[pl.BlockSpec(memory_space=pltpu.SMEM)] + [whole(a) for a in args],
        out_specs=[whole(o) for o in outs],
        scratch_shapes=[pltpu.VMEM((length, 128), BF), pltpu.VMEM((length, 128), BF)],
        compiler_params=pltpu.CompilerParams(vmem_limit_bytes=40 * 1024 * 1024),
        cost_estimate=pl.CostEstimate(flops=12 * 10**9, bytes_accessed=8 << 20, transcendentals=0),
    )(order, *args)


def attend_backward(
    hidden, q, kv, d_mixed, gain, w_heads, head_gain, cosine, sine, seg_col, seg_row
):
    length, width = hidden.shape
    shape = jax.ShapeDtypeStruct
    outs = [
        shape((length, width), BF),
        shape((width, 256), F32),
        shape((1, width), F32),
        shape((1, 256), F32),
    ]
    args = [hidden, q, kv, d_mixed, gain, w_heads, head_gain, cosine, sine, seg_col, seg_row]
    return pl.pallas_call(
        attend_back_kernel,
        out_shape=outs,
        grid=(1,),
        in_specs=[whole(a) for a in args],
        out_specs=[whole(o) for o in outs],
        scratch_shapes=[pltpu.VMEM((length, 128), BF)] * 2
        + [pltpu.VMEM((length, 128), F32)] * 3
        + [pltpu.VMEM((length, 256), BF)],
        compiler_params=pltpu.CompilerParams(vmem_limit_bytes=40 * 1024 * 1024),
        cost_estimate=pl.CostEstimate(flops=25 * 10**9, bytes_accessed=8 << 20, transcendentals=0),
    )(*args)


def halves(v):
    high = v.astype(BF)
    return high, (v - high.astype(F32)).astype(BF)


def expert_kernel(scalar_ref, *refs):
    x_own_ref, x_other_ref, g_ref, router_ref = refs[:4]
    pieces, refs = refs[4:12], refs[12:]
    out_ref, back_own_ref, back_other_ref, xe_ref, de_ref, act_ref, da_ref, db_ref = refs[:8]
    pick_ref, weight_ref, dgate_ref, eo_ref, dr_ref, w_ref = refs[8:]
    half, tok, width = x_own_ref.shape
    sources = 2 * half
    core = scalar_ref[1]
    depth = w_ref.shape[2] // 8

    for r, ref in enumerate(pieces):
        rows = pl.ds(pl.multiple_of(scalar_ref[2 + r] * depth, depth), depth)
        w_ref[:, :, rows] = ref[...]
    local, slots, hidden = act_ref.shape
    cap = slots // sources
    first = scalar_ref[0]
    lane = lax.broadcasted_iota(jnp.int32, (tok, 128), 1)
    spot = lax.broadcasted_iota(jnp.int32, (tok, local * cap), 1)
    row_expert = lax.broadcasted_iota(jnp.int32, (local * cap, 128), 0) // cap
    slot_lane = lax.broadcasted_iota(jnp.int32, (local * cap, 128), 1)
    own_lane = slot_lane == first + row_expert

    def fetch(i, carry, x_ref, offset, column):
        s = i + offset
        x = x_ref[i]
        from_g = 2 * i + column
        held = g_ref[from_g, :, width:].astype(F32)
        chosen = held >= 0.0
        logits = jnp.where(chosen, dot(x, router_ref[...], 1, 0), -1e30)
        top = jnp.max(logits, axis=1, keepdims=True)
        raised = jnp.where(chosen, jnp.exp(logits - top), 0.0)
        gates = raised / jnp.sum(raised, axis=1, keepdims=True)
        pick = jnp.zeros((tok, local * cap), F32)
        for e in range(local):
            mine = jnp.max(jnp.where(lane == first + e, held, -1.0), axis=1, keepdims=True)
            goal = jnp.where(mine >= 0.0, mine + e * cap, -1.0).astype(jnp.int32)
            pick = jnp.where(spot == goal, 1.0, pick)
        pick = pick.astype(BF)
        pick_ref[s] = pick
        rows = pl.ds(pl.multiple_of(s * cap, 16), cap)
        x_slots = dot(pick, x, 0, 0).astype(BF)
        g_slots = dot(pick, g_ref[from_g, :, :width], 0, 0).astype(BF)
        high, low = halves(gates)
        weight = dot(pick, high, 0, 0) + dot(pick, low, 0, 0)
        weight = jnp.sum(jnp.where(own_lane, weight, 0.0), axis=1, keepdims=True)
        for e in range(local):
            part = slice(e * cap, (e + 1) * cap)
            xe_ref[e, rows] = x_slots[part]
            de_ref[e, rows] = g_slots[part]
            weight_ref[e, rows] = weight[part]
        return carry

    for x_ref, offset, column in ((x_own_ref, 0, core), (x_other_ref, half, 1 - core)):
        lax.fori_loop(
            0, half, functools.partial(fetch, x_ref=x_ref, offset=offset, column=column), 0
        )
    chunk = 256

    def work(i, carry):
        e = i // (slots // chunk)
        rows = pl.ds(pl.multiple_of((i % (slots // chunk)) * chunk, chunk), chunk)
        w_gate = w_ref[e, 0]
        w_up = w_ref[e, 1]
        w_down = w_ref[e, 2]
        x = xe_ref[e, rows]
        a = dot(x, w_gate, 1, 0)
        b = dot(x, w_up, 1, 0)
        sig = 1.0 / (1.0 + jnp.exp(-a))
        silu = a * sig
        active = (silu * b).astype(BF)
        act_ref[e, rows] = active
        slope = b * (sig * (1.0 + a * (1.0 - sig)))
        weight = weight_ref[e, rows]
        g = de_ref[e, rows].astype(F32)
        result = dot(active, w_down, 1, 1).astype(BF).astype(F32)
        dgate_ref[e, rows] = jnp.sum(result * g, axis=1, keepdims=True)
        eo_ref[e, rows] = (weight * result).astype(BF)
        d_expert = (weight * g).astype(BF)
        de_ref[e, rows] = d_expert
        d_active = dot(d_expert, w_down, 1, 0)
        da = (d_active * slope).astype(BF)
        db = (d_active * silu).astype(BF)
        da_ref[e, rows] = da
        db_ref[e, rows] = db
        dr_ref[e, rows] = (dot(da, w_gate, 1, 1) + dot(db, w_up, 1, 1)).astype(BF)
        return carry

    lax.fori_loop(0, local * (slots // chunk), work, 0)

    def give(i, carry, back_ref, offset, column):
        s = i + offset
        rows = pl.ds(pl.multiple_of(s * cap, 16), cap)
        pick = pick_ref[s]
        eo = jnp.concatenate([eo_ref[e, rows] for e in range(local)], axis=0)
        dr = jnp.concatenate([dr_ref[e, rows] for e in range(local)], axis=0)
        dgate = jnp.concatenate([dgate_ref[e, rows] for e in range(local)], axis=0)
        high, low = halves(dgate)
        spread = jnp.where(own_lane, high.astype(F32), 0.0) + jnp.where(
            slot_lane == first + row_expert + 64, low.astype(F32), 0.0
        )
        out_ref[2 * i + column] = dot(pick, eo, 1, 0).astype(BF)
        back_ref[i, :, :width] = dot(pick, dr, 1, 0).astype(BF)
        back_ref[i, :, width:] = dot(pick, spread.astype(BF), 1, 0).astype(BF)
        return carry

    for back_ref, offset, column in ((back_own_ref, 0, core), (back_other_ref, half, 1 - core)):
        lax.fori_loop(
            0, half, functools.partial(give, back_ref=back_ref, offset=offset, column=column), 0
        )


def run_experts(scalars, x_own, x_other, g_all, micro, router, pieces, cap):
    half, tok, width = x_own.shape
    sources = 2 * half
    local, _, _, hidden = pieces[0].shape
    slots = sources * cap
    wide = g_all.shape[2]
    shape = jax.ShapeDtypeStruct
    outs = [
        shape((sources, tok, width), BF),
        shape((half, tok, wide), BF),
        shape((half, tok, wide), BF),
        shape((local, slots, width), BF),
        shape((local, slots, width), BF),
        shape((local, slots, hidden), BF),
        shape((local, slots, hidden), BF),
        shape((local, slots, hidden), BF),
    ]
    g_spec = pl.BlockSpec(
        (sources, tok, wide), lambda i: (0, micro, 0), pipeline_mode=pl.Buffered(1)
    )
    args = [router, *pieces]
    return pl.pallas_call(
        expert_kernel,
        out_shape=outs,
        grid=(1,),
        in_specs=[pl.BlockSpec(memory_space=pltpu.SMEM), whole(x_own), whole(x_other), g_spec]
        + [whole(a) for a in args],
        out_specs=[whole(o) for o in outs],
        scratch_shapes=[
            pltpu.VMEM((sources, tok, local * cap), BF),
            pltpu.VMEM((local, slots, 1), F32),
            pltpu.VMEM((local, slots, 1), F32),
            pltpu.VMEM((local, slots, width), BF),
            pltpu.VMEM((local, slots, width), BF),
            pltpu.VMEM((local, 3, width, hidden), BF),
        ],
        compiler_params=pltpu.CompilerParams(vmem_limit_bytes=60 * 1024 * 1024),
        cost_estimate=pl.CostEstimate(flops=40 * 10**9, bytes_accessed=40 << 20, transcendentals=0),
    )(scalars, x_own, x_other, g_all, *args)


def expert_grad_kernel(order_ref, *refs):
    kept, outs, total_ref = refs[:10], refs[10:16], refs[16]
    left = (kept[0:2], kept[0:2], kept[2:4])
    right = (kept[6:8], kept[8:10], kept[4:6])
    own_ref, other_ref = outs[:2]
    step = pl.program_id(0)
    depth = own_ref.shape[2]
    for kind in range(3):

        @pl.when(step % 3 == kind)
        def _(kind=kind):
            total = dot(left[kind][0][0], right[kind][0][0], 0, 0)
            total_ref[...] = total + dot(left[kind][1][0], right[kind][1][0], 0, 0)

    def part(r):
        rows = pl.ds(pl.multiple_of(order_ref[r] * depth, depth), depth)
        return total_ref[rows].astype(BF)

    @pl.when(step < 3)
    def _():
        for r in range(8):
            (own_ref, other_ref)[r % 2][r // 2, 0] = part(r)

    @pl.when(step >= 3)
    def _():
        for r in range(8):
            outs[2 + r // 2][r % 2, 0] = part(r)


def expert_grads(order, kept):
    local, slots, width = kept[0][0].shape
    hidden = kept[0][2].shape[2]
    args = [kept[m][i] for i in range(5) for m in range(2)]
    depth = width // 8
    shape = jax.ShapeDtypeStruct
    return pl.pallas_call(
        expert_grad_kernel,
        out_shape=[shape((4, 3, depth, hidden), BF)] * 2 + [shape((2, 3, depth, hidden), BF)] * 4,
        grid=(6,),
        in_specs=[pl.BlockSpec(memory_space=pltpu.SMEM)]
        + [pl.BlockSpec((1,) + a.shape[1:], lambda i: (i // 3, 0, 0)) for a in args],
        out_specs=[pl.BlockSpec((4, 1, depth, hidden), lambda i: (0, jnp.minimum(i, 2), 0, 0))] * 2
        + [pl.BlockSpec((2, 1, depth, hidden), lambda i: (0, jnp.maximum(i - 3, 0), 0, 0))] * 4,
        scratch_shapes=[pltpu.VMEM((width, hidden), F32)],
        compiler_params=pltpu.CompilerParams(vmem_limit_bytes=48 * 1024 * 1024),
        cost_estimate=pl.CostEstimate(flops=14 * 10**9, bytes_accessed=28 << 20, transcendentals=0),
    )(order, *args)


CTX = ("z", "yl")
GROUP = ("yh", "x")
FSDP = ("yh", "x", "core")
ALL = CTX + FSDP
UP = [(i, (i + 1) % 4) for i in range(4)]
DOWN = [(i, (i - 1) % 4) for i in range(4)]
TWO = [(i, (i + 2) % 4) for i in range(4)]
FLIP = [(0, 1), (1, 0)]


def mm(a, b):
    return jnp.dot(a, b, preferred_element_type=F32)


def mm_t(a, b):
    return lax.dot_general(a, b, (((1,), (1,)), ((), ())), preferred_element_type=F32)


def t_mm(a, b):
    return lax.dot_general(a, b, (((0,), (0,)), ((), ())), preferred_element_type=F32)


def ein(spec, a, b):
    return jnp.einsum(spec, a, b, preferred_element_type=F32)


def swap(parts, axis):
    return lax.all_to_all(parts, axis, split_axis=0, concat_axis=0, tiled=True)


def flip(block, axis):
    return lax.ppermute(block, axis, FLIP)


def ring_of(both):
    before = lax.ppermute(both, "z", UP)
    after = lax.ppermute(both, "z", DOWN)
    far_low = lax.ppermute(before[:1], "z", UP)
    far_high = lax.ppermute(after[1:], "z", DOWN)
    return [both, after, far_low, far_high, before]


class Exchange:
    def __init__(self):
        self.last = None

    def __call__(self, parts, axis):
        if self.last is not None:
            parts = after_all(parts, self.last)
        self.last = swap(parts, axis)
        return self.last

    def copies(self, block, axis, count):
        return self(jnp.broadcast_to(block[None], (count,) + block.shape), axis)


def add(a, b):
    return (a.astype(F32) + b.astype(F32)).astype(BF)


def sum_parts(parts):
    return jnp.sum(parts.astype(F32), axis=0)


def after_all(value, *others):
    return lax.optimization_barrier((value,) + others)[0]


def rope_tables(positions):
    half = DH // 2
    inverse = THETA ** (-(jnp.arange(half, dtype=F32) * 2.0) / DH)
    angles = positions.astype(F32)[:, None] * inverse[None, :]
    return (jnp.cos(angles), jnp.sin(angles))


def rms_scale(values, gain):
    return values * lax.rsqrt(jnp.mean(values * values, axis=-1, keepdims=True) + EPS) * gain


def body(
    tokens,
    segments,
    routes,
    w_query,
    w_key,
    w_value,
    w_out,
    w_router,
    attn_gain,
    mlp_gain,
    qk_gain,
    w_gate,
    w_up,
    w_down,
    cotangent,
):
    micro = tokens.shape[0]
    tok = tokens.shape[2]
    width = tokens.shape[3]
    length = segments.shape[2]
    rows = w_query.shape[0]
    n_ctx, n_fsdp = 8, 16
    n_all = n_ctx * n_fsdp
    z, yl, yh, x, core = (lax.axis_index(name) for name in ALL)
    shard = (yh * 4 + x) * 2 + core
    local = w_gate.shape[0]
    experts = local * n_fsdp
    cap = (3 * tok * TOPK + 2 * experts - 1) // (2 * experts)
    all_tok = micro * tok
    ratio = H // KV
    heads = ratio * DH
    span = heads + 2 * DH

    exchange = Exchange()
    small = jnp.concatenate(
        [
            w_router,
            attn_gain[:, None],
            mlp_gain[:, None],
            jnp.pad(qk_gain[:, None], ((0, rows - 1), (0, 0))),
        ],
        axis=1,
    )
    small = jnp.pad(small, ((0, 0), (0, 128 - small.shape[1])))
    pieces = jnp.concatenate(
        [
            w_query.reshape(rows, n_ctx, heads),
            w_key.reshape(rows, n_ctx, DH),
            w_value.reshape(rows, n_ctx, DH),
            jnp.broadcast_to(small[:, None], (rows, n_ctx, 128)),
        ],
        axis=2,
    ).transpose(1, 0, 2)
    pieces = jnp.broadcast_to(pieces[:, None], (n_ctx, n_fsdp) + pieces.shape[1:])
    both_0 = jnp.concatenate([tokens[0], flip(tokens[0], "yl")], axis=0)
    pieces = after_all(pieces, both_0)
    head_all = exchange(pieces.reshape((n_all,) + pieces.shape[2:]), ALL).reshape(width, -1)
    seq_rows = [ring_of(both_0)]
    head_all = after_all(head_all, seq_rows[0][1], seq_rows[0][4])
    w_heads = head_all[:, :span]
    small_all = head_all[:, span:]
    router = small_all[:, :experts]
    small_wide = small_all.astype(F32)
    gain_attn = small_wide[:, experts]
    gain_mlp = small_wide[:, experts + 1]
    gain_heads = small_wide[:, experts + 2].reshape(-1, rows)[:, 0]
    gain_row = gain_attn[None]
    head_row = jnp.concatenate(
        [gain_heads[:DH]] * ratio + [gain_heads[DH:], jnp.ones((DH,), F32)]
    )[None]
    router_pad = jnp.pad(router, ((0, 0), (0, 128 - experts)))

    own = exchange.copies(w_out, CTX + GROUP, n_all // 2)
    other = flip(own, "core")
    out_full = jnp.where(
        core == 0, jnp.stack([own, other], axis=1), jnp.stack([other, own], axis=1)
    ).reshape(width, width)

    stack = jnp.stack([w_gate, w_up, w_down], axis=1)
    by_yl = flip(stack, "yl")
    stack_z = after_all(stack, *seq_rows[0][1:])
    by_up = lax.ppermute(stack_z, "z", UP)
    by_down = lax.ppermute(stack_z, "z", DOWN)
    both_1 = jnp.concatenate([tokens[1], flip(tokens[1], "yl")], axis=0)
    seq_rows.append(ring_of(after_all(both_1, by_up, by_down)))
    by_two = lax.ppermute(after_all(stack, seq_rows[1][1], seq_rows[1][4]), "z", TWO)
    by_up_yl = flip(by_up, "yl")
    by_down_yl = flip(by_down, "yl")
    by_two_yl = flip(by_two, "yl")
    pieces = [stack, by_yl, by_down, by_down_yl, by_two, by_two_yl, by_up, by_up_yl]

    expert_ids = jnp.arange(experts, dtype=jnp.int32)
    cot = cotangent.reshape(all_tok, width)
    chosen = jnp.any(routes.reshape(all_tok, TOPK)[:, :, None] == expert_ids, axis=1)
    before = jnp.arange(tok, dtype=jnp.int32)
    lower = (before[:, None] >= before[None, :]).astype(BF)
    counts = ein("ut,mte->mue", lower, chosen.reshape(micro, tok, experts).astype(BF))
    held = jnp.where(chosen, counts.reshape(all_tok, experts) - 1.0, -1.0)
    held = jnp.pad(held, ((0, 0), (0, 128 - experts)), constant_values=-1.0).astype(BF)
    g_all = lax.all_gather(jnp.concatenate([cot, held], axis=1), FSDP, axis=0)

    cosine, sine = rope_tables(jnp.arange(length, dtype=jnp.int32))
    cosine = jnp.tile(cosine, (1, 4))
    sine = jnp.tile(jnp.concatenate([-sine, sine], axis=1), (1, 2))
    rel = jnp.arange(n_ctx, dtype=jnp.int32)
    order = ((z + rel // 2) % 4) * 2 + (yl + rel % 2) % 2
    scalars = jnp.concatenate([jnp.stack([shard * local, core]), order]).astype(jnp.int32)

    def to_owner(v):
        return exchange(v.reshape(n_ctx, tok, -1), CTX)

    def attention_args(m):
        seg = segments[m, 0]
        return gain_row, w_heads, head_row, cosine, sine, seg[:, None], seg[None, :]

    forward, saved = [], []
    for m in range(micro):
        mixed_h, *keep = attend_forward(order, seq_rows[m], *attention_args(m))
        saved.append(keep)
        if m == 0:
            mixed_h = after_all(mixed_h, by_up, by_down)
        else:
            mixed_h = after_all(mixed_h, by_two, by_down_yl)
        mixed = to_owner(mixed_h).transpose(1, 0, 2).reshape(tok, width)
        start = tokens[m, 0].astype(F32)
        middle = start + mm(mixed, out_full)
        normed, norm_back = jax.vjp(rms_scale, middle, gain_mlp)
        hidden_two = normed.astype(BF)
        chosen_m = chosen[m * tok : (m + 1) * tok]
        logits = jnp.where(chosen_m, mm(hidden_two, router), -1e30)
        gates = jnp.where(chosen_m, jax.nn.softmax(logits, axis=-1), 0.0)
        if m == 0:
            hidden_two_x = after_all(hidden_two, seq_rows[1][1], seq_rows[1][4], by_up_yl)
        else:
            hidden_two_x = hidden_two
        x_own = exchange.copies(hidden_two_x, GROUP, n_ctx)
        forward.append((mixed, middle, norm_back, hidden_two, gates, x_own))

    def experts_of(m, x_own):
        return run_experts(
            scalars,
            x_own,
            flip(x_own, "core"),
            g_all,
            m,
            router_pad,
            pieces,
            cap,
        )

    def back_sum(own, other):
        return add(own, flip(other, "core"))

    def middle_back(m, back):
        mixed, middle, norm_back, hidden_two, gates = forward[m][:5]
        grad_top = cot[m * tok : (m + 1) * tok].astype(F32)
        tail = back[:, width:]
        d_gates = tail[:, :experts] + tail[:, 64 : 64 + experts]
        d_select = gates * (d_gates - jnp.sum(gates * d_gates, axis=-1, keepdims=True))
        d_logits = d_select.astype(BF)
        grad_router = t_mm(hidden_two, d_logits)
        d_two = back[:, :width] + mm_t(d_logits, router)
        d_middle, grad_mlp = norm_back(d_two)
        d_middle = d_middle + grad_top
        d_branch = d_middle.astype(BF)
        grad_out = t_mm(mixed, d_branch)
        d_mixed = mm_t(d_branch, out_full).astype(BF)
        d_mixed = d_mixed.reshape(tok, n_ctx, heads).transpose(1, 0, 2)
        return d_middle, d_mixed, (grad_out, grad_router, grad_mlp)

    def attention_back(m, d_mixed):
        d_hidden, grad_heads, grad_attn, grad_qk = attend_backward(
            *saved[m], d_mixed.reshape(length, heads), *attention_args(m)
        )
        grad_qk = jnp.concatenate(
            [grad_qk[0, :DH] + grad_qk[0, DH : 2 * DH], grad_qk[0, 2 * DH : 3 * DH]]
        )
        return d_hidden, (grad_heads, grad_attn[0], grad_qk)

    def input_grad(m, d_hidden, d_middle):
        start = tokens[m, 0].astype(F32)
        inverse = lax.rsqrt(jnp.mean(start * start, axis=-1, keepdims=True) + EPS)
        u = d_hidden * gain_attn
        return (
            d_middle
            + inverse * u
            - start * (inverse**3 * jnp.mean(u * start, axis=-1, keepdims=True))
        )

    moe_0, back_own, back_other, *kept_0 = experts_of(0, forward[0][5])
    x_1, back_own, back_other, moe_0 = lax.optimization_barrier(
        (forward[1][5], back_own, back_other, moe_0)
    )
    back_0 = back_sum(back_own, back_other)
    moe_0 = lax.psum_scatter(moe_0, FSDP, scatter_dimension=0, tiled=True)[0]
    x_1 = after_all(x_1, back_0)
    back_0 = exchange(back_0, GROUP)
    moe_1, back_own, back_other, *kept_1 = experts_of(1, x_1)
    back_0, back_own, back_other, moe_1 = lax.optimization_barrier(
        (back_0, back_own, back_other, moe_1)
    )
    back_1 = back_sum(back_own, back_other)
    d_middle_0, d_mixed_0, grads_0 = middle_back(0, sum_parts(back_0))
    d_mixed_0 = exchange(d_mixed_0, CTX)
    kept_1[0], back_1 = lax.optimization_barrier((kept_1[0], back_1))
    kept_1[0] = after_all(kept_1[0], d_mixed_0)
    back_1 = exchange(back_1, GROUP)
    own_0, other_0, *parts_1 = expert_grads(order, (kept_0, kept_1))
    d_hidden_0, head_grads_0 = attention_back(0, d_mixed_0)
    back_1, d_hidden_0, own_0, other_0, parts_1 = lax.optimization_barrier(
        (back_1, d_hidden_0, own_0, other_0, parts_1)
    )
    other_0 = flip(other_0, "yl")
    from_up = lax.ppermute(parts_1[1], "z", UP)
    from_down = lax.ppermute(parts_1[3], "z", DOWN)
    from_two = lax.ppermute(parts_1[2], "z", TWO)
    d_middle_1, d_mixed_1, grads_1 = middle_back(1, sum_parts(back_1))
    d_mixed_1, moe_0 = lax.optimization_barrier((d_mixed_1, moe_0))
    moe_1 = after_all(moe_1, moe_0)
    moe_1 = lax.psum_scatter(moe_1, FSDP, scatter_dimension=0, tiled=True)[0]
    d_mixed_1 = exchange(d_mixed_1, CTX)
    d_hidden_0 = to_owner(d_hidden_0)
    d_hidden_1, head_grads_1 = attention_back(1, d_mixed_1)
    d_hidden_0, d_hidden_1, other_0, from_up, from_down = lax.optimization_barrier(
        (d_hidden_0, d_hidden_1, other_0, from_up, from_down)
    )
    own_0 = [add(own_0[k], other_0[k]) for k in range(4)]
    from_up_0 = lax.ppermute(own_0[1], "z", UP)
    from_down_0 = lax.ppermute(own_0[3], "z", DOWN)
    d_hidden_1 = to_owner(d_hidden_1)
    grad_out, grad_router, grad_mlp = jax.tree.map(jnp.add, grads_0, grads_1)
    grad_heads, grad_attn, grad_qk = jax.tree.map(jnp.add, head_grads_0, head_grads_1)
    d_hidden_1, from_two, from_up_0, from_down_0 = lax.optimization_barrier(
        (d_hidden_1, from_two, from_up_0, from_down_0)
    )
    from_two_0 = lax.ppermute(own_0[2], "z", TWO)
    second = [
        sum(part[i].astype(F32) for part in (parts_1[0], from_up, from_down, from_two))
        for i in range(2)
    ]
    from_yl = flip(second[1].astype(BF), "yl")

    grad_out = grad_out.astype(BF).reshape(n_all // 2, 2, rows, width)
    grad_own = lax.dynamic_index_in_dim(grad_out, core, axis=1, keepdims=False)
    grad_other = lax.dynamic_index_in_dim(grad_out, 1 - core, axis=1, keepdims=False)
    own_out = sum_parts(exchange(back_sum(grad_own, grad_other), CTX + GROUP))
    grad_qk = jnp.pad(grad_qk[:, None], ((0, 0), (0, rows - 1))).reshape(-1)
    grad_small = jnp.concatenate(
        [grad_router, grad_attn[:, None], grad_mlp[:, None], grad_qk[:, None]], axis=1
    )
    grad_small = jnp.pad(grad_small, ((0, 0), (0, 128 - grad_small.shape[1])))
    grad_pack = jnp.concatenate([grad_heads, grad_small], axis=1).astype(BF)
    grad_pack = exchange(grad_pack.reshape(n_all, rows, -1), ALL).astype(F32)
    own_heads = jnp.sum(grad_pack[:, :, :span].reshape(n_ctx, n_fsdp, rows, -1), axis=1)
    own_heads = own_heads.transpose(1, 0, 2)
    own_small = jnp.sum(grad_pack[:, :, span:], axis=0)
    expert_own = [
        sum(part.astype(F32) for part in (own_0[0], from_up_0, from_down_0, from_two_0)),
        second[0] + from_yl.astype(F32),
    ]
    outs = [
        (forward[0][1] + moe_0.astype(F32)).astype(BF),
        (forward[1][1] + moe_1.astype(F32)).astype(BF),
    ]
    d_inputs = [
        input_grad(0, sum_parts(d_hidden_0), d_middle_0),
        input_grad(1, sum_parts(d_hidden_1), d_middle_1),
    ]

    return (
        jnp.stack(outs)[:, None],
        jnp.stack(d_inputs)[:, None],
        own_heads[:, :, :heads].reshape(rows, -1),
        own_heads[:, :, heads : heads + DH].reshape(rows, -1),
        own_heads[:, :, heads + DH :].reshape(rows, -1),
        own_out,
        own_small[:, :experts],
        own_small[:, experts],
        own_small[:, experts + 1],
        own_small[:1, experts + 2],
        jnp.stack([part[0] for part in expert_own]),
        jnp.stack([part[1] for part in expert_own]),
        jnp.stack([part[2] for part in expert_own]),
    )


def solution(mesh):
    mesh = Mesh(mesh.devices.reshape(4, 2, 2, 4, 2), ALL)
    weight = P(ALL, None)
    gain = P(ALL)
    rows = P(None, FSDP, CTX, None)
    expert = P(FSDP, CTX, None)
    return jax.shard_map(
        body,
        mesh=mesh,
        in_specs=(rows, P(None, FSDP, None), rows)
        + (weight,) * 5
        + (gain,) * 3
        + (expert,) * 3
        + (rows,),
        out_specs=(rows, rows) + (weight,) * 5 + (gain,) * 3 + (expert,) * 3,
        check_vma=False,
    )
```

```python
import functools

import jax
import jax.numpy as jnp
from jax import lax
from jax.experimental import pallas as pl
from jax.experimental.pallas import tpu as pltpu
from jax.sharding import Mesh
from jax.sharding import PartitionSpec as P

BF = jnp.bfloat16
F32 = jnp.float32
H = 16
KV = 8
DH = 64
TOPK = 8
WINDOW = 1024
EPS = 1e-06
THETA = 10000.0


def dot(a, b, ca, cb):
    return lax.dot_general(a, b, (((ca,), (cb,)), ((), ())), preferred_element_type=F32)


def lanes_of(v):
    return lax.broadcasted_iota(jnp.int32, v.shape, v.ndim - 1)


def head_sums(v):
    low = lanes_of(v) < DH
    first = jnp.sum(jnp.where(low, v, 0.0), axis=1, keepdims=True)
    second = jnp.sum(jnp.where(low, 0.0, v), axis=1, keepdims=True)
    return jnp.where(low, first, second)


def trade(v):
    return jnp.where(
        lanes_of(v) % DH < DH // 2, pltpu.roll(v, 128 - DH // 2, 1), pltpu.roll(v, DH // 2, 1)
    )


def both_halves(v, second):
    low = lanes_of(v) < DH
    other = pltpu.roll(v, DH, 1)
    return jnp.where(low, other, v) if second else jnp.where(low, v, other)


def stack_heads(v):
    low = lanes_of(v) < DH
    zero = jnp.zeros_like(v)
    return jnp.concatenate([jnp.where(low, v, zero), jnp.where(low, zero, v)], axis=0)


def key_span(start, block, length):
    reach = WINDOW // 2 - 1
    low = max(0, start - reach) // 128 * 128
    high = min(length, -(-(start + block + reach) // 128) * 128)
    return low, high


def masked_probs(q_two, keys, seg_col, seg_row, start, low):
    block = q_two.shape[0] // 2
    scores = dot(q_two, keys, 1, 1)
    shape = (block, keys.shape[0])
    gap = (
        lax.broadcasted_iota(jnp.int32, shape, 0)
        - lax.broadcasted_iota(jnp.int32, shape, 1)
        + (start - low)
    )
    allowed = (seg_col == seg_row) & (jnp.abs(gap) < WINDOW // 2)
    bias = jnp.where(allowed, 0.0, -1e30)
    scores = scores + jnp.concatenate([bias, bias], axis=0)
    raised = jnp.exp(scores - jnp.max(scores, axis=1, keepdims=True))
    return raised * (1.0 / jnp.sum(raised, axis=1, keepdims=True))


def attend_kernel(
    order_ref,
    own_ref,
    after_ref,
    far_ref,
    before_ref,
    gain_ref,
    w_ref,
    head_gain_ref,
    cos_ref,
    sin_ref,
    seg_col_ref,
    seg_row_ref,
    mixed_ref,
    hidden_ref,
    q_ref,
    kv_ref,
    keys_ref,
    values_ref,
):
    tok, width = own_ref.shape[1:]
    length = hidden_ref.shape[0]
    pieces = [
        (own_ref, 0),
        (own_ref, 1),
        (after_ref, 0),
        (after_ref, 1),
        (far_ref, 0),
        (far_ref, 1),
        (before_ref, 0),
        (before_ref, 1),
    ]
    for r, (ref, i) in enumerate(pieces):
        x = ref[i].astype(F32)
        x = x * lax.rsqrt(jnp.mean(x * x, axis=1, keepdims=True) + EPS) * gain_ref[...]
        rows = pl.ds(pl.multiple_of(order_ref[r] * tok, tok), tok)
        hidden_ref[rows] = x.astype(BF)
    raw = dot(hidden_ref[...], w_ref[...], 1, 0)
    for half in range(2):
        u = raw[:, half * 128 : half * 128 + 128]
        gain = head_gain_ref[:, half * 128 : half * 128 + 128]
        n = u * lax.rsqrt(head_sums(u * u) * (1.0 / DH) + EPS) * gain
        turned = n * cos_ref[...] + trade(n) * sin_ref[...]
        if half == 0:
            q_ref[...] = turned.astype(BF)
        else:
            kv = jnp.where(lanes_of(u) < DH, turned, u)
            kv_ref[...] = kv.astype(BF)
            keys_ref[...] = both_halves(kv, False).astype(BF)
            values_ref[...] = both_halves(kv, True).astype(BF)
    block = 256
    for start in range(0, length, block):
        low, high = key_span(start, block, length)
        q_two = stack_heads(q_ref[start : start + block].astype(F32) * DH**-0.5).astype(BF)
        probs = masked_probs(
            q_two,
            keys_ref[low:high],
            seg_col_ref[start : start + block],
            seg_row_ref[:, low:high],
            start,
            low,
        )
        result = dot(probs.astype(BF), values_ref[low:high], 1, 0)
        first = lanes_of(result[:block]) < DH
        mixed_ref[start : start + block] = jnp.where(first, result[:block], result[block:]).astype(
            BF
        )


def attend_back_kernel(
    hidden_ref,
    q_ref,
    kv_ref,
    d_mixed_ref,
    gain_ref,
    w_ref,
    head_gain_ref,
    cos_ref,
    sin_ref,
    seg_col_ref,
    seg_row_ref,
    d_hidden_ref,
    grad_w_ref,
    grad_gain_ref,
    grad_heads_ref,
    keys_ref,
    values_ref,
    d_q_ref,
    d_k_ref,
    d_v_ref,
    d_raw_ref,
):
    length = hidden_ref.shape[0]
    kv = kv_ref[...].astype(F32)
    keys_ref[...] = both_halves(kv, False).astype(BF)
    values_ref[...] = both_halves(kv, True).astype(BF)
    d_k_ref[...] = jnp.zeros_like(d_k_ref)
    d_v_ref[...] = jnp.zeros_like(d_v_ref)
    block = 256
    for start in range(0, length, block):
        low, high = key_span(start, block, length)
        q_two = stack_heads(q_ref[start : start + block].astype(F32) * DH**-0.5).astype(BF)
        m_two = stack_heads(d_mixed_ref[start : start + block].astype(F32)).astype(BF)
        probs = masked_probs(
            q_two,
            keys_ref[low:high],
            seg_col_ref[start : start + block],
            seg_row_ref[:, low:high],
            start,
            low,
        )
        d_probs = dot(m_two, values_ref[low:high], 1, 1)
        inner = jnp.sum(probs * d_probs, axis=1, keepdims=True)
        d_scores = (probs * (d_probs - inner)).astype(BF)
        result = dot(d_scores, keys_ref[low:high], 1, 0)
        first = lanes_of(result[:block]) < DH
        d_q_ref[start : start + block] = jnp.where(first, result[:block], result[block:]) * (
            DH**-0.5
        )
        d_k_ref[low:high] += dot(d_scores, q_two, 0, 0)
        d_v_ref[low:high] += dot(probs.astype(BF), m_two, 0, 0)
    raw = dot(hidden_ref[...], w_ref[...], 1, 0)
    d_k = d_k_ref[...]
    d_k = d_k + pltpu.roll(d_k, DH, 1)
    d_v = d_v_ref[...]
    d_v = d_v + pltpu.roll(d_v, DH, 1)
    for half in range(2):
        lanes = slice(half * 128, half * 128 + 128)
        u = raw[:, lanes]
        gain = head_gain_ref[:, lanes]
        d = d_q_ref[...] if half == 0 else d_k
        d = d * cos_ref[...] + trade(d * sin_ref[...])
        r = lax.rsqrt(head_sums(u * u) * (1.0 / DH) + EPS)
        grad_heads_ref[:, lanes] = jnp.sum(d * u * r, axis=0, keepdims=True)
        d = d * gain
        d = d * r - u * (r * r * r * (head_sums(d * u) * (1.0 / DH)))
        if half == 1:
            d = jnp.where(lanes_of(d) < DH, d, d_v)
        d_raw_ref[:, lanes] = d.astype(BF)
    grad_w_ref[...] = dot(hidden_ref[...], d_raw_ref[...], 0, 0)
    total = jnp.zeros(grad_gain_ref.shape, F32)
    for start in range(0, length, block):
        rows = slice(start, start + block)
        d_hidden = dot(d_raw_ref[rows], w_ref[...], 1, 1)
        d_hidden_ref[rows] = d_hidden.astype(BF)
        total = total + jnp.sum(d_hidden * hidden_ref[rows].astype(F32), axis=0, keepdims=True)
    grad_gain_ref[...] = total / gain_ref[...]


def whole(a):
    return pl.BlockSpec(a.shape, lambda i: (0,) * len(a.shape), pipeline_mode=pl.Buffered(1))


def attend_forward(order, pieces, gain, w_heads, head_gain, cosine, sine, seg_col, seg_row):
    length = cosine.shape[0]
    width = w_heads.shape[0]
    shape = jax.ShapeDtypeStruct
    outs = [
        shape((length, 128), BF),
        shape((length, width), BF),
        shape((length, 128), BF),
        shape((length, 128), BF),
    ]
    args = list(pieces) + [gain, w_heads, head_gain, cosine, sine, seg_col, seg_row]
    return pl.pallas_call(
        attend_kernel,
        out_shape=outs,
        grid=(1,),
        in_specs=[pl.BlockSpec(memory_space=pltpu.SMEM)] + [whole(a) for a in args],
        out_specs=[whole(o) for o in outs],
        scratch_shapes=[pltpu.VMEM((length, 128), BF), pltpu.VMEM((length, 128), BF)],
        compiler_params=pltpu.CompilerParams(vmem_limit_bytes=40 * 1024 * 1024),
        cost_estimate=pl.CostEstimate(flops=12 * 10**9, bytes_accessed=8 << 20, transcendentals=0),
    )(order, *args)


def attend_backward(
    hidden, q, kv, d_mixed, gain, w_heads, head_gain, cosine, sine, seg_col, seg_row
):
    length, width = hidden.shape
    shape = jax.ShapeDtypeStruct
    outs = [
        shape((length, width), BF),
        shape((width, 256), F32),
        shape((1, width), F32),
        shape((1, 256), F32),
    ]
    args = [hidden, q, kv, d_mixed, gain, w_heads, head_gain, cosine, sine, seg_col, seg_row]
    return pl.pallas_call(
        attend_back_kernel,
        out_shape=outs,
        grid=(1,),
        in_specs=[whole(a) for a in args],
        out_specs=[whole(o) for o in outs],
        scratch_shapes=[pltpu.VMEM((length, 128), BF)] * 2
        + [pltpu.VMEM((length, 128), F32)] * 3
        + [pltpu.VMEM((length, 256), BF)],
        compiler_params=pltpu.CompilerParams(vmem_limit_bytes=40 * 1024 * 1024),
        cost_estimate=pl.CostEstimate(flops=25 * 10**9, bytes_accessed=8 << 20, transcendentals=0),
    )(*args)


def halves(v):
    high = v.astype(BF)
    return high, (v - high.astype(F32)).astype(BF)


def expert_kernel(scalar_ref, *refs, joined):
    x_own_ref, x_other_ref, g_ref, router_ref = refs[:4]
    pieces, refs = refs[4:8], refs[8:]
    outs, refs = (refs[:1], refs[1:]) if joined else (refs[:2], refs[2:])
    back_own_ref, back_other_ref, xe_ref, de_ref, act_ref, da_ref, db_ref = refs[:7]
    pick_ref, weight_ref, dgate_ref, eo_ref, dr_ref, w_ref = refs[7:]
    half, tok, width = x_own_ref.shape
    sources = 2 * half
    core = scalar_ref[1]
    depth = w_ref.shape[2] // 8

    for r in range(8):
        rows = pl.ds(pl.multiple_of(scalar_ref[2 + r] * depth, depth), depth)
        w_ref[:, :, rows] = pieces[r // 2][r % 2]
    local, slots, hidden = act_ref.shape
    cap = slots // sources
    first = scalar_ref[0]
    lane = lax.broadcasted_iota(jnp.int32, (tok, 128), 1)
    spot = lax.broadcasted_iota(jnp.int32, (tok, local * cap), 1)
    row_expert = lax.broadcasted_iota(jnp.int32, (local * cap, 128), 0) // cap
    slot_lane = lax.broadcasted_iota(jnp.int32, (local * cap, 128), 1)
    own_lane = slot_lane == first + row_expert

    def fetch(i, carry, x_ref, offset, column):
        s = i + offset
        x = x_ref[i]
        from_g = 2 * i + column
        held = g_ref[from_g, :, width:].astype(F32)
        chosen = held >= 0.0
        logits = jnp.where(chosen, dot(x, router_ref[...], 1, 0), -1e30)
        top = jnp.max(logits, axis=1, keepdims=True)
        raised = jnp.where(chosen, jnp.exp(logits - top), 0.0)
        gates = raised / jnp.sum(raised, axis=1, keepdims=True)
        pick = jnp.zeros((tok, local * cap), F32)
        for e in range(local):
            mine = jnp.max(jnp.where(lane == first + e, held, -1.0), axis=1, keepdims=True)
            goal = jnp.where(mine >= 0.0, mine + e * cap, -1.0).astype(jnp.int32)
            pick = jnp.where(spot == goal, 1.0, pick)
        pick = pick.astype(BF)
        pick_ref[s] = pick
        rows = pl.ds(pl.multiple_of(s * cap, 16), cap)
        x_slots = dot(pick, x, 0, 0).astype(BF)
        g_slots = dot(pick, g_ref[from_g, :, :width], 0, 0).astype(BF)
        high, low = halves(gates)
        weight = dot(pick, high, 0, 0) + dot(pick, low, 0, 0)
        weight = jnp.sum(jnp.where(own_lane, weight, 0.0), axis=1, keepdims=True)
        for e in range(local):
            part = slice(e * cap, (e + 1) * cap)
            xe_ref[e, rows] = x_slots[part]
            de_ref[e, rows] = g_slots[part]
            weight_ref[e, rows] = weight[part]
        return carry

    for x_ref, offset, column in ((x_own_ref, 0, core), (x_other_ref, half, 1 - core)):
        lax.fori_loop(
            0, half, functools.partial(fetch, x_ref=x_ref, offset=offset, column=column), 0
        )
    chunk = 256

    def work(i, carry):
        e = i // (slots // chunk)
        rows = pl.ds(pl.multiple_of((i % (slots // chunk)) * chunk, chunk), chunk)
        w_gate = w_ref[e, 0]
        w_up = w_ref[e, 1]
        w_down = w_ref[e, 2]
        x = xe_ref[e, rows]
        a = dot(x, w_gate, 1, 0)
        b = dot(x, w_up, 1, 0)
        sig = 1.0 / (1.0 + jnp.exp(-a))
        silu = a * sig
        active = (silu * b).astype(BF)
        act_ref[e, rows] = active
        slope = b * (sig * (1.0 + a * (1.0 - sig)))
        weight = weight_ref[e, rows]
        g = de_ref[e, rows].astype(F32)
        result = dot(active, w_down, 1, 1).astype(BF).astype(F32)
        dgate_ref[e, rows] = jnp.sum(result * g, axis=1, keepdims=True)
        eo_ref[e, rows] = (weight * result).astype(BF)
        d_expert = (weight * g).astype(BF)
        de_ref[e, rows] = d_expert
        d_active = dot(d_expert, w_down, 1, 0)
        da = (d_active * slope).astype(BF)
        db = (d_active * silu).astype(BF)
        da_ref[e, rows] = da
        db_ref[e, rows] = db
        dr_ref[e, rows] = (dot(da, w_gate, 1, 1) + dot(db, w_up, 1, 1)).astype(BF)
        return carry

    lax.fori_loop(0, local * (slots // chunk), work, 0)

    def give(i, carry, back_ref, offset, column):
        s = i + offset
        rows = pl.ds(pl.multiple_of(s * cap, 16), cap)
        pick = pick_ref[s]
        eo = jnp.concatenate([eo_ref[e, rows] for e in range(local)], axis=0)
        dr = jnp.concatenate([dr_ref[e, rows] for e in range(local)], axis=0)
        dgate = jnp.concatenate([dgate_ref[e, rows] for e in range(local)], axis=0)
        high, low = halves(dgate)
        spread = jnp.where(own_lane, high.astype(F32), 0.0) + jnp.where(
            slot_lane == first + row_expert + 64, low.astype(F32), 0.0
        )
        if joined:
            outs[0][2 * i + column] = dot(pick, eo, 1, 0).astype(BF)
        else:
            outs[offset // half][scalar_ref[10 + i]] = dot(pick, eo, 1, 0).astype(BF)
        back_ref[i, :, :width] = dot(pick, dr, 1, 0).astype(BF)
        back_ref[i, :, width:] = dot(pick, spread.astype(BF), 1, 0).astype(BF)
        return carry

    for back_ref, offset, column in ((back_own_ref, 0, core), (back_other_ref, half, 1 - core)):
        lax.fori_loop(
            0, half, functools.partial(give, back_ref=back_ref, offset=offset, column=column), 0
        )


def run_experts(scalars, x_own, x_other, g_all, micro, router, pieces, cap, joined):
    half, tok, width = x_own.shape
    sources = 2 * half
    _, local, _, _, hidden = pieces[0].shape
    slots = sources * cap
    wide = g_all.shape[2]
    shape = jax.ShapeDtypeStruct
    outs = [shape((sources, tok, width), BF)] if joined else [shape((half, tok, width), BF)] * 2
    outs += [
        shape((half, tok, wide), BF),
        shape((half, tok, wide), BF),
        shape((local, slots, width), BF),
        shape((local, slots, width), BF),
        shape((local, slots, hidden), BF),
        shape((local, slots, hidden), BF),
        shape((local, slots, hidden), BF),
    ]
    g_spec = pl.BlockSpec(
        (sources, tok, wide), lambda i: (0, micro, 0), pipeline_mode=pl.Buffered(1)
    )
    args = [router, *pieces]
    return pl.pallas_call(
        functools.partial(expert_kernel, joined=joined),
        out_shape=outs,
        grid=(1,),
        in_specs=[pl.BlockSpec(memory_space=pltpu.SMEM), whole(x_own), whole(x_other), g_spec]
        + [whole(a) for a in args],
        out_specs=[whole(o) for o in outs],
        scratch_shapes=[
            pltpu.VMEM((sources, tok, local * cap), BF),
            pltpu.VMEM((local, slots, 1), F32),
            pltpu.VMEM((local, slots, 1), F32),
            pltpu.VMEM((local, slots, width), BF),
            pltpu.VMEM((local, slots, width), BF),
            pltpu.VMEM((local, 3, width, hidden), BF),
        ],
        compiler_params=pltpu.CompilerParams(vmem_limit_bytes=60 * 1024 * 1024),
        cost_estimate=pl.CostEstimate(flops=40 * 10**9, bytes_accessed=40 << 20, transcendentals=0),
    )(scalars, x_own, x_other, g_all, *args)


def expert_grad_kernel(order_ref, *refs):
    kept, outs, total_ref = refs[:10], refs[10:14], refs[14]
    left = (kept[0:2], kept[0:2], kept[2:4])
    right = (kept[6:8], kept[8:10], kept[4:6])
    step = pl.program_id(0)
    depth = outs[0].shape[3]
    for kind in range(3):

        @pl.when(step % 3 == kind)
        def _(kind=kind):
            total = dot(left[kind][0][0], right[kind][0][0], 0, 0)
            total_ref[...] = total + dot(left[kind][1][0], right[kind][1][0], 0, 0)

    for r in range(8):
        rows = pl.ds(pl.multiple_of(order_ref[r] * depth, depth), depth)
        outs[r // 2][r % 2, 0, 0] = total_ref[rows].astype(BF)


def expert_grads(order, kept):
    local, slots, width = kept[0][0].shape
    hidden = kept[0][2].shape[2]
    args = [kept[m][i] for i in range(5) for m in range(2)]
    depth = width // 8
    shape = jax.ShapeDtypeStruct
    return pl.pallas_call(
        expert_grad_kernel,
        out_shape=[shape((2, local, 3, depth, hidden), BF)] * 4,
        grid=(3 * local,),
        in_specs=[pl.BlockSpec(memory_space=pltpu.SMEM)]
        + [pl.BlockSpec((1,) + a.shape[1:], lambda i: (i // 3, 0, 0)) for a in args],
        out_specs=[
            pl.BlockSpec((2, 1, 1, depth, hidden), lambda i: (0, i // 3, i % 3, 0, 0))
        ]
        * 4,
        scratch_shapes=[pltpu.VMEM((width, hidden), F32)],
        compiler_params=pltpu.CompilerParams(vmem_limit_bytes=48 * 1024 * 1024),
        cost_estimate=pl.CostEstimate(flops=14 * 10**9, bytes_accessed=28 << 20, transcendentals=0),
    )(order, *args)


CTX = ("z", "yl")
GROUP = ("yh", "x")
FSDP = ("yh", "x", "core")
ALL = CTX + FSDP
UP = [(i, (i + 1) % 4) for i in range(4)]
DOWN = [(i, (i - 1) % 4) for i in range(4)]
TWO = [(i, (i + 2) % 4) for i in range(4)]
FLIP = [(0, 1), (1, 0)]


def mm(a, b):
    return jnp.dot(a, b, preferred_element_type=F32)


def mm_t(a, b):
    return lax.dot_general(a, b, (((1,), (1,)), ((), ())), preferred_element_type=F32)


def t_mm(a, b):
    return lax.dot_general(a, b, (((0,), (0,)), ((), ())), preferred_element_type=F32)


def ein(spec, a, b):
    return jnp.einsum(spec, a, b, preferred_element_type=F32)


def swap(parts, axis):
    return lax.all_to_all(parts, axis, split_axis=0, concat_axis=0, tiled=True)


def flip(block, axis):
    return lax.ppermute(block, axis, FLIP)


def by_z(parts):
    return [lax.ppermute(parts[k], "z", perm) for k, perm in ((1, UP), (2, TWO), (3, DOWN))]


def along_z(both):
    before, far, after = by_z([both] * 4)
    return [both, after, far, before]


class Exchange:
    def __init__(self):
        self.last = None

    def __call__(self, parts, axis):
        if self.last is not None:
            parts = after_all(parts, self.last)
        self.last = swap(parts, axis)
        return self.last

    def copies(self, block, axis, count):
        return self(jnp.broadcast_to(block[None], (count,) + block.shape), axis)


def add(a, b):
    return (a.astype(F32) + b.astype(F32)).astype(BF)


def by_x(parts):
    return [lax.ppermute(parts[k], "x", perm) for k, perm in ((1, UP), (2, TWO), (3, DOWN))]


def pair_sum(parts, place, axis):
    own = lax.dynamic_index_in_dim(parts, place, 0, keepdims=False)
    other = lax.dynamic_index_in_dim(parts, 1 - place, 0, keepdims=False)
    return own + flip(other.astype(BF), axis).astype(F32)


def sum_parts(parts):
    return jnp.sum(parts.astype(F32), axis=0)


def after_all(value, *others):
    return lax.optimization_barrier((value,) + others)[0]


def rope_tables(positions):
    half = DH // 2
    inverse = THETA ** (-(jnp.arange(half, dtype=F32) * 2.0) / DH)
    angles = positions.astype(F32)[:, None] * inverse[None, :]
    return (jnp.cos(angles), jnp.sin(angles))


def rms_scale(values, gain):
    return values * lax.rsqrt(jnp.mean(values * values, axis=-1, keepdims=True) + EPS) * gain


def body(
    tokens,
    segments,
    routes,
    w_query,
    w_key,
    w_value,
    w_out,
    w_router,
    attn_gain,
    mlp_gain,
    qk_gain,
    w_gate,
    w_up,
    w_down,
    cotangent,
):
    micro = tokens.shape[0]
    tok = tokens.shape[2]
    width = tokens.shape[3]
    length = segments.shape[2]
    rows = w_query.shape[0]
    n_ctx, n_fsdp = 8, 16
    n_all = n_ctx * n_fsdp
    z, yl, yh, x, core = (lax.axis_index(name) for name in ALL)
    shard = (yh * 4 + x) * 2 + core
    local = w_gate.shape[0]
    experts = local * n_fsdp
    cap = (3 * tok * TOPK + 2 * experts - 1) // (2 * experts)
    all_tok = micro * tok
    ratio = H // KV
    heads = ratio * DH
    span = heads + 2 * DH

    exchange = Exchange()
    small = jnp.concatenate(
        [
            w_router,
            attn_gain[:, None],
            mlp_gain[:, None],
            jnp.pad(qk_gain[:, None], ((0, rows - 1), (0, 0))),
        ],
        axis=1,
    )
    small = jnp.pad(small, ((0, 0), (0, 128 - small.shape[1])))
    pieces = jnp.concatenate(
        [
            w_query.reshape(rows, n_ctx, heads),
            w_key.reshape(rows, n_ctx, DH),
            w_value.reshape(rows, n_ctx, DH),
            jnp.broadcast_to(small[:, None], (rows, n_ctx, 128)),
        ],
        axis=2,
    ).transpose(1, 0, 2)
    pieces = jnp.broadcast_to(pieces[:, None], (n_ctx, n_fsdp) + pieces.shape[1:])
    both_0 = jnp.concatenate([tokens[0], flip(tokens[0], "yl")], axis=0)
    both_w = jnp.stack([w_gate, w_up, w_down], axis=1)[None]
    pieces = after_all(pieces, both_0)
    head_all = exchange(pieces.reshape((n_all,) + pieces.shape[2:]), ALL).reshape(width, -1)
    both_w = jnp.concatenate([both_w, flip(both_w, "yl")], axis=0)
    seq_rows = [along_z(both_0)]
    head_all = after_all(head_all, *seq_rows[0][1:], both_w)
    w_heads = head_all[:, :span]
    small_all = head_all[:, span:]
    router = small_all[:, :experts]
    small_wide = small_all.astype(F32)
    gain_attn = small_wide[:, experts]
    gain_mlp = small_wide[:, experts + 1]
    gain_heads = small_wide[:, experts + 2].reshape(-1, rows)[:, 0]
    gain_row = gain_attn[None]
    head_row = jnp.concatenate(
        [gain_heads[:DH]] * ratio + [gain_heads[DH:], jnp.ones((DH,), F32)]
    )[None]
    router_pad = jnp.pad(router, ((0, 0), (0, 128 - experts)))

    own = exchange.copies(w_out, CTX + GROUP, n_all // 2)
    other = flip(own, "core")
    out_full = jnp.where(
        core == 0, jnp.stack([own, other], axis=1), jnp.stack([other, own], axis=1)
    ).reshape(width, width)

    weights = along_z(both_w)
    both_1 = jnp.concatenate([tokens[1], flip(tokens[1], "yl")], axis=0)
    seq_rows.append(along_z(after_all(both_1, *seq_rows[0][1:])))

    expert_ids = jnp.arange(experts, dtype=jnp.int32)
    cot = cotangent.reshape(all_tok, width)
    chosen = jnp.any(routes.reshape(all_tok, TOPK)[:, :, None] == expert_ids, axis=1)
    before = jnp.arange(tok, dtype=jnp.int32)
    lower = (before[:, None] >= before[None, :]).astype(BF)
    counts = ein("ut,mte->mue", lower, chosen.reshape(micro, tok, experts).astype(BF))
    held = jnp.where(chosen, counts.reshape(all_tok, experts) - 1.0, -1.0)
    held = jnp.pad(held, ((0, 0), (0, 128 - experts)), constant_values=-1.0).astype(BF)
    g_all = lax.all_gather(jnp.concatenate([cot, held], axis=1), FSDP, axis=0)

    cosine, sine = rope_tables(jnp.arange(length, dtype=jnp.int32))
    cosine = jnp.tile(cosine, (1, 4))
    sine = jnp.tile(jnp.concatenate([-sine, sine], axis=1), (1, 2))
    rel = jnp.arange(n_ctx, dtype=jnp.int32)
    order = ((z + rel // 2) % 4) * 2 + (yl + rel % 2) % 2
    g_rel = ((rel % 4 - x) % 4) * 2 + (rel // 4 - yh) % 2
    scalars = jnp.concatenate([jnp.stack([shard * local, core]), order, g_rel]).astype(jnp.int32)

    def to_owner(v):
        return exchange(v.reshape(n_ctx, tok, -1), CTX)

    def z_swap(v):
        return exchange(v.reshape(4, 2, tok, width), "z")

    def attention_args(m):
        seg = segments[m, 0]
        return gain_row, w_heads, head_row, cosine, sine, seg[:, None], seg[None, :]

    forward, saved = [], []
    for m in range(micro):
        mixed_h, *keep = attend_forward(order, seq_rows[m], *attention_args(m))
        saved.append(keep)
        if m == 0:
            mixed_h = after_all(mixed_h, *seq_rows[1][1:])
        else:
            mixed_h = after_all(mixed_h, weights[2])
        mixed = to_owner(mixed_h).transpose(1, 0, 2).reshape(tok, width)
        start = tokens[m, 0].astype(F32)
        middle = start + mm(mixed, out_full)
        normed, norm_back = jax.vjp(rms_scale, middle, gain_mlp)
        hidden_two = normed.astype(BF)
        chosen_m = chosen[m * tok : (m + 1) * tok]
        logits = jnp.where(chosen_m, mm(hidden_two, router), -1e30)
        gates = jnp.where(chosen_m, jax.nn.softmax(logits, axis=-1), 0.0)
        if m == 0:
            hidden_two_x = after_all(hidden_two, weights[1], weights[3])
        else:
            hidden_two_x = hidden_two
        x_own = exchange.copies(hidden_two_x, GROUP, n_ctx)
        forward.append((mixed, middle, norm_back, hidden_two, gates, x_own))

    def experts_of(m, x_own):
        return run_experts(
            scalars,
            x_own,
            flip(x_own, "core"),
            g_all,
            m,
            router_pad,
            weights,
            cap,
            m == 0,
        )

    def back_sum(own, other):
        return add(own, flip(other, "core"))

    def middle_back(m, back):
        mixed, middle, norm_back, hidden_two, gates = forward[m][:5]
        grad_top = cot[m * tok : (m + 1) * tok].astype(F32)
        tail = back[:, width:]
        d_gates = tail[:, :experts] + tail[:, 64 : 64 + experts]
        d_select = gates * (d_gates - jnp.sum(gates * d_gates, axis=-1, keepdims=True))
        d_logits = d_select.astype(BF)
        grad_router = t_mm(hidden_two, d_logits)
        d_two = back[:, :width] + mm_t(d_logits, router)
        d_middle, grad_mlp = norm_back(d_two)
        d_middle = d_middle + grad_top
        d_branch = d_middle.astype(BF)
        grad_out = t_mm(mixed, d_branch)
        d_mixed = mm_t(d_branch, out_full).astype(BF)
        d_mixed = d_mixed.reshape(tok, n_ctx, heads).transpose(1, 0, 2)
        return d_middle, d_mixed, (grad_out, grad_router, grad_mlp)

    def attention_back(m, d_mixed):
        d_hidden, grad_heads, grad_attn, grad_qk = attend_backward(
            *saved[m], d_mixed.reshape(length, heads), *attention_args(m)
        )
        grad_qk = jnp.concatenate(
            [grad_qk[0, :DH] + grad_qk[0, DH : 2 * DH], grad_qk[0, 2 * DH : 3 * DH]]
        )
        return d_hidden, (grad_heads, grad_attn[0], grad_qk)

    def input_grad(m, d_hidden, d_middle):
        start = tokens[m, 0].astype(F32)
        inverse = lax.rsqrt(jnp.mean(start * start, axis=-1, keepdims=True) + EPS)
        u = d_hidden * gain_attn
        return (
            d_middle
            + inverse * u
            - start * (inverse**3 * jnp.mean(u * start, axis=-1, keepdims=True))
        )

    moe_0, back_own, back_other, *kept_0 = experts_of(0, forward[0][5])
    x_1, back_own, back_other, moe_0 = lax.optimization_barrier(
        (forward[1][5], back_own, back_other, moe_0)
    )
    back_0 = back_sum(back_own, back_other)
    moe_0 = lax.psum_scatter(moe_0, FSDP, scatter_dimension=0, tiled=True)[0]
    x_1 = after_all(x_1, back_0)
    back_0 = exchange(back_0, GROUP)
    moe_own, moe_other, back_own, back_other, *kept_1 = experts_of(1, x_1)
    back_0, back_own, back_other, moe_own, moe_other = lax.optimization_barrier(
        (back_0, back_own, back_other, moe_own, moe_other)
    )
    back_1 = back_sum(back_own, back_other)
    d_middle_0, d_mixed_0, grads_0 = middle_back(0, sum_parts(back_0))
    d_mixed_0 = exchange(d_mixed_0, CTX)
    d_mixed_0, back_1 = lax.optimization_barrier((d_mixed_0, back_1))
    kept_1[0] = after_all(kept_1[0], d_mixed_0)
    back_1 = exchange(back_1, GROUP)
    weight_parts = expert_grads(order, (kept_0, kept_1))
    d_hidden_0, head_grads_0 = attention_back(0, d_mixed_0)
    moe_other = flip(moe_other, "core")
    back_1, d_hidden_0, weight_parts, moe_other = lax.optimization_barrier(
        (back_1, d_hidden_0, weight_parts, moe_other)
    )
    moe_1 = [add(moe_own[2 * k : 2 * k + 2], moe_other[2 * k : 2 * k + 2]) for k in range(4)]
    weight_moved = by_z(weight_parts)
    d_middle_1, d_mixed_1, grads_1 = middle_back(1, sum_parts(back_1))
    d_mixed_1 = exchange(d_mixed_1, CTX)
    d_hidden_0 = z_swap(d_hidden_0)
    d_hidden_1, head_grads_1 = attention_back(1, d_mixed_1)
    moe_moved = by_x(moe_1)
    d_hidden_0, d_hidden_1, weight_moved[0], weight_moved[2], moe_moved = (
        lax.optimization_barrier(
            (d_hidden_0, d_hidden_1, weight_moved[0], weight_moved[2], moe_moved)
        )
    )
    d_hidden_1 = z_swap(d_hidden_1)
    d_hidden_0 = pair_sum(sum_parts(d_hidden_0), yl, "yl")
    moe_1 = sum(part.astype(F32) for part in [moe_1[0]] + moe_moved)
    moe_1 = moe_1[0] + flip(moe_1[1].astype(BF), "yh").astype(F32)
    grad_out, grad_router, grad_mlp = jax.tree.map(jnp.add, grads_0, grads_1)
    grad_heads, grad_attn, grad_qk = jax.tree.map(jnp.add, head_grads_0, head_grads_1)
    d_hidden_1, weight_moved[1], moe_1 = lax.optimization_barrier(
        (d_hidden_1, weight_moved[1], moe_1)
    )
    second = [
        sum(part[i].astype(F32) for part in [weight_parts[0]] + weight_moved) for i in range(2)
    ]
    from_yl = flip(second[1].astype(BF), "yl")
    d_hidden_1 = pair_sum(sum_parts(d_hidden_1), yl, "yl")

    grad_out = grad_out.astype(BF).reshape(n_all // 2, 2, rows, width)
    grad_own = lax.dynamic_index_in_dim(grad_out, core, axis=1, keepdims=False)
    grad_other = lax.dynamic_index_in_dim(grad_out, 1 - core, axis=1, keepdims=False)
    own_out = sum_parts(exchange(back_sum(grad_own, grad_other), CTX + GROUP))
    grad_qk = jnp.pad(grad_qk[:, None], ((0, 0), (0, rows - 1))).reshape(-1)
    grad_small = jnp.concatenate(
        [grad_router, grad_attn[:, None], grad_mlp[:, None], grad_qk[:, None]], axis=1
    )
    grad_small = jnp.pad(grad_small, ((0, 0), (0, 128 - grad_small.shape[1])))
    grad_pack = jnp.concatenate([grad_heads, grad_small], axis=1).astype(BF)
    grad_pack = exchange(grad_pack.reshape(n_all, rows, -1), ALL).astype(F32)
    own_heads = jnp.sum(grad_pack[:, :, :span].reshape(n_ctx, n_fsdp, rows, -1), axis=1)
    own_heads = own_heads.transpose(1, 0, 2)
    own_small = jnp.sum(grad_pack[:, :, span:], axis=0)
    expert_own = second[0] + from_yl.astype(F32)
    outs = [
        (forward[0][1] + moe_0.astype(F32)).astype(BF),
        (forward[1][1] + moe_1).astype(BF),
    ]
    d_inputs = [
        input_grad(0, d_hidden_0, d_middle_0),
        input_grad(1, d_hidden_1, d_middle_1),
    ]

    return (
        jnp.stack(outs)[:, None],
        jnp.stack(d_inputs)[:, None],
        own_heads[:, :, :heads].reshape(rows, -1),
        own_heads[:, :, heads : heads + DH].reshape(rows, -1),
        own_heads[:, :, heads + DH :].reshape(rows, -1),
        own_out,
        own_small[:, :experts],
        own_small[:, experts],
        own_small[:, experts + 1],
        own_small[:1, experts + 2],
        expert_own[:, 0],
        expert_own[:, 1],
        expert_own[:, 2],
    )


def solution(mesh):
    mesh = Mesh(mesh.devices.reshape(4, 2, 2, 4, 2), ALL)
    weight = P(ALL, None)
    gain = P(ALL)
    rows = P(None, FSDP, CTX, None)
    expert = P(FSDP, CTX, None)
    return jax.shard_map(
        body,
        mesh=mesh,
        in_specs=(rows, P(None, FSDP, None), rows)
        + (weight,) * 5
        + (gain,) * 3
        + (expert,) * 3
        + (rows,),
        out_specs=(rows, rows) + (weight,) * 5 + (gain,) * 3 + (expert,) * 3,
        check_vma=False,
    )
```

```python
import functools

import jax
import jax.numpy as jnp
from jax import lax
from jax.experimental import pallas as pl
from jax.experimental.pallas import tpu as pltpu
from jax.sharding import Mesh
from jax.sharding import PartitionSpec as P

BF = jnp.bfloat16
F32 = jnp.float32
H = 16
KV = 8
DH = 64
TOPK = 8
WINDOW = 1024
EPS = 1e-06
THETA = 10000.0


def dot(a, b, ca, cb):
    return lax.dot_general(a, b, (((ca,), (cb,)), ((), ())), preferred_element_type=F32)


def lanes_of(v):
    return lax.broadcasted_iota(jnp.int32, v.shape, v.ndim - 1)


def head_sums(v):
    low = lanes_of(v) < DH
    first = jnp.sum(jnp.where(low, v, 0.0), axis=1, keepdims=True)
    second = jnp.sum(jnp.where(low, 0.0, v), axis=1, keepdims=True)
    return jnp.where(low, first, second)


def trade(v):
    return jnp.where(
        lanes_of(v) % DH < DH // 2, pltpu.roll(v, 128 - DH // 2, 1), pltpu.roll(v, DH // 2, 1)
    )


def both_halves(v, second):
    low = lanes_of(v) < DH
    other = pltpu.roll(v, DH, 1)
    return jnp.where(low, other, v) if second else jnp.where(low, v, other)


def stack_heads(v):
    low = lanes_of(v) < DH
    zero = jnp.zeros_like(v)
    return jnp.concatenate([jnp.where(low, v, zero), jnp.where(low, zero, v)], axis=0)


def key_span(start, block, length):
    reach = WINDOW // 2 - 1
    low = max(0, start - reach) // 128 * 128
    high = min(length, -(-(start + block + reach) // 128) * 128)
    return low, high


def masked_probs(q_two, keys, seg_col, seg_row, start, low):
    block = q_two.shape[0] // 2
    scores = dot(q_two, keys, 1, 1)
    shape = (block, keys.shape[0])
    gap = (
        lax.broadcasted_iota(jnp.int32, shape, 0)
        - lax.broadcasted_iota(jnp.int32, shape, 1)
        + (start - low)
    )
    allowed = (seg_col == seg_row) & (jnp.abs(gap) < WINDOW // 2)
    bias = jnp.where(allowed, 0.0, -1e30)
    scores = scores + jnp.concatenate([bias, bias], axis=0)
    raised = jnp.exp(scores - jnp.max(scores, axis=1, keepdims=True))
    return raised * (1.0 / jnp.sum(raised, axis=1, keepdims=True))


def attend_kernel(
    order_ref,
    *refs,
):
    pieces, refs = refs[:-13], refs[-13:]
    gain_ref, w_ref, head_gain_ref, cos_ref, sin_ref, seg_col_ref, seg_row_ref = refs[:7]
    mixed_ref, hidden_ref, q_ref, kv_ref, keys_ref, values_ref = refs[7:]
    tok, width = pieces[0].shape[1:]
    length = hidden_ref.shape[0]
    pieces = [(ref, i) for ref in pieces for i in range(ref.shape[0])]
    for r, (ref, i) in enumerate(pieces):
        x = ref[i].astype(F32)
        x = x * lax.rsqrt(jnp.mean(x * x, axis=1, keepdims=True) + EPS) * gain_ref[...]
        rows = pl.ds(pl.multiple_of(order_ref[r] * tok, tok), tok)
        hidden_ref[rows] = x.astype(BF)
    raw = dot(hidden_ref[...], w_ref[...], 1, 0)
    for half in range(2):
        u = raw[:, half * 128 : half * 128 + 128]
        gain = head_gain_ref[:, half * 128 : half * 128 + 128]
        n = u * lax.rsqrt(head_sums(u * u) * (1.0 / DH) + EPS) * gain
        turned = n * cos_ref[...] + trade(n) * sin_ref[...]
        if half == 0:
            q_ref[...] = turned.astype(BF)
        else:
            kv = jnp.where(lanes_of(u) < DH, turned, u)
            kv_ref[...] = kv.astype(BF)
            keys_ref[...] = both_halves(kv, False).astype(BF)
            values_ref[...] = both_halves(kv, True).astype(BF)
    block = 256
    for start in range(0, length, block):
        low, high = key_span(start, block, length)
        q_two = stack_heads(q_ref[start : start + block].astype(F32) * DH**-0.5).astype(BF)
        probs = masked_probs(
            q_two,
            keys_ref[low:high],
            seg_col_ref[start : start + block],
            seg_row_ref[:, low:high],
            start,
            low,
        )
        result = dot(probs.astype(BF), values_ref[low:high], 1, 0)
        first = lanes_of(result[:block]) < DH
        mixed_ref[start : start + block] = jnp.where(first, result[:block], result[block:]).astype(
            BF
        )


def attend_back_kernel(
    hidden_ref,
    q_ref,
    kv_ref,
    d_mixed_ref,
    gain_ref,
    w_ref,
    head_gain_ref,
    cos_ref,
    sin_ref,
    seg_col_ref,
    seg_row_ref,
    d_hidden_ref,
    grad_w_ref,
    grad_gain_ref,
    grad_heads_ref,
    keys_ref,
    values_ref,
    d_q_ref,
    d_k_ref,
    d_v_ref,
    d_raw_ref,
):
    length = hidden_ref.shape[0]
    kv = kv_ref[...].astype(F32)
    keys_ref[...] = both_halves(kv, False).astype(BF)
    values_ref[...] = both_halves(kv, True).astype(BF)
    d_k_ref[...] = jnp.zeros_like(d_k_ref)
    d_v_ref[...] = jnp.zeros_like(d_v_ref)
    block = 256
    for start in range(0, length, block):
        low, high = key_span(start, block, length)
        q_two = stack_heads(q_ref[start : start + block].astype(F32) * DH**-0.5).astype(BF)
        m_two = stack_heads(d_mixed_ref[start : start + block].astype(F32)).astype(BF)
        probs = masked_probs(
            q_two,
            keys_ref[low:high],
            seg_col_ref[start : start + block],
            seg_row_ref[:, low:high],
            start,
            low,
        )
        d_probs = dot(m_two, values_ref[low:high], 1, 1)
        inner = jnp.sum(probs * d_probs, axis=1, keepdims=True)
        d_scores = (probs * (d_probs - inner)).astype(BF)
        result = dot(d_scores, keys_ref[low:high], 1, 0)
        first = lanes_of(result[:block]) < DH
        d_q_ref[start : start + block] = jnp.where(first, result[:block], result[block:]) * (
            DH**-0.5
        )
        d_k_ref[low:high] += dot(d_scores, q_two, 0, 0)
        d_v_ref[low:high] += dot(probs.astype(BF), m_two, 0, 0)
    raw = dot(hidden_ref[...], w_ref[...], 1, 0)
    d_k = d_k_ref[...]
    d_k = d_k + pltpu.roll(d_k, DH, 1)
    d_v = d_v_ref[...]
    d_v = d_v + pltpu.roll(d_v, DH, 1)
    for half in range(2):
        lanes = slice(half * 128, half * 128 + 128)
        u = raw[:, lanes]
        gain = head_gain_ref[:, lanes]
        d = d_q_ref[...] if half == 0 else d_k
        d = d * cos_ref[...] + trade(d * sin_ref[...])
        r = lax.rsqrt(head_sums(u * u) * (1.0 / DH) + EPS)
        grad_heads_ref[:, lanes] = jnp.sum(d * u * r, axis=0, keepdims=True)
        d = d * gain
        d = d * r - u * (r * r * r * (head_sums(d * u) * (1.0 / DH)))
        if half == 1:
            d = jnp.where(lanes_of(d) < DH, d, d_v)
        d_raw_ref[:, lanes] = d.astype(BF)
    grad_w_ref[...] = dot(hidden_ref[...], d_raw_ref[...], 0, 0)
    total = jnp.zeros(grad_gain_ref.shape, F32)
    for start in range(0, length, block):
        rows = slice(start, start + block)
        d_hidden = dot(d_raw_ref[rows], w_ref[...], 1, 1)
        d_hidden_ref[rows] = d_hidden.astype(BF)
        total = total + jnp.sum(d_hidden * hidden_ref[rows].astype(F32), axis=0, keepdims=True)
    grad_gain_ref[...] = total / gain_ref[...]


def whole(a):
    return pl.BlockSpec(a.shape, lambda i: (0,) * len(a.shape), pipeline_mode=pl.Buffered(1))


def attend_forward(order, pieces, gain, w_heads, head_gain, cosine, sine, seg_col, seg_row):
    length = cosine.shape[0]
    width = w_heads.shape[0]
    shape = jax.ShapeDtypeStruct
    outs = [
        shape((length, 128), BF),
        shape((length, width), BF),
        shape((length, 128), BF),
        shape((length, 128), BF),
    ]
    args = list(pieces) + [gain, w_heads, head_gain, cosine, sine, seg_col, seg_row]
    return pl.pallas_call(
        attend_kernel,
        out_shape=outs,
        grid=(1,),
        in_specs=[pl.BlockSpec(memory_space=pltpu.SMEM)] + [whole(a) for a in args],
        out_specs=[whole(o) for o in outs],
        scratch_shapes=[pltpu.VMEM((length, 128), BF), pltpu.VMEM((length, 128), BF)],
        compiler_params=pltpu.CompilerParams(vmem_limit_bytes=40 * 1024 * 1024),
        cost_estimate=pl.CostEstimate(flops=12 * 10**9, bytes_accessed=8 << 20, transcendentals=0),
    )(order, *args)


def attend_backward(
    hidden, q, kv, d_mixed, gain, w_heads, head_gain, cosine, sine, seg_col, seg_row
):
    length, width = hidden.shape
    shape = jax.ShapeDtypeStruct
    outs = [
        shape((length, width), BF),
        shape((width, 256), F32),
        shape((1, width), F32),
        shape((1, 256), F32),
    ]
    args = [hidden, q, kv, d_mixed, gain, w_heads, head_gain, cosine, sine, seg_col, seg_row]
    return pl.pallas_call(
        attend_back_kernel,
        out_shape=outs,
        grid=(1,),
        in_specs=[whole(a) for a in args],
        out_specs=[whole(o) for o in outs],
        scratch_shapes=[pltpu.VMEM((length, 128), BF)] * 2
        + [pltpu.VMEM((length, 128), F32)] * 3
        + [pltpu.VMEM((length, 256), BF)],
        compiler_params=pltpu.CompilerParams(vmem_limit_bytes=40 * 1024 * 1024),
        cost_estimate=pl.CostEstimate(flops=25 * 10**9, bytes_accessed=8 << 20, transcendentals=0),
    )(*args)


def halves(v):
    high = v.astype(BF)
    return high, (v - high.astype(F32)).astype(BF)


def expert_kernel(scalar_ref, *refs, joined):
    x_own_ref, x_other_ref, g_ref, router_ref = refs[:4]
    first_refs, near_refs, far_refs, refs = refs[4:8], refs[8:12], refs[12:16], refs[16:]
    outs, refs = (refs[:1], refs[1:]) if joined else (refs[:2], refs[2:])
    back_own_ref, back_other_ref, xe_ref, de_ref, act_ref, da_ref, db_ref = refs[:7]
    pick_ref, weight_ref, dgate_ref, eo_ref, dr_ref, w_ref = refs[7:]
    half, tok, width = x_own_ref.shape
    sources = 2 * half
    core = scalar_ref[1]
    depth = w_ref.shape[2] // 8

    for r in range(8):
        rows = pl.ds(pl.multiple_of(scalar_ref[2 + r] * depth, depth), depth)
        w_ref[0, :, rows] = first_refs[r // 2][r % 2]
        w_ref[1, :, rows] = (near_refs, far_refs)[r % 2][r // 2][...]
    local, slots, hidden = act_ref.shape
    cap = slots // sources
    first = scalar_ref[0]
    lane = lax.broadcasted_iota(jnp.int32, (tok, 128), 1)
    spot = lax.broadcasted_iota(jnp.int32, (tok, local * cap), 1)
    row_expert = lax.broadcasted_iota(jnp.int32, (local * cap, 128), 0) // cap
    slot_lane = lax.broadcasted_iota(jnp.int32, (local * cap, 128), 1)
    own_lane = slot_lane == first + row_expert

    def fetch(i, carry, x_ref, offset, column):
        s = i + offset
        x = x_ref[i]
        from_g = 2 * i + column
        held = g_ref[from_g, :, width:].astype(F32)
        chosen = held >= 0.0
        logits = jnp.where(chosen, dot(x, router_ref[...], 1, 0), -1e30)
        top = jnp.max(logits, axis=1, keepdims=True)
        raised = jnp.where(chosen, jnp.exp(logits - top), 0.0)
        gates = raised / jnp.sum(raised, axis=1, keepdims=True)
        pick = jnp.zeros((tok, local * cap), F32)
        for e in range(local):
            mine = jnp.max(jnp.where(lane == first + e, held, -1.0), axis=1, keepdims=True)
            goal = jnp.where(mine >= 0.0, mine + e * cap, -1.0).astype(jnp.int32)
            pick = jnp.where(spot == goal, 1.0, pick)
        pick = pick.astype(BF)
        pick_ref[s] = pick
        rows = pl.ds(pl.multiple_of(s * cap, 16), cap)
        x_slots = dot(pick, x, 0, 0).astype(BF)
        g_slots = dot(pick, g_ref[from_g, :, :width], 0, 0).astype(BF)
        high, low = halves(gates)
        weight = dot(pick, high, 0, 0) + dot(pick, low, 0, 0)
        weight = jnp.sum(jnp.where(own_lane, weight, 0.0), axis=1, keepdims=True)
        for e in range(local):
            part = slice(e * cap, (e + 1) * cap)
            xe_ref[e, rows] = x_slots[part]
            de_ref[e, rows] = g_slots[part]
            weight_ref[e, rows] = weight[part]
        return carry

    for x_ref, offset, column in ((x_own_ref, 0, core), (x_other_ref, half, 1 - core)):
        lax.fori_loop(
            0, half, functools.partial(fetch, x_ref=x_ref, offset=offset, column=column), 0
        )
    chunk = 256

    def work(i, carry):
        e = i // (slots // chunk)
        rows = pl.ds(pl.multiple_of((i % (slots // chunk)) * chunk, chunk), chunk)
        w_gate = w_ref[e, 0]
        w_up = w_ref[e, 1]
        w_down = w_ref[e, 2]
        x = xe_ref[e, rows]
        a = dot(x, w_gate, 1, 0)
        b = dot(x, w_up, 1, 0)
        sig = 1.0 / (1.0 + jnp.exp(-a))
        silu = a * sig
        active = (silu * b).astype(BF)
        act_ref[e, rows] = active
        slope = b * (sig * (1.0 + a * (1.0 - sig)))
        weight = weight_ref[e, rows]
        g = de_ref[e, rows].astype(F32)
        result = dot(active, w_down, 1, 1).astype(BF).astype(F32)
        dgate_ref[e, rows] = jnp.sum(result * g, axis=1, keepdims=True)
        eo_ref[e, rows] = (weight * result).astype(BF)
        d_expert = (weight * g).astype(BF)
        de_ref[e, rows] = d_expert
        d_active = dot(d_expert, w_down, 1, 0)
        da = (d_active * slope).astype(BF)
        db = (d_active * silu).astype(BF)
        da_ref[e, rows] = da
        db_ref[e, rows] = db
        dr_ref[e, rows] = (dot(da, w_gate, 1, 1) + dot(db, w_up, 1, 1)).astype(BF)
        return carry

    lax.fori_loop(0, local * (slots // chunk), work, 0)

    def give(i, carry, back_ref, offset, column):
        s = i + offset
        rows = pl.ds(pl.multiple_of(s * cap, 16), cap)
        pick = pick_ref[s]
        eo = jnp.concatenate([eo_ref[e, rows] for e in range(local)], axis=0)
        dr = jnp.concatenate([dr_ref[e, rows] for e in range(local)], axis=0)
        dgate = jnp.concatenate([dgate_ref[e, rows] for e in range(local)], axis=0)
        high, low = halves(dgate)
        spread = jnp.where(own_lane, high.astype(F32), 0.0) + jnp.where(
            slot_lane == first + row_expert + 64, low.astype(F32), 0.0
        )
        if joined:
            outs[0][2 * i + column] = dot(pick, eo, 1, 0).astype(BF)
        else:
            outs[offset // half][scalar_ref[10 + i]] = dot(pick, eo, 1, 0).astype(BF)
        back_ref[i, :, :width] = dot(pick, dr, 1, 0).astype(BF)
        back_ref[i, :, width:] = dot(pick, spread.astype(BF), 1, 0).astype(BF)
        return carry

    for back_ref, offset, column in ((back_own_ref, 0, core), (back_other_ref, half, 1 - core)):
        lax.fori_loop(
            0, half, functools.partial(give, back_ref=back_ref, offset=offset, column=column), 0
        )


def run_experts(scalars, x_own, x_other, g_all, micro, router, pieces, cap, joined):
    half, tok, width = x_own.shape
    sources = 2 * half
    local, hidden = 2, pieces[0].shape[3]
    slots = sources * cap
    wide = g_all.shape[2]
    shape = jax.ShapeDtypeStruct
    outs = [shape((sources, tok, width), BF)] if joined else [shape((half, tok, width), BF)] * 2
    outs += [
        shape((half, tok, wide), BF),
        shape((half, tok, wide), BF),
        shape((local, slots, width), BF),
        shape((local, slots, width), BF),
        shape((local, slots, hidden), BF),
        shape((local, slots, hidden), BF),
        shape((local, slots, hidden), BF),
    ]
    g_spec = pl.BlockSpec(
        (sources, tok, wide), lambda i: (0, micro, 0), pipeline_mode=pl.Buffered(1)
    )
    args = [router, *pieces]
    return pl.pallas_call(
        functools.partial(expert_kernel, joined=joined),
        out_shape=outs,
        grid=(1,),
        in_specs=[pl.BlockSpec(memory_space=pltpu.SMEM), whole(x_own), whole(x_other), g_spec]
        + [whole(a) for a in args],
        out_specs=[whole(o) for o in outs],
        scratch_shapes=[
            pltpu.VMEM((sources, tok, local * cap), BF),
            pltpu.VMEM((local, slots, 1), F32),
            pltpu.VMEM((local, slots, 1), F32),
            pltpu.VMEM((local, slots, width), BF),
            pltpu.VMEM((local, slots, width), BF),
            pltpu.VMEM((local, 3, width, hidden), BF),
        ],
        compiler_params=pltpu.CompilerParams(vmem_limit_bytes=60 * 1024 * 1024),
        cost_estimate=pl.CostEstimate(flops=40 * 10**9, bytes_accessed=40 << 20, transcendentals=0),
    )(scalars, x_own, x_other, g_all, *args)


def expert_grad_kernel(order_ref, *refs):
    kept, outs, total_ref = refs[:10], refs[10:16], refs[16]
    left = (kept[0:2], kept[0:2], kept[2:4])
    right = (kept[6:8], kept[8:10], kept[4:6])
    step = pl.program_id(0)
    depth = outs[0].shape[2]
    for kind in range(3):

        @pl.when(step % 3 == kind)
        def _(kind=kind):
            total = dot(left[kind][0][0], right[kind][0][0], 0, 0)
            total_ref[...] = total + dot(left[kind][1][0], right[kind][1][0], 0, 0)

    def part(r):
        rows = pl.ds(pl.multiple_of(order_ref[r] * depth, depth), depth)
        return total_ref[rows].astype(BF)

    @pl.when(step < 3)
    def _():
        for r in range(8):
            outs[r // 2][r % 2, 0] = part(r)

    @pl.when(step >= 3)
    def _():
        for r in range(8):
            outs[4 + r % 2][r // 2, 0] = part(r)


def expert_grads(order, kept):
    local, slots, width = kept[0][0].shape
    hidden = kept[0][2].shape[2]
    args = [kept[m][i] for i in range(5) for m in range(2)]
    depth = width // 8
    shape = jax.ShapeDtypeStruct
    return pl.pallas_call(
        expert_grad_kernel,
        out_shape=[shape((2, 3, depth, hidden), BF)] * 4 + [shape((4, 3, depth, hidden), BF)] * 2,
        grid=(6,),
        in_specs=[pl.BlockSpec(memory_space=pltpu.SMEM)]
        + [pl.BlockSpec((1,) + a.shape[1:], lambda i: (i // 3, 0, 0)) for a in args],
        out_specs=[pl.BlockSpec((2, 1, depth, hidden), lambda i: (0, jnp.minimum(i, 2), 0, 0))] * 4
        + [pl.BlockSpec((4, 1, depth, hidden), lambda i: (0, jnp.maximum(i - 3, 0), 0, 0))] * 2,
        scratch_shapes=[pltpu.VMEM((width, hidden), F32)],
        compiler_params=pltpu.CompilerParams(vmem_limit_bytes=48 * 1024 * 1024),
        cost_estimate=pl.CostEstimate(flops=14 * 10**9, bytes_accessed=28 << 20, transcendentals=0),
    )(order, *args)


CTX = ("z", "yl")
GROUP = ("yh", "x")
FSDP = ("yh", "x", "core")
ALL = CTX + FSDP
UP = [(i, (i + 1) % 4) for i in range(4)]
DOWN = [(i, (i - 1) % 4) for i in range(4)]
TWO = [(i, (i + 2) % 4) for i in range(4)]
FLIP = [(0, 1), (1, 0)]


def mm(a, b):
    return jnp.dot(a, b, preferred_element_type=F32)


def mm_t(a, b):
    return lax.dot_general(a, b, (((1,), (1,)), ((), ())), preferred_element_type=F32)


def t_mm(a, b):
    return lax.dot_general(a, b, (((0,), (0,)), ((), ())), preferred_element_type=F32)


def ein(spec, a, b):
    return jnp.einsum(spec, a, b, preferred_element_type=F32)


def swap(parts, axis):
    return lax.all_to_all(parts, axis, split_axis=0, concat_axis=0, tiled=True)


def flip(block, axis):
    return lax.ppermute(block, axis, FLIP)


def by_z(parts):
    return [lax.ppermute(parts[k], "z", perm) for k, perm in ((1, UP), (2, TWO), (3, DOWN))]


def across(block):
    near = [(1, DOWN), (2, TWO), (3, UP)]
    return [
        lax.ppermute(
            block, CTX, [(2 * a + y, 2 * b + 1 - y) for a, b in perm for y in range(2)]
        )
        for _, perm in near
    ]


def interleave(first, second):
    return [block for pair in zip(first, second) for block in pair]


def along_z(both):
    before, far, after = by_z([both] * 4)
    return [both, after, far, before]


class Exchange:
    def __init__(self):
        self.last = None

    def __call__(self, parts, axis):
        if self.last is not None:
            parts = after_all(parts, self.last)
        self.last = swap(parts, axis)
        return self.last

    def copies(self, block, axis, count):
        return self(jnp.broadcast_to(block[None], (count,) + block.shape), axis)


def add(a, b):
    return (a.astype(F32) + b.astype(F32)).astype(BF)


def by_x(parts):
    return [lax.ppermute(parts[k], "x", perm) for k, perm in ((1, UP), (2, TWO), (3, DOWN))]


def pair_sum(parts, place, axis):
    own = lax.dynamic_index_in_dim(parts, place, 0, keepdims=False)
    other = lax.dynamic_index_in_dim(parts, 1 - place, 0, keepdims=False)
    return own + flip(other.astype(BF), axis).astype(F32)


def split_parts(parts):
    return list(parts[:4]), parts[4], parts[5]


def sum_parts(parts):
    return jnp.sum(parts.astype(F32), axis=0)


def after_all(value, *others):
    return lax.optimization_barrier((value,) + others)[0]


def rope_tables(positions):
    half = DH // 2
    inverse = THETA ** (-(jnp.arange(half, dtype=F32) * 2.0) / DH)
    angles = positions.astype(F32)[:, None] * inverse[None, :]
    return (jnp.cos(angles), jnp.sin(angles))


def rms_scale(values, gain):
    return values * lax.rsqrt(jnp.mean(values * values, axis=-1, keepdims=True) + EPS) * gain


def body(
    tokens,
    segments,
    routes,
    w_query,
    w_key,
    w_value,
    w_out,
    w_router,
    attn_gain,
    mlp_gain,
    qk_gain,
    w_gate,
    w_up,
    w_down,
    cotangent,
):
    micro = tokens.shape[0]
    tok = tokens.shape[2]
    width = tokens.shape[3]
    length = segments.shape[2]
    rows = w_query.shape[0]
    n_ctx, n_fsdp = 8, 16
    n_all = n_ctx * n_fsdp
    z, yl, yh, x, core = (lax.axis_index(name) for name in ALL)
    shard = (yh * 4 + x) * 2 + core
    local = w_gate.shape[0]
    experts = local * n_fsdp
    cap = (3 * tok * TOPK + 2 * experts - 1) // (2 * experts)
    all_tok = micro * tok
    ratio = H // KV
    heads = ratio * DH
    span = heads + 2 * DH

    exchange = Exchange()
    small = jnp.concatenate(
        [
            w_router,
            attn_gain[:, None],
            mlp_gain[:, None],
            jnp.pad(qk_gain[:, None], ((0, rows - 1), (0, 0))),
        ],
        axis=1,
    )
    small = jnp.pad(small, ((0, 0), (0, 128 - small.shape[1])))
    pieces = jnp.concatenate(
        [
            w_query.reshape(rows, n_ctx, heads),
            w_key.reshape(rows, n_ctx, DH),
            w_value.reshape(rows, n_ctx, DH),
            jnp.broadcast_to(small[:, None], (rows, n_ctx, 128)),
        ],
        axis=2,
    ).transpose(1, 0, 2)
    pieces = jnp.broadcast_to(pieces[:, None], (n_ctx, n_fsdp) + pieces.shape[1:])
    rows_yl = flip(tokens[0], "yl")
    seq_rows = [interleave(along_z(tokens[0]), [rows_yl] + across(tokens[0]))]
    head_all = exchange(pieces.reshape((n_all,) + pieces.shape[2:]), ALL).reshape(width, -1)
    head_all = after_all(head_all, *seq_rows[0][1:])
    w_heads = head_all[:, :span]
    small_all = head_all[:, span:]
    router = small_all[:, :experts]
    small_wide = small_all.astype(F32)
    gain_attn = small_wide[:, experts]
    gain_mlp = small_wide[:, experts + 1]
    gain_heads = small_wide[:, experts + 2].reshape(-1, rows)[:, 0]
    gain_row = gain_attn[None]
    head_row = jnp.concatenate(
        [gain_heads[:DH]] * ratio + [gain_heads[DH:], jnp.ones((DH,), F32)]
    )[None]
    router_pad = jnp.pad(router, ((0, 0), (0, 128 - experts)))

    own = exchange.copies(w_out, CTX + GROUP, n_all // 2)
    other = flip(own, "core")
    out_full = jnp.where(
        core == 0, jnp.stack([own, other], axis=1), jnp.stack([other, own], axis=1)
    ).reshape(width, width)

    stack = jnp.stack([w_gate, w_up, w_down], axis=1)
    stack = after_all(stack, *seq_rows[0][1:])
    near = along_z(stack[1])
    first = along_z(jnp.concatenate([stack[:1], flip(stack[:1], "yl")], axis=0))
    both_1 = jnp.concatenate([tokens[1], flip(tokens[1], "yl")], axis=0)
    seq_rows.append(along_z(after_all(both_1, near[1], near[3])))
    far = [flip(block, "yl") for block in near]
    weights = first + near + far

    expert_ids = jnp.arange(experts, dtype=jnp.int32)
    cot = cotangent.reshape(all_tok, width)
    chosen = jnp.any(routes.reshape(all_tok, TOPK)[:, :, None] == expert_ids, axis=1)
    before = jnp.arange(tok, dtype=jnp.int32)
    lower = (before[:, None] >= before[None, :]).astype(BF)
    counts = ein("ut,mte->mue", lower, chosen.reshape(micro, tok, experts).astype(BF))
    held = jnp.where(chosen, counts.reshape(all_tok, experts) - 1.0, -1.0)
    held = jnp.pad(held, ((0, 0), (0, 128 - experts)), constant_values=-1.0).astype(BF)
    g_all = lax.all_gather(jnp.concatenate([cot, held], axis=1), FSDP, axis=0)

    cosine, sine = rope_tables(jnp.arange(length, dtype=jnp.int32))
    cosine = jnp.tile(cosine, (1, 4))
    sine = jnp.tile(jnp.concatenate([-sine, sine], axis=1), (1, 2))
    rel = jnp.arange(n_ctx, dtype=jnp.int32)
    order = ((z + rel // 2) % 4) * 2 + (yl + rel % 2) % 2
    g_rel = ((rel % 4 - x) % 4) * 2 + (rel // 4 - yh) % 2
    scalars = jnp.concatenate([jnp.stack([shard * local, core]), order, g_rel]).astype(jnp.int32)

    def to_owner(v):
        return exchange(v.reshape(n_ctx, tok, -1), CTX)

    def z_swap(v):
        return exchange(v.reshape(4, 2, tok, width), "z")

    def attention_args(m):
        seg = segments[m, 0]
        return gain_row, w_heads, head_row, cosine, sine, seg[:, None], seg[None, :]

    def to_experts(m, mixed_h):
        mixed = to_owner(mixed_h).transpose(1, 0, 2).reshape(tok, width)
        start = tokens[m, 0].astype(F32)
        middle = start + mm(mixed, out_full)
        normed, norm_back = jax.vjp(rms_scale, middle, gain_mlp)
        hidden_two = normed.astype(BF)
        chosen_m = chosen[m * tok : (m + 1) * tok]
        logits = jnp.where(chosen_m, mm(hidden_two, router), -1e30)
        gates = jnp.where(chosen_m, jax.nn.softmax(logits, axis=-1), 0.0)
        hidden_x = hidden_two
        if m == 0:
            hidden_x = after_all(hidden_x, *seq_rows[1][1:], near[2])
        x_own = exchange.copies(hidden_x, GROUP, n_ctx)
        return [mixed, middle, norm_back, hidden_two, gates, x_own]

    mixed_0, *saved_0 = attend_forward(order, seq_rows[0], *attention_args(0))
    forward_0 = to_experts(0, after_all(mixed_0, near[1], near[3]))
    mixed_1, *saved_1 = attend_forward(order, seq_rows[1], *attention_args(1))
    saved = [saved_0, saved_1]
    forward_0[5], mixed_1, first[1], first[3] = lax.optimization_barrier(
        (forward_0[5], mixed_1, first[1], first[3])
    )
    forward = [forward_0, to_experts(1, mixed_1)]

    def experts_of(m, x_own):
        return run_experts(
            scalars,
            x_own,
            flip(x_own, "core"),
            g_all,
            m,
            router_pad,
            weights,
            cap,
            m == 0,
        )

    def back_sum(own, other):
        return add(own, flip(other, "core"))

    def middle_back(m, back):
        mixed, middle, norm_back, hidden_two, gates = forward[m][:5]
        grad_top = cot[m * tok : (m + 1) * tok].astype(F32)
        tail = back[:, width:]
        d_gates = tail[:, :experts] + tail[:, 64 : 64 + experts]
        d_select = gates * (d_gates - jnp.sum(gates * d_gates, axis=-1, keepdims=True))
        d_logits = d_select.astype(BF)
        grad_router = t_mm(hidden_two, d_logits)
        d_two = back[:, :width] + mm_t(d_logits, router)
        d_middle, grad_mlp = norm_back(d_two)
        d_middle = d_middle + grad_top
        d_branch = d_middle.astype(BF)
        grad_out = t_mm(mixed, d_branch)
        d_mixed = mm_t(d_branch, out_full).astype(BF)
        d_mixed = d_mixed.reshape(tok, n_ctx, heads).transpose(1, 0, 2)
        return d_middle, d_mixed, (grad_out, grad_router, grad_mlp)

    def attention_back(m, d_mixed):
        d_hidden, grad_heads, grad_attn, grad_qk = attend_backward(
            *saved[m], d_mixed.reshape(length, heads), *attention_args(m)
        )
        grad_qk = jnp.concatenate(
            [grad_qk[0, :DH] + grad_qk[0, DH : 2 * DH], grad_qk[0, 2 * DH : 3 * DH]]
        )
        return d_hidden, (grad_heads, grad_attn[0], grad_qk)

    def input_grad(m, d_hidden, d_middle):
        start = tokens[m, 0].astype(F32)
        inverse = lax.rsqrt(jnp.mean(start * start, axis=-1, keepdims=True) + EPS)
        u = d_hidden * gain_attn
        return (
            d_middle
            + inverse * u
            - start * (inverse**3 * jnp.mean(u * start, axis=-1, keepdims=True))
        )

    moe_0, back_own, back_other, *kept_0 = experts_of(0, forward[0][5])
    x_1, back_own, back_other, moe_0 = lax.optimization_barrier(
        (forward[1][5], back_own, back_other, moe_0)
    )
    back_0 = back_sum(back_own, back_other)
    moe_0 = lax.psum_scatter(moe_0, FSDP, scatter_dimension=0, tiled=True)[0]
    x_1 = after_all(x_1, back_0)
    back_0 = exchange(back_0, GROUP)
    moe_own, moe_other, back_own, back_other, *kept_1 = experts_of(1, x_1)
    back_0, back_own, back_other, moe_own, moe_other = lax.optimization_barrier(
        (back_0, back_own, back_other, moe_own, moe_other)
    )
    back_1 = exchange(back_sum(back_own, back_other), GROUP)
    d_middle_0, d_mixed_0, grads_0 = middle_back(0, sum_parts(back_0))
    first_parts, own_1, other_1 = split_parts(expert_grads(order, (kept_0, kept_1)))
    moe_other = flip(moe_other, "core")
    back_1, d_mixed_0, first_parts, other_1, moe_other = lax.optimization_barrier(
        (back_1, d_mixed_0, first_parts, other_1, moe_other)
    )
    d_mixed_0 = exchange(d_mixed_0, CTX)
    first_moved = by_z(first_parts)
    other_1 = flip(other_1, "yl")
    moe_1 = [add(moe_own[2 * k : 2 * k + 2], moe_other[2 * k : 2 * k + 2]) for k in range(4)]
    moe_moved = by_x(moe_1)
    d_middle_1, d_mixed_1, grads_1 = middle_back(1, sum_parts(back_1))
    d_mixed_1 = exchange(d_mixed_1, CTX)
    d_hidden_0, head_grads_0 = attention_back(0, d_mixed_0)
    d_hidden_0 = z_swap(d_hidden_0)
    d_hidden_1, head_grads_1 = attention_back(1, d_mixed_1)
    d_hidden_0, d_hidden_1, other_1, moe_moved = lax.optimization_barrier(
        (d_hidden_0, d_hidden_1, other_1, moe_moved)
    )
    own_1 = [add(own_1[k], other_1[k]) for k in range(4)]
    second_moved = by_z(own_1)
    d_hidden_1 = z_swap(d_hidden_1)
    d_hidden_0 = pair_sum(sum_parts(d_hidden_0), yl, "yl")
    moe_1 = sum(part.astype(F32) for part in [moe_1[0]] + moe_moved)
    moe_1 = moe_1[0] + flip(moe_1[1].astype(BF), "yh").astype(F32)
    grad_out, grad_router, grad_mlp = jax.tree.map(jnp.add, grads_0, grads_1)
    grad_heads, grad_attn, grad_qk = jax.tree.map(jnp.add, head_grads_0, head_grads_1)
    d_hidden_1, first_moved, moe_0 = lax.optimization_barrier((d_hidden_1, first_moved, moe_0))
    first_sums = [
        sum(part[i].astype(F32) for part in [first_parts[0]] + first_moved) for i in range(2)
    ]
    from_yl = flip(first_sums[1].astype(BF), "yl")
    d_hidden_1 = pair_sum(sum_parts(d_hidden_1), yl, "yl")

    grad_out = grad_out.astype(BF).reshape(n_all // 2, 2, rows, width)
    grad_own = lax.dynamic_index_in_dim(grad_out, core, axis=1, keepdims=False)
    grad_other = lax.dynamic_index_in_dim(grad_out, 1 - core, axis=1, keepdims=False)
    own_out = sum_parts(exchange(back_sum(grad_own, grad_other), CTX + GROUP))
    grad_qk = jnp.pad(grad_qk[:, None], ((0, 0), (0, rows - 1))).reshape(-1)
    grad_small = jnp.concatenate(
        [grad_router, grad_attn[:, None], grad_mlp[:, None], grad_qk[:, None]], axis=1
    )
    grad_small = jnp.pad(grad_small, ((0, 0), (0, 128 - grad_small.shape[1])))
    grad_pack = jnp.concatenate([grad_heads, grad_small], axis=1).astype(BF)
    grad_pack = exchange(grad_pack.reshape(n_all, rows, -1), ALL).astype(F32)
    own_heads = jnp.sum(grad_pack[:, :, :span].reshape(n_ctx, n_fsdp, rows, -1), axis=1)
    own_heads = own_heads.transpose(1, 0, 2)
    own_small = jnp.sum(grad_pack[:, :, span:], axis=0)
    expert_own = [
        first_sums[0] + from_yl.astype(F32),
        sum(part.astype(F32) for part in [own_1[0]] + second_moved),
    ]
    outs = [
        (forward[0][1] + moe_0.astype(F32)).astype(BF),
        (forward[1][1] + moe_1).astype(BF),
    ]
    d_inputs = [
        input_grad(0, d_hidden_0, d_middle_0),
        input_grad(1, d_hidden_1, d_middle_1),
    ]

    return (
        jnp.stack(outs)[:, None],
        jnp.stack(d_inputs)[:, None],
        own_heads[:, :, :heads].reshape(rows, -1),
        own_heads[:, :, heads : heads + DH].reshape(rows, -1),
        own_heads[:, :, heads + DH :].reshape(rows, -1),
        own_out,
        own_small[:, :experts],
        own_small[:, experts],
        own_small[:, experts + 1],
        own_small[:1, experts + 2],
        jnp.stack([part[0] for part in expert_own]),
        jnp.stack([part[1] for part in expert_own]),
        jnp.stack([part[2] for part in expert_own]),
    )


def solution(mesh):
    mesh = Mesh(mesh.devices.reshape(4, 2, 2, 4, 2), ALL)
    weight = P(ALL, None)
    gain = P(ALL)
    rows = P(None, FSDP, CTX, None)
    expert = P(FSDP, CTX, None)
    return jax.shard_map(
        body,
        mesh=mesh,
        in_specs=(rows, P(None, FSDP, None), rows)
        + (weight,) * 5
        + (gain,) * 3
        + (expert,) * 3
        + (rows,),
        out_specs=(rows, rows) + (weight,) * 5 + (gain,) * 3 + (expert,) * 3,
        check_vma=False,
    )
```

```python
import functools

import jax
import jax.numpy as jnp
from jax import lax
from jax.experimental import pallas as pl
from jax.experimental.pallas import tpu as pltpu
from jax.sharding import Mesh
from jax.sharding import PartitionSpec as P

BF = jnp.bfloat16
F32 = jnp.float32
H = 16
KV = 8
DH = 64
TOPK = 8
WINDOW = 1024
EPS = 1e-06
THETA = 10000.0


def dot(a, b, ca, cb):
    return lax.dot_general(a, b, (((ca,), (cb,)), ((), ())), preferred_element_type=F32)


def lanes_of(v):
    return lax.broadcasted_iota(jnp.int32, v.shape, v.ndim - 1)


def head_sums(v):
    low = lanes_of(v) < DH
    first = jnp.sum(jnp.where(low, v, 0.0), axis=1, keepdims=True)
    second = jnp.sum(jnp.where(low, 0.0, v), axis=1, keepdims=True)
    return jnp.where(low, first, second)


def trade(v):
    return jnp.where(
        lanes_of(v) % DH < DH // 2, pltpu.roll(v, 128 - DH // 2, 1), pltpu.roll(v, DH // 2, 1)
    )


def both_halves(v, second):
    low = lanes_of(v) < DH
    other = pltpu.roll(v, DH, 1)
    return jnp.where(low, other, v) if second else jnp.where(low, v, other)


def stack_heads(v):
    low = lanes_of(v) < DH
    zero = jnp.zeros_like(v)
    return jnp.concatenate([jnp.where(low, v, zero), jnp.where(low, zero, v)], axis=0)


def key_span(start, block, length):
    reach = WINDOW // 2 - 1
    low = max(0, start - reach) // 128 * 128
    high = min(length, -(-(start + block + reach) // 128) * 128)
    return low, high


def masked_probs(q_two, keys, seg_col, seg_row, start, low):
    block = q_two.shape[0] // 2
    scores = dot(q_two, keys, 1, 1)
    shape = (block, keys.shape[0])
    gap = (
        lax.broadcasted_iota(jnp.int32, shape, 0)
        - lax.broadcasted_iota(jnp.int32, shape, 1)
        + (start - low)
    )
    allowed = (seg_col == seg_row) & (jnp.abs(gap) < WINDOW // 2)
    bias = jnp.where(allowed, 0.0, -1e30)
    scores = scores + jnp.concatenate([bias, bias], axis=0)
    raised = jnp.exp(scores - jnp.max(scores, axis=1, keepdims=True))
    return raised * (1.0 / jnp.sum(raised, axis=1, keepdims=True))


def attend_kernel(
    order_ref,
    *refs,
):
    pieces, refs = refs[:-13], refs[-13:]
    gain_ref, w_ref, head_gain_ref, cos_ref, sin_ref, seg_col_ref, seg_row_ref = refs[:7]
    mixed_ref, hidden_ref, q_ref, kv_ref, keys_ref, values_ref = refs[7:]
    tok, width = pieces[0].shape[1:]
    length = hidden_ref.shape[0]
    pieces = [(ref, i) for ref in pieces for i in range(ref.shape[0])]
    for r, (ref, i) in enumerate(pieces):
        x = ref[i].astype(F32)
        x = x * lax.rsqrt(jnp.mean(x * x, axis=1, keepdims=True) + EPS) * gain_ref[...]
        rows = pl.ds(pl.multiple_of(order_ref[r] * tok, tok), tok)
        hidden_ref[rows] = x.astype(BF)
    raw = dot(hidden_ref[...], w_ref[...], 1, 0)
    for half in range(2):
        u = raw[:, half * 128 : half * 128 + 128]
        gain = head_gain_ref[:, half * 128 : half * 128 + 128]
        n = u * lax.rsqrt(head_sums(u * u) * (1.0 / DH) + EPS) * gain
        turned = n * cos_ref[...] + trade(n) * sin_ref[...]
        if half == 0:
            q_ref[...] = turned.astype(BF)
        else:
            kv = jnp.where(lanes_of(u) < DH, turned, u)
            kv_ref[...] = kv.astype(BF)
            keys_ref[...] = both_halves(kv, False).astype(BF)
            values_ref[...] = both_halves(kv, True).astype(BF)
    block = 256
    for start in range(0, length, block):
        low, high = key_span(start, block, length)
        q_two = stack_heads(q_ref[start : start + block].astype(F32) * DH**-0.5).astype(BF)
        probs = masked_probs(
            q_two,
            keys_ref[low:high],
            seg_col_ref[start : start + block],
            seg_row_ref[:, low:high],
            start,
            low,
        )
        result = dot(probs.astype(BF), values_ref[low:high], 1, 0)
        first = lanes_of(result[:block]) < DH
        mixed_ref[start : start + block] = jnp.where(first, result[:block], result[block:]).astype(
            BF
        )


def attend_back_kernel(
    order_ref,
    hidden_ref,
    q_ref,
    kv_ref,
    d_mixed_ref,
    gain_ref,
    w_ref,
    head_gain_ref,
    cos_ref,
    sin_ref,
    seg_col_ref,
    seg_row_ref,
    d_hidden_0_ref,
    d_hidden_1_ref,
    d_hidden_2_ref,
    d_hidden_3_ref,
    grad_w_ref,
    grad_gain_ref,
    grad_heads_ref,
    keys_ref,
    values_ref,
    d_q_ref,
    d_k_ref,
    d_v_ref,
    d_raw_ref,
):
    length = hidden_ref.shape[0]
    kv = kv_ref[...].astype(F32)
    keys_ref[...] = both_halves(kv, False).astype(BF)
    values_ref[...] = both_halves(kv, True).astype(BF)
    d_k_ref[...] = jnp.zeros_like(d_k_ref)
    d_v_ref[...] = jnp.zeros_like(d_v_ref)
    block = 256
    for start in range(0, length, block):
        low, high = key_span(start, block, length)
        q_two = stack_heads(q_ref[start : start + block].astype(F32) * DH**-0.5).astype(BF)
        m_two = stack_heads(d_mixed_ref[start : start + block].astype(F32)).astype(BF)
        probs = masked_probs(
            q_two,
            keys_ref[low:high],
            seg_col_ref[start : start + block],
            seg_row_ref[:, low:high],
            start,
            low,
        )
        d_probs = dot(m_two, values_ref[low:high], 1, 1)
        inner = jnp.sum(probs * d_probs, axis=1, keepdims=True)
        d_scores = (probs * (d_probs - inner)).astype(BF)
        result = dot(d_scores, keys_ref[low:high], 1, 0)
        first = lanes_of(result[:block]) < DH
        d_q_ref[start : start + block] = jnp.where(first, result[:block], result[block:]) * (
            DH**-0.5
        )
        d_k_ref[low:high] += dot(d_scores, q_two, 0, 0)
        d_v_ref[low:high] += dot(probs.astype(BF), m_two, 0, 0)
    raw = dot(hidden_ref[...], w_ref[...], 1, 0)
    d_k = d_k_ref[...]
    d_k = d_k + pltpu.roll(d_k, DH, 1)
    d_v = d_v_ref[...]
    d_v = d_v + pltpu.roll(d_v, DH, 1)
    for half in range(2):
        lanes = slice(half * 128, half * 128 + 128)
        u = raw[:, lanes]
        gain = head_gain_ref[:, lanes]
        d = d_q_ref[...] if half == 0 else d_k
        d = d * cos_ref[...] + trade(d * sin_ref[...])
        r = lax.rsqrt(head_sums(u * u) * (1.0 / DH) + EPS)
        grad_heads_ref[:, lanes] = jnp.sum(d * u * r, axis=0, keepdims=True)
        d = d * gain
        d = d * r - u * (r * r * r * (head_sums(d * u) * (1.0 / DH)))
        if half == 1:
            d = jnp.where(lanes_of(d) < DH, d, d_v)
        d_raw_ref[:, lanes] = d.astype(BF)
    grad_w_ref[...] = dot(hidden_ref[...], d_raw_ref[...], 0, 0)
    total = jnp.zeros(grad_gain_ref.shape, F32)
    outs = (d_hidden_0_ref, d_hidden_1_ref, d_hidden_2_ref, d_hidden_3_ref)
    tok = length // 8
    for r in range(8):
        rows = pl.ds(pl.multiple_of(order_ref[r] * tok, tok), tok)
        d_hidden = dot(d_raw_ref[rows], w_ref[...], 1, 1)
        outs[r // 2][r % 2] = d_hidden.astype(BF)
        total = total + jnp.sum(d_hidden * hidden_ref[rows].astype(F32), axis=0, keepdims=True)
    grad_gain_ref[...] = total / gain_ref[...]


def whole(a):
    return pl.BlockSpec(a.shape, lambda i: (0,) * len(a.shape), pipeline_mode=pl.Buffered(1))


def attend_forward(order, pieces, gain, w_heads, head_gain, cosine, sine, seg_col, seg_row):
    length = cosine.shape[0]
    width = w_heads.shape[0]
    shape = jax.ShapeDtypeStruct
    outs = [
        shape((length, 128), BF),
        shape((length, width), BF),
        shape((length, 128), BF),
        shape((length, 128), BF),
    ]
    args = list(pieces) + [gain, w_heads, head_gain, cosine, sine, seg_col, seg_row]
    return pl.pallas_call(
        attend_kernel,
        out_shape=outs,
        grid=(1,),
        in_specs=[pl.BlockSpec(memory_space=pltpu.SMEM)] + [whole(a) for a in args],
        out_specs=[whole(o) for o in outs],
        scratch_shapes=[pltpu.VMEM((length, 128), BF), pltpu.VMEM((length, 128), BF)],
        compiler_params=pltpu.CompilerParams(vmem_limit_bytes=40 * 1024 * 1024),
        cost_estimate=pl.CostEstimate(flops=12 * 10**9, bytes_accessed=8 << 20, transcendentals=0),
    )(order, *args)


def attend_backward(
    order, hidden, q, kv, d_mixed, gain, w_heads, head_gain, cosine, sine, seg_col, seg_row
):
    length, width = hidden.shape
    shape = jax.ShapeDtypeStruct
    outs = [shape((2, length // 8, width), BF)] * 4 + [
        shape((width, 256), F32),
        shape((1, width), F32),
        shape((1, 256), F32),
    ]
    args = [hidden, q, kv, d_mixed, gain, w_heads, head_gain, cosine, sine, seg_col, seg_row]
    return pl.pallas_call(
        attend_back_kernel,
        out_shape=outs,
        grid=(1,),
        in_specs=[pl.BlockSpec(memory_space=pltpu.SMEM)] + [whole(a) for a in args],
        out_specs=[whole(o) for o in outs],
        scratch_shapes=[pltpu.VMEM((length, 128), BF)] * 2
        + [pltpu.VMEM((length, 128), F32)] * 3
        + [pltpu.VMEM((length, 256), BF)],
        compiler_params=pltpu.CompilerParams(vmem_limit_bytes=40 * 1024 * 1024),
        cost_estimate=pl.CostEstimate(flops=25 * 10**9, bytes_accessed=8 << 20, transcendentals=0),
    )(order, *args)


def halves(v):
    high = v.astype(BF)
    return high, (v - high.astype(F32)).astype(BF)


def expert_kernel(scalar_ref, *refs, joined):
    x_own_ref, x_other_ref, g_ref, router_ref = refs[:4]
    pieces, refs = refs[4:8], refs[8:]
    outs, refs = (refs[:1], refs[1:]) if joined else (refs[:2], refs[2:])
    back_own_ref, back_other_ref, xe_ref, de_ref, act_ref, da_ref, db_ref = refs[:7]
    pick_ref, weight_ref, dgate_ref, eo_ref, dr_ref, w_ref = refs[7:]
    half, tok, width = x_own_ref.shape
    sources = 2 * half
    core = scalar_ref[1]
    depth = w_ref.shape[2] // 8

    for r in range(8):
        rows = pl.ds(pl.multiple_of(scalar_ref[2 + r] * depth, depth), depth)
        w_ref[:, :, rows] = pieces[r // 2][r % 2]
    local, slots, hidden = act_ref.shape
    cap = slots // sources
    first = scalar_ref[0]
    lane = lax.broadcasted_iota(jnp.int32, (tok, 128), 1)
    spot = lax.broadcasted_iota(jnp.int32, (tok, local * cap), 1)
    row_expert = lax.broadcasted_iota(jnp.int32, (local * cap, 128), 0) // cap
    slot_lane = lax.broadcasted_iota(jnp.int32, (local * cap, 128), 1)
    own_lane = slot_lane == first + row_expert

    def fetch(i, carry, x_ref, offset, column):
        s = i + offset
        x = x_ref[i]
        from_g = 2 * i + column
        held = g_ref[from_g, :, width:].astype(F32)
        chosen = held >= 0.0
        logits = jnp.where(chosen, dot(x, router_ref[...], 1, 0), -1e30)
        top = jnp.max(logits, axis=1, keepdims=True)
        raised = jnp.where(chosen, jnp.exp(logits - top), 0.0)
        gates = raised / jnp.sum(raised, axis=1, keepdims=True)
        pick = jnp.zeros((tok, local * cap), F32)
        for e in range(local):
            mine = jnp.max(jnp.where(lane == first + e, held, -1.0), axis=1, keepdims=True)
            goal = jnp.where(mine >= 0.0, mine + e * cap, -1.0).astype(jnp.int32)
            pick = jnp.where(spot == goal, 1.0, pick)
        pick = pick.astype(BF)
        pick_ref[s] = pick
        rows = pl.ds(pl.multiple_of(s * cap, 16), cap)
        x_slots = dot(pick, x, 0, 0).astype(BF)
        g_slots = dot(pick, g_ref[from_g, :, :width], 0, 0).astype(BF)
        high, low = halves(gates)
        weight = dot(pick, high, 0, 0) + dot(pick, low, 0, 0)
        weight = jnp.sum(jnp.where(own_lane, weight, 0.0), axis=1, keepdims=True)
        for e in range(local):
            part = slice(e * cap, (e + 1) * cap)
            xe_ref[e, rows] = x_slots[part]
            de_ref[e, rows] = g_slots[part]
            weight_ref[e, rows] = weight[part]
        return carry

    for x_ref, offset, column in ((x_own_ref, 0, core), (x_other_ref, half, 1 - core)):
        lax.fori_loop(
            0, half, functools.partial(fetch, x_ref=x_ref, offset=offset, column=column), 0
        )
    chunk = 256

    def work(i, carry):
        e = i // (slots // chunk)
        rows = pl.ds(pl.multiple_of((i % (slots // chunk)) * chunk, chunk), chunk)
        w_gate = w_ref[e, 0]
        w_up = w_ref[e, 1]
        w_down = w_ref[e, 2]
        x = xe_ref[e, rows]
        a = dot(x, w_gate, 1, 0)
        b = dot(x, w_up, 1, 0)
        sig = 1.0 / (1.0 + jnp.exp(-a))
        silu = a * sig
        active = (silu * b).astype(BF)
        act_ref[e, rows] = active
        slope = b * (sig * (1.0 + a * (1.0 - sig)))
        weight = weight_ref[e, rows]
        g = de_ref[e, rows].astype(F32)
        result = dot(active, w_down, 1, 1).astype(BF).astype(F32)
        dgate_ref[e, rows] = jnp.sum(result * g, axis=1, keepdims=True)
        eo_ref[e, rows] = (weight * result).astype(BF)
        d_expert = (weight * g).astype(BF)
        de_ref[e, rows] = d_expert
        d_active = dot(d_expert, w_down, 1, 0)
        da = (d_active * slope).astype(BF)
        db = (d_active * silu).astype(BF)
        da_ref[e, rows] = da
        db_ref[e, rows] = db
        dr_ref[e, rows] = (dot(da, w_gate, 1, 1) + dot(db, w_up, 1, 1)).astype(BF)
        return carry

    lax.fori_loop(0, local * (slots // chunk), work, 0)

    def give(i, carry, back_ref, offset, column):
        s = i + offset
        rows = pl.ds(pl.multiple_of(s * cap, 16), cap)
        pick = pick_ref[s]
        eo = jnp.concatenate([eo_ref[e, rows] for e in range(local)], axis=0)
        dr = jnp.concatenate([dr_ref[e, rows] for e in range(local)], axis=0)
        dgate = jnp.concatenate([dgate_ref[e, rows] for e in range(local)], axis=0)
        high, low = halves(dgate)
        spread = jnp.where(own_lane, high.astype(F32), 0.0) + jnp.where(
            slot_lane == first + row_expert + 64, low.astype(F32), 0.0
        )
        if joined:
            outs[0][2 * i + column] = dot(pick, eo, 1, 0).astype(BF)
        else:
            outs[offset // half][scalar_ref[10 + i]] = dot(pick, eo, 1, 0).astype(BF)
        back_ref[i, :, :width] = dot(pick, dr, 1, 0).astype(BF)
        back_ref[i, :, width:] = dot(pick, spread.astype(BF), 1, 0).astype(BF)
        return carry

    for back_ref, offset, column in ((back_own_ref, 0, core), (back_other_ref, half, 1 - core)):
        lax.fori_loop(
            0, half, functools.partial(give, back_ref=back_ref, offset=offset, column=column), 0
        )


def run_experts(scalars, x_own, x_other, g_all, micro, router, pieces, cap, joined):
    half, tok, width = x_own.shape
    sources = 2 * half
    _, local, _, _, hidden = pieces[0].shape
    slots = sources * cap
    wide = g_all.shape[2]
    shape = jax.ShapeDtypeStruct
    outs = [shape((sources, tok, width), BF)] if joined else [shape((half, tok, width), BF)] * 2
    outs += [
        shape((half, tok, wide), BF),
        shape((half, tok, wide), BF),
        shape((local, slots, width), BF),
        shape((local, slots, width), BF),
        shape((local, slots, hidden), BF),
        shape((local, slots, hidden), BF),
        shape((local, slots, hidden), BF),
    ]
    g_spec = pl.BlockSpec(
        (sources, tok, wide), lambda i: (0, micro, 0), pipeline_mode=pl.Buffered(1)
    )
    args = [router, *pieces]
    return pl.pallas_call(
        functools.partial(expert_kernel, joined=joined),
        out_shape=outs,
        grid=(1,),
        in_specs=[pl.BlockSpec(memory_space=pltpu.SMEM), whole(x_own), whole(x_other), g_spec]
        + [whole(a) for a in args],
        out_specs=[whole(o) for o in outs],
        scratch_shapes=[
            pltpu.VMEM((sources, tok, local * cap), BF),
            pltpu.VMEM((local, slots, 1), F32),
            pltpu.VMEM((local, slots, 1), F32),
            pltpu.VMEM((local, slots, width), BF),
            pltpu.VMEM((local, slots, width), BF),
            pltpu.VMEM((local, 3, width, hidden), BF),
        ],
        compiler_params=pltpu.CompilerParams(vmem_limit_bytes=60 * 1024 * 1024),
        cost_estimate=pl.CostEstimate(flops=40 * 10**9, bytes_accessed=40 << 20, transcendentals=0),
    )(scalars, x_own, x_other, g_all, *args)


def expert_grad_kernel(order_ref, *refs):
    kept, outs, total_ref = refs[:10], refs[10:14], refs[14]
    left = (kept[0:2], kept[0:2], kept[2:4])
    right = (kept[6:8], kept[8:10], kept[4:6])
    step = pl.program_id(0)
    depth = outs[0].shape[3]
    for kind in range(3):

        @pl.when(step % 3 == kind)
        def _(kind=kind):
            total = dot(left[kind][0][0], right[kind][0][0], 0, 0)
            total_ref[...] = total + dot(left[kind][1][0], right[kind][1][0], 0, 0)

    for r in range(8):
        rows = pl.ds(pl.multiple_of(order_ref[r] * depth, depth), depth)
        outs[r // 2][r % 2, 0, 0] = total_ref[rows].astype(BF)


def expert_grads(order, kept):
    local, slots, width = kept[0][0].shape
    hidden = kept[0][2].shape[2]
    args = [kept[m][i] for i in range(5) for m in range(2)]
    depth = width // 8
    shape = jax.ShapeDtypeStruct
    return pl.pallas_call(
        expert_grad_kernel,
        out_shape=[shape((2, local, 3, depth, hidden), BF)] * 4,
        grid=(3 * local,),
        in_specs=[pl.BlockSpec(memory_space=pltpu.SMEM)]
        + [pl.BlockSpec((1,) + a.shape[1:], lambda i: (i // 3, 0, 0)) for a in args],
        out_specs=[
            pl.BlockSpec((2, 1, 1, depth, hidden), lambda i: (0, i // 3, i % 3, 0, 0))
        ]
        * 4,
        scratch_shapes=[pltpu.VMEM((width, hidden), F32)],
        compiler_params=pltpu.CompilerParams(vmem_limit_bytes=48 * 1024 * 1024),
        cost_estimate=pl.CostEstimate(flops=14 * 10**9, bytes_accessed=28 << 20, transcendentals=0),
    )(order, *args)


CTX = ("z", "yl")
GROUP = ("yh", "x")
FSDP = ("yh", "x", "core")
ALL = CTX + FSDP
UP = [(i, (i + 1) % 4) for i in range(4)]
DOWN = [(i, (i - 1) % 4) for i in range(4)]
TWO = [(i, (i + 2) % 4) for i in range(4)]
FLIP = [(0, 1), (1, 0)]


def mm(a, b):
    return jnp.dot(a, b, preferred_element_type=F32)


def mm_t(a, b):
    return lax.dot_general(a, b, (((1,), (1,)), ((), ())), preferred_element_type=F32)


def t_mm(a, b):
    return lax.dot_general(a, b, (((0,), (0,)), ((), ())), preferred_element_type=F32)


def ein(spec, a, b):
    return jnp.einsum(spec, a, b, preferred_element_type=F32)


def swap(parts, axis):
    return lax.all_to_all(parts, axis, split_axis=0, concat_axis=0, tiled=True)


def flip(block, axis):
    return lax.ppermute(block, axis, FLIP)


def by_z(parts):
    return [lax.ppermute(parts[k], "z", perm) for k, perm in ((1, UP), (2, TWO), (3, DOWN))]


def across(block):
    return [
        lax.ppermute(
            block, CTX, [(2 * a + y, 2 * b + 1 - y) for a, b in perm for y in range(2)]
        )
        for perm in (DOWN, TWO, UP)
    ]


def interleave(first, second):
    return [block for pair in zip(first, second) for block in pair]


def along_z(both):
    before, far, after = by_z([both] * 4)
    return [both, after, far, before]


class Exchange:
    def __init__(self):
        self.last = None

    def __call__(self, parts, axis):
        if self.last is not None:
            parts = after_all(parts, self.last)
        self.last = swap(parts, axis)
        return self.last

    def copies(self, block, axis, count):
        return self(jnp.broadcast_to(block[None], (count,) + block.shape), axis)


def add(a, b):
    return (a.astype(F32) + b.astype(F32)).astype(BF)


def by_x(parts):
    return [lax.ppermute(parts[k], "x", perm) for k, perm in ((1, UP), (2, TWO), (3, DOWN))]


def pair_sums(parts, moved):
    return [sum(part[i].astype(F32) for part in [parts[0]] + moved) for i in range(2)]


def sum_parts(parts):
    return jnp.sum(parts.astype(F32), axis=0)


def after_all(value, *others):
    return lax.optimization_barrier((value,) + others)[0]


def rope_tables(positions):
    half = DH // 2
    inverse = THETA ** (-(jnp.arange(half, dtype=F32) * 2.0) / DH)
    angles = positions.astype(F32)[:, None] * inverse[None, :]
    return (jnp.cos(angles), jnp.sin(angles))


def rms_scale(values, gain):
    return values * lax.rsqrt(jnp.mean(values * values, axis=-1, keepdims=True) + EPS) * gain


def body(
    tokens,
    segments,
    routes,
    w_query,
    w_key,
    w_value,
    w_out,
    w_router,
    attn_gain,
    mlp_gain,
    qk_gain,
    w_gate,
    w_up,
    w_down,
    cotangent,
):
    micro = tokens.shape[0]
    tok = tokens.shape[2]
    width = tokens.shape[3]
    length = segments.shape[2]
    rows = w_query.shape[0]
    n_ctx, n_fsdp = 8, 16
    n_all = n_ctx * n_fsdp
    z, yl, yh, x, core = (lax.axis_index(name) for name in ALL)
    shard = (yh * 4 + x) * 2 + core
    local = w_gate.shape[0]
    experts = local * n_fsdp
    cap = (3 * tok * TOPK + 2 * experts - 1) // (2 * experts)
    all_tok = micro * tok
    ratio = H // KV
    heads = ratio * DH
    span = heads + 2 * DH

    exchange = Exchange()
    small = jnp.concatenate(
        [
            w_router,
            attn_gain[:, None],
            mlp_gain[:, None],
            jnp.pad(qk_gain[:, None], ((0, rows - 1), (0, 0))),
        ],
        axis=1,
    )
    small = jnp.pad(small, ((0, 0), (0, 128 - small.shape[1])))
    pieces = jnp.concatenate(
        [
            w_query.reshape(rows, n_ctx, heads),
            w_key.reshape(rows, n_ctx, DH),
            w_value.reshape(rows, n_ctx, DH),
            jnp.broadcast_to(small[:, None], (rows, n_ctx, 128)),
        ],
        axis=2,
    ).transpose(1, 0, 2)
    pieces = jnp.broadcast_to(pieces[:, None], (n_ctx, n_fsdp) + pieces.shape[1:])
    seq_rows = [interleave(along_z(tokens[0]), [flip(tokens[0], "yl")] + across(tokens[0]))]
    both_w = jnp.stack([w_gate, w_up, w_down], axis=1)[None]
    head_all = exchange(pieces.reshape((n_all,) + pieces.shape[2:]), ALL).reshape(width, -1)
    both_w = jnp.concatenate([both_w, flip(both_w, "yl")], axis=0)
    head_all = after_all(head_all, *seq_rows[0][1:], both_w)
    w_heads = head_all[:, :span]
    small_all = head_all[:, span:]
    router = small_all[:, :experts]
    small_wide = small_all.astype(F32)
    gain_attn = small_wide[:, experts]
    gain_mlp = small_wide[:, experts + 1]
    gain_heads = small_wide[:, experts + 2].reshape(-1, rows)[:, 0]
    gain_row = gain_attn[None]
    head_row = jnp.concatenate(
        [gain_heads[:DH]] * ratio + [gain_heads[DH:], jnp.ones((DH,), F32)]
    )[None]
    router_pad = jnp.pad(router, ((0, 0), (0, 128 - experts)))

    out_own = exchange.copies(w_out, CTX + GROUP, n_all // 2)

    weights = along_z(both_w)
    both_1 = jnp.concatenate([tokens[1], flip(tokens[1], "yl")], axis=0)
    seq_rows.append(along_z(after_all(both_1, *seq_rows[0][1:])))

    expert_ids = jnp.arange(experts, dtype=jnp.int32)
    cot = cotangent.reshape(all_tok, width)
    chosen = jnp.any(routes.reshape(all_tok, TOPK)[:, :, None] == expert_ids, axis=1)
    before = jnp.arange(tok, dtype=jnp.int32)
    lower = (before[:, None] >= before[None, :]).astype(BF)
    counts = ein("ut,mte->mue", lower, chosen.reshape(micro, tok, experts).astype(BF))
    held = jnp.where(chosen, counts.reshape(all_tok, experts) - 1.0, -1.0)
    held = jnp.pad(held, ((0, 0), (0, 128 - experts)), constant_values=-1.0).astype(BF)
    g_all = lax.all_gather(jnp.concatenate([cot, held], axis=1), FSDP, axis=0)

    cosine, sine = rope_tables(jnp.arange(length, dtype=jnp.int32))
    cosine = jnp.tile(cosine, (1, 4))
    sine = jnp.tile(jnp.concatenate([-sine, sine], axis=1), (1, 2))
    rel = jnp.arange(n_ctx, dtype=jnp.int32)
    order = ((z + rel // 2) % 4) * 2 + (yl + rel % 2) % 2
    g_rel = ((rel % 4 - x) % 4) * 2 + (rel // 4 - yh) % 2
    scalars = jnp.concatenate([jnp.stack([shard * local, core]), order, g_rel]).astype(jnp.int32)

    def to_owner(v):
        return exchange(v.reshape(n_ctx, tok, -1), CTX)

    def attention_args(m):
        seg = segments[m, 0]
        return gain_row, w_heads, head_row, cosine, sine, seg[:, None], seg[None, :]

    def to_experts(m, mixed, out_full, *before):
        start = tokens[m, 0].astype(F32)
        middle = start + mm(mixed, out_full)
        normed, norm_back = jax.vjp(rms_scale, middle, gain_mlp)
        hidden_two = normed.astype(BF)
        chosen_m = chosen[m * tok : (m + 1) * tok]
        logits = jnp.where(chosen_m, mm(hidden_two, router), -1e30)
        gates = jnp.where(chosen_m, jax.nn.softmax(logits, axis=-1), 0.0)
        x_own = exchange.copies(after_all(hidden_two, *before), GROUP, n_ctx)
        return [mixed, middle, norm_back, hidden_two, gates, x_own]

    def from_heads(mixed_h):
        return to_owner(mixed_h).transpose(1, 0, 2).reshape(tok, width)

    mixed_0, *saved_0 = attend_forward(order, seq_rows[0], *attention_args(0))
    out_own, mixed_0 = lax.optimization_barrier((out_own, mixed_0))
    out_other = flip(out_own, "core")
    mixed_0 = from_heads(mixed_0)
    out_full = jnp.where(
        core == 0,
        jnp.stack([out_own, out_other], axis=1),
        jnp.stack([out_other, out_own], axis=1),
    ).reshape(width, width)
    forward_0 = to_experts(0, mixed_0, out_full, weights[1], weights[3], *seq_rows[1][1:])
    mixed_1, *saved_1 = attend_forward(order, seq_rows[1], *attention_args(1))
    saved = [saved_0, saved_1]
    forward_0[5], mixed_1 = lax.optimization_barrier((forward_0[5], mixed_1))
    mixed_1 = from_heads(after_all(mixed_1, weights[2]))
    forward = [forward_0, to_experts(1, mixed_1, out_full)]

    def experts_of(m, x_own):
        return run_experts(
            scalars,
            x_own,
            flip(x_own, "core"),
            g_all,
            m,
            router_pad,
            weights,
            cap,
            m == 0,
        )

    def back_sum(own, other):
        return add(own, flip(other, "core"))

    def middle_back(m, back):
        mixed, middle, norm_back, hidden_two, gates = forward[m][:5]
        grad_top = cot[m * tok : (m + 1) * tok].astype(F32)
        tail = back[:, width:]
        d_gates = tail[:, :experts] + tail[:, 64 : 64 + experts]
        d_select = gates * (d_gates - jnp.sum(gates * d_gates, axis=-1, keepdims=True))
        d_logits = d_select.astype(BF)
        grad_router = t_mm(hidden_two, d_logits)
        d_two = back[:, :width] + mm_t(d_logits, router)
        d_middle, grad_mlp = norm_back(d_two)
        d_middle = d_middle + grad_top
        d_branch = d_middle.astype(BF)
        grad_out = t_mm(mixed, d_branch)
        d_mixed = mm_t(d_branch, out_full).astype(BF)
        d_mixed = d_mixed.reshape(tok, n_ctx, heads).transpose(1, 0, 2)
        return d_middle, d_mixed, (grad_out, grad_router, grad_mlp)

    def attention_back(m, d_mixed):
        *d_hidden, grad_heads, grad_attn, grad_qk = attend_backward(
            order, *saved[m], d_mixed.reshape(length, heads), *attention_args(m)
        )
        grad_qk = jnp.concatenate(
            [grad_qk[0, :DH] + grad_qk[0, DH : 2 * DH], grad_qk[0, 2 * DH : 3 * DH]]
        )
        return d_hidden, (grad_heads, grad_attn[0], grad_qk)

    def input_grad(m, d_hidden, d_middle):
        start = tokens[m, 0].astype(F32)
        inverse = lax.rsqrt(jnp.mean(start * start, axis=-1, keepdims=True) + EPS)
        u = d_hidden * gain_attn
        return (
            d_middle
            + inverse * u
            - start * (inverse**3 * jnp.mean(u * start, axis=-1, keepdims=True))
        )

    moe_0, back_own, back_other, *kept_0 = experts_of(0, forward[0][5])
    x_1, back_own, back_other, moe_0 = lax.optimization_barrier(
        (forward[1][5], back_own, back_other, moe_0)
    )
    back_0 = back_sum(back_own, back_other)
    moe_0 = lax.psum_scatter(moe_0, FSDP, scatter_dimension=0, tiled=True)[0]
    x_1 = after_all(x_1, back_0)
    back_0 = exchange(back_0, GROUP)
    moe_own, moe_other, back_own, back_other, *kept_1 = experts_of(1, x_1)
    back_0, back_own, back_other, moe_own, moe_other = lax.optimization_barrier(
        (back_0, back_own, back_other, moe_own, moe_other)
    )
    back_1 = back_sum(back_own, back_other)
    d_middle_0, d_mixed_0, grads_0 = middle_back(0, sum_parts(back_0))
    d_mixed_0 = exchange(d_mixed_0, CTX)
    d_mixed_0, back_1 = lax.optimization_barrier((d_mixed_0, back_1))
    back_1 = exchange(back_1, GROUP)
    d_hidden_0, head_grads_0 = attention_back(0, d_mixed_0)
    kept_1[0] = after_all(kept_1[0], head_grads_0[0])
    weight_parts = expert_grads(order, (kept_0, kept_1))
    hidden_moved_0 = by_z(d_hidden_0)
    moe_other = flip(moe_other, "core")
    back_1, weight_parts, moe_other = lax.optimization_barrier((back_1, weight_parts, moe_other))
    weight_moved = by_z(weight_parts)
    moe_1 = [add(moe_own[2 * k : 2 * k + 2], moe_other[2 * k : 2 * k + 2]) for k in range(4)]
    moe_moved = by_x(moe_1)
    d_middle_1, d_mixed_1, grads_1 = middle_back(1, sum_parts(back_1))
    d_mixed_1, hidden_moved_0 = lax.optimization_barrier((d_mixed_1, hidden_moved_0))
    d_mixed_1 = exchange(d_mixed_1, CTX)
    grad_out, grad_router, grad_mlp = jax.tree.map(jnp.add, grads_0, grads_1)
    grad_out = grad_out.astype(BF).reshape(n_all // 2, 2, rows, width)
    grad_own = lax.dynamic_index_in_dim(grad_out, core, axis=1, keepdims=False)
    grad_other = lax.dynamic_index_in_dim(grad_out, 1 - core, axis=1, keepdims=False)
    grad_out = exchange(back_sum(grad_own, grad_other), CTX + GROUP)
    d_hidden_1, head_grads_1 = attention_back(1, d_mixed_1)
    d_hidden_1, weight_moved[0], weight_moved[2], moe_moved = lax.optimization_barrier(
        (d_hidden_1, weight_moved[0], weight_moved[2], moe_moved)
    )
    hidden_moved_1 = by_z(d_hidden_1)
    hidden_sums = pair_sums(d_hidden_0, hidden_moved_0)
    d_hidden_0 = hidden_sums[0] + flip(hidden_sums[1].astype(BF), "yl").astype(F32)
    moe_sums = pair_sums(moe_1, moe_moved)
    moe_1 = moe_sums[0] + flip(moe_sums[1].astype(BF), "yh").astype(F32)
    grad_heads, grad_attn, grad_qk = jax.tree.map(jnp.add, head_grads_0, head_grads_1)

    grad_qk = jnp.pad(grad_qk[:, None], ((0, 0), (0, rows - 1))).reshape(-1)
    grad_small = jnp.concatenate(
        [grad_router, grad_attn[:, None], grad_mlp[:, None], grad_qk[:, None]], axis=1
    )
    grad_small = jnp.pad(grad_small, ((0, 0), (0, 128 - grad_small.shape[1])))
    grad_pack = jnp.concatenate([grad_heads, grad_small], axis=1).astype(BF)
    grad_pack = exchange(grad_pack.reshape(n_all, rows, -1), ALL).astype(F32)
    own_heads = jnp.sum(grad_pack[:, :, :span].reshape(n_ctx, n_fsdp, rows, -1), axis=1)
    own_heads = own_heads.transpose(1, 0, 2)
    own_small = jnp.sum(grad_pack[:, :, span:], axis=0)
    own_out = sum_parts(grad_out)
    weight_moved[1], hidden_moved_1, moe_0 = lax.optimization_barrier(
        (weight_moved[1], hidden_moved_1, after_all(moe_0, grad_pack))
    )
    weight_sums = pair_sums(weight_parts, weight_moved)
    hidden_sums = pair_sums(d_hidden_1, hidden_moved_1)
    d_hidden_1 = hidden_sums[0] + flip(hidden_sums[1].astype(BF), "yl").astype(F32)
    expert_own = weight_sums[0] + flip(weight_sums[1].astype(BF), "yl").astype(F32)
    outs = [
        (forward[0][1] + moe_0.astype(F32)).astype(BF),
        (forward[1][1] + moe_1).astype(BF),
    ]
    d_inputs = [
        input_grad(0, d_hidden_0, d_middle_0),
        input_grad(1, d_hidden_1, d_middle_1),
    ]

    return (
        jnp.stack(outs)[:, None],
        jnp.stack(d_inputs)[:, None],
        own_heads[:, :, :heads].reshape(rows, -1),
        own_heads[:, :, heads : heads + DH].reshape(rows, -1),
        own_heads[:, :, heads + DH :].reshape(rows, -1),
        own_out,
        own_small[:, :experts],
        own_small[:, experts],
        own_small[:, experts + 1],
        own_small[:1, experts + 2],
        expert_own[:, 0],
        expert_own[:, 1],
        expert_own[:, 2],
    )


def solution(mesh):
    mesh = Mesh(mesh.devices.reshape(4, 2, 2, 4, 2), ALL)
    weight = P(ALL, None)
    gain = P(ALL)
    rows = P(None, FSDP, CTX, None)
    expert = P(FSDP, CTX, None)
    return jax.shard_map(
        body,
        mesh=mesh,
        in_specs=(rows, P(None, FSDP, None), rows)
        + (weight,) * 5
        + (gain,) * 3
        + (expert,) * 3
        + (rows,),
        out_specs=(rows, rows) + (weight,) * 5 + (gain,) * 3 + (expert,) * 3,
        check_vma=False,
    )
```

```python
import functools

import jax
import jax.numpy as jnp
from jax import lax
from jax.experimental import pallas as pl
from jax.experimental.pallas import tpu as pltpu
from jax.sharding import Mesh
from jax.sharding import PartitionSpec as P

BF = jnp.bfloat16
F32 = jnp.float32
H = 16
KV = 8
DH = 64
TOPK = 8
WINDOW = 1024
EPS = 1e-06
THETA = 10000.0


def dot(a, b, ca, cb):
    return lax.dot_general(a, b, (((ca,), (cb,)), ((), ())), preferred_element_type=F32)


def lanes_of(v):
    return lax.broadcasted_iota(jnp.int32, v.shape, v.ndim - 1)


def head_sums(v):
    low = lanes_of(v) < DH
    first = jnp.sum(jnp.where(low, v, 0.0), axis=1, keepdims=True)
    second = jnp.sum(jnp.where(low, 0.0, v), axis=1, keepdims=True)
    return jnp.where(low, first, second)


def trade(v):
    return jnp.where(
        lanes_of(v) % DH < DH // 2, pltpu.roll(v, 128 - DH // 2, 1), pltpu.roll(v, DH // 2, 1)
    )


def both_halves(v, second):
    low = lanes_of(v) < DH
    other = pltpu.roll(v, DH, 1)
    return jnp.where(low, other, v) if second else jnp.where(low, v, other)


def stack_heads(v):
    low = lanes_of(v) < DH
    zero = jnp.zeros_like(v)
    return jnp.concatenate([jnp.where(low, v, zero), jnp.where(low, zero, v)], axis=0)


def key_span(start, block, length):
    reach = WINDOW // 2 - 1
    low = max(0, start - reach) // 128 * 128
    high = min(length, -(-(start + block + reach) // 128) * 128)
    return low, high


def masked_probs(q_two, keys, seg_col, seg_row, start, low):
    block = q_two.shape[0] // 2
    scores = dot(q_two, keys, 1, 1)
    shape = (block, keys.shape[0])
    gap = (
        lax.broadcasted_iota(jnp.int32, shape, 0)
        - lax.broadcasted_iota(jnp.int32, shape, 1)
        + (start - low)
    )
    allowed = (seg_col == seg_row) & (jnp.abs(gap) < WINDOW // 2)
    bias = jnp.where(allowed, 0.0, -1e30)
    scores = scores + jnp.concatenate([bias, bias], axis=0)
    raised = jnp.exp(scores - jnp.max(scores, axis=1, keepdims=True))
    return raised * (1.0 / jnp.sum(raised, axis=1, keepdims=True))


def attend_kernel(
    order_ref,
    *refs,
):
    pieces, refs = refs[:-13], refs[-13:]
    gain_ref, w_ref, head_gain_ref, cos_ref, sin_ref, seg_col_ref, seg_row_ref = refs[:7]
    mixed_ref, hidden_ref, q_ref, kv_ref, keys_ref, values_ref = refs[7:]
    tok, width = pieces[0].shape[1:]
    length = hidden_ref.shape[0]
    pieces = [(ref, i) for ref in pieces for i in range(ref.shape[0])]
    for r, (ref, i) in enumerate(pieces):
        x = ref[i].astype(F32)
        x = x * lax.rsqrt(jnp.mean(x * x, axis=1, keepdims=True) + EPS) * gain_ref[...]
        rows = pl.ds(pl.multiple_of(order_ref[r] * tok, tok), tok)
        hidden_ref[rows] = x.astype(BF)
    raw = dot(hidden_ref[...], w_ref[...], 1, 0)
    for half in range(2):
        u = raw[:, half * 128 : half * 128 + 128]
        gain = head_gain_ref[:, half * 128 : half * 128 + 128]
        n = u * lax.rsqrt(head_sums(u * u) * (1.0 / DH) + EPS) * gain
        turned = n * cos_ref[...] + trade(n) * sin_ref[...]
        if half == 0:
            q_ref[...] = turned.astype(BF)
        else:
            kv = jnp.where(lanes_of(u) < DH, turned, u)
            kv_ref[...] = kv.astype(BF)
            keys_ref[...] = both_halves(kv, False).astype(BF)
            values_ref[...] = both_halves(kv, True).astype(BF)
    block = 256
    for start in range(0, length, block):
        low, high = key_span(start, block, length)
        q_two = stack_heads(q_ref[start : start + block].astype(F32) * DH**-0.5).astype(BF)
        probs = masked_probs(
            q_two,
            keys_ref[low:high],
            seg_col_ref[start : start + block],
            seg_row_ref[:, low:high],
            start,
            low,
        )
        result = dot(probs.astype(BF), values_ref[low:high], 1, 0)
        first = lanes_of(result[:block]) < DH
        mixed_ref[start : start + block] = jnp.where(first, result[:block], result[block:]).astype(
            BF
        )


def attend_back_kernel(
    order_ref,
    hidden_ref,
    q_ref,
    kv_ref,
    d_mixed_ref,
    gain_ref,
    w_ref,
    head_gain_ref,
    cos_ref,
    sin_ref,
    seg_col_ref,
    seg_row_ref,
    d_hidden_0_ref,
    d_hidden_1_ref,
    d_hidden_2_ref,
    d_hidden_3_ref,
    grad_w_ref,
    grad_gain_ref,
    grad_heads_ref,
    keys_ref,
    values_ref,
    d_q_ref,
    d_k_ref,
    d_v_ref,
    d_raw_ref,
):
    length = hidden_ref.shape[0]
    kv = kv_ref[...].astype(F32)
    keys_ref[...] = both_halves(kv, False).astype(BF)
    values_ref[...] = both_halves(kv, True).astype(BF)
    d_k_ref[...] = jnp.zeros_like(d_k_ref)
    d_v_ref[...] = jnp.zeros_like(d_v_ref)
    block = 256
    for start in range(0, length, block):
        low, high = key_span(start, block, length)
        q_two = stack_heads(q_ref[start : start + block].astype(F32) * DH**-0.5).astype(BF)
        m_two = stack_heads(d_mixed_ref[start : start + block].astype(F32)).astype(BF)
        probs = masked_probs(
            q_two,
            keys_ref[low:high],
            seg_col_ref[start : start + block],
            seg_row_ref[:, low:high],
            start,
            low,
        )
        d_probs = dot(m_two, values_ref[low:high], 1, 1)
        inner = jnp.sum(probs * d_probs, axis=1, keepdims=True)
        d_scores = (probs * (d_probs - inner)).astype(BF)
        result = dot(d_scores, keys_ref[low:high], 1, 0)
        first = lanes_of(result[:block]) < DH
        d_q_ref[start : start + block] = jnp.where(first, result[:block], result[block:]) * (
            DH**-0.5
        )
        d_k_ref[low:high] += dot(d_scores, q_two, 0, 0)
        d_v_ref[low:high] += dot(probs.astype(BF), m_two, 0, 0)
    raw = dot(hidden_ref[...], w_ref[...], 1, 0)
    d_k = d_k_ref[...]
    d_k = d_k + pltpu.roll(d_k, DH, 1)
    d_v = d_v_ref[...]
    d_v = d_v + pltpu.roll(d_v, DH, 1)
    for half in range(2):
        lanes = slice(half * 128, half * 128 + 128)
        u = raw[:, lanes]
        gain = head_gain_ref[:, lanes]
        d = d_q_ref[...] if half == 0 else d_k
        d = d * cos_ref[...] + trade(d * sin_ref[...])
        r = lax.rsqrt(head_sums(u * u) * (1.0 / DH) + EPS)
        grad_heads_ref[:, lanes] = jnp.sum(d * u * r, axis=0, keepdims=True)
        d = d * gain
        d = d * r - u * (r * r * r * (head_sums(d * u) * (1.0 / DH)))
        if half == 1:
            d = jnp.where(lanes_of(d) < DH, d, d_v)
        d_raw_ref[:, lanes] = d.astype(BF)
    grad_w_ref[...] = dot(hidden_ref[...], d_raw_ref[...], 0, 0)
    total = jnp.zeros(grad_gain_ref.shape, F32)
    outs = (d_hidden_0_ref, d_hidden_1_ref, d_hidden_2_ref, d_hidden_3_ref)
    tok = length // 8
    for r in range(8):
        rows = pl.ds(pl.multiple_of(order_ref[r] * tok, tok), tok)
        d_hidden = dot(d_raw_ref[rows], w_ref[...], 1, 1)
        outs[r // 2][r % 2] = d_hidden.astype(BF)
        total = total + jnp.sum(d_hidden * hidden_ref[rows].astype(F32), axis=0, keepdims=True)
    grad_gain_ref[...] = total / gain_ref[...]


def whole(a):
    return pl.BlockSpec(a.shape, lambda i: (0,) * len(a.shape), pipeline_mode=pl.Buffered(1))


def attend_forward(order, pieces, gain, w_heads, head_gain, cosine, sine, seg_col, seg_row):
    length = cosine.shape[0]
    width = w_heads.shape[0]
    shape = jax.ShapeDtypeStruct
    outs = [
        shape((length, 128), BF),
        shape((length, width), BF),
        shape((length, 128), BF),
        shape((length, 128), BF),
    ]
    args = list(pieces) + [gain, w_heads, head_gain, cosine, sine, seg_col, seg_row]
    return pl.pallas_call(
        attend_kernel,
        out_shape=outs,
        grid=(1,),
        in_specs=[pl.BlockSpec(memory_space=pltpu.SMEM)] + [whole(a) for a in args],
        out_specs=[whole(o) for o in outs],
        scratch_shapes=[pltpu.VMEM((length, 128), BF), pltpu.VMEM((length, 128), BF)],
        compiler_params=pltpu.CompilerParams(vmem_limit_bytes=40 * 1024 * 1024),
        cost_estimate=pl.CostEstimate(flops=12 * 10**9, bytes_accessed=8 << 20, transcendentals=0),
    )(order, *args)


def attend_backward(
    order, hidden, q, kv, d_mixed, gain, w_heads, head_gain, cosine, sine, seg_col, seg_row
):
    length, width = hidden.shape
    shape = jax.ShapeDtypeStruct
    outs = [shape((2, length // 8, width), BF)] * 4 + [
        shape((width, 256), F32),
        shape((1, width), F32),
        shape((1, 256), F32),
    ]
    args = [hidden, q, kv, d_mixed, gain, w_heads, head_gain, cosine, sine, seg_col, seg_row]
    return pl.pallas_call(
        attend_back_kernel,
        out_shape=outs,
        grid=(1,),
        in_specs=[pl.BlockSpec(memory_space=pltpu.SMEM)] + [whole(a) for a in args],
        out_specs=[whole(o) for o in outs],
        scratch_shapes=[pltpu.VMEM((length, 128), BF)] * 2
        + [pltpu.VMEM((length, 128), F32)] * 3
        + [pltpu.VMEM((length, 256), BF)],
        compiler_params=pltpu.CompilerParams(vmem_limit_bytes=40 * 1024 * 1024),
        cost_estimate=pl.CostEstimate(flops=25 * 10**9, bytes_accessed=8 << 20, transcendentals=0),
    )(order, *args)


def halves(v):
    high = v.astype(BF)
    return high, (v - high.astype(F32)).astype(BF)


def expert_kernel(scalar_ref, *refs, joined):
    x_own_ref, x_other_ref, g_ref, router_ref = refs[:4]
    pieces, refs = refs[4:9], refs[9:]
    outs, refs = (refs[:1], refs[1:]) if joined else (refs[:2], refs[2:])
    back_own_ref, back_other_ref, xe_ref, de_ref, act_ref, da_ref, db_ref = refs[:7]
    pick_ref, weight_ref, dgate_ref, eo_ref, dr_ref, w_ref = refs[7:]
    half, tok, width = x_own_ref.shape
    sources = 2 * half
    core = scalar_ref[1]
    depth = w_ref.shape[2] // 8

    pieces = [(ref, i) for ref in pieces for i in range(ref.shape[0])]
    for r, (ref, i) in enumerate(pieces):
        rows = pl.ds(pl.multiple_of(scalar_ref[2 + r] * depth, depth), depth)
        w_ref[:, :, rows] = ref[i]
    local, slots, hidden = act_ref.shape
    cap = slots // sources
    first = scalar_ref[0]
    lane = lax.broadcasted_iota(jnp.int32, (tok, 128), 1)
    spot = lax.broadcasted_iota(jnp.int32, (tok, local * cap), 1)
    row_expert = lax.broadcasted_iota(jnp.int32, (local * cap, 128), 0) // cap
    slot_lane = lax.broadcasted_iota(jnp.int32, (local * cap, 128), 1)
    own_lane = slot_lane == first + row_expert

    def fetch(i, carry, x_ref, offset, column):
        s = i + offset
        x = x_ref[i]
        from_g = 2 * i + column
        held = g_ref[from_g, :, width:].astype(F32)
        chosen = held >= 0.0
        logits = jnp.where(chosen, dot(x, router_ref[...], 1, 0), -1e30)
        top = jnp.max(logits, axis=1, keepdims=True)
        raised = jnp.where(chosen, jnp.exp(logits - top), 0.0)
        gates = raised / jnp.sum(raised, axis=1, keepdims=True)
        pick = jnp.zeros((tok, local * cap), F32)
        for e in range(local):
            mine = jnp.max(jnp.where(lane == first + e, held, -1.0), axis=1, keepdims=True)
            goal = jnp.where(mine >= 0.0, mine + e * cap, -1.0).astype(jnp.int32)
            pick = jnp.where(spot == goal, 1.0, pick)
        pick = pick.astype(BF)
        pick_ref[s] = pick
        rows = pl.ds(pl.multiple_of(s * cap, 16), cap)
        x_slots = dot(pick, x, 0, 0).astype(BF)
        g_slots = dot(pick, g_ref[from_g, :, :width], 0, 0).astype(BF)
        high, low = halves(gates)
        weight = dot(pick, high, 0, 0) + dot(pick, low, 0, 0)
        weight = jnp.sum(jnp.where(own_lane, weight, 0.0), axis=1, keepdims=True)
        for e in range(local):
            part = slice(e * cap, (e + 1) * cap)
            xe_ref[e, rows] = x_slots[part]
            de_ref[e, rows] = g_slots[part]
            weight_ref[e, rows] = weight[part]
        return carry

    for x_ref, offset, column in ((x_own_ref, 0, core), (x_other_ref, half, 1 - core)):
        lax.fori_loop(
            0, half, functools.partial(fetch, x_ref=x_ref, offset=offset, column=column), 0
        )
    chunk = 256

    def work(i, carry):
        e = i // (slots // chunk)
        rows = pl.ds(pl.multiple_of((i % (slots // chunk)) * chunk, chunk), chunk)
        w_gate = w_ref[e, 0]
        w_up = w_ref[e, 1]
        w_down = w_ref[e, 2]
        x = xe_ref[e, rows]
        a = dot(x, w_gate, 1, 0)
        b = dot(x, w_up, 1, 0)
        sig = 1.0 / (1.0 + jnp.exp(-a))
        silu = a * sig
        active = (silu * b).astype(BF)
        act_ref[e, rows] = active
        slope = b * (sig * (1.0 + a * (1.0 - sig)))
        weight = weight_ref[e, rows]
        g = de_ref[e, rows].astype(F32)
        result = dot(active, w_down, 1, 1).astype(BF).astype(F32)
        dgate_ref[e, rows] = jnp.sum(result * g, axis=1, keepdims=True)
        eo_ref[e, rows] = (weight * result).astype(BF)
        d_expert = (weight * g).astype(BF)
        de_ref[e, rows] = d_expert
        d_active = dot(d_expert, w_down, 1, 0)
        da = (d_active * slope).astype(BF)
        db = (d_active * silu).astype(BF)
        da_ref[e, rows] = da
        db_ref[e, rows] = db
        dr_ref[e, rows] = (dot(da, w_gate, 1, 1) + dot(db, w_up, 1, 1)).astype(BF)
        return carry

    lax.fori_loop(0, local * (slots // chunk), work, 0)

    def give(i, carry, back_ref, offset, column):
        s = i + offset
        rows = pl.ds(pl.multiple_of(s * cap, 16), cap)
        pick = pick_ref[s]
        eo = jnp.concatenate([eo_ref[e, rows] for e in range(local)], axis=0)
        dr = jnp.concatenate([dr_ref[e, rows] for e in range(local)], axis=0)
        dgate = jnp.concatenate([dgate_ref[e, rows] for e in range(local)], axis=0)
        high, low = halves(dgate)
        spread = jnp.where(own_lane, high.astype(F32), 0.0) + jnp.where(
            slot_lane == first + row_expert + 64, low.astype(F32), 0.0
        )
        if joined:
            outs[0][2 * i + column] = dot(pick, eo, 1, 0).astype(BF)
        else:
            outs[offset // half][scalar_ref[10 + i]] = dot(pick, eo, 1, 0).astype(BF)
        back_ref[i, :, :width] = dot(pick, dr, 1, 0).astype(BF)
        back_ref[i, :, width:] = dot(pick, spread.astype(BF), 1, 0).astype(BF)
        return carry

    for back_ref, offset, column in ((back_own_ref, 0, core), (back_other_ref, half, 1 - core)):
        lax.fori_loop(
            0, half, functools.partial(give, back_ref=back_ref, offset=offset, column=column), 0
        )


def run_experts(scalars, x_own, x_other, g_all, micro, router, pieces, cap, joined):
    half, tok, width = x_own.shape
    sources = 2 * half
    _, local, _, _, hidden = pieces[0].shape
    slots = sources * cap
    wide = g_all.shape[2]
    shape = jax.ShapeDtypeStruct
    outs = [shape((sources, tok, width), BF)] if joined else [shape((half, tok, width), BF)] * 2
    outs += [
        shape((half, tok, wide), BF),
        shape((half, tok, wide), BF),
        shape((local, slots, width), BF),
        shape((local, slots, width), BF),
        shape((local, slots, hidden), BF),
        shape((local, slots, hidden), BF),
        shape((local, slots, hidden), BF),
    ]
    g_spec = pl.BlockSpec(
        (sources, tok, wide), lambda i: (0, micro, 0), pipeline_mode=pl.Buffered(1)
    )
    args = [router, *pieces]
    return pl.pallas_call(
        functools.partial(expert_kernel, joined=joined),
        out_shape=outs,
        grid=(1,),
        in_specs=[pl.BlockSpec(memory_space=pltpu.SMEM), whole(x_own), whole(x_other), g_spec]
        + [whole(a) for a in args],
        out_specs=[whole(o) for o in outs],
        scratch_shapes=[
            pltpu.VMEM((sources, tok, local * cap), BF),
            pltpu.VMEM((local, slots, 1), F32),
            pltpu.VMEM((local, slots, 1), F32),
            pltpu.VMEM((local, slots, width), BF),
            pltpu.VMEM((local, slots, width), BF),
            pltpu.VMEM((local, 3, width, hidden), BF),
        ],
        compiler_params=pltpu.CompilerParams(vmem_limit_bytes=60 * 1024 * 1024),
        cost_estimate=pl.CostEstimate(flops=40 * 10**9, bytes_accessed=40 << 20, transcendentals=0),
    )(scalars, x_own, x_other, g_all, *args)


def expert_grad_kernel(order_ref, *refs):
    kept, outs, total_ref = refs[:10], refs[10:14], refs[14]
    left = (kept[0:2], kept[0:2], kept[2:4])
    right = (kept[6:8], kept[8:10], kept[4:6])
    step = pl.program_id(0)
    depth = outs[0].shape[3]
    for kind in range(3):

        @pl.when(step % 3 == kind)
        def _(kind=kind):
            total = dot(left[kind][0][0], right[kind][0][0], 0, 0)
            total_ref[...] = total + dot(left[kind][1][0], right[kind][1][0], 0, 0)

    for r in range(8):
        rows = pl.ds(pl.multiple_of(order_ref[r] * depth, depth), depth)
        outs[r // 2][r % 2, 0, 0] = total_ref[rows].astype(BF)


def expert_grads(order, kept):
    local, slots, width = kept[0][0].shape
    hidden = kept[0][2].shape[2]
    args = [kept[m][i] for i in range(5) for m in range(2)]
    depth = width // 8
    shape = jax.ShapeDtypeStruct
    return pl.pallas_call(
        expert_grad_kernel,
        out_shape=[shape((2, local, 3, depth, hidden), BF)] * 4,
        grid=(3 * local,),
        in_specs=[pl.BlockSpec(memory_space=pltpu.SMEM)]
        + [pl.BlockSpec((1,) + a.shape[1:], lambda i: (i // 3, 0, 0)) for a in args],
        out_specs=[
            pl.BlockSpec((2, 1, 1, depth, hidden), lambda i: (0, i // 3, i % 3, 0, 0))
        ]
        * 4,
        scratch_shapes=[pltpu.VMEM((width, hidden), F32)],
        compiler_params=pltpu.CompilerParams(vmem_limit_bytes=48 * 1024 * 1024),
        cost_estimate=pl.CostEstimate(flops=14 * 10**9, bytes_accessed=28 << 20, transcendentals=0),
    )(order, *args)


CTX = ("z", "yl")
GROUP = ("yh", "x")
FSDP = ("yh", "x", "core")
ALL = CTX + FSDP
UP = [(i, (i + 1) % 4) for i in range(4)]
DOWN = [(i, (i - 1) % 4) for i in range(4)]
TWO = [(i, (i + 2) % 4) for i in range(4)]
FLIP = [(0, 1), (1, 0)]


def mm(a, b):
    return jnp.dot(a, b, preferred_element_type=F32)


def mm_t(a, b):
    return lax.dot_general(a, b, (((1,), (1,)), ((), ())), preferred_element_type=F32)


def t_mm(a, b):
    return lax.dot_general(a, b, (((0,), (0,)), ((), ())), preferred_element_type=F32)


def ein(spec, a, b):
    return jnp.einsum(spec, a, b, preferred_element_type=F32)


def swap(parts, axis):
    return lax.all_to_all(parts, axis, split_axis=0, concat_axis=0, tiled=True)


def flip(block, axis):
    return lax.ppermute(block, axis, FLIP)


def by_z(parts):
    return [lax.ppermute(parts[k], "z", perm) for k, perm in ((1, UP), (2, TWO), (3, DOWN))]


def along_z(both):
    before, far, after = by_z([both] * 4)
    return [both, after, far, before]


class Exchange:
    def __init__(self):
        self.last = None

    def __call__(self, parts, axis):
        if self.last is not None:
            parts = after_all(parts, self.last)
        self.last = swap(parts, axis)
        return self.last

    def copies(self, block, axis, count):
        return self(jnp.broadcast_to(block[None], (count,) + block.shape), axis)


def add(a, b):
    return (a.astype(F32) + b.astype(F32)).astype(BF)


def by_x(parts):
    return [lax.ppermute(parts[k], "x", perm) for k, perm in ((1, UP), (2, TWO), (3, DOWN))]


def add_part(parts, i, more):
    pieces = [parts[:1], parts[1:]]
    pieces[i] = add(pieces[i], more)
    return jnp.concatenate(pieces, axis=0)


def pair_sums(parts, moved):
    return [sum(part[i].astype(F32) for part in [parts[0]] + moved) for i in range(2)]


def sum_parts(parts):
    return jnp.sum(parts.astype(F32), axis=0)


def after_all(value, *others):
    return lax.optimization_barrier((value,) + others)[0]


def rope_tables(positions):
    half = DH // 2
    inverse = THETA ** (-(jnp.arange(half, dtype=F32) * 2.0) / DH)
    angles = positions.astype(F32)[:, None] * inverse[None, :]
    return (jnp.cos(angles), jnp.sin(angles))


def rms_scale(values, gain):
    return values * lax.rsqrt(jnp.mean(values * values, axis=-1, keepdims=True) + EPS) * gain


def body(
    tokens,
    segments,
    routes,
    w_query,
    w_key,
    w_value,
    w_out,
    w_router,
    attn_gain,
    mlp_gain,
    qk_gain,
    w_gate,
    w_up,
    w_down,
    cotangent,
):
    micro = tokens.shape[0]
    tok = tokens.shape[2]
    width = tokens.shape[3]
    length = segments.shape[2]
    rows = w_query.shape[0]
    n_ctx, n_fsdp = 8, 16
    n_all = n_ctx * n_fsdp
    z, yl, yh, x, core = (lax.axis_index(name) for name in ALL)
    shard = (yh * 4 + x) * 2 + core
    local = w_gate.shape[0]
    experts = local * n_fsdp
    cap = (3 * tok * TOPK + 2 * experts - 1) // (2 * experts)
    all_tok = micro * tok
    ratio = H // KV
    heads = ratio * DH
    span = heads + 2 * DH

    exchange = Exchange()
    small = jnp.concatenate(
        [
            w_router,
            attn_gain[:, None],
            mlp_gain[:, None],
            jnp.pad(qk_gain[:, None], ((0, rows - 1), (0, 0))),
        ],
        axis=1,
    )
    small = jnp.pad(small, ((0, 0), (0, 128 - small.shape[1])))
    pieces = jnp.concatenate(
        [
            w_query.reshape(rows, n_ctx, heads),
            w_key.reshape(rows, n_ctx, DH),
            w_value.reshape(rows, n_ctx, DH),
            jnp.broadcast_to(small[:, None], (rows, n_ctx, 128)),
        ],
        axis=2,
    ).transpose(1, 0, 2)
    pieces = jnp.broadcast_to(pieces[:, None], (n_ctx, n_fsdp) + pieces.shape[1:])
    both_0, both_1 = (
        jnp.concatenate([tokens[m], flip(tokens[m], "yl")], axis=0) for m in range(micro)
    )
    both_w = jnp.stack([w_gate, w_up, w_down], axis=1)[None]
    head_all = exchange(pieces.reshape((n_all,) + pieces.shape[2:]), ALL).reshape(width, -1)
    both_w = jnp.concatenate([both_w, flip(both_w, "yl")], axis=0)
    seq_rows = [along_z(both_0)]
    seq_rows.append(along_z(after_all(both_1, *seq_rows[0][1:])))
    head_all = after_all(head_all, *seq_rows[0][1:], both_w)
    w_heads = head_all[:, :span]
    small_all = head_all[:, span:]
    router = small_all[:, :experts]
    small_wide = small_all.astype(F32)
    gain_attn = small_wide[:, experts]
    gain_mlp = small_wide[:, experts + 1]
    gain_heads = small_wide[:, experts + 2].reshape(-1, rows)[:, 0]
    gain_row = gain_attn[None]
    head_row = jnp.concatenate(
        [gain_heads[:DH]] * ratio + [gain_heads[DH:], jnp.ones((DH,), F32)]
    )[None]
    router_pad = jnp.pad(router, ((0, 0), (0, 128 - experts)))

    out_own = exchange.copies(w_out, CTX + GROUP, n_all // 2)

    both_w = after_all(both_w, *seq_rows[1][1:])
    w_before = lax.ppermute(both_w, "z", UP)
    w_after = lax.ppermute(both_w, "z", DOWN)
    w_far = [lax.ppermute(w_before[:1], "z", UP), lax.ppermute(w_after[1:], "z", DOWN)]

    expert_ids = jnp.arange(experts, dtype=jnp.int32)
    cot = cotangent.reshape(all_tok, width)
    chosen = jnp.any(routes.reshape(all_tok, TOPK)[:, :, None] == expert_ids, axis=1)
    before = jnp.arange(tok, dtype=jnp.int32)
    lower = (before[:, None] >= before[None, :]).astype(BF)
    counts = ein("ut,mte->mue", lower, chosen.reshape(micro, tok, experts).astype(BF))
    held = jnp.where(chosen, counts.reshape(all_tok, experts) - 1.0, -1.0)
    held = jnp.pad(held, ((0, 0), (0, 128 - experts)), constant_values=-1.0).astype(BF)
    g_all = lax.all_gather(jnp.concatenate([cot, held], axis=1), FSDP, axis=0)

    cosine, sine = rope_tables(jnp.arange(length, dtype=jnp.int32))
    cosine = jnp.tile(cosine, (1, 4))
    sine = jnp.tile(jnp.concatenate([-sine, sine], axis=1), (1, 2))
    rel = jnp.arange(n_ctx, dtype=jnp.int32)
    order = ((z + rel // 2) % 4) * 2 + (yl + rel % 2) % 2
    g_rel = ((rel % 4 - x) % 4) * 2 + (rel // 4 - yh) % 2
    scalars = jnp.concatenate([jnp.stack([shard * local, core]), order, g_rel]).astype(jnp.int32)

    def to_owner(v):
        return exchange(v.reshape(n_ctx, tok, -1), CTX)

    def attention_args(m):
        seg = segments[m, 0]
        return gain_row, w_heads, head_row, cosine, sine, seg[:, None], seg[None, :]

    mixed_0, *saved_0 = attend_forward(order, seq_rows[0], *attention_args(0))
    mixed_1, *saved_1 = attend_forward(order, seq_rows[1], *attention_args(1))
    saved = [saved_0, saved_1]
    out_own, mixed_0, mixed_1 = lax.optimization_barrier((out_own, mixed_0, mixed_1))
    out_other = flip(out_own, "core")
    mixed = jnp.stack([mixed_0, mixed_1]).reshape(micro, n_ctx, tok, heads).transpose(1, 0, 2, 3)
    mixed = exchange(mixed.reshape(n_ctx, all_tok, heads), CTX)
    mixed = mixed.transpose(1, 0, 2).reshape(all_tok, width)
    out_full = jnp.where(
        core == 0,
        jnp.stack([out_own, out_other], axis=1),
        jnp.stack([out_other, out_own], axis=1),
    ).reshape(width, width)
    middle = tokens.reshape(all_tok, width).astype(F32) + mm(mixed, out_full)
    inv_two = lax.rsqrt(jnp.mean(middle * middle, axis=-1, keepdims=True) + EPS)
    hidden_two = (middle * inv_two * gain_mlp).astype(BF)
    x_0 = after_all(hidden_two[:tok], w_before, w_after)
    x_0 = exchange.copies(x_0, GROUP, n_ctx)
    x_0, *w_far = lax.optimization_barrier((x_0, *w_far))
    x_1 = exchange.copies(hidden_two[tok:], GROUP, n_ctx)
    weights = [both_w, w_after, *w_far, w_before]
    logits = jnp.where(chosen, mm(hidden_two, router), -1e30)
    gates_all = jnp.where(chosen, jax.nn.softmax(logits, axis=-1), 0.0)

    def own_rows(v, m):
        return v[m * tok : (m + 1) * tok]

    def experts_of(m, x_own):
        return run_experts(
            scalars,
            x_own,
            flip(x_own, "core"),
            g_all,
            m,
            router_pad,
            weights,
            cap,
            m == 0,
        )

    def back_sum(own, other):
        return add(own, flip(other, "core"))

    def middle_back(m, back):
        rows_mixed, rows_middle, inv, hidden, gates = (
            own_rows(v, m) for v in (mixed, middle, inv_two, hidden_two, gates_all)
        )
        grad_top = own_rows(cot, m).astype(F32)
        tail = back[:, width:]
        d_gates = tail[:, :experts] + tail[:, 64 : 64 + experts]
        d_select = gates * (d_gates - jnp.sum(gates * d_gates, axis=-1, keepdims=True))
        d_logits = d_select.astype(BF)
        grad_router = t_mm(hidden, d_logits)
        d_two = back[:, :width] + mm_t(d_logits, router)
        grad_mlp = jnp.sum(d_two * rows_middle * inv, axis=0)
        u = d_two * gain_mlp
        d_middle = (
            grad_top
            + inv * u
            - rows_middle * (inv**3 * jnp.mean(u * rows_middle, axis=-1, keepdims=True))
        )
        d_branch = d_middle.astype(BF)
        grad_out = t_mm(rows_mixed, d_branch)
        d_mixed = mm_t(d_branch, out_full).astype(BF)
        d_mixed = d_mixed.reshape(tok, n_ctx, heads).transpose(1, 0, 2)
        return d_middle, d_mixed, (grad_out, grad_router, grad_mlp)

    def attention_back(m, d_mixed):
        *d_hidden, grad_heads, grad_attn, grad_qk = attend_backward(
            order, *saved[m], d_mixed.reshape(length, heads), *attention_args(m)
        )
        grad_qk = jnp.concatenate(
            [grad_qk[0, :DH] + grad_qk[0, DH : 2 * DH], grad_qk[0, 2 * DH : 3 * DH]]
        )
        return d_hidden, (grad_heads, grad_attn[0], grad_qk)

    def input_grad(m, d_hidden, d_middle):
        start = tokens[m, 0].astype(F32)
        inverse = lax.rsqrt(jnp.mean(start * start, axis=-1, keepdims=True) + EPS)
        u = d_hidden * gain_attn
        return (
            d_middle
            + inverse * u
            - start * (inverse**3 * jnp.mean(u * start, axis=-1, keepdims=True))
        )

    moe_0, back_own, back_other, *kept_0 = experts_of(0, x_0)
    x_1, back_own, back_other, moe_0 = lax.optimization_barrier(
        (x_1, back_own, back_other, moe_0)
    )
    back_0 = back_sum(back_own, back_other)
    moe_0 = lax.psum_scatter(moe_0, FSDP, scatter_dimension=0, tiled=True)[0]
    x_1 = after_all(x_1, back_0)
    back_0 = exchange(back_0, GROUP)
    moe_own, moe_other, back_own, back_other, *kept_1 = experts_of(1, x_1)
    back_0, back_own, back_other, moe_own, moe_other = lax.optimization_barrier(
        (back_0, back_own, back_other, moe_own, moe_other)
    )
    back_1 = back_sum(back_own, back_other)
    d_middle_0, d_mixed_0, grads_0 = middle_back(0, sum_parts(back_0))
    d_mixed_0 = exchange(d_mixed_0, CTX)
    d_mixed_0, back_1 = lax.optimization_barrier((d_mixed_0, back_1))
    back_1 = exchange(back_1, GROUP)
    kept_1[0] = after_all(kept_1[0], d_mixed_0)
    weight_parts = expert_grads(order, (kept_0, kept_1))
    weight_far = [
        lax.ppermute(weight_parts[2][:1], "z", UP),
        lax.ppermute(weight_parts[2][1:], "z", DOWN),
    ]
    d_hidden_0, head_grads_0 = attention_back(0, after_all(d_mixed_0, weight_parts[0]))
    hidden_moved_0 = by_z(d_hidden_0)
    moe_other = flip(moe_other, "core")
    back_1, d_hidden_0[0], moe_other, *weight_far = lax.optimization_barrier(
        (back_1, d_hidden_0[0], moe_other, *weight_far)
    )
    d_middle_1, d_mixed_1, grads_1 = middle_back(1, sum_parts(back_1))
    weight_after = add_part(weight_parts[1], 0, weight_far[0])
    weight_before = add_part(weight_parts[3], 1, weight_far[1])
    moe_1 = [add(moe_own[2 * k : 2 * k + 2], moe_other[2 * k : 2 * k + 2]) for k in range(4)]
    d_mixed_1, hidden_moved_0 = lax.optimization_barrier((d_mixed_1, hidden_moved_0))
    weight_moved = [
        lax.ppermute(weight_after, "z", UP),
        lax.ppermute(weight_before, "z", DOWN),
    ]
    d_mixed_1 = exchange(d_mixed_1, CTX)
    moe_moved = by_x(moe_1)
    grad_out, grad_router, grad_mlp = jax.tree.map(jnp.add, grads_0, grads_1)
    grad_out = grad_out.astype(BF).reshape(n_all // 2, 2, rows, width)
    grad_own = lax.dynamic_index_in_dim(grad_out, core, axis=1, keepdims=False)
    grad_other = lax.dynamic_index_in_dim(grad_out, 1 - core, axis=1, keepdims=False)
    grad_out = back_sum(grad_own, grad_other)
    d_hidden_1, head_grads_1 = attention_back(1, d_mixed_1)
    grad_out = exchange(grad_out, CTX + GROUP)
    hidden_moved_1 = by_z(d_hidden_1)
    hidden_sums = pair_sums(d_hidden_0, hidden_moved_0)
    d_hidden_0 = hidden_sums[0] + flip(hidden_sums[1].astype(BF), "yl").astype(F32)
    grad_out, hidden_moved_1, weight_moved, moe_moved = lax.optimization_barrier(
        (grad_out, hidden_moved_1, weight_moved, moe_moved)
    )
    exchange.last = grad_out
    weight_sums = pair_sums(weight_parts, weight_moved)
    weight_yl = flip(weight_sums[1].astype(BF), "yl")
    hidden_sums = pair_sums(d_hidden_1, hidden_moved_1)
    hidden_yl = flip(hidden_sums[1].astype(BF), "yl")
    moe_sums = pair_sums(moe_1, moe_moved)
    moe_yh = flip(moe_sums[1].astype(BF), "yh")
    grad_heads, grad_attn, grad_qk = jax.tree.map(jnp.add, head_grads_0, head_grads_1)

    grad_qk = jnp.pad(grad_qk[:, None], ((0, 0), (0, rows - 1))).reshape(-1)
    grad_small = jnp.concatenate(
        [grad_router, grad_attn[:, None], grad_mlp[:, None], grad_qk[:, None]], axis=1
    )
    grad_small = jnp.pad(grad_small, ((0, 0), (0, 128 - grad_small.shape[1])))
    grad_pack = jnp.concatenate([grad_heads, grad_small], axis=1).astype(BF)
    grad_pack = exchange(grad_pack.reshape(n_all, rows, -1), ALL).astype(F32)
    own_heads = jnp.sum(grad_pack[:, :, :span].reshape(n_ctx, n_fsdp, rows, -1), axis=1)
    own_heads = own_heads.transpose(1, 0, 2)
    own_small = jnp.sum(grad_pack[:, :, span:], axis=0)
    own_out = sum_parts(grad_out)
    moe_0 = after_all(moe_0, grad_pack)
    d_hidden_1 = hidden_sums[0] + hidden_yl.astype(F32)
    expert_own = weight_sums[0] + weight_yl.astype(F32)
    moe_1 = moe_sums[0] + moe_yh.astype(F32)
    outs = [
        (own_rows(middle, 0) + moe_0.astype(F32)).astype(BF),
        (own_rows(middle, 1) + moe_1).astype(BF),
    ]
    d_inputs = [
        input_grad(0, d_hidden_0, d_middle_0),
        input_grad(1, d_hidden_1, d_middle_1),
    ]

    return (
        jnp.stack(outs)[:, None],
        jnp.stack(d_inputs)[:, None],
        own_heads[:, :, :heads].reshape(rows, -1),
        own_heads[:, :, heads : heads + DH].reshape(rows, -1),
        own_heads[:, :, heads + DH :].reshape(rows, -1),
        own_out,
        own_small[:, :experts],
        own_small[:, experts],
        own_small[:, experts + 1],
        own_small[:1, experts + 2],
        expert_own[:, 0],
        expert_own[:, 1],
        expert_own[:, 2],
    )


def solution(mesh):
    mesh = Mesh(mesh.devices.reshape(4, 2, 2, 4, 2), ALL)
    weight = P(ALL, None)
    gain = P(ALL)
    rows = P(None, FSDP, CTX, None)
    expert = P(FSDP, CTX, None)
    return jax.shard_map(
        body,
        mesh=mesh,
        in_specs=(rows, P(None, FSDP, None), rows)
        + (weight,) * 5
        + (gain,) * 3
        + (expert,) * 3
        + (rows,),
        out_specs=(rows, rows) + (weight,) * 5 + (gain,) * 3 + (expert,) * 3,
        check_vma=False,
    )
```

```python
import functools

import jax
import jax.numpy as jnp
from jax import lax
from jax.experimental import pallas as pl
from jax.experimental.pallas import tpu as pltpu
from jax.sharding import Mesh
from jax.sharding import PartitionSpec as P

BF = jnp.bfloat16
F32 = jnp.float32
H = 16
KV = 8
DH = 64
TOPK = 8
WINDOW = 1024
EPS = 1e-06
THETA = 10000.0
COST = pl.CostEstimate(flops=10**7, bytes_accessed=10**5, transcendentals=0)


def dot(a, b, ca, cb):
    return lax.dot_general(a, b, (((ca,), (cb,)), ((), ())), preferred_element_type=F32)


def lanes_of(v):
    return lax.broadcasted_iota(jnp.int32, v.shape, v.ndim - 1)


def head_sums(v):
    low = lanes_of(v) < DH
    first = jnp.sum(jnp.where(low, v, 0.0), axis=1, keepdims=True)
    second = jnp.sum(jnp.where(low, 0.0, v), axis=1, keepdims=True)
    return jnp.where(low, first, second)


def trade(v):
    return jnp.where(
        lanes_of(v) % DH < DH // 2, pltpu.roll(v, 128 - DH // 2, 1), pltpu.roll(v, DH // 2, 1)
    )


def both_halves(v, second):
    low = lanes_of(v) < DH
    other = pltpu.roll(v, DH, 1)
    return jnp.where(low, other, v) if second else jnp.where(low, v, other)


def stack_heads(v):
    low = lanes_of(v) < DH
    zero = jnp.zeros_like(v)
    return jnp.concatenate([jnp.where(low, v, zero), jnp.where(low, zero, v)], axis=0)


def key_span(start, block, length):
    reach = WINDOW // 2 - 1
    low = max(0, start - reach) // 128 * 128
    high = min(length, -(-(start + block + reach) // 128) * 128)
    return low, high


def masked_probs(q_two, keys, seg_col, seg_row, start, low):
    block = q_two.shape[0] // 2
    scores = dot(q_two, keys, 1, 1)
    shape = (block, keys.shape[0])
    gap = (
        lax.broadcasted_iota(jnp.int32, shape, 0)
        - lax.broadcasted_iota(jnp.int32, shape, 1)
        + (start - low)
    )
    allowed = (seg_col == seg_row) & (jnp.abs(gap) < WINDOW // 2)
    bias = jnp.where(allowed, 0.0, -1e30)
    scores = scores + jnp.concatenate([bias, bias], axis=0)
    raised = jnp.exp(scores - jnp.max(scores, axis=1, keepdims=True))
    return raised * (1.0 / jnp.sum(raised, axis=1, keepdims=True))


def attend_kernel(
    order_ref,
    *refs,
):
    pieces, refs = refs[:-13], refs[-13:]
    gain_ref, w_ref, head_gain_ref, cos_ref, sin_ref, seg_col_ref, seg_row_ref = refs[:7]
    mixed_ref, hidden_ref, q_ref, kv_ref, keys_ref, values_ref = refs[7:]
    tok, width = pieces[0].shape[1:]
    length = hidden_ref.shape[0]
    pieces = [(ref, i) for ref in pieces for i in range(ref.shape[0])]
    for r, (ref, i) in enumerate(pieces):
        x = ref[i].astype(F32)
        x = x * lax.rsqrt(jnp.mean(x * x, axis=1, keepdims=True) + EPS) * gain_ref[...]
        rows = pl.ds(pl.multiple_of(order_ref[r] * tok, tok), tok)
        hidden_ref[rows] = x.astype(BF)
    raw = dot(hidden_ref[...], w_ref[...], 1, 0)
    for half in range(2):
        u = raw[:, half * 128 : half * 128 + 128]
        gain = head_gain_ref[:, half * 128 : half * 128 + 128]
        n = u * lax.rsqrt(head_sums(u * u) * (1.0 / DH) + EPS) * gain
        turned = n * cos_ref[...] + trade(n) * sin_ref[...]
        if half == 0:
            q_ref[...] = turned.astype(BF)
        else:
            kv = jnp.where(lanes_of(u) < DH, turned, u)
            kv_ref[...] = kv.astype(BF)
            keys_ref[...] = both_halves(kv, False).astype(BF)
            values_ref[...] = both_halves(kv, True).astype(BF)
    block = 256
    for start in range(0, length, block):
        low, high = key_span(start, block, length)
        q_two = stack_heads(q_ref[start : start + block].astype(F32) * DH**-0.5).astype(BF)
        probs = masked_probs(
            q_two,
            keys_ref[low:high],
            seg_col_ref[start : start + block],
            seg_row_ref[:, low:high],
            start,
            low,
        )
        result = dot(probs.astype(BF), values_ref[low:high], 1, 0)
        first = lanes_of(result[:block]) < DH
        mixed_ref[start : start + block] = jnp.where(first, result[:block], result[block:]).astype(
            BF
        )


def attend_back_kernel(
    order_ref,
    hidden_ref,
    q_ref,
    kv_ref,
    d_mixed_ref,
    gain_ref,
    w_ref,
    head_gain_ref,
    cos_ref,
    sin_ref,
    seg_col_ref,
    seg_row_ref,
    d_hidden_0_ref,
    d_hidden_1_ref,
    d_hidden_2_ref,
    d_hidden_3_ref,
    grad_w_ref,
    grad_gain_ref,
    grad_heads_ref,
    keys_ref,
    values_ref,
    d_q_ref,
    d_k_ref,
    d_v_ref,
    d_raw_ref,
):
    length = hidden_ref.shape[0]
    kv = kv_ref[...].astype(F32)
    keys_ref[...] = both_halves(kv, False).astype(BF)
    values_ref[...] = both_halves(kv, True).astype(BF)
    d_k_ref[...] = jnp.zeros_like(d_k_ref)
    d_v_ref[...] = jnp.zeros_like(d_v_ref)
    block = 256
    for start in range(0, length, block):
        low, high = key_span(start, block, length)
        q_two = stack_heads(q_ref[start : start + block].astype(F32) * DH**-0.5).astype(BF)
        m_two = stack_heads(d_mixed_ref[start : start + block].astype(F32)).astype(BF)
        probs = masked_probs(
            q_two,
            keys_ref[low:high],
            seg_col_ref[start : start + block],
            seg_row_ref[:, low:high],
            start,
            low,
        )
        d_probs = dot(m_two, values_ref[low:high], 1, 1)
        inner = jnp.sum(probs * d_probs, axis=1, keepdims=True)
        d_scores = (probs * (d_probs - inner)).astype(BF)
        result = dot(d_scores, keys_ref[low:high], 1, 0)
        first = lanes_of(result[:block]) < DH
        d_q_ref[start : start + block] = jnp.where(first, result[:block], result[block:]) * (
            DH**-0.5
        )
        d_k_ref[low:high] += dot(d_scores, q_two, 0, 0)
        d_v_ref[low:high] += dot(probs.astype(BF), m_two, 0, 0)
    raw = dot(hidden_ref[...], w_ref[...], 1, 0)
    d_k = d_k_ref[...]
    d_k = d_k + pltpu.roll(d_k, DH, 1)
    d_v = d_v_ref[...]
    d_v = d_v + pltpu.roll(d_v, DH, 1)
    for half in range(2):
        lanes = slice(half * 128, half * 128 + 128)
        u = raw[:, lanes]
        gain = head_gain_ref[:, lanes]
        d = d_q_ref[...] if half == 0 else d_k
        d = d * cos_ref[...] + trade(d * sin_ref[...])
        r = lax.rsqrt(head_sums(u * u) * (1.0 / DH) + EPS)
        grad_heads_ref[:, lanes] = jnp.sum(d * u * r, axis=0, keepdims=True)
        d = d * gain
        d = d * r - u * (r * r * r * (head_sums(d * u) * (1.0 / DH)))
        if half == 1:
            d = jnp.where(lanes_of(d) < DH, d, d_v)
        d_raw_ref[:, lanes] = d.astype(BF)
    grad_w_ref[...] = dot(hidden_ref[...], d_raw_ref[...], 0, 0)
    total = jnp.zeros(grad_gain_ref.shape, F32)
    outs = (d_hidden_0_ref, d_hidden_1_ref, d_hidden_2_ref, d_hidden_3_ref)
    tok = length // 8
    for step in range(4):
        rows = pl.ds(pl.multiple_of(order_ref[2 * step] // 2 * (2 * tok), 2 * tok), 2 * tok)
        d_hidden = dot(d_raw_ref[rows], w_ref[...], 1, 1)
        own = order_ref[0] % 2
        outs[step][own] = d_hidden[:tok].astype(BF)
        outs[step][1 - own] = d_hidden[tok:].astype(BF)
        total = total + jnp.sum(d_hidden * hidden_ref[rows].astype(F32), axis=0, keepdims=True)
    grad_gain_ref[...] = total / gain_ref[...]


def whole(a):
    return pl.BlockSpec(a.shape, lambda i: (0,) * len(a.shape), pipeline_mode=pl.Buffered(1))


def attend_forward(order, pieces, gain, w_heads, head_gain, cosine, sine, seg_col, seg_row):
    length = cosine.shape[0]
    width = w_heads.shape[0]
    shape = jax.ShapeDtypeStruct
    outs = [
        shape((length, 128), BF),
        shape((length, width), BF),
        shape((length, 128), BF),
        shape((length, 128), BF),
    ]
    args = list(pieces) + [gain, w_heads, head_gain, cosine, sine, seg_col, seg_row]
    return pl.pallas_call(
        attend_kernel,
        out_shape=outs,
        grid=(1,),
        in_specs=[pl.BlockSpec(memory_space=pltpu.SMEM)] + [whole(a) for a in args],
        out_specs=[whole(o) for o in outs],
        scratch_shapes=[pltpu.VMEM((length, 128), BF), pltpu.VMEM((length, 128), BF)],
        compiler_params=pltpu.CompilerParams(vmem_limit_bytes=40 * 1024 * 1024),
        cost_estimate=COST,
    )(order, *args)


def attend_backward(
    order, hidden, q, kv, d_mixed, gain, w_heads, head_gain, cosine, sine, seg_col, seg_row
):
    length, width = hidden.shape
    shape = jax.ShapeDtypeStruct
    outs = [shape((2, length // 8, width), BF)] * 4 + [
        shape((width, 256), F32),
        shape((1, width), F32),
        shape((1, 256), F32),
    ]
    args = [hidden, q, kv, d_mixed, gain, w_heads, head_gain, cosine, sine, seg_col, seg_row]
    return pl.pallas_call(
        attend_back_kernel,
        out_shape=outs,
        grid=(1,),
        in_specs=[pl.BlockSpec(memory_space=pltpu.SMEM)] + [whole(a) for a in args],
        out_specs=[whole(o) for o in outs],
        scratch_shapes=[pltpu.VMEM((length, 128), BF)] * 2
        + [pltpu.VMEM((length, 128), F32)] * 3
        + [pltpu.VMEM((length, 256), BF)],
        compiler_params=pltpu.CompilerParams(vmem_limit_bytes=40 * 1024 * 1024),
        cost_estimate=COST,
    )(order, *args)


def halves(v):
    high = v.astype(BF)
    return high, (v - high.astype(F32)).astype(BF)


def expert_kernel(scalar_ref, *refs, again):
    x_own_ref, x_other_ref, g_ref, router_ref = refs[:4]
    pieces, refs = (refs[4:9], refs[9:14]), refs[14:]
    if again:
        refs = refs[1:]
    out_ref, refs = refs[0], refs[1:]
    back_own_ref, back_other_ref, xe_ref, de_ref, act_ref, da_ref, db_ref = refs[:7]
    pick_ref, weight_ref, dgate_ref, eo_ref, dr_ref, w_ref = refs[7:]
    half, tok, width = x_own_ref.shape
    sources = 2 * half
    core = scalar_ref[1]
    depth = w_ref.shape[2] // 8

    for e in range(2):
        blocks = [(ref, i) for ref in pieces[e] for i in range(ref.shape[0])]
        for r, (ref, i) in enumerate(blocks):
            rows = pl.ds(pl.multiple_of(scalar_ref[2 + r] * depth, depth), depth)
            w_ref[e, :, rows] = ref[i]
    local, slots, hidden = act_ref.shape
    cap = slots // sources
    first = scalar_ref[0]
    lane = lax.broadcasted_iota(jnp.int32, (tok, 128), 1)
    spot = lax.broadcasted_iota(jnp.int32, (tok, local * cap), 1)
    row_expert = lax.broadcasted_iota(jnp.int32, (local * cap, 128), 0) // cap
    slot_lane = lax.broadcasted_iota(jnp.int32, (local * cap, 128), 1)
    own_lane = slot_lane == first + row_expert

    def fetch(i, carry, x_ref, offset, column):
        s = i + offset
        x = x_ref[i]
        from_g = 2 * i + column
        held = g_ref[from_g, :, width:].astype(F32)
        chosen = held >= 0.0
        logits = jnp.where(chosen, dot(x, router_ref[...], 1, 0), -1e30)
        top = jnp.max(logits, axis=1, keepdims=True)
        raised = jnp.where(chosen, jnp.exp(logits - top), 0.0)
        gates = raised / jnp.sum(raised, axis=1, keepdims=True)
        pick = jnp.zeros((tok, local * cap), F32)
        for e in range(local):
            mine = jnp.max(jnp.where(lane == first + e, held, -1.0), axis=1, keepdims=True)
            goal = jnp.where(mine >= 0.0, mine + e * cap, -1.0).astype(jnp.int32)
            pick = jnp.where(spot == goal, 1.0, pick)
        pick = pick.astype(BF)
        pick_ref[s] = pick
        rows = pl.ds(pl.multiple_of(s * cap, 16), cap)
        x_slots = dot(pick, x, 0, 0).astype(BF)
        g_slots = dot(pick, g_ref[from_g, :, :width], 0, 0).astype(BF)
        high, low = halves(gates)
        weight = dot(pick, high, 0, 0) + dot(pick, low, 0, 0)
        weight = jnp.sum(jnp.where(own_lane, weight, 0.0), axis=1, keepdims=True)
        for e in range(local):
            part = slice(e * cap, (e + 1) * cap)
            xe_ref[e, rows] = x_slots[part]
            de_ref[e, rows] = g_slots[part]
            weight_ref[e, rows] = weight[part]
        return carry

    for x_ref, offset, column in ((x_own_ref, 0, core), (x_other_ref, half, 1 - core)):
        lax.fori_loop(
            0, half, functools.partial(fetch, x_ref=x_ref, offset=offset, column=column), 0
        )
    chunk = 256

    def work(i, carry):
        e = i // (slots // chunk)
        rows = pl.ds(pl.multiple_of((i % (slots // chunk)) * chunk, chunk), chunk)
        w_gate = w_ref[e, 0]
        w_up = w_ref[e, 1]
        w_down = w_ref[e, 2]
        x = xe_ref[e, rows]
        a = dot(x, w_gate, 1, 0)
        b = dot(x, w_up, 1, 0)
        sig = 1.0 / (1.0 + jnp.exp(-a))
        silu = a * sig
        active = (silu * b).astype(BF)
        act_ref[e, rows] = active
        slope = b * (sig * (1.0 + a * (1.0 - sig)))
        weight = weight_ref[e, rows]
        g = de_ref[e, rows].astype(F32)
        result = dot(active, w_down, 1, 1).astype(BF).astype(F32)
        dgate_ref[e, rows] = jnp.sum(result * g, axis=1, keepdims=True)
        eo_ref[e, rows] = (weight * result).astype(BF)
        d_expert = (weight * g).astype(BF)
        de_ref[e, rows] = d_expert
        d_active = dot(d_expert, w_down, 1, 0)
        da = (d_active * slope).astype(BF)
        db = (d_active * silu).astype(BF)
        da_ref[e, rows] = da
        db_ref[e, rows] = db
        dr_ref[e, rows] = (dot(da, w_gate, 1, 1) + dot(db, w_up, 1, 1)).astype(BF)
        return carry

    lax.fori_loop(0, local * (slots // chunk), work, 0)

    def give(i, carry, back_ref, offset, column):
        s = i + offset
        rows = pl.ds(pl.multiple_of(s * cap, 16), cap)
        pick = pick_ref[s]
        eo = jnp.concatenate([eo_ref[e, rows] for e in range(local)], axis=0)
        dr = jnp.concatenate([dr_ref[e, rows] for e in range(local)], axis=0)
        dgate = jnp.concatenate([dgate_ref[e, rows] for e in range(local)], axis=0)
        high, low = halves(dgate)
        spread = jnp.where(own_lane, high.astype(F32), 0.0) + jnp.where(
            slot_lane == first + row_expert + 64, low.astype(F32), 0.0
        )
        out_ref[2 * i + column, 0] = dot(pick, eo, 1, 0).astype(BF)
        back_ref[i, :, :width] = dot(pick, dr, 1, 0).astype(BF)
        back_ref[i, :, width:] = dot(pick, spread.astype(BF), 1, 0).astype(BF)
        return carry

    for back_ref, offset, column in ((back_own_ref, 0, core), (back_other_ref, half, 1 - core)):
        lax.fori_loop(
            0, half, functools.partial(give, back_ref=back_ref, offset=offset, column=column), 0
        )


def run_experts(scalars, x_own, x_other, g_all, micro, router, pieces, cap, moe=None):
    half, tok, width = x_own.shape
    sources = 2 * half
    local, hidden = len(pieces), pieces[0][0].shape[3]
    slots = sources * cap
    wide = g_all.shape[2]
    shape = jax.ShapeDtypeStruct
    outs = [
        shape((sources, 2, tok, width), BF),
        shape((half, tok, wide), BF),
        shape((half, tok, wide), BF),
        shape((local, slots, width), BF),
        shape((local, slots, width), BF),
        shape((local, slots, hidden), BF),
        shape((local, slots, hidden), BF),
        shape((local, slots, hidden), BF),
    ]
    g_spec = pl.BlockSpec(
        (sources, tok, wide), lambda i: (0, micro, 0), pipeline_mode=pl.Buffered(1)
    )
    args = [router, *pieces[0], *pieces[1]]
    held = [] if moe is None else [moe]
    moe_spec = pl.BlockSpec(
        (sources, 1, tok, width), lambda i: (0, micro, 0, 0), pipeline_mode=pl.Buffered(1)
    )
    return pl.pallas_call(
        functools.partial(expert_kernel, again=moe is not None),
        out_shape=outs,
        grid=(1,),
        in_specs=[pl.BlockSpec(memory_space=pltpu.SMEM), whole(x_own), whole(x_other), g_spec]
        + [whole(a) for a in args]
        + [pl.BlockSpec(memory_space=pl.ANY)] * len(held),
        out_specs=[moe_spec] + [whole(o) for o in outs[1:]],
        input_output_aliases={4 + len(args): 0} if held else {},
        scratch_shapes=[
            pltpu.VMEM((sources, tok, local * cap), BF),
            pltpu.VMEM((local, slots, 1), F32),
            pltpu.VMEM((local, slots, 1), F32),
            pltpu.VMEM((local, slots, width), BF),
            pltpu.VMEM((local, slots, width), BF),
            pltpu.VMEM((local, 3, width, hidden), BF),
        ],
        compiler_params=pltpu.CompilerParams(vmem_limit_bytes=60 * 1024 * 1024),
        cost_estimate=COST,
    )(scalars, x_own, x_other, g_all, *args, *held)


def expert_grad_kernel(order_ref, *refs):
    kept, outs, total_ref = refs[:10], refs[10:14], refs[14]
    left = (kept[0:2], kept[0:2], kept[2:4])
    right = (kept[6:8], kept[8:10], kept[4:6])
    step = pl.program_id(0)
    depth = outs[0].shape[2]
    for kind in range(3):

        @pl.when(step == kind)
        def _(kind=kind):
            total = dot(left[kind][0][0], right[kind][0][0], 0, 0)
            total_ref[...] = total + dot(left[kind][1][0], right[kind][1][0], 0, 0)

    for r in range(8):
        rows = pl.ds(pl.multiple_of(order_ref[r] * depth, depth), depth)
        outs[r // 2][r % 2, 0] = total_ref[rows].astype(BF)


def expert_grads(order, kept, expert):
    _, slots, width = kept[0][0].shape
    hidden = kept[0][2].shape[2]
    args = [kept[m][i] for i in range(5) for m in range(2)]
    depth = width // 8
    shape = jax.ShapeDtypeStruct
    return pl.pallas_call(
        expert_grad_kernel,
        out_shape=[shape((2, 3, depth, hidden), BF)] * 4,
        grid=(3,),
        in_specs=[pl.BlockSpec(memory_space=pltpu.SMEM)]
        + [pl.BlockSpec((1,) + a.shape[1:], lambda i: (expert, 0, 0)) for a in args],
        out_specs=[pl.BlockSpec((2, 1, depth, hidden), lambda i: (0, i, 0, 0))] * 4,
        scratch_shapes=[pltpu.VMEM((width, hidden), F32)],
        compiler_params=pltpu.CompilerParams(vmem_limit_bytes=48 * 1024 * 1024),
        cost_estimate=COST,
    )(order, *args)


CTX = ("z", "yl")
GROUP = ("yh", "x")
FSDP = ("yh", "x", "core")
ALL = CTX + FSDP
UP = [(i, (i + 1) % 4) for i in range(4)]
DOWN = [(i, (i - 1) % 4) for i in range(4)]
TWO = [(i, (i + 2) % 4) for i in range(4)]
FLIP = [(0, 1), (1, 0)]


def mm(a, b):
    return jnp.dot(a, b, preferred_element_type=F32)


def mm_t(a, b):
    return lax.dot_general(a, b, (((1,), (1,)), ((), ())), preferred_element_type=F32)


def t_mm(a, b):
    return lax.dot_general(a, b, (((0,), (0,)), ((), ())), preferred_element_type=F32)


def ein(spec, a, b):
    return jnp.einsum(spec, a, b, preferred_element_type=F32)


def swap(parts, axis):
    return lax.all_to_all(parts, axis, split_axis=0, concat_axis=0, tiled=True)


def flip(block, axis):
    return lax.ppermute(block, axis, FLIP)


def by_z(parts):
    return [lax.ppermute(parts[k], "z", perm) for k, perm in ((1, UP), (2, TWO), (3, DOWN))]


def along_z(both):
    before, far, after = by_z([both] * 4)
    return [both, after, far, before]


class Exchange:
    def __init__(self):
        self.last = None

    def __call__(self, parts, axis):
        if self.last is not None:
            parts = after_all(parts, self.last)
        self.last = swap(parts, axis)
        return self.last

    def copies(self, block, axis, count):
        return self(jnp.broadcast_to(block[None], (count,) + block.shape), axis)


def add(a, b):
    return (a.astype(F32) + b.astype(F32)).astype(BF)


def add_part(parts, i, more):
    pieces = [parts[:1], parts[1:]]
    pieces[i] = add(pieces[i], more)
    return jnp.concatenate(pieces, axis=0)


def relay(far):
    return [lax.ppermute(far[:1], "z", UP), lax.ppermute(far[1:], "z", DOWN)]


def ring_sums(parts, far):
    return [
        lax.ppermute(add_part(parts[1], 0, far[0]), "z", UP),
        lax.ppermute(add_part(parts[3], 1, far[1]), "z", DOWN),
    ]


def pair_sums(parts, moved):
    return [sum(part[i].astype(F32) for part in [parts[0]] + moved) for i in range(2)]


def sum_parts(parts):
    return jnp.sum(parts.astype(F32), axis=0)


def after_all(value, *others):
    return lax.optimization_barrier((value,) + others)[0]


def rope_tables(positions):
    half = DH // 2
    inverse = THETA ** (-(jnp.arange(half, dtype=F32) * 2.0) / DH)
    angles = positions.astype(F32)[:, None] * inverse[None, :]
    return (jnp.cos(angles), jnp.sin(angles))


def rms_scale(values, gain):
    return values * lax.rsqrt(jnp.mean(values * values, axis=-1, keepdims=True) + EPS) * gain


def body(
    tokens,
    segments,
    routes,
    w_query,
    w_key,
    w_value,
    w_out,
    w_router,
    attn_gain,
    mlp_gain,
    qk_gain,
    w_gate,
    w_up,
    w_down,
    cotangent,
):
    micro = tokens.shape[0]
    tok = tokens.shape[2]
    width = tokens.shape[3]
    length = segments.shape[2]
    rows = w_query.shape[0]
    n_ctx, n_fsdp = 8, 16
    n_all = n_ctx * n_fsdp
    z, yl, yh, x, core = (lax.axis_index(name) for name in ALL)
    shard = (yh * 4 + x) * 2 + core
    local = w_gate.shape[0]
    experts = local * n_fsdp
    cap = (3 * tok * TOPK + 2 * experts - 1) // (2 * experts)
    all_tok = micro * tok
    ratio = H // KV
    heads = ratio * DH
    span = heads + 2 * DH

    exchange = Exchange()
    small = jnp.concatenate(
        [
            w_router,
            attn_gain[:, None],
            mlp_gain[:, None],
            jnp.pad(qk_gain[:, None], ((0, rows - 1), (0, 0))),
        ],
        axis=1,
    )
    small = jnp.pad(small, ((0, 0), (0, 128 - small.shape[1])))
    pieces = jnp.concatenate(
        [
            w_query.reshape(rows, n_ctx, heads),
            w_key.reshape(rows, n_ctx, DH),
            w_value.reshape(rows, n_ctx, DH),
            jnp.broadcast_to(small[:, None], (rows, n_ctx, 128)),
        ],
        axis=2,
    ).transpose(1, 0, 2)
    pieces = jnp.broadcast_to(pieces[:, None], (n_ctx, n_fsdp) + pieces.shape[1:])
    both_0, both_1 = (
        jnp.concatenate([tokens[m], flip(tokens[m], "yl")], axis=0) for m in range(micro)
    )
    both_w = jnp.stack([w_gate, w_up, w_down], axis=1)
    head_all = exchange(pieces.reshape((n_all,) + pieces.shape[2:]), ALL).reshape(width, -1)
    other_w = flip(both_w, "yl")
    both_w = [jnp.stack([both_w[e], other_w[e]]) for e in range(local)]
    seq_rows = [along_z(both_0)]
    seq_rows.append(along_z(after_all(both_1, *seq_rows[0][1:])))
    head_all = after_all(head_all, *seq_rows[1][1:], *both_w)
    w_heads = head_all[:, :span]
    small_all = head_all[:, span:]
    router = small_all[:, :experts]
    small_wide = small_all.astype(F32)
    gain_attn = small_wide[:, experts]
    gain_mlp = small_wide[:, experts + 1]
    gain_heads = small_wide[:, experts + 2].reshape(-1, rows)[:, 0]
    gain_row = gain_attn[None]
    head_row = jnp.concatenate(
        [gain_heads[:DH]] * ratio + [gain_heads[DH:], jnp.ones((DH,), F32)]
    )[None]
    router_pad = jnp.pad(router, ((0, 0), (0, 128 - experts)))

    out_own = exchange.copies(w_out, CTX + GROUP, n_all // 2)

    moved_w = []
    last = seq_rows[1][1:]
    for e in range(local):
        block = after_all(both_w[e], *last)
        last = [lax.ppermute(block, "z", UP), lax.ppermute(block, "z", DOWN)]
        moved_w.append(last)

    expert_ids = jnp.arange(experts, dtype=jnp.int32)
    cot = cotangent.reshape(all_tok, width)
    chosen = jnp.any(routes.reshape(all_tok, TOPK)[:, :, None] == expert_ids, axis=1)
    before = jnp.arange(tok, dtype=jnp.int32)
    lower = (before[:, None] >= before[None, :]).astype(BF)
    counts = ein("ut,mte->mue", lower, chosen.reshape(micro, tok, experts).astype(BF))
    held = jnp.where(chosen, counts.reshape(all_tok, experts) - 1.0, -1.0)
    held = jnp.pad(held, ((0, 0), (0, 128 - experts)), constant_values=-1.0).astype(BF)
    pack = after_all(jnp.concatenate([cot, held], axis=1), both_0, both_1)
    g_all = lax.all_gather(pack, FSDP, axis=0)

    cosine, sine = rope_tables(jnp.arange(length, dtype=jnp.int32))
    cosine = jnp.tile(cosine, (1, 4))
    sine = jnp.tile(jnp.concatenate([-sine, sine], axis=1), (1, 2))
    rel = jnp.arange(n_ctx, dtype=jnp.int32)
    order = ((z + rel // 2) % 4) * 2 + (yl + rel % 2) % 2
    scalars = jnp.concatenate([jnp.stack([shard * local, core]), order]).astype(jnp.int32)

    def to_owner(v):
        return exchange(v.reshape(n_ctx, tok, -1), CTX)

    def attention_args(m):
        seg = segments[m, 0]
        return gain_row, w_heads, head_row, cosine, sine, seg[:, None], seg[None, :]

    mixed_0, *saved_0 = attend_forward(order, seq_rows[0], *attention_args(0))
    mixed_1, *saved_1 = attend_forward(order, seq_rows[1], *attention_args(1))
    saved = [saved_0, saved_1]
    out_own, mixed_0, mixed_1 = lax.optimization_barrier((out_own, mixed_0, mixed_1))
    mixed_1 = after_all(mixed_1, *moved_w[0], *moved_w[1])
    out_other = flip(out_own, "core")
    mixed = jnp.stack([mixed_0, mixed_1]).reshape(micro, n_ctx, tok, heads).transpose(1, 0, 2, 3)
    mixed = exchange(mixed.reshape(n_ctx, all_tok, heads), CTX)
    mixed = mixed.transpose(1, 0, 2).reshape(all_tok, width)
    out_full = jnp.where(
        core == 0,
        jnp.stack([out_own, out_other], axis=1),
        jnp.stack([out_other, out_own], axis=1),
    ).reshape(width, width)
    middle = tokens.reshape(all_tok, width).astype(F32) + mm(mixed, out_full)
    inv_two = lax.rsqrt(jnp.mean(middle * middle, axis=-1, keepdims=True) + EPS)
    hidden_two = (middle * inv_two * gain_mlp).astype(BF)
    x_0 = hidden_two[:tok]
    weights = []
    for e, (w_before, w_after) in enumerate(moved_w):
        w_far = [lax.ppermute(w_before[:1], "z", UP), lax.ppermute(w_after[1:], "z", DOWN)]
        weights.append([both_w[e], w_after, *w_far, w_before])
    x_0 = exchange.copies(x_0, GROUP, n_ctx)
    x_0, weights = lax.optimization_barrier((x_0, weights))
    x_1 = exchange.copies(hidden_two[tok:], GROUP, n_ctx)
    logits = jnp.where(chosen, mm(hidden_two, router), -1e30)
    gates_all = jnp.where(chosen, jax.nn.softmax(logits, axis=-1), 0.0)

    def own_rows(v, m):
        return v[m * tok : (m + 1) * tok]

    def experts_of(m, x_own, *moe):
        return run_experts(
            scalars,
            x_own,
            flip(x_own, "core"),
            g_all,
            m,
            router_pad,
            weights,
            cap,
            *moe,
        )

    def back_sum(own, other):
        return add(own, flip(other, "core"))

    def middle_back(m, back):
        rows_mixed, rows_middle, inv, hidden, gates = (
            own_rows(v, m) for v in (mixed, middle, inv_two, hidden_two, gates_all)
        )
        grad_top = own_rows(cot, m).astype(F32)
        tail = back[:, width:]
        d_gates = tail[:, :experts] + tail[:, 64 : 64 + experts]
        d_select = gates * (d_gates - jnp.sum(gates * d_gates, axis=-1, keepdims=True))
        d_logits = d_select.astype(BF)
        grad_router = t_mm(hidden, d_logits)
        d_two = back[:, :width] + mm_t(d_logits, router)
        grad_mlp = jnp.sum(d_two * rows_middle * inv, axis=0)
        u = d_two * gain_mlp
        d_middle = (
            grad_top
            + inv * u
            - rows_middle * (inv**3 * jnp.mean(u * rows_middle, axis=-1, keepdims=True))
        )
        d_branch = d_middle.astype(BF)
        grad_out = t_mm(rows_mixed, d_branch)
        d_mixed = mm_t(d_branch, out_full).astype(BF)
        d_mixed = d_mixed.reshape(tok, n_ctx, heads).transpose(1, 0, 2)
        return d_middle, d_mixed, (grad_out, grad_router, grad_mlp)

    def attention_back(m, d_mixed):
        *d_hidden, grad_heads, grad_attn, grad_qk = attend_backward(
            order, *saved[m], d_mixed.reshape(length, heads), *attention_args(m)
        )
        grad_qk = jnp.concatenate(
            [grad_qk[0, :DH] + grad_qk[0, DH : 2 * DH], grad_qk[0, 2 * DH : 3 * DH]]
        )
        return d_hidden, (grad_heads, grad_attn[0], grad_qk)

    def input_grad(m, d_hidden, d_middle):
        start = tokens[m, 0].astype(F32)
        inverse = lax.rsqrt(jnp.mean(start * start, axis=-1, keepdims=True) + EPS)
        u = d_hidden * gain_attn
        return (
            d_middle
            + inverse * u
            - start * (inverse**3 * jnp.mean(u * start, axis=-1, keepdims=True))
        )

    moe, back_own, back_other, *kept_0 = experts_of(0, x_0)
    x_1, back_own, back_other = lax.optimization_barrier((x_1, back_own, back_other))
    back_0 = back_sum(back_own, back_other)
    x_1 = after_all(x_1, back_0)
    back_0 = exchange(back_0, GROUP)
    moe, back_own, back_other, *kept_1 = experts_of(1, x_1, moe)
    back_0, back_own, back_other, moe = lax.optimization_barrier(
        (back_0, back_own, back_other, moe)
    )
    moe = lax.psum_scatter(moe, FSDP, scatter_dimension=0, tiled=True)[0]
    back_1 = back_sum(back_own, back_other)
    d_middle_0, d_mixed_0, grads_0 = middle_back(0, sum_parts(back_0))
    d_mixed_0 = exchange(d_mixed_0, CTX)
    d_mixed_0, back_1 = lax.optimization_barrier((d_mixed_0, back_1))
    back_1 = exchange(back_1, GROUP)
    kept_1[0] = after_all(kept_1[0], d_mixed_0)
    parts = [expert_grads(order, (kept_0, kept_1), 0)]
    far = [relay(parts[0][2])]
    d_hidden_0, head_grads_0 = attention_back(0, after_all(d_mixed_0, parts[0][0]))
    hidden_moved_0 = by_z(d_hidden_0)
    back_1, d_hidden_0[0], far[0] = lax.optimization_barrier((back_1, d_hidden_0[0], far[0]))
    d_middle_1, d_mixed_1, grads_1 = middle_back(1, sum_parts(back_1))
    d_mixed_1 = exchange(d_mixed_1, CTX)
    kept_1[0] = after_all(kept_1[0], back_1)
    parts.append(expert_grads(order, (kept_0, kept_1), 1))
    moved = [ring_sums(parts[0], far[0])]
    grad_out, grad_router, grad_mlp = jax.tree.map(jnp.add, grads_0, grads_1)
    grad_out = grad_out.astype(BF).reshape(n_all // 2, 2, rows, width)
    grad_own = lax.dynamic_index_in_dim(grad_out, core, axis=1, keepdims=False)
    grad_other = lax.dynamic_index_in_dim(grad_out, 1 - core, axis=1, keepdims=False)
    grad_out = back_sum(grad_own, grad_other)
    d_mixed_1, parts[1], hidden_moved_0, grad_out = lax.optimization_barrier(
        (d_mixed_1, parts[1], hidden_moved_0, grad_out)
    )
    far.append(relay(parts[1][2]))
    grad_out = exchange(grad_out, CTX + GROUP)
    d_hidden_1, head_grads_1 = attention_back(1, d_mixed_1)
    d_hidden_1, grad_out, far[1], moved[0] = lax.optimization_barrier(
        (d_hidden_1, grad_out, far[1], moved[0])
    )
    hidden_moved_1 = by_z(d_hidden_1)
    moved.append(ring_sums(parts[1], after_all(far[1], hidden_moved_1[0])))
    hidden_sums = pair_sums(d_hidden_0, hidden_moved_0)
    d_hidden_0 = hidden_sums[0] + flip(hidden_sums[1].astype(BF), "yl").astype(F32)
    exchange.last = grad_out
    weight_sums = [pair_sums(p, q) for p, q in zip(parts, moved)]
    weight_yl = [flip(sums[1].astype(BF), "yl") for sums in weight_sums]
    hidden_sums = pair_sums(d_hidden_1, hidden_moved_1)
    hidden_yl = flip(hidden_sums[1].astype(BF), "yl")
    grad_heads, grad_attn, grad_qk = jax.tree.map(jnp.add, head_grads_0, head_grads_1)

    grad_qk = jnp.pad(grad_qk[:, None], ((0, 0), (0, rows - 1))).reshape(-1)
    grad_small = jnp.concatenate(
        [grad_router, grad_attn[:, None], grad_mlp[:, None], grad_qk[:, None]], axis=1
    )
    grad_small = jnp.pad(grad_small, ((0, 0), (0, 128 - grad_small.shape[1])))
    grad_pack = jnp.concatenate([grad_heads, grad_small], axis=1).astype(BF)
    grad_pack = exchange(grad_pack.reshape(n_all, rows, -1), ALL).astype(F32)
    own_heads = jnp.sum(grad_pack[:, :, :span].reshape(n_ctx, n_fsdp, rows, -1), axis=1)
    own_heads = own_heads.transpose(1, 0, 2)
    own_small = jnp.sum(grad_pack[:, :, span:], axis=0)
    own_out = sum_parts(grad_out)
    moe = after_all(moe, grad_pack)
    d_hidden_1 = hidden_sums[0] + hidden_yl.astype(F32)
    expert_own = [sums[0] + other.astype(F32) for sums, other in zip(weight_sums, weight_yl)]
    out = (middle.reshape(moe.shape) + moe.astype(F32)).astype(BF)
    d_inputs = [
        input_grad(0, d_hidden_0, d_middle_0),
        input_grad(1, d_hidden_1, d_middle_1),
    ]

    return (
        out[:, None],
        jnp.stack(d_inputs)[:, None],
        own_heads[:, :, :heads].reshape(rows, -1),
        own_heads[:, :, heads : heads + DH].reshape(rows, -1),
        own_heads[:, :, heads + DH :].reshape(rows, -1),
        own_out,
        own_small[:, :experts],
        own_small[:, experts],
        own_small[:, experts + 1],
        own_small[:1, experts + 2],
        jnp.stack([part[0] for part in expert_own]),
        jnp.stack([part[1] for part in expert_own]),
        jnp.stack([part[2] for part in expert_own]),
    )


def solution(mesh):
    mesh = Mesh(mesh.devices.reshape(4, 2, 2, 4, 2), ALL)
    weight = P(ALL, None)
    gain = P(ALL)
    rows = P(None, FSDP, CTX, None)
    expert = P(FSDP, CTX, None)
    return jax.shard_map(
        body,
        mesh=mesh,
        in_specs=(rows, P(None, FSDP, None), rows)
        + (weight,) * 5
        + (gain,) * 3
        + (expert,) * 3
        + (rows,),
        out_specs=(rows, rows) + (weight,) * 5 + (gain,) * 3 + (expert,) * 3,
        check_vma=False,
    )
```

```python
import functools

import jax
import jax.numpy as jnp
from jax import lax
from jax.experimental import pallas as pl
from jax.experimental.pallas import tpu as pltpu
from jax.sharding import Mesh
from jax.sharding import PartitionSpec as P

BF = jnp.bfloat16
F32 = jnp.float32
H = 16
KV = 8
DH = 64
TOPK = 8
WINDOW = 1024
EPS = 1e-06
THETA = 10000.0
COST = pl.CostEstimate(flops=10**7, bytes_accessed=10**5, transcendentals=0)


def dot(a, b, ca, cb):
    return lax.dot_general(a, b, (((ca,), (cb,)), ((), ())), preferred_element_type=F32)


def lanes_of(v):
    return lax.broadcasted_iota(jnp.int32, v.shape, v.ndim - 1)


def head_sums(v):
    low = lanes_of(v) < DH
    first = jnp.sum(jnp.where(low, v, 0.0), axis=1, keepdims=True)
    second = jnp.sum(jnp.where(low, 0.0, v), axis=1, keepdims=True)
    return jnp.where(low, first, second)


def trade(v):
    return jnp.where(
        lanes_of(v) % DH < DH // 2, pltpu.roll(v, 128 - DH // 2, 1), pltpu.roll(v, DH // 2, 1)
    )


def both_halves(v, second):
    low = lanes_of(v) < DH
    other = pltpu.roll(v, DH, 1)
    return jnp.where(low, other, v) if second else jnp.where(low, v, other)


def stack_heads(v):
    low = lanes_of(v) < DH
    zero = jnp.zeros_like(v)
    return jnp.concatenate([jnp.where(low, v, zero), jnp.where(low, zero, v)], axis=0)


def key_span(start, block, length):
    reach = WINDOW // 2 - 1
    low = max(0, start - reach) // 128 * 128
    high = min(length, -(-(start + block + reach) // 128) * 128)
    return low, high


def masked_probs(q_two, keys, seg_col, seg_row, start, low):
    block = q_two.shape[0] // 2
    scores = dot(q_two, keys, 1, 1)
    shape = (block, keys.shape[0])
    gap = (
        lax.broadcasted_iota(jnp.int32, shape, 0)
        - lax.broadcasted_iota(jnp.int32, shape, 1)
        + (start - low)
    )
    allowed = (seg_col == seg_row) & (jnp.abs(gap) < WINDOW // 2)
    bias = jnp.where(allowed, 0.0, -1e30)
    scores = scores + jnp.concatenate([bias, bias], axis=0)
    raised = jnp.exp(scores - jnp.max(scores, axis=1, keepdims=True))
    return raised * (1.0 / jnp.sum(raised, axis=1, keepdims=True))


def attend_kernel(
    order_ref,
    *refs,
):
    pieces, refs = refs[:-13], refs[-13:]
    gain_ref, w_ref, head_gain_ref, cos_ref, sin_ref, seg_col_ref, seg_row_ref = refs[:7]
    mixed_ref, hidden_ref, q_ref, kv_ref, keys_ref, values_ref = refs[7:]
    tok, width = pieces[0].shape[1:]
    length = hidden_ref.shape[0]
    pieces = [(ref, i) for ref in pieces for i in range(ref.shape[0])]
    for r, (ref, i) in enumerate(pieces):
        x = ref[i].astype(F32)
        x = x * lax.rsqrt(jnp.mean(x * x, axis=1, keepdims=True) + EPS) * gain_ref[...]
        rows = pl.ds(pl.multiple_of(order_ref[r] * tok, tok), tok)
        hidden_ref[rows] = x.astype(BF)
    raw = dot(hidden_ref[...], w_ref[...], 1, 0)
    for half in range(2):
        u = raw[:, half * 128 : half * 128 + 128]
        gain = head_gain_ref[:, half * 128 : half * 128 + 128]
        n = u * lax.rsqrt(head_sums(u * u) * (1.0 / DH) + EPS) * gain
        turned = n * cos_ref[...] + trade(n) * sin_ref[...]
        if half == 0:
            q_ref[...] = turned.astype(BF)
        else:
            kv = jnp.where(lanes_of(u) < DH, turned, u)
            kv_ref[...] = kv.astype(BF)
            keys_ref[...] = both_halves(kv, False).astype(BF)
            values_ref[...] = both_halves(kv, True).astype(BF)
    block = 256
    for start in range(0, length, block):
        low, high = key_span(start, block, length)
        q_two = stack_heads(q_ref[start : start + block].astype(F32) * DH**-0.5).astype(BF)
        probs = masked_probs(
            q_two,
            keys_ref[low:high],
            seg_col_ref[start : start + block],
            seg_row_ref[:, low:high],
            start,
            low,
        )
        result = dot(probs.astype(BF), values_ref[low:high], 1, 0)
        first = lanes_of(result[:block]) < DH
        mixed_ref[start : start + block] = jnp.where(first, result[:block], result[block:]).astype(
            BF
        )


def attend_back_kernel(
    order_ref,
    hidden_ref,
    q_ref,
    kv_ref,
    d_mixed_ref,
    gain_ref,
    w_ref,
    head_gain_ref,
    cos_ref,
    sin_ref,
    seg_col_ref,
    seg_row_ref,
    d_hidden_0_ref,
    d_hidden_1_ref,
    d_hidden_2_ref,
    d_hidden_3_ref,
    grad_w_ref,
    grad_gain_ref,
    grad_heads_ref,
    keys_ref,
    values_ref,
    d_q_ref,
    d_k_ref,
    d_v_ref,
    d_raw_ref,
):
    length = hidden_ref.shape[0]
    kv = kv_ref[...].astype(F32)
    keys_ref[...] = both_halves(kv, False).astype(BF)
    values_ref[...] = both_halves(kv, True).astype(BF)
    d_k_ref[...] = jnp.zeros_like(d_k_ref)
    d_v_ref[...] = jnp.zeros_like(d_v_ref)
    block = 256
    for start in range(0, length, block):
        low, high = key_span(start, block, length)
        q_two = stack_heads(q_ref[start : start + block].astype(F32) * DH**-0.5).astype(BF)
        m_two = stack_heads(d_mixed_ref[start : start + block].astype(F32)).astype(BF)
        probs = masked_probs(
            q_two,
            keys_ref[low:high],
            seg_col_ref[start : start + block],
            seg_row_ref[:, low:high],
            start,
            low,
        )
        d_probs = dot(m_two, values_ref[low:high], 1, 1)
        inner = jnp.sum(probs * d_probs, axis=1, keepdims=True)
        d_scores = (probs * (d_probs - inner)).astype(BF)
        result = dot(d_scores, keys_ref[low:high], 1, 0)
        first = lanes_of(result[:block]) < DH
        d_q_ref[start : start + block] = jnp.where(first, result[:block], result[block:]) * (
            DH**-0.5
        )
        d_k_ref[low:high] += dot(d_scores, q_two, 0, 0)
        d_v_ref[low:high] += dot(probs.astype(BF), m_two, 0, 0)
    raw = dot(hidden_ref[...], w_ref[...], 1, 0)
    d_k = d_k_ref[...]
    d_k = d_k + pltpu.roll(d_k, DH, 1)
    d_v = d_v_ref[...]
    d_v = d_v + pltpu.roll(d_v, DH, 1)
    for half in range(2):
        lanes = slice(half * 128, half * 128 + 128)
        u = raw[:, lanes]
        gain = head_gain_ref[:, lanes]
        d = d_q_ref[...] if half == 0 else d_k
        d = d * cos_ref[...] + trade(d * sin_ref[...])
        r = lax.rsqrt(head_sums(u * u) * (1.0 / DH) + EPS)
        grad_heads_ref[:, lanes] = jnp.sum(d * u * r, axis=0, keepdims=True)
        d = d * gain
        d = d * r - u * (r * r * r * (head_sums(d * u) * (1.0 / DH)))
        if half == 1:
            d = jnp.where(lanes_of(d) < DH, d, d_v)
        d_raw_ref[:, lanes] = d.astype(BF)
    grad_w_ref[...] = dot(hidden_ref[...], d_raw_ref[...], 0, 0)
    total = jnp.zeros(grad_gain_ref.shape, F32)
    outs = (d_hidden_0_ref, d_hidden_1_ref, d_hidden_2_ref, d_hidden_3_ref)
    tok = length // 8
    for step in range(4):
        rows = pl.ds(pl.multiple_of(order_ref[2 * step] // 2 * (2 * tok), 2 * tok), 2 * tok)
        d_hidden = dot(d_raw_ref[rows], w_ref[...], 1, 1)
        own = order_ref[0] % 2
        outs[step][own] = d_hidden[:tok].astype(BF)
        outs[step][1 - own] = d_hidden[tok:].astype(BF)
        total = total + jnp.sum(d_hidden * hidden_ref[rows].astype(F32), axis=0, keepdims=True)
    grad_gain_ref[...] = total / gain_ref[...]


def whole(a):
    return pl.BlockSpec(a.shape, lambda i: (0,) * len(a.shape), pipeline_mode=pl.Buffered(1))


def attend_forward(order, pieces, gain, w_heads, head_gain, cosine, sine, seg_col, seg_row):
    length = cosine.shape[0]
    width = w_heads.shape[0]
    shape = jax.ShapeDtypeStruct
    outs = [
        shape((length, 128), BF),
        shape((length, width), BF),
        shape((length, 128), BF),
        shape((length, 128), BF),
    ]
    args = list(pieces) + [gain, w_heads, head_gain, cosine, sine, seg_col, seg_row]
    return pl.pallas_call(
        attend_kernel,
        out_shape=outs,
        grid=(1,),
        in_specs=[pl.BlockSpec(memory_space=pltpu.SMEM)] + [whole(a) for a in args],
        out_specs=[whole(o) for o in outs],
        scratch_shapes=[pltpu.VMEM((length, 128), BF), pltpu.VMEM((length, 128), BF)],
        compiler_params=pltpu.CompilerParams(vmem_limit_bytes=40 * 1024 * 1024),
        cost_estimate=COST,
    )(order, *args)


def attend_backward(
    order, hidden, q, kv, d_mixed, gain, w_heads, head_gain, cosine, sine, seg_col, seg_row
):
    length, width = hidden.shape
    shape = jax.ShapeDtypeStruct
    outs = [shape((2, length // 8, width), BF)] * 4 + [
        shape((width, 256), F32),
        shape((1, width), F32),
        shape((1, 256), F32),
    ]
    args = [hidden, q, kv, d_mixed, gain, w_heads, head_gain, cosine, sine, seg_col, seg_row]
    return pl.pallas_call(
        attend_back_kernel,
        out_shape=outs,
        grid=(1,),
        in_specs=[pl.BlockSpec(memory_space=pltpu.SMEM)] + [whole(a) for a in args],
        out_specs=[whole(o) for o in outs],
        scratch_shapes=[pltpu.VMEM((length, 128), BF)] * 2
        + [pltpu.VMEM((length, 128), F32)] * 3
        + [pltpu.VMEM((length, 256), BF)],
        compiler_params=pltpu.CompilerParams(vmem_limit_bytes=40 * 1024 * 1024),
        cost_estimate=COST,
    )(order, *args)


def halves(v):
    high = v.astype(BF)
    return high, (v - high.astype(F32)).astype(BF)


def expert_kernel(scalar_ref, *refs, again):
    x_own_ref, x_other_ref, g_ref, router_ref = refs[:4]
    pieces, refs = (refs[4:9], refs[9:14]), refs[14:]
    if again:
        refs = refs[1:]
    out_ref, refs = refs[0], refs[1:]
    back_own_ref, back_other_ref, xe_ref, de_ref, act_ref, da_ref, db_ref = refs[:7]
    pick_ref, weight_ref, dgate_ref, eo_ref, dr_ref, w_ref = refs[7:]
    half, tok, width = x_own_ref.shape
    sources = 2 * half
    core = scalar_ref[1]
    depth = w_ref.shape[2] // 8

    for e in range(2):
        blocks = [(ref, i) for ref in pieces[e] for i in range(ref.shape[0])]
        for r, (ref, i) in enumerate(blocks):
            rows = pl.ds(pl.multiple_of(scalar_ref[2 + r] * depth, depth), depth)
            w_ref[e, :, rows] = ref[i]
    local, slots, hidden = act_ref.shape
    cap = slots // sources
    first = scalar_ref[0]
    lane = lax.broadcasted_iota(jnp.int32, (tok, 128), 1)
    spot = lax.broadcasted_iota(jnp.int32, (tok, local * cap), 1)
    row_expert = lax.broadcasted_iota(jnp.int32, (local * cap, 128), 0) // cap
    slot_lane = lax.broadcasted_iota(jnp.int32, (local * cap, 128), 1)
    own_lane = slot_lane == first + row_expert

    def fetch(i, carry, x_ref, offset, column):
        s = i + offset
        x = x_ref[i]
        from_g = 2 * i + column
        held = g_ref[from_g, :, width:].astype(F32)
        chosen = held >= 0.0
        logits = jnp.where(chosen, dot(x, router_ref[...], 1, 0), -1e30)
        top = jnp.max(logits, axis=1, keepdims=True)
        raised = jnp.where(chosen, jnp.exp(logits - top), 0.0)
        gates = raised / jnp.sum(raised, axis=1, keepdims=True)
        pick = jnp.zeros((tok, local * cap), F32)
        for e in range(local):
            mine = jnp.max(jnp.where(lane == first + e, held, -1.0), axis=1, keepdims=True)
            goal = jnp.where(mine >= 0.0, mine + e * cap, -1.0).astype(jnp.int32)
            pick = jnp.where(spot == goal, 1.0, pick)
        pick = pick.astype(BF)
        pick_ref[s] = pick
        rows = pl.ds(pl.multiple_of(s * cap, 16), cap)
        x_slots = dot(pick, x, 0, 0).astype(BF)
        g_slots = dot(pick, g_ref[from_g, :, :width], 0, 0).astype(BF)
        high, low = halves(gates)
        weight = dot(pick, high, 0, 0) + dot(pick, low, 0, 0)
        weight = jnp.sum(jnp.where(own_lane, weight, 0.0), axis=1, keepdims=True)
        for e in range(local):
            part = slice(e * cap, (e + 1) * cap)
            xe_ref[e, rows] = x_slots[part]
            de_ref[e, rows] = g_slots[part]
            weight_ref[e, rows] = weight[part]
        return carry

    for x_ref, offset, column in ((x_own_ref, 0, core), (x_other_ref, half, 1 - core)):
        lax.fori_loop(
            0, half, functools.partial(fetch, x_ref=x_ref, offset=offset, column=column), 0
        )
    chunk = 256

    def work(i, carry):
        e = i // (slots // chunk)
        rows = pl.ds(pl.multiple_of((i % (slots // chunk)) * chunk, chunk), chunk)
        w_gate = w_ref[e, 0]
        w_up = w_ref[e, 1]
        w_down = w_ref[e, 2]
        x = xe_ref[e, rows]
        a = dot(x, w_gate, 1, 0)
        b = dot(x, w_up, 1, 0)
        sig = 1.0 / (1.0 + jnp.exp(-a))
        silu = a * sig
        active = (silu * b).astype(BF)
        act_ref[e, rows] = active
        slope = b * (sig * (1.0 + a * (1.0 - sig)))
        weight = weight_ref[e, rows]
        g = de_ref[e, rows].astype(F32)
        result = dot(active, w_down, 1, 1).astype(BF).astype(F32)
        dgate_ref[e, rows] = jnp.sum(result * g, axis=1, keepdims=True)
        eo_ref[e, rows] = (weight * result).astype(BF)
        d_expert = (weight * g).astype(BF)
        de_ref[e, rows] = d_expert
        d_active = dot(d_expert, w_down, 1, 0)
        da = (d_active * slope).astype(BF)
        db = (d_active * silu).astype(BF)
        da_ref[e, rows] = da
        db_ref[e, rows] = db
        dr_ref[e, rows] = (dot(da, w_gate, 1, 1) + dot(db, w_up, 1, 1)).astype(BF)
        return carry

    lax.fori_loop(0, local * (slots // chunk), work, 0)

    def give(i, carry, back_ref, offset, column):
        s = i + offset
        rows = pl.ds(pl.multiple_of(s * cap, 16), cap)
        pick = pick_ref[s]
        eo = jnp.concatenate([eo_ref[e, rows] for e in range(local)], axis=0)
        dr = jnp.concatenate([dr_ref[e, rows] for e in range(local)], axis=0)
        dgate = jnp.concatenate([dgate_ref[e, rows] for e in range(local)], axis=0)
        high, low = halves(dgate)
        spread = jnp.where(own_lane, high.astype(F32), 0.0) + jnp.where(
            slot_lane == first + row_expert + 64, low.astype(F32), 0.0
        )
        out_ref[2 * i + column, 0] = dot(pick, eo, 1, 0).astype(BF)
        back_ref[i, :, :width] = dot(pick, dr, 1, 0).astype(BF)
        back_ref[i, :, width:] = dot(pick, spread.astype(BF), 1, 0).astype(BF)
        return carry

    for back_ref, offset, column in ((back_own_ref, 0, core), (back_other_ref, half, 1 - core)):
        lax.fori_loop(
            0, half, functools.partial(give, back_ref=back_ref, offset=offset, column=column), 0
        )


def run_experts(scalars, x_own, x_other, g_all, micro, router, pieces, cap, moe=None):
    half, tok, width = x_own.shape
    sources = 2 * half
    local, hidden = len(pieces), pieces[0][0].shape[3]
    slots = sources * cap
    wide = g_all.shape[2]
    shape = jax.ShapeDtypeStruct
    outs = [
        shape((sources, 2, tok, width), BF),
        shape((half, tok, wide), BF),
        shape((half, tok, wide), BF),
        shape((local, slots, width), BF),
        shape((local, slots, width), BF),
        shape((local, slots, hidden), BF),
        shape((local, slots, hidden), BF),
        shape((local, slots, hidden), BF),
    ]
    g_spec = pl.BlockSpec(
        (sources, tok, wide), lambda i: (0, micro, 0), pipeline_mode=pl.Buffered(1)
    )
    args = [router, *pieces[0], *pieces[1]]
    held = [] if moe is None else [moe]
    moe_spec = pl.BlockSpec(
        (sources, 1, tok, width), lambda i: (0, micro, 0, 0), pipeline_mode=pl.Buffered(1)
    )
    return pl.pallas_call(
        functools.partial(expert_kernel, again=moe is not None),
        out_shape=outs,
        grid=(1,),
        in_specs=[pl.BlockSpec(memory_space=pltpu.SMEM), whole(x_own), whole(x_other), g_spec]
        + [whole(a) for a in args]
        + [pl.BlockSpec(memory_space=pl.ANY)] * len(held),
        out_specs=[moe_spec] + [whole(o) for o in outs[1:]],
        input_output_aliases={4 + len(args): 0} if held else {},
        scratch_shapes=[
            pltpu.VMEM((sources, tok, local * cap), BF),
            pltpu.VMEM((local, slots, 1), F32),
            pltpu.VMEM((local, slots, 1), F32),
            pltpu.VMEM((local, slots, width), BF),
            pltpu.VMEM((local, slots, width), BF),
            pltpu.VMEM((local, 3, width, hidden), BF),
        ],
        compiler_params=pltpu.CompilerParams(vmem_limit_bytes=60 * 1024 * 1024),
        cost_estimate=COST,
    )(scalars, x_own, x_other, g_all, *args, *held)


def expert_grad_kernel(order_ref, *refs):
    kept, outs, total_ref = refs[:10], refs[10:14], refs[14]
    left = (kept[0:2], kept[0:2], kept[2:4])
    right = (kept[6:8], kept[8:10], kept[4:6])
    step = pl.program_id(0)
    depth = outs[0].shape[2]
    for kind in range(3):

        @pl.when(step == kind)
        def _(kind=kind):
            total = dot(left[kind][0][0], right[kind][0][0], 0, 0)
            total_ref[...] = total + dot(left[kind][1][0], right[kind][1][0], 0, 0)

    for r in range(8):
        rows = pl.ds(pl.multiple_of(order_ref[r] * depth, depth), depth)
        outs[r // 2][r % 2, 0] = total_ref[rows].astype(BF)


def expert_grads(order, kept, expert):
    _, slots, width = kept[0][0].shape
    hidden = kept[0][2].shape[2]
    args = [kept[m][i] for i in range(5) for m in range(2)]
    depth = width // 8
    shape = jax.ShapeDtypeStruct
    return pl.pallas_call(
        expert_grad_kernel,
        out_shape=[shape((2, 3, depth, hidden), BF)] * 4,
        grid=(3,),
        in_specs=[pl.BlockSpec(memory_space=pltpu.SMEM)]
        + [pl.BlockSpec((1,) + a.shape[1:], lambda i: (expert, 0, 0)) for a in args],
        out_specs=[pl.BlockSpec((2, 1, depth, hidden), lambda i: (0, i, 0, 0))] * 4,
        scratch_shapes=[pltpu.VMEM((width, hidden), F32)],
        compiler_params=pltpu.CompilerParams(vmem_limit_bytes=48 * 1024 * 1024),
        cost_estimate=COST,
    )(order, *args)


CTX = ("z", "yl")
GROUP = ("yh", "x")
FSDP = ("yh", "x", "core")
ALL = CTX + FSDP
UP = [(i, (i + 1) % 4) for i in range(4)]
DOWN = [(i, (i - 1) % 4) for i in range(4)]
TWO = [(i, (i + 2) % 4) for i in range(4)]
FLIP = [(0, 1), (1, 0)]


def mm(a, b):
    return jnp.dot(a, b, preferred_element_type=F32)


def mm_t(a, b):
    return lax.dot_general(a, b, (((1,), (1,)), ((), ())), preferred_element_type=F32)


def t_mm(a, b):
    return lax.dot_general(a, b, (((0,), (0,)), ((), ())), preferred_element_type=F32)


def ein(spec, a, b):
    return jnp.einsum(spec, a, b, preferred_element_type=F32)


def swap(parts, axis):
    return lax.all_to_all(parts, axis, split_axis=0, concat_axis=0, tiled=True)


def flip(block, axis):
    return lax.ppermute(block, axis, FLIP)


def by_z(parts):
    return [lax.ppermute(parts[k], "z", perm) for k, perm in ((1, UP), (2, TWO), (3, DOWN))]


def along_z(both):
    before, far, after = by_z([both] * 4)
    return [both, after, far, before]


class Exchange:
    def __init__(self):
        self.last = None

    def __call__(self, parts, axis):
        if self.last is not None:
            parts = after_all(parts, self.last)
        self.last = swap(parts, axis)
        return self.last

    def copies(self, block, axis, count):
        return self(jnp.broadcast_to(block[None], (count,) + block.shape), axis)


def add(a, b):
    return (a.astype(F32) + b.astype(F32)).astype(BF)


def add_part(parts, i, more):
    pieces = [parts[:1], parts[1:]]
    pieces[i] = add(pieces[i], more)
    return jnp.concatenate(pieces, axis=0)


def relay(far):
    return [lax.ppermute(far[:1], "z", UP), lax.ppermute(far[1:], "z", DOWN)]


def ring_sums(parts, far):
    return [
        lax.ppermute(add_part(parts[1], 0, far[0]), "z", UP),
        lax.ppermute(add_part(parts[3], 1, far[1]), "z", DOWN),
    ]


def pair_sums(parts, moved):
    return [sum(part[i].astype(F32) for part in [parts[0]] + moved) for i in range(2)]


def sum_parts(parts):
    return jnp.sum(parts.astype(F32), axis=0)


def after_all(value, *others):
    return lax.optimization_barrier((value,) + others)[0]


def rope_tables(positions):
    half = DH // 2
    inverse = THETA ** (-(jnp.arange(half, dtype=F32) * 2.0) / DH)
    angles = positions.astype(F32)[:, None] * inverse[None, :]
    return (jnp.cos(angles), jnp.sin(angles))


def rms_scale(values, gain):
    return values * lax.rsqrt(jnp.mean(values * values, axis=-1, keepdims=True) + EPS) * gain


def body(
    tokens,
    segments,
    routes,
    w_query,
    w_key,
    w_value,
    w_out,
    w_router,
    attn_gain,
    mlp_gain,
    qk_gain,
    w_gate,
    w_up,
    w_down,
    cotangent,
):
    micro = tokens.shape[0]
    tok = tokens.shape[2]
    width = tokens.shape[3]
    length = segments.shape[2]
    rows = w_query.shape[0]
    n_ctx, n_fsdp = 8, 16
    n_all = n_ctx * n_fsdp
    z, yl, yh, x, core = (lax.axis_index(name) for name in ALL)
    shard = (yh * 4 + x) * 2 + core
    local = w_gate.shape[0]
    experts = local * n_fsdp
    cap = (3 * tok * TOPK + 2 * experts - 1) // (2 * experts)
    all_tok = micro * tok
    ratio = H // KV
    heads = ratio * DH
    span = heads + 2 * DH

    exchange = Exchange()
    small = jnp.concatenate(
        [
            w_router,
            attn_gain[:, None],
            mlp_gain[:, None],
            jnp.pad(qk_gain[:, None], ((0, rows - 1), (0, 0))),
        ],
        axis=1,
    )
    small = jnp.pad(small, ((0, 0), (0, 128 - small.shape[1])))
    pieces = jnp.concatenate(
        [
            w_query.reshape(rows, n_ctx, heads),
            w_key.reshape(rows, n_ctx, DH),
            w_value.reshape(rows, n_ctx, DH),
            jnp.broadcast_to(small[:, None], (rows, n_ctx, 128)),
        ],
        axis=2,
    ).transpose(1, 0, 2)
    pieces = jnp.broadcast_to(pieces[:, None], (n_ctx, n_fsdp) + pieces.shape[1:])
    both_0, both_1 = (
        jnp.concatenate([tokens[m], flip(tokens[m], "yl")], axis=0) for m in range(micro)
    )
    both_w = jnp.stack([w_gate, w_up, w_down], axis=1)
    head_all = exchange(pieces.reshape((n_all,) + pieces.shape[2:]), ALL).reshape(width, -1)
    other_w = flip(both_w, "yl")
    both_w = [jnp.stack([both_w[e], other_w[e]]) for e in range(local)]
    seq_rows = [along_z(both_0)]
    seq_rows.append(along_z(after_all(both_1, *seq_rows[0][1:])))
    head_all = after_all(head_all, *seq_rows[0][1:], other_w)
    w_heads = head_all[:, :span]
    small_all = head_all[:, span:]
    router = small_all[:, :experts]
    small_wide = small_all.astype(F32)
    gain_attn = small_wide[:, experts]
    gain_mlp = small_wide[:, experts + 1]
    gain_heads = small_wide[:, experts + 2].reshape(-1, rows)[:, 0]
    gain_row = gain_attn[None]
    head_row = jnp.concatenate(
        [gain_heads[:DH]] * ratio + [gain_heads[DH:], jnp.ones((DH,), F32)]
    )[None]
    router_pad = jnp.pad(router, ((0, 0), (0, 128 - experts)))

    out_own = exchange.copies(w_out, CTX + GROUP, n_all // 2)

    moved_w = []
    last = seq_rows[1][1:]
    for e in range(local):
        block = after_all(both_w[e], *last)
        last = [lax.ppermute(block, "z", UP), lax.ppermute(block, "z", DOWN)]
        moved_w.append(last)

    expert_ids = jnp.arange(experts, dtype=jnp.int32)
    cot = cotangent.reshape(all_tok, width)
    chosen = jnp.any(routes.reshape(all_tok, TOPK)[:, :, None] == expert_ids, axis=1)
    before = jnp.arange(tok, dtype=jnp.int32)
    lower = (before[:, None] >= before[None, :]).astype(BF)
    counts = ein("ut,mte->mue", lower, chosen.reshape(micro, tok, experts).astype(BF))
    held = jnp.where(chosen, counts.reshape(all_tok, experts) - 1.0, -1.0)
    held = jnp.pad(held, ((0, 0), (0, 128 - experts)), constant_values=-1.0).astype(BF)
    pack = after_all(jnp.concatenate([cot, held], axis=1), both_0, both_1)
    g_all = lax.all_gather(pack, FSDP, axis=0)

    cosine, sine = rope_tables(jnp.arange(length, dtype=jnp.int32))
    cosine = jnp.tile(cosine, (1, 4))
    sine = jnp.tile(jnp.concatenate([-sine, sine], axis=1), (1, 2))
    rel = jnp.arange(n_ctx, dtype=jnp.int32)
    order = ((z + rel // 2) % 4) * 2 + (yl + rel % 2) % 2
    scalars = jnp.concatenate([jnp.stack([shard * local, core]), order]).astype(jnp.int32)

    def to_owner(v):
        return exchange(v.reshape(n_ctx, tok, -1), CTX)

    def attention_args(m):
        seg = segments[m, 0]
        return gain_row, w_heads, head_row, cosine, sine, seg[:, None], seg[None, :]

    mixed_0, *saved_0 = attend_forward(order, seq_rows[0], *attention_args(0))
    seq_rows[1], mixed_0 = lax.optimization_barrier((seq_rows[1], mixed_0))
    mixed_1, *saved_1 = attend_forward(order, seq_rows[1], *attention_args(1))
    saved = [saved_0, saved_1]
    out_own, mixed_0, mixed_1 = lax.optimization_barrier((out_own, mixed_0, mixed_1))
    out_other = flip(out_own, "core")
    mixed = jnp.stack([mixed_0, mixed_1]).reshape(micro, n_ctx, tok, heads).transpose(1, 0, 2, 3)
    mixed = exchange(mixed.reshape(n_ctx, all_tok, heads), CTX)
    mixed, moved_w[0] = lax.optimization_barrier((mixed, moved_w[0]))
    mixed = mixed.transpose(1, 0, 2).reshape(all_tok, width)
    out_full = jnp.where(
        core == 0,
        jnp.stack([out_own, out_other], axis=1),
        jnp.stack([out_other, out_own], axis=1),
    ).reshape(width, width)
    middle = tokens.reshape(all_tok, width).astype(F32) + mm(mixed, out_full)
    inv_two = lax.rsqrt(jnp.mean(middle * middle, axis=-1, keepdims=True) + EPS)
    hidden_two = (middle * inv_two * gain_mlp).astype(BF)
    x_0 = exchange.copies(hidden_two[:tok], GROUP, n_ctx)
    weights = []
    for e, (w_before, w_after) in enumerate(moved_w):
        w_far = [lax.ppermute(w_before[:1], "z", UP), lax.ppermute(w_after[1:], "z", DOWN)]
        weights.append([both_w[e], w_after, *w_far, w_before])
    x_0, weights = lax.optimization_barrier((x_0, weights))
    x_1 = exchange.copies(hidden_two[tok:], GROUP, n_ctx)
    logits = jnp.where(chosen, mm(hidden_two, router), -1e30)
    gates_all = jnp.where(chosen, jax.nn.softmax(logits, axis=-1), 0.0)

    def own_rows(v, m):
        return v[m * tok : (m + 1) * tok]

    def experts_of(m, x_own, *moe):
        return run_experts(
            scalars,
            x_own,
            flip(x_own, "core"),
            g_all,
            m,
            router_pad,
            weights,
            cap,
            *moe,
        )

    def back_sum(own, other):
        return add(own, flip(other, "core"))

    def middle_back(m, back, before):
        rows_middle, inv, gates = (own_rows(v, m) for v in (middle, inv_two, gates_all))
        grad_top = own_rows(cot, m).astype(F32)
        tail = back[:, width:]
        d_gates = tail[:, :experts] + tail[:, 64 : 64 + experts]
        d_select = gates * (d_gates - jnp.sum(gates * d_gates, axis=-1, keepdims=True))
        d_logits = d_select.astype(BF)
        d_two = back[:, :width] + mm_t(d_logits, router)
        u = d_two * gain_mlp
        d_middle = (
            grad_top
            + inv * u
            - rows_middle * (inv**3 * jnp.mean(u * rows_middle, axis=-1, keepdims=True))
        )
        d_branch = d_middle.astype(BF)
        d_mixed = mm_t(d_branch, out_full).astype(BF)
        d_mixed = d_mixed.reshape(tok, n_ctx, heads).transpose(1, 0, 2)
        return d_middle, d_mixed, before + [(d_branch, d_logits, d_two)]

    def weight_grads(saved_rows):
        grad_out = grad_router = grad_mlp = 0.0
        for m, (d_branch, d_logits, d_two) in enumerate(saved_rows):
            rows_mixed, rows_middle, inv, hidden = (
                own_rows(v, m) for v in (mixed, middle, inv_two, hidden_two)
            )
            grad_out = grad_out + t_mm(rows_mixed, d_branch)
            grad_router = grad_router + t_mm(hidden, d_logits)
            grad_mlp = grad_mlp + jnp.sum(d_two * rows_middle * inv, axis=0)
        return grad_out, grad_router, grad_mlp

    def pack_grads(grad_heads, grad_router, grad_attn, grad_mlp, grad_qk):
        grad_qk = jnp.pad(grad_qk[:, None], ((0, 0), (0, rows - 1))).reshape(-1)
        grad_small = jnp.concatenate(
            [grad_router, grad_attn[:, None], grad_mlp[:, None], grad_qk[:, None]], axis=1
        )
        grad_small = jnp.pad(grad_small, ((0, 0), (0, 128 - grad_small.shape[1])))
        grad_pack = jnp.concatenate([grad_heads, grad_small], axis=1).astype(BF)
        return grad_pack.reshape(n_all, rows, -1)

    def attention_back(m, d_mixed):
        *d_hidden, grad_heads, grad_attn, grad_qk = attend_backward(
            order, *saved[m], d_mixed.reshape(length, heads), *attention_args(m)
        )
        grad_qk = jnp.concatenate(
            [grad_qk[0, :DH] + grad_qk[0, DH : 2 * DH], grad_qk[0, 2 * DH : 3 * DH]]
        )
        return d_hidden, (grad_heads, grad_attn[0], grad_qk)

    def input_grad(m, d_hidden, d_middle):
        start = tokens[m, 0].astype(F32)
        inverse = lax.rsqrt(jnp.mean(start * start, axis=-1, keepdims=True) + EPS)
        u = d_hidden * gain_attn
        return (
            d_middle
            + inverse * u
            - start * (inverse**3 * jnp.mean(u * start, axis=-1, keepdims=True))
        )

    moe, back_own, back_other, *kept_0 = experts_of(0, x_0)
    x_1, back_own, back_other = lax.optimization_barrier((x_1, back_own, back_other))
    back_0 = back_sum(back_own, back_other)
    x_1 = after_all(x_1, back_0)
    back_0 = exchange(back_0, GROUP)
    moe, back_own, back_other, *kept_1 = experts_of(1, x_1, moe)
    back_0, back_own, back_other, moe = lax.optimization_barrier(
        (back_0, back_own, back_other, moe)
    )
    moe = lax.psum_scatter(moe, FSDP, scatter_dimension=0, tiled=True)[0]
    back_1 = back_sum(back_own, back_other)
    d_middle_0, d_mixed_0, d_branches = middle_back(0, sum_parts(back_0), [])
    d_mixed_0 = exchange(d_mixed_0, CTX)
    d_mixed_0, back_1 = lax.optimization_barrier((d_mixed_0, back_1))
    back_1 = exchange(back_1, GROUP)
    kept_1[0] = after_all(kept_1[0], d_mixed_0)
    parts = [expert_grads(order, (kept_0, kept_1), 0)]
    far = [relay(parts[0][2])]
    d_hidden_0, head_grads_0 = attention_back(0, after_all(d_mixed_0, parts[0][0]))
    hidden_moved_0 = by_z(d_hidden_0)
    back_1, d_hidden_0[0], far[0] = lax.optimization_barrier((back_1, d_hidden_0[0], far[0]))
    d_middle_1, d_mixed_1, d_branches = middle_back(1, sum_parts(back_1), d_branches)
    far[0], d_mixed_1 = lax.optimization_barrier((far[0], d_mixed_1))
    d_mixed_1 = exchange(d_mixed_1, CTX)
    moved = [ring_sums(parts[0], far[0])]
    d_mixed_1, hidden_moved_0 = lax.optimization_barrier((d_mixed_1, hidden_moved_0))
    d_hidden_1, head_grads_1 = attention_back(1, d_mixed_1)
    d_hidden_1, d_branches, hidden_moved_0, moved[0], kept_1 = lax.optimization_barrier(
        (d_hidden_1, d_branches, hidden_moved_0, moved[0], kept_1)
    )
    hidden_moved_1 = by_z(d_hidden_1)
    grad_heads, grad_attn, grad_qk = jax.tree.map(jnp.add, head_grads_0, head_grads_1)
    grad_out, grad_router, grad_mlp = weight_grads(d_branches)
    grad_pack = pack_grads(grad_heads, grad_router, grad_attn, grad_mlp, grad_qk)
    grad_pack = exchange(grad_pack, ALL)
    parts.append(expert_grads(order, (kept_0, kept_1), 1))
    far.append(relay(parts[1][2]))
    grad_out = grad_out.astype(BF).reshape(n_all // 2, 2, rows, width)
    grad_own = lax.dynamic_index_in_dim(grad_out, core, axis=1, keepdims=False)
    grad_other = lax.dynamic_index_in_dim(grad_out, 1 - core, axis=1, keepdims=False)
    grad_out = back_sum(grad_own, grad_other)
    grad_pack, grad_out, hidden_moved_1, far[1] = lax.optimization_barrier(
        (grad_pack, grad_out, hidden_moved_1, far[1])
    )
    exchange.last = grad_pack
    grad_out = exchange(grad_out, CTX + GROUP)
    moved.append(ring_sums(parts[1], far[1]))
    hidden_sums = pair_sums(d_hidden_0, hidden_moved_0)
    d_hidden_0 = hidden_sums[0] + flip(hidden_sums[1].astype(BF), "yl").astype(F32)
    grad_out, moved[1] = lax.optimization_barrier((grad_out, moved[1]))
    weight_sums = [pair_sums(p, q) for p, q in zip(parts, moved)]
    weight_yl = [flip(sums[1].astype(BF), "yl") for sums in weight_sums]
    hidden_sums = pair_sums(d_hidden_1, hidden_moved_1)
    hidden_yl = flip(hidden_sums[1].astype(BF), "yl")

    grad_pack = grad_pack.astype(F32)
    own_heads = jnp.sum(grad_pack[:, :, :span].reshape(n_ctx, n_fsdp, rows, -1), axis=1)
    own_heads = own_heads.transpose(1, 0, 2)
    own_small = jnp.sum(grad_pack[:, :, span:], axis=0)
    own_out = sum_parts(grad_out)
    moe = after_all(moe, grad_pack)
    d_hidden_1 = hidden_sums[0] + hidden_yl.astype(F32)
    expert_own = [sums[0] + other.astype(F32) for sums, other in zip(weight_sums, weight_yl)]
    out = (middle.reshape(moe.shape) + moe.astype(F32)).astype(BF)
    d_inputs = [
        input_grad(0, d_hidden_0, d_middle_0),
        input_grad(1, d_hidden_1, d_middle_1),
    ]

    return (
        out[:, None],
        jnp.stack(d_inputs)[:, None],
        own_heads[:, :, :heads].reshape(rows, -1),
        own_heads[:, :, heads : heads + DH].reshape(rows, -1),
        own_heads[:, :, heads + DH :].reshape(rows, -1),
        own_out,
        own_small[:, :experts],
        own_small[:, experts],
        own_small[:, experts + 1],
        own_small[:1, experts + 2],
        jnp.stack([part[0] for part in expert_own]),
        jnp.stack([part[1] for part in expert_own]),
        jnp.stack([part[2] for part in expert_own]),
    )


def solution(mesh):
    mesh = Mesh(mesh.devices.reshape(4, 2, 2, 4, 2), ALL)
    weight = P(ALL, None)
    gain = P(ALL)
    rows = P(None, FSDP, CTX, None)
    expert = P(FSDP, CTX, None)
    return jax.shard_map(
        body,
        mesh=mesh,
        in_specs=(rows, P(None, FSDP, None), rows)
        + (weight,) * 5
        + (gain,) * 3
        + (expert,) * 3
        + (rows,),
        out_specs=(rows, rows) + (weight,) * 5 + (gain,) * 3 + (expert,) * 3,
        check_vma=False,
    )
```

```python
import functools

import jax
import jax.numpy as jnp
from jax import lax
from jax.experimental import pallas as pl
from jax.experimental.pallas import tpu as pltpu
from jax.sharding import Mesh
from jax.sharding import PartitionSpec as P

BF = jnp.bfloat16
F32 = jnp.float32
H = 16
KV = 8
DH = 64
TOPK = 8
WINDOW = 1024
EPS = 1e-06
THETA = 10000.0
COST = pl.CostEstimate(flops=10**7, bytes_accessed=10**5, transcendentals=0)


def dot(a, b, ca, cb):
    return lax.dot_general(a, b, (((ca,), (cb,)), ((), ())), preferred_element_type=F32)


def lanes_of(v):
    return lax.broadcasted_iota(jnp.int32, v.shape, v.ndim - 1)


def head_sums(v):
    low = lanes_of(v) < DH
    first = jnp.sum(jnp.where(low, v, 0.0), axis=1, keepdims=True)
    second = jnp.sum(jnp.where(low, 0.0, v), axis=1, keepdims=True)
    return jnp.where(low, first, second)


def trade(v):
    return jnp.where(
        lanes_of(v) % DH < DH // 2, pltpu.roll(v, 128 - DH // 2, 1), pltpu.roll(v, DH // 2, 1)
    )


def both_halves(v, second):
    low = lanes_of(v) < DH
    other = pltpu.roll(v, DH, 1)
    return jnp.where(low, other, v) if second else jnp.where(low, v, other)


def stack_heads(v):
    low = lanes_of(v) < DH
    zero = jnp.zeros_like(v)
    return jnp.concatenate([jnp.where(low, v, zero), jnp.where(low, zero, v)], axis=0)


def key_span(start, block, length):
    reach = WINDOW // 2 - 1
    low = max(0, start - reach) // 128 * 128
    high = min(length, -(-(start + block + reach) // 128) * 128)
    return low, high


def masked_probs(q_two, keys, seg_col, seg_row, start, low):
    block = q_two.shape[0] // 2
    scores = dot(q_two, keys, 1, 1)
    shape = (block, keys.shape[0])
    gap = (
        lax.broadcasted_iota(jnp.int32, shape, 0)
        - lax.broadcasted_iota(jnp.int32, shape, 1)
        + (start - low)
    )
    allowed = (seg_col == seg_row) & (jnp.abs(gap) < WINDOW // 2)
    bias = jnp.where(allowed, 0.0, -1e30)
    scores = scores + jnp.concatenate([bias, bias], axis=0)
    raised = jnp.exp(scores - jnp.max(scores, axis=1, keepdims=True))
    return raised * (1.0 / jnp.sum(raised, axis=1, keepdims=True))


def attend_kernel(
    order_ref,
    *refs,
):
    pieces, refs = refs[:-13], refs[-13:]
    gain_ref, w_ref, head_gain_ref, cos_ref, sin_ref, seg_col_ref, seg_row_ref = refs[:7]
    mixed_ref, hidden_ref, q_ref, kv_ref, keys_ref, values_ref = refs[7:]
    tok, width = pieces[0].shape[1:]
    length = hidden_ref.shape[0]
    pieces = [(ref, i) for ref in pieces for i in range(ref.shape[0])]
    for r, (ref, i) in enumerate(pieces):
        x = ref[i].astype(F32)
        x = x * lax.rsqrt(jnp.mean(x * x, axis=1, keepdims=True) + EPS) * gain_ref[...]
        rows = pl.ds(pl.multiple_of(order_ref[r] * tok, tok), tok)
        hidden_ref[rows] = x.astype(BF)
    raw = dot(hidden_ref[...], w_ref[...], 1, 0)
    for half in range(2):
        u = raw[:, half * 128 : half * 128 + 128]
        gain = head_gain_ref[:, half * 128 : half * 128 + 128]
        n = u * lax.rsqrt(head_sums(u * u) * (1.0 / DH) + EPS) * gain
        turned = n * cos_ref[...] + trade(n) * sin_ref[...]
        if half == 0:
            q_ref[...] = turned.astype(BF)
        else:
            kv = jnp.where(lanes_of(u) < DH, turned, u)
            kv_ref[...] = kv.astype(BF)
            keys_ref[...] = both_halves(kv, False).astype(BF)
            values_ref[...] = both_halves(kv, True).astype(BF)
    block = 256
    for start in range(0, length, block):
        low, high = key_span(start, block, length)
        q_two = stack_heads(q_ref[start : start + block].astype(F32) * DH**-0.5).astype(BF)
        probs = masked_probs(
            q_two,
            keys_ref[low:high],
            seg_col_ref[start : start + block],
            seg_row_ref[:, low:high],
            start,
            low,
        )
        result = dot(probs.astype(BF), values_ref[low:high], 1, 0)
        first = lanes_of(result[:block]) < DH
        mixed_ref[start : start + block] = jnp.where(first, result[:block], result[block:]).astype(
            BF
        )


def attend_back_kernel(
    order_ref,
    hidden_ref,
    q_ref,
    kv_ref,
    d_mixed_ref,
    gain_ref,
    w_ref,
    head_gain_ref,
    cos_ref,
    sin_ref,
    seg_col_ref,
    seg_row_ref,
    d_hidden_0_ref,
    d_hidden_1_ref,
    d_hidden_2_ref,
    d_hidden_3_ref,
    grad_w_ref,
    grad_gain_ref,
    grad_heads_ref,
    keys_ref,
    values_ref,
    d_q_ref,
    d_k_ref,
    d_v_ref,
    d_raw_ref,
):
    length = hidden_ref.shape[0]
    kv = kv_ref[...].astype(F32)
    keys_ref[...] = both_halves(kv, False).astype(BF)
    values_ref[...] = both_halves(kv, True).astype(BF)
    d_k_ref[...] = jnp.zeros_like(d_k_ref)
    d_v_ref[...] = jnp.zeros_like(d_v_ref)
    block = 256
    for start in range(0, length, block):
        low, high = key_span(start, block, length)
        q_two = stack_heads(q_ref[start : start + block].astype(F32) * DH**-0.5).astype(BF)
        m_two = stack_heads(d_mixed_ref[start : start + block].astype(F32)).astype(BF)
        probs = masked_probs(
            q_two,
            keys_ref[low:high],
            seg_col_ref[start : start + block],
            seg_row_ref[:, low:high],
            start,
            low,
        )
        d_probs = dot(m_two, values_ref[low:high], 1, 1)
        inner = jnp.sum(probs * d_probs, axis=1, keepdims=True)
        d_scores = (probs * (d_probs - inner)).astype(BF)
        result = dot(d_scores, keys_ref[low:high], 1, 0)
        first = lanes_of(result[:block]) < DH
        d_q_ref[start : start + block] = jnp.where(first, result[:block], result[block:]) * (
            DH**-0.5
        )
        d_k_ref[low:high] += dot(d_scores, q_two, 0, 0)
        d_v_ref[low:high] += dot(probs.astype(BF), m_two, 0, 0)
    raw = dot(hidden_ref[...], w_ref[...], 1, 0)
    d_k = d_k_ref[...]
    d_k = d_k + pltpu.roll(d_k, DH, 1)
    d_v = d_v_ref[...]
    d_v = d_v + pltpu.roll(d_v, DH, 1)
    for half in range(2):
        lanes = slice(half * 128, half * 128 + 128)
        u = raw[:, lanes]
        gain = head_gain_ref[:, lanes]
        d = d_q_ref[...] if half == 0 else d_k
        d = d * cos_ref[...] + trade(d * sin_ref[...])
        r = lax.rsqrt(head_sums(u * u) * (1.0 / DH) + EPS)
        grad_heads_ref[:, lanes] = jnp.sum(d * u * r, axis=0, keepdims=True)
        d = d * gain
        d = d * r - u * (r * r * r * (head_sums(d * u) * (1.0 / DH)))
        if half == 1:
            d = jnp.where(lanes_of(d) < DH, d, d_v)
        d_raw_ref[:, lanes] = d.astype(BF)
    grad_w_ref[...] = dot(hidden_ref[...], d_raw_ref[...], 0, 0)
    total = jnp.zeros(grad_gain_ref.shape, F32)
    outs = (d_hidden_0_ref, d_hidden_1_ref, d_hidden_2_ref, d_hidden_3_ref)
    tok = length // 8
    for step in range(4):
        rows = pl.ds(pl.multiple_of(order_ref[2 * step] // 2 * (2 * tok), 2 * tok), 2 * tok)
        d_hidden = dot(d_raw_ref[rows], w_ref[...], 1, 1)
        own = order_ref[0] % 2
        outs[step][own] = d_hidden[:tok].astype(BF)
        outs[step][1 - own] = d_hidden[tok:].astype(BF)
        total = total + jnp.sum(d_hidden * hidden_ref[rows].astype(F32), axis=0, keepdims=True)
    grad_gain_ref[...] = total / gain_ref[...]


def whole(a):
    return pl.BlockSpec(a.shape, lambda i: (0,) * len(a.shape), pipeline_mode=pl.Buffered(1))


def attend_forward(order, pieces, gain, w_heads, head_gain, cosine, sine, seg_col, seg_row):
    length = cosine.shape[0]
    width = w_heads.shape[0]
    shape = jax.ShapeDtypeStruct
    outs = [
        shape((length, 128), BF),
        shape((length, width), BF),
        shape((length, 128), BF),
        shape((length, 128), BF),
    ]
    args = list(pieces) + [gain, w_heads, head_gain, cosine, sine, seg_col, seg_row]
    return pl.pallas_call(
        attend_kernel,
        out_shape=outs,
        grid=(1,),
        in_specs=[pl.BlockSpec(memory_space=pltpu.SMEM)] + [whole(a) for a in args],
        out_specs=[whole(o) for o in outs],
        scratch_shapes=[pltpu.VMEM((length, 128), BF), pltpu.VMEM((length, 128), BF)],
        compiler_params=pltpu.CompilerParams(vmem_limit_bytes=40 * 1024 * 1024),
        cost_estimate=COST,
    )(order, *args)


def attend_backward(
    order, hidden, q, kv, d_mixed, gain, w_heads, head_gain, cosine, sine, seg_col, seg_row
):
    length, width = hidden.shape
    shape = jax.ShapeDtypeStruct
    outs = [shape((2, length // 8, width), BF)] * 4 + [
        shape((width, 256), F32),
        shape((1, width), F32),
        shape((1, 256), F32),
    ]
    args = [hidden, q, kv, d_mixed, gain, w_heads, head_gain, cosine, sine, seg_col, seg_row]
    return pl.pallas_call(
        attend_back_kernel,
        out_shape=outs,
        grid=(1,),
        in_specs=[pl.BlockSpec(memory_space=pltpu.SMEM)] + [whole(a) for a in args],
        out_specs=[whole(o) for o in outs],
        scratch_shapes=[pltpu.VMEM((length, 128), BF)] * 2
        + [pltpu.VMEM((length, 128), F32)] * 3
        + [pltpu.VMEM((length, 256), BF)],
        compiler_params=pltpu.CompilerParams(vmem_limit_bytes=40 * 1024 * 1024),
        cost_estimate=COST,
    )(order, *args)


def halves(v):
    high = v.astype(BF)
    return high, (v - high.astype(F32)).astype(BF)


def expert_kernel(scalar_ref, *refs, again):
    x_own_ref, x_other_ref, g_ref, router_ref = refs[:4]
    pieces, refs = (refs[4:9], refs[9:14]), refs[14:]
    if again:
        refs = refs[1:]
    out_ref, refs = refs[0], refs[1:]
    back_own_ref, back_other_ref, xe_ref, de_ref, act_ref, da_ref, db_ref = refs[:7]
    pick_ref, weight_ref, dgate_ref, eo_ref, dr_ref, w_ref = refs[7:]
    half, tok, width = x_own_ref.shape
    sources = 2 * half
    core = scalar_ref[1]
    depth = w_ref.shape[2] // 8

    for e in range(2):
        blocks = [(ref, i) for ref in pieces[e] for i in range(ref.shape[0])]
        for r, (ref, i) in enumerate(blocks):
            rows = pl.ds(pl.multiple_of(scalar_ref[2 + r] * depth, depth), depth)
            w_ref[e, :, rows] = ref[i]
    local, slots, hidden = act_ref.shape
    cap = slots // sources
    first = scalar_ref[0]
    lane = lax.broadcasted_iota(jnp.int32, (tok, 128), 1)
    spot = lax.broadcasted_iota(jnp.int32, (tok, local * cap), 1)
    row_expert = lax.broadcasted_iota(jnp.int32, (local * cap, 128), 0) // cap
    slot_lane = lax.broadcasted_iota(jnp.int32, (local * cap, 128), 1)
    own_lane = slot_lane == first + row_expert

    def fetch(i, carry, x_ref, offset, column):
        s = i + offset
        x = x_ref[i]
        from_g = 2 * i + column
        held = g_ref[from_g, :, width:].astype(F32)
        chosen = held >= 0.0
        logits = jnp.where(chosen, dot(x, router_ref[...], 1, 0), -1e30)
        top = jnp.max(logits, axis=1, keepdims=True)
        raised = jnp.where(chosen, jnp.exp(logits - top), 0.0)
        gates = raised / jnp.sum(raised, axis=1, keepdims=True)
        pick = jnp.zeros((tok, local * cap), F32)
        for e in range(local):
            mine = jnp.max(jnp.where(lane == first + e, held, -1.0), axis=1, keepdims=True)
            goal = jnp.where(mine >= 0.0, mine + e * cap, -1.0).astype(jnp.int32)
            pick = jnp.where(spot == goal, 1.0, pick)
        pick = pick.astype(BF)
        pick_ref[s] = pick
        rows = pl.ds(pl.multiple_of(s * cap, 16), cap)
        x_slots = dot(pick, x, 0, 0).astype(BF)
        g_slots = dot(pick, g_ref[from_g, :, :width], 0, 0).astype(BF)
        high, low = halves(gates)
        weight = dot(pick, high, 0, 0) + dot(pick, low, 0, 0)
        weight = jnp.sum(jnp.where(own_lane, weight, 0.0), axis=1, keepdims=True)
        for e in range(local):
            part = slice(e * cap, (e + 1) * cap)
            xe_ref[e, rows] = x_slots[part]
            de_ref[e, rows] = g_slots[part]
            weight_ref[e, rows] = weight[part]
        return carry

    for x_ref, offset, column in ((x_own_ref, 0, core), (x_other_ref, half, 1 - core)):
        lax.fori_loop(
            0, half, functools.partial(fetch, x_ref=x_ref, offset=offset, column=column), 0
        )
    chunk = 256

    def work(i, carry):
        e = i // (slots // chunk)
        rows = pl.ds(pl.multiple_of((i % (slots // chunk)) * chunk, chunk), chunk)
        w_gate = w_ref[e, 0]
        w_up = w_ref[e, 1]
        w_down = w_ref[e, 2]
        x = xe_ref[e, rows]
        a = dot(x, w_gate, 1, 0)
        b = dot(x, w_up, 1, 0)
        sig = 1.0 / (1.0 + jnp.exp(-a))
        silu = a * sig
        active = (silu * b).astype(BF)
        act_ref[e, rows] = active
        slope = b * (sig * (1.0 + a * (1.0 - sig)))
        weight = weight_ref[e, rows]
        g = de_ref[e, rows].astype(F32)
        result = dot(active, w_down, 1, 1).astype(BF).astype(F32)
        dgate_ref[e, rows] = jnp.sum(result * g, axis=1, keepdims=True)
        eo_ref[e, rows] = (weight * result).astype(BF)
        d_expert = (weight * g).astype(BF)
        de_ref[e, rows] = d_expert
        d_active = dot(d_expert, w_down, 1, 0)
        da = (d_active * slope).astype(BF)
        db = (d_active * silu).astype(BF)
        da_ref[e, rows] = da
        db_ref[e, rows] = db
        dr_ref[e, rows] = (dot(da, w_gate, 1, 1) + dot(db, w_up, 1, 1)).astype(BF)
        return carry

    lax.fori_loop(0, local * (slots // chunk), work, 0)

    def give(i, carry, back_ref, offset, column):
        s = i + offset
        rows = pl.ds(pl.multiple_of(s * cap, 16), cap)
        pick = pick_ref[s]
        eo = jnp.concatenate([eo_ref[e, rows] for e in range(local)], axis=0)
        dr = jnp.concatenate([dr_ref[e, rows] for e in range(local)], axis=0)
        dgate = jnp.concatenate([dgate_ref[e, rows] for e in range(local)], axis=0)
        high, low = halves(dgate)
        spread = jnp.where(own_lane, high.astype(F32), 0.0) + jnp.where(
            slot_lane == first + row_expert + 64, low.astype(F32), 0.0
        )
        out_ref[2 * i + column, 0] = dot(pick, eo, 1, 0).astype(BF)
        back_ref[i, :, :width] = dot(pick, dr, 1, 0).astype(BF)
        back_ref[i, :, width:] = dot(pick, spread.astype(BF), 1, 0).astype(BF)
        return carry

    for back_ref, offset, column in ((back_own_ref, 0, core), (back_other_ref, half, 1 - core)):
        lax.fori_loop(
            0, half, functools.partial(give, back_ref=back_ref, offset=offset, column=column), 0
        )


def run_experts(scalars, x_own, x_other, g_all, micro, router, pieces, cap, moe=None):
    half, tok, width = x_own.shape
    sources = 2 * half
    local, hidden = len(pieces), pieces[0][0].shape[3]
    slots = sources * cap
    wide = g_all.shape[2]
    shape = jax.ShapeDtypeStruct
    outs = [
        shape((sources, 2, tok, width), BF),
        shape((half, tok, wide), BF),
        shape((half, tok, wide), BF),
        shape((local, slots, width), BF),
        shape((local, slots, width), BF),
        shape((local, slots, hidden), BF),
        shape((local, slots, hidden), BF),
        shape((local, slots, hidden), BF),
    ]
    g_spec = pl.BlockSpec(
        (sources, tok, wide), lambda i: (0, micro, 0), pipeline_mode=pl.Buffered(1)
    )
    args = [router, *pieces[0], *pieces[1]]
    held = [] if moe is None else [moe]
    moe_spec = pl.BlockSpec(
        (sources, 1, tok, width), lambda i: (0, micro, 0, 0), pipeline_mode=pl.Buffered(1)
    )
    return pl.pallas_call(
        functools.partial(expert_kernel, again=moe is not None),
        out_shape=outs,
        grid=(1,),
        in_specs=[pl.BlockSpec(memory_space=pltpu.SMEM), whole(x_own), whole(x_other), g_spec]
        + [whole(a) for a in args]
        + [pl.BlockSpec(memory_space=pl.ANY)] * len(held),
        out_specs=[moe_spec] + [whole(o) for o in outs[1:]],
        input_output_aliases={4 + len(args): 0} if held else {},
        scratch_shapes=[
            pltpu.VMEM((sources, tok, local * cap), BF),
            pltpu.VMEM((local, slots, 1), F32),
            pltpu.VMEM((local, slots, 1), F32),
            pltpu.VMEM((local, slots, width), BF),
            pltpu.VMEM((local, slots, width), BF),
            pltpu.VMEM((local, 3, width, hidden), BF),
        ],
        compiler_params=pltpu.CompilerParams(vmem_limit_bytes=60 * 1024 * 1024),
        cost_estimate=COST,
    )(scalars, x_own, x_other, g_all, *args, *held)


def expert_grad_kernel(order_ref, *refs):
    kept, outs, total_ref = refs[:10], refs[10:14], refs[14]
    left = (kept[0:2], kept[0:2], kept[2:4])
    right = (kept[6:8], kept[8:10], kept[4:6])
    step = pl.program_id(0)
    depth = outs[0].shape[2]
    for kind in range(3):

        @pl.when(step == kind)
        def _(kind=kind):
            total = dot(left[kind][0][0], right[kind][0][0], 0, 0)
            total_ref[...] = total + dot(left[kind][1][0], right[kind][1][0], 0, 0)

    for r in range(8):
        rows = pl.ds(pl.multiple_of(order_ref[r] * depth, depth), depth)
        outs[r // 2][r % 2, 0] = total_ref[rows].astype(BF)


def expert_grads(order, kept, expert):
    _, slots, width = kept[0][0].shape
    hidden = kept[0][2].shape[2]
    args = [kept[m][i] for i in range(5) for m in range(2)]
    depth = width // 8
    shape = jax.ShapeDtypeStruct
    return pl.pallas_call(
        expert_grad_kernel,
        out_shape=[shape((2, 3, depth, hidden), BF)] * 4,
        grid=(3,),
        in_specs=[pl.BlockSpec(memory_space=pltpu.SMEM)]
        + [pl.BlockSpec((1,) + a.shape[1:], lambda i: (expert, 0, 0)) for a in args],
        out_specs=[pl.BlockSpec((2, 1, depth, hidden), lambda i: (0, i, 0, 0))] * 4,
        scratch_shapes=[pltpu.VMEM((width, hidden), F32)],
        compiler_params=pltpu.CompilerParams(vmem_limit_bytes=48 * 1024 * 1024),
        cost_estimate=COST,
    )(order, *args)


CTX = ("z", "yl")
GROUP = ("yh", "x")
FSDP = ("yh", "x", "core")
ALL = CTX + FSDP
UP = [(i, (i + 1) % 4) for i in range(4)]
DOWN = [(i, (i - 1) % 4) for i in range(4)]
TWO = [(i, (i + 2) % 4) for i in range(4)]
FLIP = [(0, 1), (1, 0)]


def mm(a, b):
    return jnp.dot(a, b, preferred_element_type=F32)


def mm_t(a, b):
    return lax.dot_general(a, b, (((1,), (1,)), ((), ())), preferred_element_type=F32)


def t_mm(a, b):
    return lax.dot_general(a, b, (((0,), (0,)), ((), ())), preferred_element_type=F32)


def ein(spec, a, b):
    return jnp.einsum(spec, a, b, preferred_element_type=F32)


def swap(parts, axis):
    return lax.all_to_all(parts, axis, split_axis=0, concat_axis=0, tiled=True)


def flip(block, axis):
    return lax.ppermute(block, axis, FLIP)


def by_z(parts):
    return [lax.ppermute(parts[k], "z", perm) for k, perm in ((1, UP), (2, TWO), (3, DOWN))]


def along_z(both):
    before, far, after = by_z([both] * 4)
    return [both, after, far, before]


class Exchange:
    def __init__(self):
        self.last = None

    def __call__(self, parts, axis):
        if self.last is not None:
            parts = after_all(parts, self.last)
        self.last = swap(parts, axis)
        return self.last

    def copies(self, block, axis, count):
        return self(jnp.broadcast_to(block[None], (count,) + block.shape), axis)


def add(a, b):
    return (a.astype(F32) + b.astype(F32)).astype(BF)


def add_part(parts, i, more):
    pieces = [parts[:1], parts[1:]]
    pieces[i] = add(pieces[i], more)
    return jnp.concatenate(pieces, axis=0)


def relay(far):
    return [lax.ppermute(far[:1], "z", UP), lax.ppermute(far[1:], "z", DOWN)]


def ring_sums(parts, far):
    return [
        lax.ppermute(add_part(parts[1], 0, far[0]), "z", UP),
        lax.ppermute(add_part(parts[3], 1, far[1]), "z", DOWN),
    ]


def pair_sums(parts, moved):
    return [sum(part[i].astype(F32) for part in [parts[0]] + moved) for i in range(2)]


def sum_parts(parts):
    return jnp.sum(parts.astype(F32), axis=0)


def after_all(value, *others):
    return lax.optimization_barrier((value,) + others)[0]


def rope_tables(positions):
    half = DH // 2
    inverse = THETA ** (-(jnp.arange(half, dtype=F32) * 2.0) / DH)
    angles = positions.astype(F32)[:, None] * inverse[None, :]
    return (jnp.cos(angles), jnp.sin(angles))


def rms_scale(values, gain):
    return values * lax.rsqrt(jnp.mean(values * values, axis=-1, keepdims=True) + EPS) * gain


def body(
    tokens,
    segments,
    routes,
    w_query,
    w_key,
    w_value,
    w_out,
    w_router,
    attn_gain,
    mlp_gain,
    qk_gain,
    w_gate,
    w_up,
    w_down,
    cotangent,
):
    micro = tokens.shape[0]
    tok = tokens.shape[2]
    width = tokens.shape[3]
    length = segments.shape[2]
    rows = w_query.shape[0]
    n_ctx, n_fsdp = 8, 16
    n_all = n_ctx * n_fsdp
    z, yl, yh, x, core = (lax.axis_index(name) for name in ALL)
    shard = (yh * 4 + x) * 2 + core
    local = w_gate.shape[0]
    experts = local * n_fsdp
    cap = (3 * tok * TOPK + 2 * experts - 1) // (2 * experts)
    all_tok = micro * tok
    ratio = H // KV
    heads = ratio * DH
    span = heads + 2 * DH

    exchange = Exchange()
    small = jnp.concatenate(
        [
            w_router,
            attn_gain[:, None],
            mlp_gain[:, None],
            jnp.pad(qk_gain[:, None], ((0, rows - 1), (0, 0))),
        ],
        axis=1,
    )
    small = jnp.pad(small, ((0, 0), (0, 128 - small.shape[1])))
    pieces = jnp.concatenate(
        [
            w_query.reshape(rows, n_ctx, heads),
            w_key.reshape(rows, n_ctx, DH),
            w_value.reshape(rows, n_ctx, DH),
            jnp.broadcast_to(small[:, None], (rows, n_ctx, 128)),
        ],
        axis=2,
    ).transpose(1, 0, 2)
    pieces = jnp.broadcast_to(pieces[:, None], (n_ctx, n_fsdp) + pieces.shape[1:])
    both_0, both_1 = (
        jnp.concatenate([tokens[m], flip(tokens[m], "yl")], axis=0) for m in range(micro)
    )
    both_w = jnp.stack([w_gate, w_up, w_down], axis=1)
    head_all = exchange(pieces.reshape((n_all,) + pieces.shape[2:]), ALL).reshape(width, -1)
    other_w = flip(both_w, "yl")
    both_w = [jnp.stack([both_w[e], other_w[e]]) for e in range(local)]
    seq_rows = [along_z(both_0)]
    seq_rows.append(along_z(after_all(both_1, *seq_rows[0][1:])))
    head_all = after_all(head_all, *seq_rows[0][1:], other_w)
    w_heads = head_all[:, :span]
    small_all = head_all[:, span:]
    router = small_all[:, :experts]
    small_wide = small_all.astype(F32)
    gain_attn = small_wide[:, experts]
    gain_mlp = small_wide[:, experts + 1]
    gain_heads = small_wide[:, experts + 2].reshape(-1, rows)[:, 0]
    gain_row = gain_attn[None]
    head_row = jnp.concatenate(
        [gain_heads[:DH]] * ratio + [gain_heads[DH:], jnp.ones((DH,), F32)]
    )[None]
    router_pad = jnp.pad(router, ((0, 0), (0, 128 - experts)))

    out_own = exchange.copies(w_out, CTX + GROUP, n_all // 2)

    moved_w = []
    last = seq_rows[1][1:]
    for e in range(local):
        block = after_all(both_w[e], *last)
        last = [lax.ppermute(block, "z", UP), lax.ppermute(block, "z", DOWN)]
        moved_w.append(last)

    expert_ids = jnp.arange(experts, dtype=jnp.int32)
    cot = cotangent.reshape(all_tok, width)
    chosen = jnp.any(routes.reshape(all_tok, TOPK)[:, :, None] == expert_ids, axis=1)
    before = jnp.arange(tok, dtype=jnp.int32)
    lower = (before[:, None] >= before[None, :]).astype(BF)
    counts = ein("ut,mte->mue", lower, chosen.reshape(micro, tok, experts).astype(BF))
    held = jnp.where(chosen, counts.reshape(all_tok, experts) - 1.0, -1.0)
    held = jnp.pad(held, ((0, 0), (0, 128 - experts)), constant_values=-1.0).astype(BF)
    pack = after_all(jnp.concatenate([cot, held], axis=1), both_0, both_1)
    g_all = lax.all_gather(pack, FSDP, axis=0)

    cosine, sine = rope_tables(jnp.arange(length, dtype=jnp.int32))
    cosine = jnp.tile(cosine, (1, 4))
    sine = jnp.tile(jnp.concatenate([-sine, sine], axis=1), (1, 2))
    rel = jnp.arange(n_ctx, dtype=jnp.int32)
    order = ((z + rel // 2) % 4) * 2 + (yl + rel % 2) % 2
    scalars = jnp.concatenate([jnp.stack([shard * local, core]), order]).astype(jnp.int32)

    def to_owner(v):
        return exchange(v.reshape(n_ctx, tok, -1), CTX)

    def attention_args(m):
        seg = segments[m, 0]
        return gain_row, w_heads, head_row, cosine, sine, seg[:, None], seg[None, :]

    mixed_0, *saved_0 = attend_forward(order, seq_rows[0], *attention_args(0))
    seq_rows[1], mixed_0 = lax.optimization_barrier((seq_rows[1], mixed_0))
    mixed_1, *saved_1 = attend_forward(order, seq_rows[1], *attention_args(1))
    saved = [saved_0, saved_1]
    out_own, mixed_0, mixed_1 = lax.optimization_barrier((out_own, mixed_0, mixed_1))
    out_other = flip(out_own, "core")
    mixed = jnp.stack([mixed_0, mixed_1]).reshape(micro, n_ctx, tok, heads).transpose(1, 0, 2, 3)
    mixed = exchange(mixed.reshape(n_ctx, all_tok, heads), CTX)
    mixed, moved_w[0] = lax.optimization_barrier((mixed, moved_w[0]))
    mixed = mixed.transpose(1, 0, 2).reshape(all_tok, width)
    out_full = jnp.where(
        core == 0,
        jnp.stack([out_own, out_other], axis=1),
        jnp.stack([out_other, out_own], axis=1),
    ).reshape(width, width)
    middle = tokens.reshape(all_tok, width).astype(F32) + mm(mixed, out_full)
    inv_two = lax.rsqrt(jnp.mean(middle * middle, axis=-1, keepdims=True) + EPS)
    hidden_two = (middle * inv_two * gain_mlp).astype(BF)
    x_0 = exchange.copies(hidden_two[:tok], GROUP, n_ctx)
    weights = []
    for e, (w_before, w_after) in enumerate(moved_w):
        w_far = [lax.ppermute(w_before[:1], "z", UP), lax.ppermute(w_after[1:], "z", DOWN)]
        weights.append([both_w[e], w_after, *w_far, w_before])
    x_0, weights = lax.optimization_barrier((x_0, weights))
    x_1 = exchange.copies(hidden_two[tok:], GROUP, n_ctx)
    logits = jnp.where(chosen, mm(hidden_two, router), -1e30)
    gates_all = jnp.where(chosen, jax.nn.softmax(logits, axis=-1), 0.0)

    def experts_of(m, x_own, *moe):
        return run_experts(
            scalars,
            x_own,
            flip(x_own, "core"),
            g_all,
            m,
            router_pad,
            weights,
            cap,
            *moe,
        )

    def back_sum(own, other):
        return add(own, flip(other, "core"))

    def middle_back(back):
        tail = back[:, width:]
        d_gates = tail[:, :experts] + tail[:, 64 : 64 + experts]
        d_select = gates_all * (d_gates - jnp.sum(gates_all * d_gates, axis=-1, keepdims=True))
        d_logits = d_select.astype(BF)
        d_two = back[:, :width] + mm_t(d_logits, router)
        u = d_two * gain_mlp
        d_middle = (
            cot.astype(F32)
            + inv_two * u
            - middle * (inv_two**3 * jnp.mean(u * middle, axis=-1, keepdims=True))
        )
        d_branch = d_middle.astype(BF)
        d_mixed = mm_t(d_branch, out_full).astype(BF)
        d_mixed = d_mixed.reshape(all_tok, n_ctx, heads).transpose(1, 0, 2)
        return d_middle, d_mixed, (d_branch, d_logits, d_two)

    def weight_grads(d_branch, d_logits, d_two):
        grad_mlp = jnp.sum(d_two * middle * inv_two, axis=0)
        return t_mm(mixed, d_branch), t_mm(hidden_two, d_logits), grad_mlp

    def pack_grads(grad_heads, grad_router, grad_attn, grad_mlp, grad_qk):
        grad_qk = jnp.pad(grad_qk[:, None], ((0, 0), (0, rows - 1))).reshape(-1)
        grad_small = jnp.concatenate(
            [grad_router, grad_attn[:, None], grad_mlp[:, None], grad_qk[:, None]], axis=1
        )
        grad_small = jnp.pad(grad_small, ((0, 0), (0, 128 - grad_small.shape[1])))
        grad_pack = jnp.concatenate([grad_heads, grad_small], axis=1).astype(BF)
        return grad_pack.reshape(n_all, rows, -1)

    def attention_back(m, d_mixed):
        *d_hidden, grad_heads, grad_attn, grad_qk = attend_backward(
            order, *saved[m], d_mixed.reshape(length, heads), *attention_args(m)
        )
        grad_qk = jnp.concatenate(
            [grad_qk[0, :DH] + grad_qk[0, DH : 2 * DH], grad_qk[0, 2 * DH : 3 * DH]]
        )
        return d_hidden, (grad_heads, grad_attn[0], grad_qk)

    moe, back_own, back_other, *kept_0 = experts_of(0, x_0)
    x_1, back_own, back_other = lax.optimization_barrier((x_1, back_own, back_other))
    back_0 = back_sum(back_own, back_other)
    x_1 = after_all(x_1, back_0)
    back_0 = exchange(back_0, GROUP)
    moe, back_own, back_other, *kept_1 = experts_of(1, x_1, moe)
    back_0, back_own, back_other, moe = lax.optimization_barrier(
        (back_0, back_own, back_other, moe)
    )
    moe = lax.psum_scatter(moe, FSDP, scatter_dimension=0, tiled=True)[0]
    back_1 = back_sum(back_own, back_other)
    kept_1[0], back_1 = lax.optimization_barrier((kept_1[0], back_1))
    back_1 = exchange(back_1, GROUP)
    parts = [expert_grads(order, (kept_0, kept_1), e) for e in range(local)]
    far = [relay(part[2]) for part in parts]
    back_1, parts, far[0] = lax.optimization_barrier((back_1, parts, far[0]))
    d_middle, d_mixed, d_rows = middle_back(
        jnp.concatenate([sum_parts(back_0), sum_parts(back_1)], axis=0)
    )
    d_mixed, far[0] = lax.optimization_barrier((d_mixed, far[0]))
    d_mixed = exchange(d_mixed, CTX)
    moved = [ring_sums(parts[0], far[0])]
    d_mixed, far[1], moved[0] = lax.optimization_barrier((d_mixed, far[1], moved[0]))
    moved.append(ring_sums(parts[1], far[1]))
    d_mixed = d_mixed.reshape(n_ctx, micro, tok, heads)
    d_hidden_0, head_grads_0 = attention_back(0, d_mixed[:, 0])
    d_hidden_0, d_mixed, moved[1] = lax.optimization_barrier((d_hidden_0, d_mixed, moved[1]))
    hidden_moved_0 = by_z(d_hidden_0)
    d_hidden_1, head_grads_1 = attention_back(1, d_mixed[:, 1])
    d_hidden_1, d_rows, parts, moved = lax.optimization_barrier(
        (d_hidden_1, d_rows, parts, moved)
    )
    hidden_moved_1 = by_z(d_hidden_1)
    grad_heads, grad_attn, grad_qk = jax.tree.map(jnp.add, head_grads_0, head_grads_1)
    grad_out, grad_router, grad_mlp = weight_grads(*d_rows)
    grad_pack = pack_grads(grad_heads, grad_router, grad_attn, grad_mlp, grad_qk)
    grad_pack = exchange(grad_pack, ALL)
    grad_out = grad_out.astype(BF).reshape(n_all // 2, 2, rows, width)
    grad_own = lax.dynamic_index_in_dim(grad_out, core, axis=1, keepdims=False)
    grad_other = lax.dynamic_index_in_dim(grad_out, 1 - core, axis=1, keepdims=False)
    grad_out = back_sum(grad_own, grad_other)
    weight_sums = [pair_sums(p, q) for p, q in zip(parts, moved)]
    weight_yl = [flip(sums[1].astype(BF), "yl") for sums in weight_sums]
    grad_pack, grad_out, hidden_moved_0, hidden_moved_1, weight_yl = lax.optimization_barrier(
        (grad_pack, grad_out, hidden_moved_0, hidden_moved_1, weight_yl)
    )
    exchange.last = grad_pack
    grad_out = exchange(grad_out, CTX + GROUP)
    hidden_sums = [
        jnp.stack(sums)
        for sums in zip(
            pair_sums(d_hidden_0, hidden_moved_0), pair_sums(d_hidden_1, hidden_moved_1)
        )
    ]
    hidden_yl = flip(hidden_sums[1].astype(BF), "yl")

    grad_pack = grad_pack.astype(F32)
    own_heads = jnp.sum(grad_pack[:, :, :span].reshape(n_ctx, n_fsdp, rows, -1), axis=1)
    own_heads = own_heads.transpose(1, 0, 2)
    own_small = jnp.sum(grad_pack[:, :, span:], axis=0)
    own_out = sum_parts(grad_out)
    moe = after_all(moe, grad_pack)
    d_hidden = (hidden_sums[0] + hidden_yl.astype(F32)).reshape(all_tok, width)
    expert_own = [sums[0] + other.astype(F32) for sums, other in zip(weight_sums, weight_yl)]
    out = (middle.reshape(moe.shape) + moe.astype(F32)).astype(BF)
    start = tokens.reshape(all_tok, width).astype(F32)
    inv_one = lax.rsqrt(jnp.mean(start * start, axis=-1, keepdims=True) + EPS)
    u = d_hidden * gain_attn
    d_input = (
        d_middle
        + inv_one * u
        - start * (inv_one**3 * jnp.mean(u * start, axis=-1, keepdims=True))
    )

    return (
        out[:, None],
        d_input.reshape(tokens.shape),
        own_heads[:, :, :heads].reshape(rows, -1),
        own_heads[:, :, heads : heads + DH].reshape(rows, -1),
        own_heads[:, :, heads + DH :].reshape(rows, -1),
        own_out,
        own_small[:, :experts],
        own_small[:, experts],
        own_small[:, experts + 1],
        own_small[:1, experts + 2],
        jnp.stack([part[0] for part in expert_own]),
        jnp.stack([part[1] for part in expert_own]),
        jnp.stack([part[2] for part in expert_own]),
    )


def solution(mesh):
    mesh = Mesh(mesh.devices.reshape(4, 2, 2, 4, 2), ALL)
    weight = P(ALL, None)
    gain = P(ALL)
    rows = P(None, FSDP, CTX, None)
    expert = P(FSDP, CTX, None)
    return jax.shard_map(
        body,
        mesh=mesh,
        in_specs=(rows, P(None, FSDP, None), rows)
        + (weight,) * 5
        + (gain,) * 3
        + (expert,) * 3
        + (rows,),
        out_specs=(rows, rows) + (weight,) * 5 + (gain,) * 3 + (expert,) * 3,
        check_vma=False,
    )
```

```python
import functools

import jax
import jax.numpy as jnp
from jax import lax
from jax.experimental import pallas as pl
from jax.experimental.pallas import tpu as pltpu
from jax.sharding import Mesh
from jax.sharding import PartitionSpec as P

BF = jnp.bfloat16
F32 = jnp.float32
H = 16
KV = 8
DH = 64
TOPK = 8
WINDOW = 1024
EPS = 1e-06
THETA = 10000.0
COST = pl.CostEstimate(flops=10**7, bytes_accessed=10**5, transcendentals=0)


def dot(a, b, ca, cb):
    return lax.dot_general(a, b, (((ca,), (cb,)), ((), ())), preferred_element_type=F32)


def lanes_of(v):
    return lax.broadcasted_iota(jnp.int32, v.shape, v.ndim - 1)


def head_sums(v):
    low = lanes_of(v) < DH
    first = jnp.sum(jnp.where(low, v, 0.0), axis=1, keepdims=True)
    second = jnp.sum(jnp.where(low, 0.0, v), axis=1, keepdims=True)
    return jnp.where(low, first, second)


def trade(v):
    return jnp.where(
        lanes_of(v) % DH < DH // 2, pltpu.roll(v, 128 - DH // 2, 1), pltpu.roll(v, DH // 2, 1)
    )


def both_halves(v, second):
    low = lanes_of(v) < DH
    other = pltpu.roll(v, DH, 1)
    return jnp.where(low, other, v) if second else jnp.where(low, v, other)


def stack_heads(v):
    low = lanes_of(v) < DH
    zero = jnp.zeros_like(v)
    return jnp.concatenate([jnp.where(low, v, zero), jnp.where(low, zero, v)], axis=0)


def key_span(start, block, length):
    reach = WINDOW // 2 - 1
    low = max(0, start - reach) // 128 * 128
    high = min(length, -(-(start + block + reach) // 128) * 128)
    return low, high


def masked_probs(q_two, keys, seg_col, seg_row, start, low):
    block = q_two.shape[0] // 2
    scores = dot(q_two, keys, 1, 1)
    shape = (block, keys.shape[0])
    gap = (
        lax.broadcasted_iota(jnp.int32, shape, 0)
        - lax.broadcasted_iota(jnp.int32, shape, 1)
        + (start - low)
    )
    allowed = (seg_col == seg_row) & (jnp.abs(gap) < WINDOW // 2)
    bias = jnp.where(allowed, 0.0, -1e30)
    scores = scores + jnp.concatenate([bias, bias], axis=0)
    raised = jnp.exp(scores - jnp.max(scores, axis=1, keepdims=True))
    return raised * (1.0 / jnp.sum(raised, axis=1, keepdims=True))


def attend_kernel(
    order_ref,
    *refs,
):
    pieces, refs = refs[:-13], refs[-13:]
    gain_ref, w_ref, head_gain_ref, cos_ref, sin_ref, seg_col_ref, seg_row_ref = refs[:7]
    mixed_ref, hidden_ref, q_ref, kv_ref, keys_ref, values_ref = refs[7:]
    tok, width = pieces[0].shape[1:]
    length = hidden_ref.shape[0]
    pieces = [(ref, i) for ref in pieces for i in range(ref.shape[0])]
    for r, (ref, i) in enumerate(pieces):
        x = ref[i].astype(F32)
        x = x * lax.rsqrt(jnp.mean(x * x, axis=1, keepdims=True) + EPS) * gain_ref[...]
        rows = pl.ds(pl.multiple_of(order_ref[r] * tok, tok), tok)
        hidden_ref[rows] = x.astype(BF)
    raw = dot(hidden_ref[...], w_ref[...], 1, 0)
    for half in range(2):
        u = raw[:, half * 128 : half * 128 + 128]
        gain = head_gain_ref[:, half * 128 : half * 128 + 128]
        n = u * lax.rsqrt(head_sums(u * u) * (1.0 / DH) + EPS) * gain
        turned = n * cos_ref[...] + trade(n) * sin_ref[...]
        if half == 0:
            q_ref[...] = turned.astype(BF)
        else:
            kv = jnp.where(lanes_of(u) < DH, turned, u)
            kv_ref[...] = kv.astype(BF)
            keys_ref[...] = both_halves(kv, False).astype(BF)
            values_ref[...] = both_halves(kv, True).astype(BF)
    block = 256
    for start in range(0, length, block):
        low, high = key_span(start, block, length)
        q_two = stack_heads(q_ref[start : start + block].astype(F32) * DH**-0.5).astype(BF)
        probs = masked_probs(
            q_two,
            keys_ref[low:high],
            seg_col_ref[start : start + block],
            seg_row_ref[:, low:high],
            start,
            low,
        )
        result = dot(probs.astype(BF), values_ref[low:high], 1, 0)
        first = lanes_of(result[:block]) < DH
        mixed_ref[start : start + block] = jnp.where(first, result[:block], result[block:]).astype(
            BF
        )


def attend_back_kernel(
    order_ref,
    hidden_ref,
    q_ref,
    kv_ref,
    d_mixed_ref,
    gain_ref,
    w_ref,
    head_gain_ref,
    cos_ref,
    sin_ref,
    seg_col_ref,
    seg_row_ref,
    d_hidden_0_ref,
    d_hidden_1_ref,
    d_hidden_2_ref,
    d_hidden_3_ref,
    grad_w_ref,
    grad_gain_ref,
    grad_heads_ref,
    keys_ref,
    values_ref,
    d_q_ref,
    d_k_ref,
    d_v_ref,
    d_raw_ref,
):
    length = hidden_ref.shape[0]
    kv = kv_ref[...].astype(F32)
    keys_ref[...] = both_halves(kv, False).astype(BF)
    values_ref[...] = both_halves(kv, True).astype(BF)
    d_k_ref[...] = jnp.zeros_like(d_k_ref)
    d_v_ref[...] = jnp.zeros_like(d_v_ref)
    block = 256
    for start in range(0, length, block):
        low, high = key_span(start, block, length)
        q_two = stack_heads(q_ref[start : start + block].astype(F32) * DH**-0.5).astype(BF)
        m_two = stack_heads(d_mixed_ref[start : start + block].astype(F32)).astype(BF)
        probs = masked_probs(
            q_two,
            keys_ref[low:high],
            seg_col_ref[start : start + block],
            seg_row_ref[:, low:high],
            start,
            low,
        )
        d_probs = dot(m_two, values_ref[low:high], 1, 1)
        inner = jnp.sum(probs * d_probs, axis=1, keepdims=True)
        d_scores = (probs * (d_probs - inner)).astype(BF)
        result = dot(d_scores, keys_ref[low:high], 1, 0)
        first = lanes_of(result[:block]) < DH
        d_q_ref[start : start + block] = jnp.where(first, result[:block], result[block:]) * (
            DH**-0.5
        )
        d_k_ref[low:high] += dot(d_scores, q_two, 0, 0)
        d_v_ref[low:high] += dot(probs.astype(BF), m_two, 0, 0)
    raw = dot(hidden_ref[...], w_ref[...], 1, 0)
    d_k = d_k_ref[...]
    d_k = d_k + pltpu.roll(d_k, DH, 1)
    d_v = d_v_ref[...]
    d_v = d_v + pltpu.roll(d_v, DH, 1)
    for half in range(2):
        lanes = slice(half * 128, half * 128 + 128)
        u = raw[:, lanes]
        gain = head_gain_ref[:, lanes]
        d = d_q_ref[...] if half == 0 else d_k
        d = d * cos_ref[...] + trade(d * sin_ref[...])
        r = lax.rsqrt(head_sums(u * u) * (1.0 / DH) + EPS)
        grad_heads_ref[:, lanes] = jnp.sum(d * u * r, axis=0, keepdims=True)
        d = d * gain
        d = d * r - u * (r * r * r * (head_sums(d * u) * (1.0 / DH)))
        if half == 1:
            d = jnp.where(lanes_of(d) < DH, d, d_v)
        d_raw_ref[:, lanes] = d.astype(BF)
    grad_w_ref[...] = dot(hidden_ref[...], d_raw_ref[...], 0, 0)
    total = jnp.zeros(grad_gain_ref.shape, F32)
    outs = (d_hidden_0_ref, d_hidden_1_ref, d_hidden_2_ref, d_hidden_3_ref)
    tok = length // 8
    for step in range(4):
        rows = pl.ds(pl.multiple_of(order_ref[2 * step] // 2 * (2 * tok), 2 * tok), 2 * tok)
        d_hidden = dot(d_raw_ref[rows], w_ref[...], 1, 1)
        own = order_ref[0] % 2
        outs[step][own] = d_hidden[:tok].astype(BF)
        outs[step][1 - own] = d_hidden[tok:].astype(BF)
        total = total + jnp.sum(d_hidden * hidden_ref[rows].astype(F32), axis=0, keepdims=True)
    grad_gain_ref[...] = total / gain_ref[...]


def whole(a):
    return pl.BlockSpec(a.shape, lambda i: (0,) * len(a.shape), pipeline_mode=pl.Buffered(1))


def attend_forward(order, pieces, gain, w_heads, head_gain, cosine, sine, seg_col, seg_row):
    length = cosine.shape[0]
    width = w_heads.shape[0]
    shape = jax.ShapeDtypeStruct
    outs = [
        shape((length, 128), BF),
        shape((length, width), BF),
        shape((length, 128), BF),
        shape((length, 128), BF),
    ]
    args = list(pieces) + [gain, w_heads, head_gain, cosine, sine, seg_col, seg_row]
    return pl.pallas_call(
        attend_kernel,
        out_shape=outs,
        grid=(1,),
        in_specs=[pl.BlockSpec(memory_space=pltpu.SMEM)] + [whole(a) for a in args],
        out_specs=[whole(o) for o in outs],
        scratch_shapes=[pltpu.VMEM((length, 128), BF), pltpu.VMEM((length, 128), BF)],
        compiler_params=pltpu.CompilerParams(vmem_limit_bytes=40 * 1024 * 1024),
        cost_estimate=COST,
    )(order, *args)


def attend_backward(
    order, hidden, q, kv, d_mixed, gain, w_heads, head_gain, cosine, sine, seg_col, seg_row
):
    length, width = hidden.shape
    shape = jax.ShapeDtypeStruct
    outs = [shape((2, length // 8, width), BF)] * 4 + [
        shape((width, 256), F32),
        shape((1, width), F32),
        shape((1, 256), F32),
    ]
    args = [hidden, q, kv, d_mixed, gain, w_heads, head_gain, cosine, sine, seg_col, seg_row]
    return pl.pallas_call(
        attend_back_kernel,
        out_shape=outs,
        grid=(1,),
        in_specs=[pl.BlockSpec(memory_space=pltpu.SMEM)] + [whole(a) for a in args],
        out_specs=[whole(o) for o in outs],
        scratch_shapes=[pltpu.VMEM((length, 128), BF)] * 2
        + [pltpu.VMEM((length, 128), F32)] * 3
        + [pltpu.VMEM((length, 256), BF)],
        compiler_params=pltpu.CompilerParams(vmem_limit_bytes=40 * 1024 * 1024),
        cost_estimate=COST,
    )(order, *args)


def halves(v):
    high = v.astype(BF)
    return high, (v - high.astype(F32)).astype(BF)


def expert_kernel(scalar_ref, *refs, again):
    x_own_ref, x_other_ref, g_ref, router_ref = refs[:4]
    pieces, refs = (refs[4:9], refs[9:14]), refs[14:]
    if again:
        refs = refs[1:]
    out_ref, refs = refs[0], refs[1:]
    back_own_ref, back_other_ref, xe_ref, de_ref, act_ref, da_ref, db_ref = refs[:7]
    pick_ref, weight_ref, dgate_ref, eo_ref, dr_ref, w_ref = refs[7:]
    half, tok, width = x_own_ref.shape
    sources = 2 * half
    core = scalar_ref[1]
    depth = w_ref.shape[2] // 8

    for e in range(2):
        blocks = [(ref, i) for ref in pieces[e] for i in range(ref.shape[0])]
        for r, (ref, i) in enumerate(blocks):
            rows = pl.ds(pl.multiple_of(scalar_ref[2 + r] * depth, depth), depth)
            w_ref[e, :, rows] = ref[i]
    local, slots, hidden = act_ref.shape
    cap = slots // sources
    first = scalar_ref[0]
    lane = lax.broadcasted_iota(jnp.int32, (tok, 128), 1)
    spot = lax.broadcasted_iota(jnp.int32, (tok, local * cap), 1)
    row_expert = lax.broadcasted_iota(jnp.int32, (local * cap, 128), 0) // cap
    slot_lane = lax.broadcasted_iota(jnp.int32, (local * cap, 128), 1)
    own_lane = slot_lane == first + row_expert

    def fetch(i, carry, x_ref, offset, column):
        s = i + offset
        x = x_ref[i]
        from_g = 2 * i + column
        held = g_ref[from_g, :, width:].astype(F32)
        chosen = held >= 0.0
        logits = jnp.where(chosen, dot(x, router_ref[...], 1, 0), -1e30)
        top = jnp.max(logits, axis=1, keepdims=True)
        raised = jnp.where(chosen, jnp.exp(logits - top), 0.0)
        gates = raised / jnp.sum(raised, axis=1, keepdims=True)
        pick = jnp.zeros((tok, local * cap), F32)
        for e in range(local):
            mine = jnp.max(jnp.where(lane == first + e, held, -1.0), axis=1, keepdims=True)
            goal = jnp.where(mine >= 0.0, mine + e * cap, -1.0).astype(jnp.int32)
            pick = jnp.where(spot == goal, 1.0, pick)
        pick = pick.astype(BF)
        pick_ref[s] = pick
        rows = pl.ds(pl.multiple_of(s * cap, 16), cap)
        x_slots = dot(pick, x, 0, 0).astype(BF)
        g_slots = dot(pick, g_ref[from_g, :, :width], 0, 0).astype(BF)
        high, low = halves(gates)
        weight = dot(pick, high, 0, 0) + dot(pick, low, 0, 0)
        weight = jnp.sum(jnp.where(own_lane, weight, 0.0), axis=1, keepdims=True)
        for e in range(local):
            part = slice(e * cap, (e + 1) * cap)
            xe_ref[e, rows] = x_slots[part]
            de_ref[e, rows] = g_slots[part]
            weight_ref[e, rows] = weight[part]
        return carry

    for x_ref, offset, column in ((x_own_ref, 0, core), (x_other_ref, half, 1 - core)):
        lax.fori_loop(
            0, half, functools.partial(fetch, x_ref=x_ref, offset=offset, column=column), 0
        )
    chunk = 256

    def work(i, carry):
        e = i // (slots // chunk)
        rows = pl.ds(pl.multiple_of((i % (slots // chunk)) * chunk, chunk), chunk)
        w_gate = w_ref[e, 0]
        w_up = w_ref[e, 1]
        w_down = w_ref[e, 2]
        x = xe_ref[e, rows]
        a = dot(x, w_gate, 1, 0)
        b = dot(x, w_up, 1, 0)
        sig = 1.0 / (1.0 + jnp.exp(-a))
        silu = a * sig
        active = (silu * b).astype(BF)
        act_ref[e, rows] = active
        slope = b * (sig * (1.0 + a * (1.0 - sig)))
        weight = weight_ref[e, rows]
        g = de_ref[e, rows].astype(F32)
        result = dot(active, w_down, 1, 1).astype(BF).astype(F32)
        dgate_ref[e, rows] = jnp.sum(result * g, axis=1, keepdims=True)
        eo_ref[e, rows] = (weight * result).astype(BF)
        d_expert = (weight * g).astype(BF)
        de_ref[e, rows] = d_expert
        d_active = dot(d_expert, w_down, 1, 0)
        da = (d_active * slope).astype(BF)
        db = (d_active * silu).astype(BF)
        da_ref[e, rows] = da
        db_ref[e, rows] = db
        dr_ref[e, rows] = (dot(da, w_gate, 1, 1) + dot(db, w_up, 1, 1)).astype(BF)
        return carry

    lax.fori_loop(0, local * (slots // chunk), work, 0)

    def give(i, carry, back_ref, offset, column):
        s = i + offset
        rows = pl.ds(pl.multiple_of(s * cap, 16), cap)
        pick = pick_ref[s]
        eo = jnp.concatenate([eo_ref[e, rows] for e in range(local)], axis=0)
        dr = jnp.concatenate([dr_ref[e, rows] for e in range(local)], axis=0)
        dgate = jnp.concatenate([dgate_ref[e, rows] for e in range(local)], axis=0)
        high, low = halves(dgate)
        spread = jnp.where(own_lane, high.astype(F32), 0.0) + jnp.where(
            slot_lane == first + row_expert + 64, low.astype(F32), 0.0
        )
        out_ref[2 * i + column, 0] = dot(pick, eo, 1, 0).astype(BF)
        back_ref[i, :, :width] = dot(pick, dr, 1, 0).astype(BF)
        back_ref[i, :, width:] = dot(pick, spread.astype(BF), 1, 0).astype(BF)
        return carry

    for back_ref, offset, column in ((back_own_ref, 0, core), (back_other_ref, half, 1 - core)):
        lax.fori_loop(
            0, half, functools.partial(give, back_ref=back_ref, offset=offset, column=column), 0
        )


def run_experts(scalars, x_own, x_other, g_all, micro, router, pieces, cap, moe=None):
    half, tok, width = x_own.shape
    sources = 2 * half
    local, hidden = len(pieces), pieces[0][0].shape[3]
    slots = sources * cap
    wide = g_all.shape[2]
    shape = jax.ShapeDtypeStruct
    outs = [
        shape((sources, 2, tok, width), BF),
        shape((half, tok, wide), BF),
        shape((half, tok, wide), BF),
        shape((local, slots, width), BF),
        shape((local, slots, width), BF),
        shape((local, slots, hidden), BF),
        shape((local, slots, hidden), BF),
        shape((local, slots, hidden), BF),
    ]
    g_spec = pl.BlockSpec(
        (sources, tok, wide), lambda i: (0, micro, 0), pipeline_mode=pl.Buffered(1)
    )
    args = [router, *pieces[0], *pieces[1]]
    held = [] if moe is None else [moe]
    moe_spec = pl.BlockSpec(
        (sources, 1, tok, width), lambda i: (0, micro, 0, 0), pipeline_mode=pl.Buffered(1)
    )
    return pl.pallas_call(
        functools.partial(expert_kernel, again=moe is not None),
        out_shape=outs,
        grid=(1,),
        in_specs=[pl.BlockSpec(memory_space=pltpu.SMEM), whole(x_own), whole(x_other), g_spec]
        + [whole(a) for a in args]
        + [pl.BlockSpec(memory_space=pl.ANY)] * len(held),
        out_specs=[moe_spec] + [whole(o) for o in outs[1:]],
        input_output_aliases={4 + len(args): 0} if held else {},
        scratch_shapes=[
            pltpu.VMEM((sources, tok, local * cap), BF),
            pltpu.VMEM((local, slots, 1), F32),
            pltpu.VMEM((local, slots, 1), F32),
            pltpu.VMEM((local, slots, width), BF),
            pltpu.VMEM((local, slots, width), BF),
            pltpu.VMEM((local, 3, width, hidden), BF),
        ],
        compiler_params=pltpu.CompilerParams(vmem_limit_bytes=60 * 1024 * 1024),
        cost_estimate=COST,
    )(scalars, x_own, x_other, g_all, *args, *held)


def expert_grad_kernel(order_ref, *refs):
    kept, outs, total_ref = refs[:10], refs[10:14], refs[14]
    left = (kept[0:2], kept[0:2], kept[2:4])
    right = (kept[6:8], kept[8:10], kept[4:6])
    step = pl.program_id(0)
    depth = outs[0].shape[2]
    for kind in range(3):

        @pl.when(step == kind)
        def _(kind=kind):
            total = dot(left[kind][0][0], right[kind][0][0], 0, 0)
            total_ref[...] = total + dot(left[kind][1][0], right[kind][1][0], 0, 0)

    for r in range(8):
        rows = pl.ds(pl.multiple_of(order_ref[r] * depth, depth), depth)
        outs[r // 2][r % 2, 0] = total_ref[rows].astype(BF)


def expert_grads(order, kept, expert):
    _, slots, width = kept[0][0].shape
    hidden = kept[0][2].shape[2]
    args = [kept[m][i] for i in range(5) for m in range(2)]
    depth = width // 8
    shape = jax.ShapeDtypeStruct
    return pl.pallas_call(
        expert_grad_kernel,
        out_shape=[shape((2, 3, depth, hidden), BF)] * 4,
        grid=(3,),
        in_specs=[pl.BlockSpec(memory_space=pltpu.SMEM)]
        + [pl.BlockSpec((1,) + a.shape[1:], lambda i: (expert, 0, 0)) for a in args],
        out_specs=[pl.BlockSpec((2, 1, depth, hidden), lambda i: (0, i, 0, 0))] * 4,
        scratch_shapes=[pltpu.VMEM((width, hidden), F32)],
        compiler_params=pltpu.CompilerParams(vmem_limit_bytes=48 * 1024 * 1024),
        cost_estimate=COST,
    )(order, *args)


CTX = ("z", "yl")
GROUP = ("yh", "x")
FSDP = ("yh", "x", "core")
ALL = CTX + FSDP
UP = [(i, (i + 1) % 4) for i in range(4)]
DOWN = [(i, (i - 1) % 4) for i in range(4)]
TWO = [(i, (i + 2) % 4) for i in range(4)]
FLIP = [(0, 1), (1, 0)]


def mm(a, b):
    return jnp.dot(a, b, preferred_element_type=F32)


def mm_t(a, b):
    return lax.dot_general(a, b, (((1,), (1,)), ((), ())), preferred_element_type=F32)


def t_mm(a, b):
    return lax.dot_general(a, b, (((0,), (0,)), ((), ())), preferred_element_type=F32)


def ein(spec, a, b):
    return jnp.einsum(spec, a, b, preferred_element_type=F32)


def swap(parts, axis):
    return lax.all_to_all(parts, axis, split_axis=0, concat_axis=0, tiled=True)


def flip(block, axis):
    return lax.ppermute(block, axis, FLIP)


def by_z(parts):
    return [lax.ppermute(parts[k], "z", perm) for k, perm in ((1, UP), (2, TWO), (3, DOWN))]


def along_z(both):
    before, far, after = by_z([both] * 4)
    return [both, after, far, before]


class Exchange:
    def __init__(self):
        self.last = None

    def __call__(self, parts, axis):
        if self.last is not None:
            parts = after_all(parts, self.last)
        self.last = swap(parts, axis)
        return self.last

    def copies(self, block, axis, count):
        return self(jnp.broadcast_to(block[None], (count,) + block.shape), axis)


def add(a, b):
    return (a.astype(F32) + b.astype(F32)).astype(BF)


def add_part(parts, i, more):
    pieces = [parts[:1], parts[1:]]
    pieces[i] = add(pieces[i], more)
    return jnp.concatenate(pieces, axis=0)


def relay(far):
    return [lax.ppermute(far[:1], "z", UP), lax.ppermute(far[1:], "z", DOWN)]


def ring_sums(parts, far):
    return [
        lax.ppermute(add_part(parts[1], 0, far[0]), "z", UP),
        lax.ppermute(add_part(parts[3], 1, far[1]), "z", DOWN),
    ]


def pair_sums(parts, moved):
    return [sum(part[i].astype(F32) for part in [parts[0]] + moved) for i in range(2)]


def sum_parts(parts):
    return jnp.sum(parts.astype(F32), axis=0)


def after_all(value, *others):
    return lax.optimization_barrier((value,) + others)[0]


def rope_tables(positions):
    half = DH // 2
    inverse = THETA ** (-(jnp.arange(half, dtype=F32) * 2.0) / DH)
    angles = positions.astype(F32)[:, None] * inverse[None, :]
    return (jnp.cos(angles), jnp.sin(angles))


def rms_scale(values, gain):
    return values * lax.rsqrt(jnp.mean(values * values, axis=-1, keepdims=True) + EPS) * gain


def body(
    tokens,
    segments,
    routes,
    w_query,
    w_key,
    w_value,
    w_out,
    w_router,
    attn_gain,
    mlp_gain,
    qk_gain,
    w_gate,
    w_up,
    w_down,
    cotangent,
):
    micro = tokens.shape[0]
    tok = tokens.shape[2]
    width = tokens.shape[3]
    length = segments.shape[2]
    rows = w_query.shape[0]
    n_ctx, n_fsdp = 8, 16
    n_all = n_ctx * n_fsdp
    z, yl, yh, x, core = (lax.axis_index(name) for name in ALL)
    shard = (yh * 4 + x) * 2 + core
    local = w_gate.shape[0]
    experts = local * n_fsdp
    cap = (3 * tok * TOPK + 2 * experts - 1) // (2 * experts)
    all_tok = micro * tok
    ratio = H // KV
    heads = ratio * DH
    span = heads + 2 * DH

    exchange = Exchange()
    small = jnp.concatenate(
        [
            w_router,
            attn_gain[:, None],
            mlp_gain[:, None],
            jnp.pad(qk_gain[:, None], ((0, rows - 1), (0, 0))),
        ],
        axis=1,
    )
    small = jnp.pad(small, ((0, 0), (0, 128 - small.shape[1])))
    pieces = jnp.concatenate(
        [
            w_query.reshape(rows, n_ctx, heads),
            w_key.reshape(rows, n_ctx, DH),
            w_value.reshape(rows, n_ctx, DH),
            jnp.broadcast_to(small[:, None], (rows, n_ctx, 128)),
        ],
        axis=2,
    ).transpose(1, 0, 2)
    pieces = jnp.broadcast_to(pieces[:, None], (n_ctx, n_fsdp) + pieces.shape[1:])
    both_0, both_1 = (
        jnp.concatenate([tokens[m], flip(tokens[m], "yl")], axis=0) for m in range(micro)
    )
    both_w = jnp.stack([w_gate, w_up, w_down], axis=1)
    head_all = exchange(pieces.reshape((n_all,) + pieces.shape[2:]), ALL).reshape(width, -1)
    other_w = flip(both_w, "yl")
    both_w = [jnp.stack([both_w[e], other_w[e]]) for e in range(local)]
    seq_rows = [along_z(both_0)]
    seq_rows.append(along_z(after_all(both_1, *seq_rows[0][1:])))
    head_all = after_all(head_all, *seq_rows[0][1:], other_w)
    w_heads = head_all[:, :span]
    small_all = head_all[:, span:]
    router = small_all[:, :experts]
    small_wide = small_all.astype(F32)
    gain_attn = small_wide[:, experts]
    gain_mlp = small_wide[:, experts + 1]
    gain_heads = small_wide[:, experts + 2].reshape(-1, rows)[:, 0]
    gain_row = gain_attn[None]
    head_row = jnp.concatenate(
        [gain_heads[:DH]] * ratio + [gain_heads[DH:], jnp.ones((DH,), F32)]
    )[None]
    router_pad = jnp.pad(router, ((0, 0), (0, 128 - experts)))

    out_own = exchange.copies(w_out, CTX + GROUP, n_all // 2)

    moved_w = []
    last = seq_rows[1][1:]
    for e in range(local):
        block = after_all(both_w[e], *last)
        last = [lax.ppermute(block, "z", UP), lax.ppermute(block, "z", DOWN)]
        moved_w.append(last)

    expert_ids = jnp.arange(experts, dtype=jnp.int32)
    cot = cotangent.reshape(all_tok, width)
    chosen = jnp.any(routes.reshape(all_tok, TOPK)[:, :, None] == expert_ids, axis=1)
    before = jnp.arange(tok, dtype=jnp.int32)
    lower = (before[:, None] >= before[None, :]).astype(BF)
    counts = ein("ut,mte->mue", lower, chosen.reshape(micro, tok, experts).astype(BF))
    held = jnp.where(chosen, counts.reshape(all_tok, experts) - 1.0, -1.0)
    held = jnp.pad(held, ((0, 0), (0, 128 - experts)), constant_values=-1.0).astype(BF)
    pack = after_all(jnp.concatenate([cot, held], axis=1), both_0, both_1)
    g_all = lax.all_gather(pack, FSDP, axis=0)

    cosine, sine = rope_tables(jnp.arange(length, dtype=jnp.int32))
    cosine = jnp.tile(cosine, (1, 4))
    sine = jnp.tile(jnp.concatenate([-sine, sine], axis=1), (1, 2))
    rel = jnp.arange(n_ctx, dtype=jnp.int32)
    order = ((z + rel // 2) % 4) * 2 + (yl + rel % 2) % 2
    scalars = jnp.concatenate([jnp.stack([shard * local, core]), order]).astype(jnp.int32)

    def to_owner(v):
        return exchange(v.reshape(n_ctx, tok, -1), CTX)

    def attention_args(m):
        seg = segments[m, 0]
        return gain_row, w_heads, head_row, cosine, sine, seg[:, None], seg[None, :]

    mixed_0, *saved_0 = attend_forward(order, seq_rows[0], *attention_args(0))
    seq_rows[1], mixed_0 = lax.optimization_barrier((seq_rows[1], mixed_0))
    mixed_1, *saved_1 = attend_forward(order, seq_rows[1], *attention_args(1))
    mixed_1, moved_w[0] = lax.optimization_barrier((mixed_1, moved_w[0]))
    saved = [saved_0, saved_1]
    out_own, mixed_0, mixed_1 = lax.optimization_barrier((out_own, mixed_0, mixed_1))
    out_other = flip(out_own, "core")
    mixed = jnp.stack([mixed_0, mixed_1]).reshape(micro, n_ctx, tok, heads).transpose(1, 0, 2, 3)
    mixed = exchange(mixed.reshape(n_ctx, all_tok, heads), CTX)
    mixed, moved_w[1] = lax.optimization_barrier((mixed, moved_w[1]))
    mixed = mixed.transpose(1, 0, 2).reshape(all_tok, width)
    out_full = jnp.where(
        core == 0,
        jnp.stack([out_own, out_other], axis=1),
        jnp.stack([out_other, out_own], axis=1),
    ).reshape(width, width)
    middle = tokens.reshape(all_tok, width).astype(F32) + mm(mixed, out_full)
    inv_two = lax.rsqrt(jnp.mean(middle * middle, axis=-1, keepdims=True) + EPS)
    hidden_two = (middle * inv_two * gain_mlp).astype(BF)
    x_0 = exchange.copies(hidden_two[:tok], GROUP, n_ctx)
    weights = []
    for e, (w_before, w_after) in enumerate(moved_w):
        w_far = [lax.ppermute(w_before[:1], "z", UP), lax.ppermute(w_after[1:], "z", DOWN)]
        weights.append([both_w[e], w_after, *w_far, w_before])
    x_0, weights = lax.optimization_barrier((x_0, weights))
    x_1 = exchange.copies(hidden_two[tok:], GROUP, n_ctx)
    logits = jnp.where(chosen, mm(hidden_two, router), -1e30)
    gates_all = jnp.where(chosen, jax.nn.softmax(logits, axis=-1), 0.0)

    def experts_of(m, x_own, *moe):
        return run_experts(
            scalars,
            x_own,
            flip(x_own, "core"),
            g_all,
            m,
            router_pad,
            weights,
            cap,
            *moe,
        )

    def back_sum(own, other):
        return add(own, flip(other, "core"))

    def middle_back(back):
        tail = back[:, width:]
        d_gates = tail[:, :experts] + tail[:, 64 : 64 + experts]
        d_select = gates_all * (d_gates - jnp.sum(gates_all * d_gates, axis=-1, keepdims=True))
        d_logits = d_select.astype(BF)
        d_two = back[:, :width] + mm_t(d_logits, router)
        u = d_two * gain_mlp
        d_middle = (
            cot.astype(F32)
            + inv_two * u
            - middle * (inv_two**3 * jnp.mean(u * middle, axis=-1, keepdims=True))
        )
        d_branch = d_middle.astype(BF)
        d_mixed = mm_t(d_branch, out_full).astype(BF)
        d_mixed = d_mixed.reshape(all_tok, n_ctx, heads).transpose(1, 0, 2)
        return d_middle, d_mixed, (d_branch, d_logits, d_two)

    def weight_grads(d_branch, d_logits, d_two):
        grad_mlp = jnp.sum(d_two * middle * inv_two, axis=0)
        return t_mm(mixed, d_branch), t_mm(hidden_two, d_logits), grad_mlp

    def pack_grads(grad_heads, grad_router, grad_attn, grad_mlp, grad_qk):
        grad_qk = jnp.pad(grad_qk[:, None], ((0, 0), (0, rows - 1))).reshape(-1)
        grad_small = jnp.concatenate(
            [grad_router, grad_attn[:, None], grad_mlp[:, None], grad_qk[:, None]], axis=1
        )
        grad_small = jnp.pad(grad_small, ((0, 0), (0, 128 - grad_small.shape[1])))
        grad_pack = jnp.concatenate([grad_heads, grad_small], axis=1).astype(BF)
        return grad_pack.reshape(n_all, rows, -1)

    def attention_back(m, d_mixed):
        *d_hidden, grad_heads, grad_attn, grad_qk = attend_backward(
            order, *saved[m], d_mixed.reshape(length, heads), *attention_args(m)
        )
        grad_qk = jnp.concatenate(
            [grad_qk[0, :DH] + grad_qk[0, DH : 2 * DH], grad_qk[0, 2 * DH : 3 * DH]]
        )
        return d_hidden, (grad_heads, grad_attn[0], grad_qk)

    moe, back_own, back_other, *kept_0 = experts_of(0, x_0)
    x_1, back_own, back_other = lax.optimization_barrier((x_1, back_own, back_other))
    back_0 = back_sum(back_own, back_other)
    x_1 = after_all(x_1, back_0)
    back_0 = exchange(back_0, GROUP)
    moe, back_own, back_other, *kept_1 = experts_of(1, x_1, moe)
    back_0, back_own, back_other, moe = lax.optimization_barrier(
        (back_0, back_own, back_other, moe)
    )
    moe = lax.psum_scatter(moe, FSDP, scatter_dimension=0, tiled=True)[0]
    back_1 = back_sum(back_own, back_other)
    kept_1[0], back_1 = lax.optimization_barrier((kept_1[0], back_1))
    back_1 = exchange(back_1, GROUP)
    parts = [expert_grads(order, (kept_0, kept_1), e) for e in range(local)]
    far = [relay(part[2]) for part in parts]
    back_1, parts = lax.optimization_barrier((back_1, parts))
    d_middle, d_mixed, d_rows = middle_back(
        jnp.concatenate([sum_parts(back_0), sum_parts(back_1)], axis=0)
    )
    d_mixed, far = lax.optimization_barrier((d_mixed, far))
    d_mixed = exchange(d_mixed, CTX)
    moved = [ring_sums(parts[0], far[0])]
    grad_out, grad_router, grad_mlp = weight_grads(*d_rows)
    grad_out = grad_out.astype(BF).reshape(n_all // 2, 2, rows, width)
    grad_own = lax.dynamic_index_in_dim(grad_out, core, axis=1, keepdims=False)
    grad_other = lax.dynamic_index_in_dim(grad_out, 1 - core, axis=1, keepdims=False)
    grad_out = back_sum(grad_own, grad_other)
    d_mixed, moved[0], grad_out, grad_router, grad_mlp = lax.optimization_barrier(
        (d_mixed, moved[0], grad_out, grad_router, grad_mlp)
    )
    grad_out = exchange(grad_out, CTX + GROUP)
    moved.append(ring_sums(parts[1], far[1]))
    d_mixed = d_mixed.reshape(n_ctx, micro, tok, heads)
    d_hidden_0, head_grads_0 = attention_back(0, d_mixed[:, 0])
    d_hidden_0, d_mixed, moved[1] = lax.optimization_barrier((d_hidden_0, d_mixed, moved[1]))
    hidden_moved_0 = by_z(d_hidden_0)
    d_hidden_1, head_grads_1 = attention_back(1, d_mixed[:, 1])
    d_hidden_1, hidden_moved_0, grad_out = lax.optimization_barrier(
        (d_hidden_1, hidden_moved_0, grad_out)
    )
    hidden_moved_1 = by_z(d_hidden_1)
    grad_heads, grad_attn, grad_qk = jax.tree.map(jnp.add, head_grads_0, head_grads_1)
    grad_pack = pack_grads(grad_heads, grad_router, grad_attn, grad_mlp, grad_qk)
    grad_pack = exchange(grad_pack, ALL)
    hidden_moved_1, parts, moved = lax.optimization_barrier((hidden_moved_1, parts, moved))
    weight_sums = [pair_sums(p, q) for p, q in zip(parts, moved)]
    weight_yl = [flip(sums[1].astype(BF), "yl") for sums in weight_sums]
    hidden_sums = [
        jnp.stack(sums)
        for sums in zip(
            pair_sums(d_hidden_0, hidden_moved_0), pair_sums(d_hidden_1, hidden_moved_1)
        )
    ]
    hidden_yl = flip(hidden_sums[1].astype(BF), "yl")

    grad_pack = grad_pack.astype(F32)
    own_heads = jnp.sum(grad_pack[:, :, :span].reshape(n_ctx, n_fsdp, rows, -1), axis=1)
    own_heads = own_heads.transpose(1, 0, 2)
    own_small = jnp.sum(grad_pack[:, :, span:], axis=0)
    own_out = sum_parts(grad_out)
    moe = after_all(moe, grad_pack)
    d_hidden = (hidden_sums[0] + hidden_yl.astype(F32)).reshape(all_tok, width)
    expert_own = [sums[0] + other.astype(F32) for sums, other in zip(weight_sums, weight_yl)]
    out = (middle.reshape(moe.shape) + moe.astype(F32)).astype(BF)
    start = tokens.reshape(all_tok, width).astype(F32)
    inv_one = lax.rsqrt(jnp.mean(start * start, axis=-1, keepdims=True) + EPS)
    u = d_hidden * gain_attn
    d_input = (
        d_middle
        + inv_one * u
        - start * (inv_one**3 * jnp.mean(u * start, axis=-1, keepdims=True))
    )

    return (
        out[:, None],
        d_input.reshape(tokens.shape),
        own_heads[:, :, :heads].reshape(rows, -1),
        own_heads[:, :, heads : heads + DH].reshape(rows, -1),
        own_heads[:, :, heads + DH :].reshape(rows, -1),
        own_out,
        own_small[:, :experts],
        own_small[:, experts],
        own_small[:, experts + 1],
        own_small[:1, experts + 2],
        jnp.stack([part[0] for part in expert_own]),
        jnp.stack([part[1] for part in expert_own]),
        jnp.stack([part[2] for part in expert_own]),
    )


def solution(mesh):
    mesh = Mesh(mesh.devices.reshape(4, 2, 2, 4, 2), ALL)
    weight = P(ALL, None)
    gain = P(ALL)
    rows = P(None, FSDP, CTX, None)
    expert = P(FSDP, CTX, None)
    return jax.shard_map(
        body,
        mesh=mesh,
        in_specs=(rows, P(None, FSDP, None), rows)
        + (weight,) * 5
        + (gain,) * 3
        + (expert,) * 3
        + (rows,),
        out_specs=(rows, rows) + (weight,) * 5 + (gain,) * 3 + (expert,) * 3,
        check_vma=False,
    )
```

```python
import functools

import jax
import jax.numpy as jnp
from jax import lax
from jax.experimental import pallas as pl
from jax.experimental.pallas import tpu as pltpu
from jax.sharding import Mesh
from jax.sharding import PartitionSpec as P

BF = jnp.bfloat16
F32 = jnp.float32
H = 16
KV = 8
DH = 64
TOPK = 8
WINDOW = 1024
EPS = 1e-06
THETA = 10000.0
COST = pl.CostEstimate(flops=10**7, bytes_accessed=10**5, transcendentals=0)


def dot(a, b, ca, cb):
    return lax.dot_general(a, b, (((ca,), (cb,)), ((), ())), preferred_element_type=F32)


def lanes_of(v):
    return lax.broadcasted_iota(jnp.int32, v.shape, v.ndim - 1)


def head_sums(v):
    low = lanes_of(v) < DH
    first = jnp.sum(jnp.where(low, v, 0.0), axis=1, keepdims=True)
    second = jnp.sum(jnp.where(low, 0.0, v), axis=1, keepdims=True)
    return jnp.where(low, first, second)


def trade(v):
    return jnp.where(
        lanes_of(v) % DH < DH // 2, pltpu.roll(v, 128 - DH // 2, 1), pltpu.roll(v, DH // 2, 1)
    )


def both_halves(v, second):
    low = lanes_of(v) < DH
    other = pltpu.roll(v, DH, 1)
    return jnp.where(low, other, v) if second else jnp.where(low, v, other)


def stack_heads(v):
    low = lanes_of(v) < DH
    zero = jnp.zeros_like(v)
    return jnp.concatenate([jnp.where(low, v, zero), jnp.where(low, zero, v)], axis=0)


def key_span(start, block, length):
    reach = WINDOW // 2 - 1
    low = max(0, start - reach) // 128 * 128
    high = min(length, -(-(start + block + reach) // 128) * 128)
    return low, high


def masked_probs(q_two, keys, seg_col, seg_row, start, low):
    block = q_two.shape[0] // 2
    scores = dot(q_two, keys, 1, 1)
    shape = (block, keys.shape[0])
    gap = (
        lax.broadcasted_iota(jnp.int32, shape, 0)
        - lax.broadcasted_iota(jnp.int32, shape, 1)
        + (start - low)
    )
    allowed = (seg_col == seg_row) & (jnp.abs(gap) < WINDOW // 2)
    bias = jnp.where(allowed, 0.0, -1e30)
    scores = scores + jnp.concatenate([bias, bias], axis=0)
    raised = jnp.exp(scores - jnp.max(scores, axis=1, keepdims=True))
    return raised * (1.0 / jnp.sum(raised, axis=1, keepdims=True))


def attend_kernel(
    order_ref,
    *refs,
):
    pieces, refs = refs[:-13], refs[-13:]
    gain_ref, w_ref, head_gain_ref, cos_ref, sin_ref, seg_col_ref, seg_row_ref = refs[:7]
    mixed_ref, hidden_ref, q_ref, kv_ref, keys_ref, values_ref = refs[7:]
    tok, width = pieces[0].shape[1:]
    length = hidden_ref.shape[0]
    pieces = [(ref, i) for ref in pieces for i in range(ref.shape[0])]
    for r, (ref, i) in enumerate(pieces):
        x = ref[i].astype(F32)
        x = x * lax.rsqrt(jnp.mean(x * x, axis=1, keepdims=True) + EPS) * gain_ref[...]
        rows = pl.ds(pl.multiple_of(order_ref[r] * tok, tok), tok)
        hidden_ref[rows] = x.astype(BF)
    raw = dot(hidden_ref[...], w_ref[...], 1, 0)
    for half in range(2):
        u = raw[:, half * 128 : half * 128 + 128]
        gain = head_gain_ref[:, half * 128 : half * 128 + 128]
        n = u * lax.rsqrt(head_sums(u * u) * (1.0 / DH) + EPS) * gain
        turned = n * cos_ref[...] + trade(n) * sin_ref[...]
        if half == 0:
            q_ref[...] = turned.astype(BF)
        else:
            kv = jnp.where(lanes_of(u) < DH, turned, u)
            kv_ref[...] = kv.astype(BF)
            keys_ref[...] = both_halves(kv, False).astype(BF)
            values_ref[...] = both_halves(kv, True).astype(BF)
    block = 256
    for start in range(0, length, block):
        low, high = key_span(start, block, length)
        q_two = stack_heads(q_ref[start : start + block].astype(F32) * DH**-0.5).astype(BF)
        probs = masked_probs(
            q_two,
            keys_ref[low:high],
            seg_col_ref[start : start + block],
            seg_row_ref[:, low:high],
            start,
            low,
        )
        result = dot(probs.astype(BF), values_ref[low:high], 1, 0)
        first = lanes_of(result[:block]) < DH
        mixed_ref[start : start + block] = jnp.where(first, result[:block], result[block:]).astype(
            BF
        )


def attend_back_kernel(
    order_ref,
    hidden_ref,
    q_ref,
    kv_ref,
    d_mixed_ref,
    gain_ref,
    w_ref,
    head_gain_ref,
    cos_ref,
    sin_ref,
    seg_col_ref,
    seg_row_ref,
    d_hidden_0_ref,
    d_hidden_1_ref,
    d_hidden_2_ref,
    d_hidden_3_ref,
    grad_w_ref,
    grad_gain_ref,
    grad_heads_ref,
    keys_ref,
    values_ref,
    d_q_ref,
    d_k_ref,
    d_v_ref,
    d_raw_ref,
):
    length = hidden_ref.shape[0]
    kv = kv_ref[...].astype(F32)
    keys_ref[...] = both_halves(kv, False).astype(BF)
    values_ref[...] = both_halves(kv, True).astype(BF)
    d_k_ref[...] = jnp.zeros_like(d_k_ref)
    d_v_ref[...] = jnp.zeros_like(d_v_ref)
    block = 256
    for start in range(0, length, block):
        low, high = key_span(start, block, length)
        q_two = stack_heads(q_ref[start : start + block].astype(F32) * DH**-0.5).astype(BF)
        m_two = stack_heads(d_mixed_ref[start : start + block].astype(F32)).astype(BF)
        probs = masked_probs(
            q_two,
            keys_ref[low:high],
            seg_col_ref[start : start + block],
            seg_row_ref[:, low:high],
            start,
            low,
        )
        d_probs = dot(m_two, values_ref[low:high], 1, 1)
        inner = jnp.sum(probs * d_probs, axis=1, keepdims=True)
        d_scores = (probs * (d_probs - inner)).astype(BF)
        result = dot(d_scores, keys_ref[low:high], 1, 0)
        first = lanes_of(result[:block]) < DH
        d_q_ref[start : start + block] = jnp.where(first, result[:block], result[block:]) * (
            DH**-0.5
        )
        d_k_ref[low:high] += dot(d_scores, q_two, 0, 0)
        d_v_ref[low:high] += dot(probs.astype(BF), m_two, 0, 0)
    raw = dot(hidden_ref[...], w_ref[...], 1, 0)
    d_k = d_k_ref[...]
    d_k = d_k + pltpu.roll(d_k, DH, 1)
    d_v = d_v_ref[...]
    d_v = d_v + pltpu.roll(d_v, DH, 1)
    for half in range(2):
        lanes = slice(half * 128, half * 128 + 128)
        u = raw[:, lanes]
        gain = head_gain_ref[:, lanes]
        d = d_q_ref[...] if half == 0 else d_k
        d = d * cos_ref[...] + trade(d * sin_ref[...])
        r = lax.rsqrt(head_sums(u * u) * (1.0 / DH) + EPS)
        grad_heads_ref[:, lanes] = jnp.sum(d * u * r, axis=0, keepdims=True)
        d = d * gain
        d = d * r - u * (r * r * r * (head_sums(d * u) * (1.0 / DH)))
        if half == 1:
            d = jnp.where(lanes_of(d) < DH, d, d_v)
        d_raw_ref[:, lanes] = d.astype(BF)
    grad_w_ref[...] = dot(hidden_ref[...], d_raw_ref[...], 0, 0)
    total = jnp.zeros(grad_gain_ref.shape, F32)
    outs = (d_hidden_0_ref, d_hidden_1_ref, d_hidden_2_ref, d_hidden_3_ref)
    tok = length // 8
    for step in range(4):
        rows = pl.ds(pl.multiple_of(order_ref[2 * step] // 2 * (2 * tok), 2 * tok), 2 * tok)
        d_hidden = dot(d_raw_ref[rows], w_ref[...], 1, 1)
        own = order_ref[0] % 2
        outs[step][own] = d_hidden[:tok].astype(BF)
        outs[step][1 - own] = d_hidden[tok:].astype(BF)
        total = total + jnp.sum(d_hidden * hidden_ref[rows].astype(F32), axis=0, keepdims=True)
    grad_gain_ref[...] = total / gain_ref[...]


def whole(a):
    return pl.BlockSpec(a.shape, lambda i: (0,) * len(a.shape), pipeline_mode=pl.Buffered(1))


def attend_forward(order, pieces, gain, w_heads, head_gain, cosine, sine, seg_col, seg_row):
    length = cosine.shape[0]
    width = w_heads.shape[0]
    shape = jax.ShapeDtypeStruct
    outs = [
        shape((length, 128), BF),
        shape((length, width), BF),
        shape((length, 128), BF),
        shape((length, 128), BF),
    ]
    args = list(pieces) + [gain, w_heads, head_gain, cosine, sine, seg_col, seg_row]
    return pl.pallas_call(
        attend_kernel,
        out_shape=outs,
        grid=(1,),
        in_specs=[pl.BlockSpec(memory_space=pltpu.SMEM)] + [whole(a) for a in args],
        out_specs=[whole(o) for o in outs],
        scratch_shapes=[pltpu.VMEM((length, 128), BF), pltpu.VMEM((length, 128), BF)],
        compiler_params=pltpu.CompilerParams(vmem_limit_bytes=40 * 1024 * 1024),
        cost_estimate=COST,
    )(order, *args)


def attend_backward(
    order, hidden, q, kv, d_mixed, gain, w_heads, head_gain, cosine, sine, seg_col, seg_row
):
    length, width = hidden.shape
    shape = jax.ShapeDtypeStruct
    outs = [shape((2, length // 8, width), BF)] * 4 + [
        shape((width, 256), F32),
        shape((1, width), F32),
        shape((1, 256), F32),
    ]
    args = [hidden, q, kv, d_mixed, gain, w_heads, head_gain, cosine, sine, seg_col, seg_row]
    return pl.pallas_call(
        attend_back_kernel,
        out_shape=outs,
        grid=(1,),
        in_specs=[pl.BlockSpec(memory_space=pltpu.SMEM)] + [whole(a) for a in args],
        out_specs=[whole(o) for o in outs],
        scratch_shapes=[pltpu.VMEM((length, 128), BF)] * 2
        + [pltpu.VMEM((length, 128), F32)] * 3
        + [pltpu.VMEM((length, 256), BF)],
        compiler_params=pltpu.CompilerParams(vmem_limit_bytes=40 * 1024 * 1024),
        cost_estimate=COST,
    )(order, *args)


def halves(v):
    high = v.astype(BF)
    return high, (v - high.astype(F32)).astype(BF)


def expert_kernel(scalar_ref, *refs, again):
    x_own_ref, x_other_ref, g_ref, router_ref = refs[:4]
    pieces, refs = (refs[4:9], refs[9:14]), refs[14:]
    if again:
        refs = refs[1:]
    out_ref, back_own_ref, back_other_ref = refs[:3]
    kept_refs, refs = refs[3:8], refs[8:]
    xe_ref, de_ref, act_ref, da_ref, db_ref, *refs = refs
    pick_ref, weight_ref, dgate_ref, eo_ref, dr_ref, w_ref, in_sem, out_sem = refs
    half, tok, width = x_own_ref.shape
    sources = 2 * half
    core = scalar_ref[1]
    depth = w_ref.shape[2] // 8

    loads = []
    for e in range(2):
        blocks = [(ref, i) for ref in pieces[e] for i in range(ref.shape[0])]
        for r, (ref, i) in enumerate(blocks):
            rows = pl.ds(pl.multiple_of(scalar_ref[2 + r] * depth, depth), depth)
            loads.append(
                pltpu.make_async_copy(ref.at[i], w_ref.at[e, :, rows], in_sem.at[8 * e + r])
            )
            loads[-1].start()
    local, slots, hidden = act_ref.shape
    cap = slots // sources
    first = scalar_ref[0]
    lane = lax.broadcasted_iota(jnp.int32, (tok, 128), 1)
    spot = lax.broadcasted_iota(jnp.int32, (tok, local * cap), 1)
    row_expert = lax.broadcasted_iota(jnp.int32, (local * cap, 128), 0) // cap
    slot_lane = lax.broadcasted_iota(jnp.int32, (local * cap, 128), 1)
    own_lane = slot_lane == first + row_expert

    def fetch(i, carry, x_ref, offset, column):
        s = i + offset
        x = x_ref[i]
        from_g = 2 * i + column
        held = g_ref[from_g, :, width:].astype(F32)
        chosen = held >= 0.0
        logits = jnp.where(chosen, dot(x, router_ref[...], 1, 0), -1e30)
        top = jnp.max(logits, axis=1, keepdims=True)
        raised = jnp.where(chosen, jnp.exp(logits - top), 0.0)
        gates = raised / jnp.sum(raised, axis=1, keepdims=True)
        pick = jnp.zeros((tok, local * cap), F32)
        for e in range(local):
            mine = jnp.max(jnp.where(lane == first + e, held, -1.0), axis=1, keepdims=True)
            goal = jnp.where(mine >= 0.0, mine + e * cap, -1.0).astype(jnp.int32)
            pick = jnp.where(spot == goal, 1.0, pick)
        pick = pick.astype(BF)
        pick_ref[s] = pick
        rows = pl.ds(pl.multiple_of(s * cap, 16), cap)
        x_slots = dot(pick, x, 0, 0).astype(BF)
        g_slots = dot(pick, g_ref[from_g, :, :width], 0, 0).astype(BF)
        high, low = halves(gates)
        weight = dot(pick, high, 0, 0) + dot(pick, low, 0, 0)
        weight = jnp.sum(jnp.where(own_lane, weight, 0.0), axis=1, keepdims=True)
        for e in range(local):
            part = slice(e * cap, (e + 1) * cap)
            xe_ref[e, rows] = x_slots[part]
            de_ref[e, rows] = g_slots[part]
            weight_ref[e, rows] = weight[part]
        return carry

    for x_ref, offset, column in ((x_own_ref, 0, core), (x_other_ref, half, 1 - core)):
        step = functools.partial(fetch, x_ref=x_ref, offset=offset, column=column)
        lax.fori_loop(0, half, step, 0, unroll=4)
    for load in loads:
        load.wait()
    chunk = 384

    def work(i, carry):
        e = i // (slots // chunk)
        rows = pl.ds(pl.multiple_of((i % (slots // chunk)) * chunk, chunk), chunk)
        w_gate = w_ref[e, 0]
        w_up = w_ref[e, 1]
        w_down = w_ref[e, 2]
        x = xe_ref[e, rows]
        a = dot(x, w_gate, 1, 0)
        b = dot(x, w_up, 1, 0)
        sig = 1.0 / (1.0 + jnp.exp(-a))
        silu = a * sig
        active = (silu * b).astype(BF)
        act_ref[e, rows] = active
        slope = b * (sig * (1.0 + a * (1.0 - sig)))
        weight = weight_ref[e, rows]
        g = de_ref[e, rows].astype(F32)
        result = dot(active, w_down, 1, 1).astype(BF).astype(F32)
        dgate_ref[e, rows] = jnp.sum(result * g, axis=1, keepdims=True)
        eo_ref[e, rows] = (weight * result).astype(BF)
        d_expert = (weight * g).astype(BF)
        de_ref[e, rows] = d_expert
        d_active = dot(d_expert, w_down, 1, 0)
        da = (d_active * slope).astype(BF)
        db = (d_active * silu).astype(BF)
        da_ref[e, rows] = da
        db_ref[e, rows] = db
        dr_ref[e, rows] = (dot(da, w_gate, 1, 1) + dot(db, w_up, 1, 1)).astype(BF)
        return carry

    lax.fori_loop(0, local * (slots // chunk), work, 0)
    stores = [
        pltpu.make_async_copy(ref, kept, out_sem.at[n])
        for n, (ref, kept) in enumerate(
            zip((xe_ref, de_ref, act_ref, da_ref, db_ref), kept_refs)
        )
    ]
    for store in stores:
        store.start()

    def give(i, carry, back_ref, offset, column):
        s = i + offset
        rows = pl.ds(pl.multiple_of(s * cap, 16), cap)
        pick = pick_ref[s]
        eo = jnp.concatenate([eo_ref[e, rows] for e in range(local)], axis=0)
        dr = jnp.concatenate([dr_ref[e, rows] for e in range(local)], axis=0)
        dgate = jnp.concatenate([dgate_ref[e, rows] for e in range(local)], axis=0)
        high, low = halves(dgate)
        spread = jnp.where(own_lane, high.astype(F32), 0.0) + jnp.where(
            slot_lane == first + row_expert + 64, low.astype(F32), 0.0
        )
        out_ref[2 * i + column, 0] = dot(pick, eo, 1, 0).astype(BF)
        back_ref[i, :, :width] = dot(pick, dr, 1, 0).astype(BF)
        back_ref[i, :, width:] = dot(pick, spread.astype(BF), 1, 0).astype(BF)
        return carry

    for back_ref, offset, column in ((back_own_ref, 0, core), (back_other_ref, half, 1 - core)):
        step = functools.partial(give, back_ref=back_ref, offset=offset, column=column)
        lax.fori_loop(0, half, step, 0, unroll=4)
    for store in stores:
        store.wait()


def run_experts(scalars, x_own, x_other, g_all, micro, router, pieces, cap, moe=None):
    half, tok, width = x_own.shape
    sources = 2 * half
    local, hidden = len(pieces), pieces[0][0].shape[3]
    slots = sources * cap
    wide = g_all.shape[2]
    shape = jax.ShapeDtypeStruct
    outs = [
        shape((sources, 2, tok, width), BF),
        shape((half, tok, wide), BF),
        shape((half, tok, wide), BF),
        shape((local, slots, width), BF),
        shape((local, slots, width), BF),
        shape((local, slots, hidden), BF),
        shape((local, slots, hidden), BF),
        shape((local, slots, hidden), BF),
    ]
    g_spec = pl.BlockSpec(
        (sources, tok, wide), lambda i: (0, micro, 0), pipeline_mode=pl.Buffered(1)
    )
    args = [*pieces[0], *pieces[1]]
    any_place = pl.BlockSpec(memory_space=pl.ANY)
    held = [] if moe is None else [moe]
    moe_spec = pl.BlockSpec(
        (sources, 1, tok, width), lambda i: (0, micro, 0, 0), pipeline_mode=pl.Buffered(1)
    )
    return pl.pallas_call(
        functools.partial(expert_kernel, again=moe is not None),
        out_shape=outs,
        grid=(1,),
        in_specs=[pl.BlockSpec(memory_space=pltpu.SMEM), whole(x_own), whole(x_other), g_spec]
        + [whole(router)]
        + [any_place] * (len(args) + len(held)),
        out_specs=[moe_spec] + [whole(o) for o in outs[1:3]] + [any_place] * 5,
        input_output_aliases={5 + len(args): 0} if held else {},
        scratch_shapes=[pltpu.VMEM(o.shape, o.dtype) for o in outs[3:]]
        + [
            pltpu.VMEM((sources, tok, local * cap), BF),
            pltpu.VMEM((local, slots, 1), F32),
            pltpu.VMEM((local, slots, 1), F32),
            pltpu.VMEM((local, slots, width), BF),
            pltpu.VMEM((local, slots, width), BF),
            pltpu.VMEM((local, 3, width, hidden), BF),
            pltpu.SemaphoreType.DMA((16,)),
            pltpu.SemaphoreType.DMA((5,)),
        ],
        compiler_params=pltpu.CompilerParams(vmem_limit_bytes=60 * 1024 * 1024),
        cost_estimate=COST,
    )(scalars, x_own, x_other, g_all, router, *args, *held)


def expert_grad_kernel(order_ref, *refs):
    kept, outs, total_ref = refs[:10], refs[10:14], refs[14]
    left = (kept[0:2], kept[0:2], kept[2:4])
    right = (kept[6:8], kept[8:10], kept[4:6])
    step = pl.program_id(0)
    depth = outs[0].shape[2]
    for kind in range(3):

        @pl.when(step == kind)
        def _(kind=kind):
            total = dot(left[kind][0][0], right[kind][0][0], 0, 0)
            total_ref[...] = total + dot(left[kind][1][0], right[kind][1][0], 0, 0)

    for r in range(8):
        rows = pl.ds(pl.multiple_of(order_ref[r] * depth, depth), depth)
        outs[r // 2][r % 2, 0] = total_ref[rows].astype(BF)


def expert_grads(order, kept, expert):
    _, slots, width = kept[0][0].shape
    hidden = kept[0][2].shape[2]
    args = [kept[m][i] for i in range(5) for m in range(2)]
    depth = width // 8
    shape = jax.ShapeDtypeStruct
    return pl.pallas_call(
        expert_grad_kernel,
        out_shape=[shape((2, 3, depth, hidden), BF)] * 4,
        grid=(3,),
        in_specs=[pl.BlockSpec(memory_space=pltpu.SMEM)]
        + [pl.BlockSpec((1,) + a.shape[1:], lambda i: (expert, 0, 0)) for a in args],
        out_specs=[pl.BlockSpec((2, 1, depth, hidden), lambda i: (0, i, 0, 0))] * 4,
        scratch_shapes=[pltpu.VMEM((width, hidden), F32)],
        compiler_params=pltpu.CompilerParams(vmem_limit_bytes=48 * 1024 * 1024),
        cost_estimate=COST,
    )(order, *args)


CTX = ("z", "yl")
GROUP = ("yh", "x")
FSDP = ("yh", "x", "core")
ALL = CTX + FSDP
UP = [(i, (i + 1) % 4) for i in range(4)]
DOWN = [(i, (i - 1) % 4) for i in range(4)]
TWO = [(i, (i + 2) % 4) for i in range(4)]
FLIP = [(0, 1), (1, 0)]


def mm(a, b):
    return jnp.dot(a, b, preferred_element_type=F32)


def mm_t(a, b):
    return lax.dot_general(a, b, (((1,), (1,)), ((), ())), preferred_element_type=F32)


def t_mm(a, b):
    return lax.dot_general(a, b, (((0,), (0,)), ((), ())), preferred_element_type=F32)


def ein(spec, a, b):
    return jnp.einsum(spec, a, b, preferred_element_type=F32)


def swap(parts, axis):
    return lax.all_to_all(parts, axis, split_axis=0, concat_axis=0, tiled=True)


def flip(block, axis):
    return lax.ppermute(block, axis, FLIP)


def by_z(parts):
    return [lax.ppermute(parts[k], "z", perm) for k, perm in ((1, UP), (2, TWO), (3, DOWN))]


def along_z(both):
    before, far, after = by_z([both] * 4)
    return [both, after, far, before]


class Exchange:
    def __init__(self):
        self.last = None

    def __call__(self, parts, axis):
        if self.last is not None:
            parts = after_all(parts, self.last)
        self.last = swap(parts, axis)
        return self.last

    def copies(self, block, axis, count):
        return self(jnp.broadcast_to(block[None], (count,) + block.shape), axis)


def add(a, b):
    return (a.astype(F32) + b.astype(F32)).astype(BF)


def add_part(parts, i, more):
    pieces = [parts[:1], parts[1:]]
    pieces[i] = add(pieces[i], more)
    return jnp.concatenate(pieces, axis=0)


def relay(far):
    return [lax.ppermute(far[:1], "z", UP), lax.ppermute(far[1:], "z", DOWN)]


def ring_sums(parts, far):
    return [
        lax.ppermute(add_part(parts[1], 0, far[0]), "z", UP),
        lax.ppermute(add_part(parts[3], 1, far[1]), "z", DOWN),
    ]


def pair_sums(parts, moved):
    return [sum(part[i].astype(F32) for part in [parts[0]] + moved) for i in range(2)]


def sum_parts(parts):
    return jnp.sum(parts.astype(F32), axis=0)


def after_all(value, *others):
    return lax.optimization_barrier((value,) + others)[0]


def rope_tables(positions):
    half = DH // 2
    inverse = THETA ** (-(jnp.arange(half, dtype=F32) * 2.0) / DH)
    angles = positions.astype(F32)[:, None] * inverse[None, :]
    return (jnp.cos(angles), jnp.sin(angles))


def rms_scale(values, gain):
    return values * lax.rsqrt(jnp.mean(values * values, axis=-1, keepdims=True) + EPS) * gain


def body(
    tokens,
    segments,
    routes,
    w_query,
    w_key,
    w_value,
    w_out,
    w_router,
    attn_gain,
    mlp_gain,
    qk_gain,
    w_gate,
    w_up,
    w_down,
    cotangent,
):
    micro = tokens.shape[0]
    tok = tokens.shape[2]
    width = tokens.shape[3]
    length = segments.shape[2]
    rows = w_query.shape[0]
    n_ctx, n_fsdp = 8, 16
    n_all = n_ctx * n_fsdp
    z, yl, yh, x, core = (lax.axis_index(name) for name in ALL)
    shard = (yh * 4 + x) * 2 + core
    local = w_gate.shape[0]
    experts = local * n_fsdp
    cap = (3 * tok * TOPK + 2 * experts - 1) // (2 * experts)
    all_tok = micro * tok
    ratio = H // KV
    heads = ratio * DH
    span = heads + 2 * DH

    exchange = Exchange()
    small = jnp.concatenate(
        [
            w_router,
            attn_gain[:, None],
            mlp_gain[:, None],
            jnp.pad(qk_gain[:, None], ((0, rows - 1), (0, 0))),
        ],
        axis=1,
    )
    small = jnp.pad(small, ((0, 0), (0, 128 - small.shape[1])))
    pieces = jnp.concatenate(
        [
            w_query.reshape(rows, n_ctx, heads),
            w_key.reshape(rows, n_ctx, DH),
            w_value.reshape(rows, n_ctx, DH),
            jnp.broadcast_to(small[:, None], (rows, n_ctx, 128)),
        ],
        axis=2,
    ).transpose(1, 0, 2)
    pieces = jnp.broadcast_to(pieces[:, None], (n_ctx, n_fsdp) + pieces.shape[1:])
    both_0, both_1 = (
        jnp.concatenate([tokens[m], flip(tokens[m], "yl")], axis=0) for m in range(micro)
    )
    both_w = jnp.stack([w_gate, w_up, w_down], axis=1)
    head_all = exchange(pieces.reshape((n_all,) + pieces.shape[2:]), ALL).reshape(width, -1)
    other_w = flip(both_w, "yl")
    both_w = [jnp.stack([both_w[e], other_w[e]]) for e in range(local)]
    seq_rows = [along_z(both_0)]
    seq_rows.append(along_z(after_all(both_1, *seq_rows[0][1:])))
    head_all = after_all(head_all, *seq_rows[0][1:], other_w)
    w_heads = head_all[:, :span]
    small_all = head_all[:, span:]
    router = small_all[:, :experts]
    small_wide = small_all.astype(F32)
    gain_attn = small_wide[:, experts]
    gain_mlp = small_wide[:, experts + 1]
    gain_heads = small_wide[:, experts + 2].reshape(-1, rows)[:, 0]
    gain_row = gain_attn[None]
    head_row = jnp.concatenate(
        [gain_heads[:DH]] * ratio + [gain_heads[DH:], jnp.ones((DH,), F32)]
    )[None]
    router_pad = jnp.pad(router, ((0, 0), (0, 128 - experts)))

    out_own = exchange.copies(w_out, CTX + GROUP, n_all // 2)

    moved_w = []
    last = seq_rows[1][1:]
    for e in range(local):
        block = after_all(both_w[e], *last)
        last = [lax.ppermute(block, "z", UP), lax.ppermute(block, "z", DOWN)]
        moved_w.append(last)

    expert_ids = jnp.arange(experts, dtype=jnp.int32)
    cot = cotangent.reshape(all_tok, width)
    chosen = jnp.any(routes.reshape(all_tok, TOPK)[:, :, None] == expert_ids, axis=1)
    before = jnp.arange(tok, dtype=jnp.int32)
    lower = (before[:, None] >= before[None, :]).astype(BF)
    counts = ein("ut,mte->mue", lower, chosen.reshape(micro, tok, experts).astype(BF))
    held = jnp.where(chosen, counts.reshape(all_tok, experts) - 1.0, -1.0)
    held = jnp.pad(held, ((0, 0), (0, 128 - experts)), constant_values=-1.0).astype(BF)
    pack = after_all(jnp.concatenate([cot, held], axis=1), both_0, both_1)
    g_all = lax.all_gather(pack, FSDP, axis=0)

    cosine, sine = rope_tables(jnp.arange(length, dtype=jnp.int32))
    cosine = jnp.tile(cosine, (1, 4))
    sine = jnp.tile(jnp.concatenate([-sine, sine], axis=1), (1, 2))
    rel = jnp.arange(n_ctx, dtype=jnp.int32)
    order = ((z + rel // 2) % 4) * 2 + (yl + rel % 2) % 2
    scalars = jnp.concatenate([jnp.stack([shard * local, core]), order]).astype(jnp.int32)

    def to_owner(v):
        return exchange(v.reshape(n_ctx, tok, -1), CTX)

    def attention_args(m):
        seg = segments[m, 0]
        return gain_row, w_heads, head_row, cosine, sine, seg[:, None], seg[None, :]

    mixed_0, *saved_0 = attend_forward(order, seq_rows[0], *attention_args(0))
    seq_rows[1], mixed_0 = lax.optimization_barrier((seq_rows[1], mixed_0))
    mixed_1, *saved_1 = attend_forward(order, seq_rows[1], *attention_args(1))
    saved = [saved_0, saved_1]
    out_own, mixed_0, mixed_1 = lax.optimization_barrier((out_own, mixed_0, mixed_1))
    out_other = flip(out_own, "core")
    mixed = jnp.stack([mixed_0, mixed_1]).reshape(micro, n_ctx, tok, heads).transpose(1, 0, 2, 3)
    mixed = exchange(mixed.reshape(n_ctx, all_tok, heads), CTX)
    mixed, moved_w[0] = lax.optimization_barrier((mixed, moved_w[0]))
    mixed = mixed.transpose(1, 0, 2).reshape(all_tok, width)
    out_full = jnp.where(
        core == 0,
        jnp.stack([out_own, out_other], axis=1),
        jnp.stack([out_other, out_own], axis=1),
    ).reshape(width, width)
    middle = tokens.reshape(all_tok, width).astype(F32) + mm(mixed, out_full)
    inv_two = lax.rsqrt(jnp.mean(middle * middle, axis=-1, keepdims=True) + EPS)
    hidden_two = (middle * inv_two * gain_mlp).astype(BF)
    x_0 = exchange.copies(hidden_two[:tok], GROUP, n_ctx)
    weights = []
    for e, (w_before, w_after) in enumerate(moved_w):
        w_far = [lax.ppermute(w_before[:1], "z", UP), lax.ppermute(w_after[1:], "z", DOWN)]
        weights.append([both_w[e], w_after, *w_far, w_before])
    x_0, weights = lax.optimization_barrier((x_0, weights))
    x_1 = exchange.copies(hidden_two[tok:], GROUP, n_ctx)
    logits = jnp.where(chosen, mm(hidden_two, router), -1e30)
    gates_all = jnp.where(chosen, jax.nn.softmax(logits, axis=-1), 0.0)

    def experts_of(m, x_own, *moe):
        return run_experts(
            scalars,
            x_own,
            flip(x_own, "core"),
            g_all,
            m,
            router_pad,
            weights,
            cap,
            *moe,
        )

    def back_sum(own, other):
        return add(own, flip(other, "core"))

    def middle_back(back):
        tail = back[:, width:]
        d_gates = tail[:, :experts] + tail[:, 64 : 64 + experts]
        d_select = gates_all * (d_gates - jnp.sum(gates_all * d_gates, axis=-1, keepdims=True))
        d_logits = d_select.astype(BF)
        d_two = back[:, :width] + mm_t(d_logits, router)
        u = d_two * gain_mlp
        d_middle = (
            cot.astype(F32)
            + inv_two * u
            - middle * (inv_two**3 * jnp.mean(u * middle, axis=-1, keepdims=True))
        )
        d_branch = d_middle.astype(BF)
        d_mixed = mm_t(d_branch, out_full).astype(BF)
        d_mixed = d_mixed.reshape(all_tok, n_ctx, heads).transpose(1, 0, 2)
        return d_middle, d_mixed, (d_branch, d_logits, d_two)

    def weight_grads(d_branch, d_logits, d_two):
        grad_mlp = jnp.sum(d_two * middle * inv_two, axis=0)
        return t_mm(mixed, d_branch), t_mm(hidden_two, d_logits), grad_mlp

    def pack_grads(grad_heads, grad_router, grad_attn, grad_mlp, grad_qk):
        grad_qk = jnp.pad(grad_qk[:, None], ((0, 0), (0, rows - 1))).reshape(-1)
        grad_small = jnp.concatenate(
            [grad_router, grad_attn[:, None], grad_mlp[:, None], grad_qk[:, None]], axis=1
        )
        grad_small = jnp.pad(grad_small, ((0, 0), (0, 128 - grad_small.shape[1])))
        grad_pack = jnp.concatenate([grad_heads, grad_small], axis=1).astype(BF)
        return grad_pack.reshape(n_all, rows, -1)

    def attention_back(m, d_mixed):
        *d_hidden, grad_heads, grad_attn, grad_qk = attend_backward(
            order, *saved[m], d_mixed.reshape(length, heads), *attention_args(m)
        )
        grad_qk = jnp.concatenate(
            [grad_qk[0, :DH] + grad_qk[0, DH : 2 * DH], grad_qk[0, 2 * DH : 3 * DH]]
        )
        return d_hidden, (grad_heads, grad_attn[0], grad_qk)

    moe, back_own, back_other, *kept_0 = experts_of(0, x_0)
    x_1, back_own, back_other = lax.optimization_barrier((x_1, back_own, back_other))
    back_0 = back_sum(back_own, back_other)
    x_1 = after_all(x_1, back_0)
    back_0 = exchange(back_0, GROUP)
    moe, back_own, back_other, *kept_1 = experts_of(1, x_1, moe)
    back_0, back_own, back_other, moe = lax.optimization_barrier(
        (back_0, back_own, back_other, moe)
    )
    moe = lax.psum_scatter(moe, FSDP, scatter_dimension=0, tiled=True)[0]
    back_1 = back_sum(back_own, back_other)
    kept_1[0], back_1 = lax.optimization_barrier((kept_1[0], back_1))
    back_1 = exchange(back_1, GROUP)
    parts = [expert_grads(order, (kept_0, kept_1), e) for e in range(local)]
    far = [relay(part[2]) for part in parts]
    back_1, parts = lax.optimization_barrier((back_1, parts))
    d_middle, d_mixed, d_rows = middle_back(
        jnp.concatenate([sum_parts(back_0), sum_parts(back_1)], axis=0)
    )
    d_mixed, far = lax.optimization_barrier((d_mixed, far))
    d_mixed = exchange(d_mixed, CTX)
    d_mixed, far = lax.optimization_barrier((d_mixed, far))
    moved = [ring_sums(part, f) for part, f in zip(parts, far)]
    d_mixed = d_mixed.reshape(n_ctx, micro, tok, heads)
    d_hidden_0, head_grads_0 = attention_back(0, d_mixed[:, 0])
    d_hidden_0, d_mixed, moved[0] = lax.optimization_barrier((d_hidden_0, d_mixed, moved[0]))
    d_hidden_1, head_grads_1 = attention_back(1, d_mixed[:, 1])
    d_hidden_1, d_hidden_0, moved[1], d_rows = lax.optimization_barrier(
        (d_hidden_1, d_hidden_0, moved[1], d_rows)
    )
    hidden_moved_0 = by_z(d_hidden_0)
    hidden_moved_1 = by_z(d_hidden_1)
    grad_out, grad_router, grad_mlp = weight_grads(*d_rows)
    grad_heads, grad_attn, grad_qk = jax.tree.map(jnp.add, head_grads_0, head_grads_1)
    grad_pack = pack_grads(grad_heads, grad_router, grad_attn, grad_mlp, grad_qk)
    grad_pack = exchange(grad_pack, ALL)
    grad_out = grad_out.astype(BF).reshape(n_all // 2, 2, rows, width)
    grad_own = lax.dynamic_index_in_dim(grad_out, core, axis=1, keepdims=False)
    grad_other = lax.dynamic_index_in_dim(grad_out, 1 - core, axis=1, keepdims=False)
    grad_out = back_sum(grad_own, grad_other)
    weight_sums = [pair_sums(p, q) for p, q in zip(parts, moved)]
    weight_yl = [flip(sums[1].astype(BF), "yl") for sums in weight_sums]
    grad_pack, grad_out, hidden_moved_0, weight_yl = lax.optimization_barrier(
        (grad_pack, grad_out, hidden_moved_0, weight_yl)
    )
    exchange.last = grad_pack
    grad_out = exchange(grad_out, CTX + GROUP)
    hidden_sums_0 = pair_sums(d_hidden_0, hidden_moved_0)
    hidden_sums_1 = pair_sums(d_hidden_1, hidden_moved_1)
    hidden_sums = [jnp.stack(sums) for sums in zip(hidden_sums_0, hidden_sums_1)]
    hidden_yl = flip(hidden_sums[1].astype(BF), "yl")
    grad_out, hidden_yl = lax.optimization_barrier((grad_out, hidden_yl))

    grad_pack = grad_pack.astype(F32)
    own_heads = jnp.sum(grad_pack[:, :, :span].reshape(n_ctx, n_fsdp, rows, -1), axis=1)
    own_heads = own_heads.transpose(1, 0, 2)
    own_small = jnp.sum(grad_pack[:, :, span:], axis=0)
    own_out = sum_parts(grad_out)
    moe = after_all(moe, grad_pack)
    d_hidden = (hidden_sums[0] + hidden_yl.astype(F32)).reshape(all_tok, width)
    expert_own = [sums[0] + other.astype(F32) for sums, other in zip(weight_sums, weight_yl)]
    out = (middle.reshape(moe.shape) + moe.astype(F32)).astype(BF)
    start = tokens.reshape(all_tok, width).astype(F32)
    inv_one = lax.rsqrt(jnp.mean(start * start, axis=-1, keepdims=True) + EPS)
    u = d_hidden * gain_attn
    d_input = (
        d_middle
        + inv_one * u
        - start * (inv_one**3 * jnp.mean(u * start, axis=-1, keepdims=True))
    )

    return (
        out[:, None],
        d_input.reshape(tokens.shape),
        own_heads[:, :, :heads].reshape(rows, -1),
        own_heads[:, :, heads : heads + DH].reshape(rows, -1),
        own_heads[:, :, heads + DH :].reshape(rows, -1),
        own_out,
        own_small[:, :experts],
        own_small[:, experts],
        own_small[:, experts + 1],
        own_small[:1, experts + 2],
        jnp.stack([part[0] for part in expert_own]),
        jnp.stack([part[1] for part in expert_own]),
        jnp.stack([part[2] for part in expert_own]),
    )


def solution(mesh):
    mesh = Mesh(mesh.devices.reshape(4, 2, 2, 4, 2), ALL)
    weight = P(ALL, None)
    gain = P(ALL)
    rows = P(None, FSDP, CTX, None)
    expert = P(FSDP, CTX, None)
    return jax.shard_map(
        body,
        mesh=mesh,
        in_specs=(rows, P(None, FSDP, None), rows)
        + (weight,) * 5
        + (gain,) * 3
        + (expert,) * 3
        + (rows,),
        out_specs=(rows, rows) + (weight,) * 5 + (gain,) * 3 + (expert,) * 3,
        check_vma=False,
    )
```

```python
import functools

import jax
import jax.numpy as jnp
from jax import lax
from jax.experimental import pallas as pl
from jax.experimental.pallas import tpu as pltpu
from jax.sharding import Mesh
from jax.sharding import PartitionSpec as P

BF = jnp.bfloat16
F32 = jnp.float32
H = 16
KV = 8
DH = 64
TOPK = 8
WINDOW = 1024
EPS = 1e-06
THETA = 10000.0
COST = pl.CostEstimate(flops=10**7, bytes_accessed=10**5, transcendentals=0)


def dot(a, b, ca, cb):
    return lax.dot_general(a, b, (((ca,), (cb,)), ((), ())), preferred_element_type=F32)


def lanes_of(v):
    return lax.broadcasted_iota(jnp.int32, v.shape, v.ndim - 1)


def head_sums(v):
    low = lanes_of(v) < DH
    first = jnp.sum(jnp.where(low, v, 0.0), axis=1, keepdims=True)
    second = jnp.sum(jnp.where(low, 0.0, v), axis=1, keepdims=True)
    return jnp.where(low, first, second)


def trade(v):
    return jnp.where(
        lanes_of(v) % DH < DH // 2, pltpu.roll(v, 128 - DH // 2, 1), pltpu.roll(v, DH // 2, 1)
    )


def both_halves(v, second):
    low = lanes_of(v) < DH
    other = pltpu.roll(v, DH, 1)
    return jnp.where(low, other, v) if second else jnp.where(low, v, other)


def stack_heads(v):
    low = lanes_of(v) < DH
    zero = jnp.zeros_like(v)
    return jnp.concatenate([jnp.where(low, v, zero), jnp.where(low, zero, v)], axis=0)


def key_span(start, block, length):
    reach = WINDOW // 2 - 1
    low = max(0, start - reach) // 128 * 128
    high = min(length, -(-(start + block + reach) // 128) * 128)
    return low, high


def masked_probs(q_two, keys, seg_col, seg_row, start, low):
    block = q_two.shape[0] // 2
    scores = dot(q_two, keys, 1, 1)
    shape = (block, keys.shape[0])
    gap = (
        lax.broadcasted_iota(jnp.int32, shape, 0)
        - lax.broadcasted_iota(jnp.int32, shape, 1)
        + (start - low)
    )
    allowed = (seg_col == seg_row) & (jnp.abs(gap) < WINDOW // 2)
    bias = jnp.where(allowed, 0.0, -1e30)
    scores = scores + jnp.concatenate([bias, bias], axis=0)
    raised = jnp.exp(scores - jnp.max(scores, axis=1, keepdims=True))
    return raised * (1.0 / jnp.sum(raised, axis=1, keepdims=True))


def attend_kernel(
    order_ref,
    *refs,
):
    pieces, refs = refs[:-13], refs[-13:]
    gain_ref, w_ref, head_gain_ref, cos_ref, sin_ref, seg_col_ref, seg_row_ref = refs[:7]
    mixed_ref, hidden_ref, q_ref, kv_ref, keys_ref, values_ref = refs[7:]
    tok, width = pieces[0].shape[1:]
    length = hidden_ref.shape[0]
    pieces = [(ref, i) for ref in pieces for i in range(ref.shape[0])]
    for r, (ref, i) in enumerate(pieces):
        x = ref[i].astype(F32)
        x = x * lax.rsqrt(jnp.mean(x * x, axis=1, keepdims=True) + EPS) * gain_ref[...]
        rows = pl.ds(pl.multiple_of(order_ref[r] * tok, tok), tok)
        hidden_ref[rows] = x.astype(BF)
    raw = dot(hidden_ref[...], w_ref[...], 1, 0)
    for half in range(2):
        u = raw[:, half * 128 : half * 128 + 128]
        gain = head_gain_ref[:, half * 128 : half * 128 + 128]
        n = u * lax.rsqrt(head_sums(u * u) * (1.0 / DH) + EPS) * gain
        turned = n * cos_ref[...] + trade(n) * sin_ref[...]
        if half == 0:
            q_ref[...] = turned.astype(BF)
        else:
            kv = jnp.where(lanes_of(u) < DH, turned, u)
            kv_ref[...] = kv.astype(BF)
            keys_ref[...] = both_halves(kv, False).astype(BF)
            values_ref[...] = both_halves(kv, True).astype(BF)
    block = 256
    for start in range(0, length, block):
        low, high = key_span(start, block, length)
        q_two = stack_heads(q_ref[start : start + block].astype(F32) * DH**-0.5).astype(BF)
        probs = masked_probs(
            q_two,
            keys_ref[low:high],
            seg_col_ref[start : start + block],
            seg_row_ref[:, low:high],
            start,
            low,
        )
        result = dot(probs.astype(BF), values_ref[low:high], 1, 0)
        first = lanes_of(result[:block]) < DH
        mixed_ref[start : start + block] = jnp.where(first, result[:block], result[block:]).astype(
            BF
        )


def attend_back_kernel(order_ref, *refs, again):
    hidden_ref, q_ref, kv_ref, d_mixed_ref, gain_ref, w_ref, head_gain_ref = refs[:7]
    cos_ref, sin_ref, seg_col_ref, seg_row_ref = refs[7:11]
    refs = refs[15:] if again else refs[11:]
    outs, refs = refs[:4], refs[4:]
    grad_w_ref, grad_gain_ref, grad_heads_ref = refs[:3]
    keys_ref, values_ref, d_q_ref, d_k_ref, d_v_ref, d_raw_ref = refs[3:]
    length = hidden_ref.shape[0]
    kv = kv_ref[...].astype(F32)
    keys_ref[...] = both_halves(kv, False).astype(BF)
    values_ref[...] = both_halves(kv, True).astype(BF)
    d_k_ref[...] = jnp.zeros_like(d_k_ref)
    d_v_ref[...] = jnp.zeros_like(d_v_ref)
    block = 256
    for start in range(0, length, block):
        low, high = key_span(start, block, length)
        q_two = stack_heads(q_ref[start : start + block].astype(F32) * DH**-0.5).astype(BF)
        m_two = stack_heads(d_mixed_ref[start : start + block].astype(F32)).astype(BF)
        probs = masked_probs(
            q_two,
            keys_ref[low:high],
            seg_col_ref[start : start + block],
            seg_row_ref[:, low:high],
            start,
            low,
        )
        d_probs = dot(m_two, values_ref[low:high], 1, 1)
        inner = jnp.sum(probs * d_probs, axis=1, keepdims=True)
        d_scores = (probs * (d_probs - inner)).astype(BF)
        result = dot(d_scores, keys_ref[low:high], 1, 0)
        first = lanes_of(result[:block]) < DH
        d_q_ref[start : start + block] = jnp.where(first, result[:block], result[block:]) * (
            DH**-0.5
        )
        d_k_ref[low:high] += dot(d_scores, q_two, 0, 0)
        d_v_ref[low:high] += dot(probs.astype(BF), m_two, 0, 0)
    raw = dot(hidden_ref[...], w_ref[...], 1, 0)
    d_k = d_k_ref[...]
    d_k = d_k + pltpu.roll(d_k, DH, 1)
    d_v = d_v_ref[...]
    d_v = d_v + pltpu.roll(d_v, DH, 1)
    for half in range(2):
        lanes = slice(half * 128, half * 128 + 128)
        u = raw[:, lanes]
        gain = head_gain_ref[:, lanes]
        d = d_q_ref[...] if half == 0 else d_k
        d = d * cos_ref[...] + trade(d * sin_ref[...])
        r = lax.rsqrt(head_sums(u * u) * (1.0 / DH) + EPS)
        grad_heads_ref[:, lanes] = jnp.sum(d * u * r, axis=0, keepdims=True)
        d = d * gain
        d = d * r - u * (r * r * r * (head_sums(d * u) * (1.0 / DH)))
        if half == 1:
            d = jnp.where(lanes_of(d) < DH, d, d_v)
        d_raw_ref[:, lanes] = d.astype(BF)
    grad_w_ref[...] = dot(hidden_ref[...], d_raw_ref[...], 0, 0)
    total = jnp.zeros(grad_gain_ref.shape, F32)
    tok = length // 8
    for step in range(4):
        rows = pl.ds(pl.multiple_of(order_ref[2 * step] // 2 * (2 * tok), 2 * tok), 2 * tok)
        d_hidden = dot(d_raw_ref[rows], w_ref[...], 1, 1)
        own = order_ref[0] % 2
        outs[step][0, own] = d_hidden[:tok].astype(BF)
        outs[step][0, 1 - own] = d_hidden[tok:].astype(BF)
        total = total + jnp.sum(d_hidden * hidden_ref[rows].astype(F32), axis=0, keepdims=True)
    grad_gain_ref[...] = total / gain_ref[...]


def whole(a):
    return pl.BlockSpec(a.shape, lambda i: (0,) * len(a.shape), pipeline_mode=pl.Buffered(1))


def attend_forward(order, pieces, gain, w_heads, head_gain, cosine, sine, seg_col, seg_row):
    length = cosine.shape[0]
    width = w_heads.shape[0]
    shape = jax.ShapeDtypeStruct
    outs = [
        shape((length, 128), BF),
        shape((length, width), BF),
        shape((length, 128), BF),
        shape((length, 128), BF),
    ]
    args = list(pieces) + [gain, w_heads, head_gain, cosine, sine, seg_col, seg_row]
    return pl.pallas_call(
        attend_kernel,
        out_shape=outs,
        grid=(1,),
        in_specs=[pl.BlockSpec(memory_space=pltpu.SMEM)] + [whole(a) for a in args],
        out_specs=[whole(o) for o in outs],
        scratch_shapes=[pltpu.VMEM((length, 128), BF), pltpu.VMEM((length, 128), BF)],
        compiler_params=pltpu.CompilerParams(vmem_limit_bytes=40 * 1024 * 1024),
        cost_estimate=COST,
    )(order, *args)


def attend_backward(micro, held, order, *args):
    length, width = args[0].shape
    shape = jax.ShapeDtypeStruct
    outs = [shape((2, 2, length // 8, width), BF)] * 4 + [
        shape((width, 256), F32),
        shape((1, width), F32),
        shape((1, 256), F32),
    ]
    part = pl.BlockSpec(
        (1, 2, length // 8, width), lambda i: (micro, 0, 0, 0), pipeline_mode=pl.Buffered(1)
    )
    return pl.pallas_call(
        functools.partial(attend_back_kernel, again=len(held) > 0),
        out_shape=outs,
        grid=(1,),
        in_specs=[pl.BlockSpec(memory_space=pltpu.SMEM)]
        + [whole(a) for a in args]
        + [pl.BlockSpec(memory_space=pl.ANY)] * len(held),
        out_specs=[part] * 4 + [whole(o) for o in outs[4:]],
        input_output_aliases={1 + len(args) + n: n for n in range(len(held))},
        scratch_shapes=[pltpu.VMEM((length, 128), BF)] * 2
        + [pltpu.VMEM((length, 128), F32)] * 3
        + [pltpu.VMEM((length, 256), BF)],
        compiler_params=pltpu.CompilerParams(vmem_limit_bytes=40 * 1024 * 1024),
        cost_estimate=COST,
    )(order, *args, *held)


def halves(v):
    high = v.astype(BF)
    return high, (v - high.astype(F32)).astype(BF)


def expert_kernel(scalar_ref, *refs, again):
    x_own_ref, x_other_ref, g_ref, router_ref = refs[:4]
    pieces, refs = refs[4:9], refs[9:]
    if again:
        refs = refs[1:]
    out_ref, back_own_ref, back_other_ref = refs[:3]
    kept_refs, refs = refs[3:8], refs[8:]
    xe_ref, de_ref, act_ref, da_ref, db_ref, *refs = refs
    pick_ref, weight_ref, dgate_ref, eo_ref, dr_ref, w_ref, in_sem, out_sem = refs
    half, tok, width = x_own_ref.shape
    sources = 2 * half
    core = scalar_ref[1]
    depth = w_ref.shape[2] // 8

    loads = []
    blocks = [(ref, i) for ref in pieces for i in range(ref.shape[0])]
    for r, (ref, i) in enumerate(blocks):
        rows = pl.ds(pl.multiple_of(scalar_ref[2 + r] * depth, depth), depth)
        loads.append(pltpu.make_async_copy(ref.at[i], w_ref.at[:, :, rows], in_sem.at[r]))
        loads[-1].start()
    local, slots, hidden = act_ref.shape
    cap = slots // sources
    first = scalar_ref[0]
    lane = lax.broadcasted_iota(jnp.int32, (tok, 128), 1)
    spot = lax.broadcasted_iota(jnp.int32, (tok, local * cap), 1)
    row_expert = lax.broadcasted_iota(jnp.int32, (local * cap, 128), 0) // cap
    slot_lane = lax.broadcasted_iota(jnp.int32, (local * cap, 128), 1)
    own_lane = slot_lane == first + row_expert

    def fetch(i, carry, x_ref, offset, column):
        s = i + offset
        x = x_ref[i]
        from_g = 2 * i + column
        held = g_ref[from_g, :, width:].astype(F32)
        chosen = held >= 0.0
        logits = jnp.where(chosen, dot(x, router_ref[...], 1, 0), -1e30)
        top = jnp.max(logits, axis=1, keepdims=True)
        raised = jnp.where(chosen, jnp.exp(logits - top), 0.0)
        gates = raised / jnp.sum(raised, axis=1, keepdims=True)
        pick = jnp.zeros((tok, local * cap), F32)
        for e in range(local):
            mine = jnp.max(jnp.where(lane == first + e, held, -1.0), axis=1, keepdims=True)
            goal = jnp.where(mine >= 0.0, mine + e * cap, -1.0).astype(jnp.int32)
            pick = jnp.where(spot == goal, 1.0, pick)
        pick = pick.astype(BF)
        pick_ref[s] = pick
        rows = pl.ds(pl.multiple_of(s * cap, 16), cap)
        x_slots = dot(pick, x, 0, 0).astype(BF)
        g_slots = dot(pick, g_ref[from_g, :, :width], 0, 0).astype(BF)
        high, low = halves(gates)
        weight = dot(pick, high, 0, 0) + dot(pick, low, 0, 0)
        weight = jnp.sum(jnp.where(own_lane, weight, 0.0), axis=1, keepdims=True)
        for e in range(local):
            part = slice(e * cap, (e + 1) * cap)
            xe_ref[e, rows] = x_slots[part]
            de_ref[e, rows] = g_slots[part]
            weight_ref[e, rows] = weight[part]
        return carry

    for x_ref, offset, column in ((x_own_ref, 0, core), (x_other_ref, half, 1 - core)):
        step = functools.partial(fetch, x_ref=x_ref, offset=offset, column=column)
        lax.fori_loop(0, half, step, 0, unroll=4)
    for load in loads:
        load.wait()
    chunk = 384

    def work(i, carry):
        e = i // (slots // chunk)
        rows = pl.ds(pl.multiple_of((i % (slots // chunk)) * chunk, chunk), chunk)
        w_gate = w_ref[e, 0]
        w_up = w_ref[e, 1]
        w_down = w_ref[e, 2]
        x = xe_ref[e, rows]
        a = dot(x, w_gate, 1, 0)
        b = dot(x, w_up, 1, 0)
        sig = 1.0 / (1.0 + jnp.exp(-a))
        silu = a * sig
        active = (silu * b).astype(BF)
        act_ref[e, rows] = active
        slope = b * (sig * (1.0 + a * (1.0 - sig)))
        weight = weight_ref[e, rows]
        g = de_ref[e, rows].astype(F32)
        result = dot(active, w_down, 1, 1).astype(BF).astype(F32)
        dgate_ref[e, rows] = jnp.sum(result * g, axis=1, keepdims=True)
        eo_ref[e, rows] = (weight * result).astype(BF)
        d_expert = (weight * g).astype(BF)
        de_ref[e, rows] = d_expert
        d_active = dot(d_expert, w_down, 1, 0)
        da = (d_active * slope).astype(BF)
        db = (d_active * silu).astype(BF)
        da_ref[e, rows] = da
        db_ref[e, rows] = db
        dr_ref[e, rows] = (dot(da, w_gate, 1, 1) + dot(db, w_up, 1, 1)).astype(BF)
        return carry

    lax.fori_loop(0, local * (slots // chunk), work, 0)
    stores = [
        pltpu.make_async_copy(ref, kept, out_sem.at[n])
        for n, (ref, kept) in enumerate(
            zip((xe_ref, de_ref, act_ref, da_ref, db_ref), kept_refs)
        )
    ]
    for store in stores:
        store.start()

    def give(i, carry, back_ref, offset, column):
        s = i + offset
        rows = pl.ds(pl.multiple_of(s * cap, 16), cap)
        pick = pick_ref[s]
        eo = jnp.concatenate([eo_ref[e, rows] for e in range(local)], axis=0)
        dr = jnp.concatenate([dr_ref[e, rows] for e in range(local)], axis=0)
        dgate = jnp.concatenate([dgate_ref[e, rows] for e in range(local)], axis=0)
        high, low = halves(dgate)
        spread = jnp.where(own_lane, high.astype(F32), 0.0) + jnp.where(
            slot_lane == first + row_expert + 64, low.astype(F32), 0.0
        )
        out_ref[2 * i + column, 0] = dot(pick, eo, 1, 0).astype(BF)
        back_ref[i, :, :width] = dot(pick, dr, 1, 0).astype(BF)
        back_ref[i, :, width:] = dot(pick, spread.astype(BF), 1, 0).astype(BF)
        return carry

    for back_ref, offset, column in ((back_own_ref, 0, core), (back_other_ref, half, 1 - core)):
        step = functools.partial(give, back_ref=back_ref, offset=offset, column=column)
        lax.fori_loop(0, half, step, 0, unroll=4)
    for store in stores:
        store.wait()


def run_experts(scalars, x_own, x_other, g_all, micro, router, pieces, cap, moe=None):
    half, tok, width = x_own.shape
    sources = 2 * half
    _, local, _, _, hidden = pieces[0].shape
    slots = sources * cap
    wide = g_all.shape[2]
    shape = jax.ShapeDtypeStruct
    outs = [
        shape((sources, 2, tok, width), BF),
        shape((half, tok, wide), BF),
        shape((half, tok, wide), BF),
        shape((local, slots, width), BF),
        shape((local, slots, width), BF),
        shape((local, slots, hidden), BF),
        shape((local, slots, hidden), BF),
        shape((local, slots, hidden), BF),
    ]
    g_spec = pl.BlockSpec(
        (sources, tok, wide), lambda i: (0, micro, 0), pipeline_mode=pl.Buffered(1)
    )
    args = list(pieces)
    any_place = pl.BlockSpec(memory_space=pl.ANY)
    held = [] if moe is None else [moe]
    moe_spec = pl.BlockSpec(
        (sources, 1, tok, width), lambda i: (0, micro, 0, 0), pipeline_mode=pl.Buffered(1)
    )
    return pl.pallas_call(
        functools.partial(expert_kernel, again=moe is not None),
        out_shape=outs,
        grid=(1,),
        in_specs=[pl.BlockSpec(memory_space=pltpu.SMEM), whole(x_own), whole(x_other), g_spec]
        + [whole(router)]
        + [any_place] * (len(args) + len(held)),
        out_specs=[moe_spec] + [whole(o) for o in outs[1:3]] + [any_place] * 5,
        input_output_aliases={5 + len(args): 0} if held else {},
        scratch_shapes=[pltpu.VMEM(o.shape, o.dtype) for o in outs[3:]]
        + [
            pltpu.VMEM((sources, tok, local * cap), BF),
            pltpu.VMEM((local, slots, 1), F32),
            pltpu.VMEM((local, slots, 1), F32),
            pltpu.VMEM((local, slots, width), BF),
            pltpu.VMEM((local, slots, width), BF),
            pltpu.VMEM((local, 3, width, hidden), BF),
            pltpu.SemaphoreType.DMA((8,)),
            pltpu.SemaphoreType.DMA((5,)),
        ],
        compiler_params=pltpu.CompilerParams(vmem_limit_bytes=60 * 1024 * 1024),
        cost_estimate=COST,
    )(scalars, x_own, x_other, g_all, router, *args, *held)


def expert_grad_kernel(order_ref, *refs):
    kept, outs, total_ref = refs[:10], refs[10:14], refs[14]
    left = (kept[0:2], kept[0:2], kept[2:4])
    right = (kept[6:8], kept[8:10], kept[4:6])
    step = pl.program_id(0)
    depth = outs[0].shape[3]
    for kind in range(3):

        @pl.when(step % 3 == kind)
        def _(kind=kind):
            total = dot(left[kind][0][0], right[kind][0][0], 0, 0)
            total_ref[...] = total + dot(left[kind][1][0], right[kind][1][0], 0, 0)

    for r in range(8):
        rows = pl.ds(pl.multiple_of(order_ref[r] * depth, depth), depth)
        outs[r // 2][r % 2, 0, 0] = total_ref[rows].astype(BF)


def expert_grads(order, kept):
    local, slots, width = kept[0][0].shape
    hidden = kept[0][2].shape[2]
    args = [kept[m][i] for i in range(5) for m in range(2)]
    depth = width // 8
    shape = jax.ShapeDtypeStruct
    return pl.pallas_call(
        expert_grad_kernel,
        out_shape=[shape((2, local, 3, depth, hidden), BF)] * 4,
        grid=(3 * local,),
        in_specs=[pl.BlockSpec(memory_space=pltpu.SMEM)]
        + [pl.BlockSpec((1,) + a.shape[1:], lambda i: (i // 3, 0, 0)) for a in args],
        out_specs=[
            pl.BlockSpec((2, 1, 1, depth, hidden), lambda i: (0, i // 3, i % 3, 0, 0))
        ]
        * 4,
        scratch_shapes=[pltpu.VMEM((width, hidden), F32)],
        compiler_params=pltpu.CompilerParams(vmem_limit_bytes=48 * 1024 * 1024),
        cost_estimate=COST,
    )(order, *args)


CTX = ("z", "yl")
GROUP = ("yh", "x")
FSDP = ("yh", "x", "core")
ALL = CTX + FSDP
UP = [(i, (i + 1) % 4) for i in range(4)]
DOWN = [(i, (i - 1) % 4) for i in range(4)]
TWO = [(i, (i + 2) % 4) for i in range(4)]
FLIP = [(0, 1), (1, 0)]


def mm(a, b):
    return jnp.dot(a, b, preferred_element_type=F32)


def mm_t(a, b):
    return lax.dot_general(a, b, (((1,), (1,)), ((), ())), preferred_element_type=F32)


def t_mm(a, b):
    return lax.dot_general(a, b, (((0,), (0,)), ((), ())), preferred_element_type=F32)


def ein(spec, a, b):
    return jnp.einsum(spec, a, b, preferred_element_type=F32)


def swap(parts, axis):
    return lax.all_to_all(parts, axis, split_axis=0, concat_axis=0, tiled=True)


def flip(block, axis):
    return lax.ppermute(block, axis, FLIP)


def by_z(parts):
    return [lax.ppermute(parts[k], "z", perm) for k, perm in ((1, UP), (2, TWO), (3, DOWN))]


def along_z(both):
    before, far, after = by_z([both] * 4)
    return [both, after, far, before]


class Exchange:
    def __init__(self):
        self.last = None

    def __call__(self, parts, axis):
        if self.last is not None:
            parts = after_all(parts, self.last)
        self.last = swap(parts, axis)
        return self.last

    def copies(self, block, axis, count):
        return self(jnp.broadcast_to(block[None], (count,) + block.shape), axis)


def add(a, b):
    return (a.astype(F32) + b.astype(F32)).astype(BF)


def add_part(parts, i, more):
    pieces = [parts[:1], parts[1:]]
    pieces[i] = add(pieces[i], more)
    return jnp.concatenate(pieces, axis=0)


def relay(far):
    return [lax.ppermute(far[:1], "z", UP), lax.ppermute(far[1:], "z", DOWN)]


def ring_sums(parts, far):
    return [
        lax.ppermute(add_part(parts[1], 0, far[0]), "z", UP),
        lax.ppermute(add_part(parts[3], 1, far[1]), "z", DOWN),
    ]


def pair_sums(parts, moved):
    return [sum(part[i].astype(F32) for part in [parts[0]] + moved) for i in range(2)]


def sum_parts(parts):
    return jnp.sum(parts.astype(F32), axis=0)


def after_all(value, *others):
    return lax.optimization_barrier((value,) + others)[0]


def rope_tables(positions):
    half = DH // 2
    inverse = THETA ** (-(jnp.arange(half, dtype=F32) * 2.0) / DH)
    angles = positions.astype(F32)[:, None] * inverse[None, :]
    return (jnp.cos(angles), jnp.sin(angles))


def rms_scale(values, gain):
    return values * lax.rsqrt(jnp.mean(values * values, axis=-1, keepdims=True) + EPS) * gain


def body(
    tokens,
    segments,
    routes,
    w_query,
    w_key,
    w_value,
    w_out,
    w_router,
    attn_gain,
    mlp_gain,
    qk_gain,
    w_gate,
    w_up,
    w_down,
    cotangent,
):
    micro = tokens.shape[0]
    tok = tokens.shape[2]
    width = tokens.shape[3]
    length = segments.shape[2]
    rows = w_query.shape[0]
    n_ctx, n_fsdp = 8, 16
    n_all = n_ctx * n_fsdp
    z, yl, yh, x, core = (lax.axis_index(name) for name in ALL)
    shard = (yh * 4 + x) * 2 + core
    local = w_gate.shape[0]
    experts = local * n_fsdp
    cap = (3 * tok * TOPK + 2 * experts - 1) // (2 * experts)
    all_tok = micro * tok
    ratio = H // KV
    heads = ratio * DH
    span = heads + 2 * DH

    exchange = Exchange()
    small = jnp.concatenate(
        [
            w_router,
            attn_gain[:, None],
            mlp_gain[:, None],
            jnp.pad(qk_gain[:, None], ((0, rows - 1), (0, 0))),
        ],
        axis=1,
    )
    small = jnp.pad(small, ((0, 0), (0, 128 - small.shape[1])))
    pieces = jnp.concatenate(
        [
            w_query.reshape(rows, n_ctx, heads),
            w_key.reshape(rows, n_ctx, DH),
            w_value.reshape(rows, n_ctx, DH),
            jnp.broadcast_to(small[:, None], (rows, n_ctx, 128)),
        ],
        axis=2,
    ).transpose(1, 0, 2)
    pieces = jnp.broadcast_to(pieces[:, None], (n_ctx, n_fsdp) + pieces.shape[1:])
    both_0, both_1 = (
        jnp.concatenate([tokens[m], flip(tokens[m], "yl")], axis=0) for m in range(micro)
    )
    both_w = jnp.stack([w_gate, w_up, w_down], axis=1)
    head_all = exchange(pieces.reshape((n_all,) + pieces.shape[2:]), ALL).reshape(width, -1)
    other_w = flip(both_w, "yl")
    both_w = jnp.stack([both_w, other_w])
    seq_rows = [along_z(both_0)]
    seq_rows.append(along_z(after_all(both_1, *seq_rows[0][1:])))
    head_all = after_all(head_all, *seq_rows[0][1:], other_w)
    w_heads = head_all[:, :span]
    small_all = head_all[:, span:]
    router = small_all[:, :experts]
    small_wide = small_all.astype(F32)
    gain_attn = small_wide[:, experts]
    gain_mlp = small_wide[:, experts + 1]
    gain_heads = small_wide[:, experts + 2].reshape(-1, rows)[:, 0]
    gain_row = gain_attn[None]
    head_row = jnp.concatenate(
        [gain_heads[:DH]] * ratio + [gain_heads[DH:], jnp.ones((DH,), F32)]
    )[None]
    router_pad = jnp.pad(router, ((0, 0), (0, 128 - experts)))

    out_own = exchange.copies(after_all(w_out, *seq_rows[0][1:]), CTX + GROUP, n_all // 2)

    both_w = after_all(both_w, *seq_rows[1][1:])
    w_before = lax.ppermute(both_w, "z", UP)
    w_after = lax.ppermute(both_w, "z", DOWN)

    expert_ids = jnp.arange(experts, dtype=jnp.int32)
    cot = cotangent.reshape(all_tok, width)
    chosen = jnp.any(routes.reshape(all_tok, TOPK)[:, :, None] == expert_ids, axis=1)
    before = jnp.arange(tok, dtype=jnp.int32)
    lower = (before[:, None] >= before[None, :]).astype(BF)
    counts = ein("ut,mte->mue", lower, chosen.reshape(micro, tok, experts).astype(BF))
    held = jnp.where(chosen, counts.reshape(all_tok, experts) - 1.0, -1.0)
    held = jnp.pad(held, ((0, 0), (0, 128 - experts)), constant_values=-1.0).astype(BF)
    pack = after_all(jnp.concatenate([cot, held], axis=1), both_0, both_1)
    g_all = lax.all_gather(pack, FSDP, axis=0)

    cosine, sine = rope_tables(jnp.arange(length, dtype=jnp.int32))
    cosine = jnp.tile(cosine, (1, 4))
    sine = jnp.tile(jnp.concatenate([-sine, sine], axis=1), (1, 2))
    rel = jnp.arange(n_ctx, dtype=jnp.int32)
    order = ((z + rel // 2) % 4) * 2 + (yl + rel % 2) % 2
    scalars = jnp.concatenate([jnp.stack([shard * local, core]), order]).astype(jnp.int32)

    def to_owner(v):
        return exchange(v.reshape(n_ctx, tok, -1), CTX)

    def attention_args(m):
        seg = segments[m, 0]
        return gain_row, w_heads, head_row, cosine, sine, seg[:, None], seg[None, :]

    mixed_0, *saved_0 = attend_forward(order, seq_rows[0], *attention_args(0))
    seq_rows[1], mixed_0 = lax.optimization_barrier((seq_rows[1], mixed_0))
    mixed_1, *saved_1 = attend_forward(order, seq_rows[1], *attention_args(1))
    saved = [saved_0, saved_1]
    out_own, mixed_0, mixed_1 = lax.optimization_barrier((out_own, mixed_0, mixed_1))
    out_other = flip(out_own, "core")
    mixed = jnp.stack([mixed_0, mixed_1]).reshape(micro, n_ctx, tok, heads).transpose(1, 0, 2, 3)
    mixed = exchange(mixed.reshape(n_ctx, all_tok, heads), CTX)
    mixed, w_before, w_after = lax.optimization_barrier((mixed, w_before, w_after))
    mixed = mixed.transpose(1, 0, 2).reshape(all_tok, width)
    out_full = jnp.where(
        core == 0,
        jnp.stack([out_own, out_other], axis=1),
        jnp.stack([out_other, out_own], axis=1),
    ).reshape(width, width)
    middle = tokens.reshape(all_tok, width).astype(F32) + mm(mixed, out_full)
    inv_two = lax.rsqrt(jnp.mean(middle * middle, axis=-1, keepdims=True) + EPS)
    hidden_two = (middle * inv_two * gain_mlp).astype(BF)
    x_0 = exchange.copies(hidden_two[:tok], GROUP, n_ctx)
    w_far = [lax.ppermute(w_before[:1], "z", UP), lax.ppermute(w_after[1:], "z", DOWN)]
    weights = [both_w, w_after, *w_far, w_before]
    x_0, weights = lax.optimization_barrier((x_0, weights))
    x_1 = exchange.copies(hidden_two[tok:], GROUP, n_ctx)
    logits = jnp.where(chosen, mm(hidden_two, router), -1e30)
    gates_all = jnp.where(chosen, jax.nn.softmax(logits, axis=-1), 0.0)

    def experts_of(m, x_own, *moe):
        return run_experts(
            scalars,
            x_own,
            flip(x_own, "core"),
            g_all,
            m,
            router_pad,
            weights,
            cap,
            *moe,
        )

    def back_sum(own, other):
        return add(own, flip(other, "core"))

    def middle_back(back):
        tail = back[:, width:]
        d_gates = tail[:, :experts] + tail[:, 64 : 64 + experts]
        d_select = gates_all * (d_gates - jnp.sum(gates_all * d_gates, axis=-1, keepdims=True))
        d_logits = d_select.astype(BF)
        d_two = back[:, :width] + mm_t(d_logits, router)
        u = d_two * gain_mlp
        d_middle = (
            cot.astype(F32)
            + inv_two * u
            - middle * (inv_two**3 * jnp.mean(u * middle, axis=-1, keepdims=True))
        )
        d_branch = d_middle.astype(BF)
        d_mixed = mm_t(d_branch, out_full).astype(BF)
        d_mixed = d_mixed.reshape(all_tok, n_ctx, heads).transpose(1, 0, 2)
        return d_middle, d_mixed, (d_branch, d_logits, d_two)

    def weight_grads(d_branch, d_logits, d_two):
        grad_mlp = jnp.sum(d_two * middle * inv_two, axis=0)
        return t_mm(mixed, d_branch), t_mm(hidden_two, d_logits), grad_mlp

    def pack_grads(grad_heads, grad_router, grad_attn, grad_mlp, grad_qk):
        grad_qk = jnp.pad(grad_qk[:, None], ((0, 0), (0, rows - 1))).reshape(-1)
        grad_small = jnp.concatenate(
            [grad_router, grad_attn[:, None], grad_mlp[:, None], grad_qk[:, None]], axis=1
        )
        grad_small = jnp.pad(grad_small, ((0, 0), (0, 128 - grad_small.shape[1])))
        grad_pack = jnp.concatenate([grad_heads, grad_small], axis=1).astype(BF)
        return grad_pack.reshape(n_all, rows, -1)

    def attention_back(m, d_mixed, held):
        *d_hidden, grad_heads, grad_attn, grad_qk = attend_backward(
            m, held, order, *saved[m], d_mixed.reshape(length, heads), *attention_args(m)
        )
        grad_qk = jnp.concatenate(
            [grad_qk[0, :DH] + grad_qk[0, DH : 2 * DH], grad_qk[0, 2 * DH : 3 * DH]]
        )
        return d_hidden, (grad_heads, grad_attn[0], grad_qk)

    moe, back_own, back_other, *kept_0 = experts_of(0, x_0)
    x_1, back_own, back_other = lax.optimization_barrier((x_1, back_own, back_other))
    back_0 = back_sum(back_own, back_other)
    x_1 = after_all(x_1, back_0)
    back_0 = exchange(back_0, GROUP)
    moe, back_own, back_other, *kept_1 = experts_of(1, x_1, moe)
    back_0, back_own, back_other, moe = lax.optimization_barrier(
        (back_0, back_own, back_other, moe)
    )
    moe = lax.psum_scatter(moe, FSDP, scatter_dimension=0, tiled=True)[0]
    back_1 = back_sum(back_own, back_other)
    kept_1[0], back_1 = lax.optimization_barrier((kept_1[0], back_1))
    back_1 = exchange(back_1, GROUP)
    parts = expert_grads(order, (kept_0, kept_1))
    far = relay(parts[2])
    back_1, parts = lax.optimization_barrier((back_1, parts))
    d_middle, d_mixed, d_rows = middle_back(
        jnp.concatenate([sum_parts(back_0), sum_parts(back_1)], axis=0)
    )
    d_mixed, far = lax.optimization_barrier((d_mixed, far))
    d_mixed = exchange(d_mixed, CTX)
    d_mixed, far = lax.optimization_barrier((d_mixed, far))
    moved = ring_sums(parts, far)
    d_mixed = d_mixed.reshape(n_ctx, micro, tok, heads)
    d_hidden, head_grads_0 = attention_back(0, d_mixed[:, 0], [])
    d_hidden, head_grads_1 = attention_back(1, d_mixed[:, 1], d_hidden)
    d_hidden, moved, d_rows = lax.optimization_barrier((d_hidden, moved, d_rows))
    hidden_moved = by_z(d_hidden)
    grad_out, grad_router, grad_mlp = weight_grads(*d_rows)
    grad_heads, grad_attn, grad_qk = jax.tree.map(jnp.add, head_grads_0, head_grads_1)
    grad_pack = pack_grads(grad_heads, grad_router, grad_attn, grad_mlp, grad_qk)
    grad_pack = exchange(grad_pack, ALL)
    grad_out = grad_out.astype(BF).reshape(n_all // 2, 2, rows, width)
    grad_own = lax.dynamic_index_in_dim(grad_out, core, axis=1, keepdims=False)
    grad_other = lax.dynamic_index_in_dim(grad_out, 1 - core, axis=1, keepdims=False)
    grad_out = back_sum(grad_own, grad_other)
    weight_sums = pair_sums(parts, moved)
    weight_yl = flip(weight_sums[1].astype(BF), "yl")
    grad_pack, grad_out, weight_yl = lax.optimization_barrier((grad_pack, grad_out, weight_yl))
    exchange.last = grad_pack
    grad_out = exchange(grad_out, CTX + GROUP)
    hidden_sums = [
        sum(part[:, i].astype(F32) for part in [d_hidden[0]] + hidden_moved) for i in range(2)
    ]
    hidden_yl = flip(hidden_sums[1].astype(BF), "yl")
    grad_out, hidden_yl = lax.optimization_barrier((grad_out, hidden_yl))

    grad_pack = grad_pack.astype(F32)
    own_heads = jnp.sum(grad_pack[:, :, :span].reshape(n_ctx, n_fsdp, rows, -1), axis=1)
    own_heads = own_heads.transpose(1, 0, 2)
    own_small = jnp.sum(grad_pack[:, :, span:], axis=0)
    own_out = sum_parts(grad_out)
    moe = after_all(moe, grad_pack)
    d_hidden = (hidden_sums[0] + hidden_yl.astype(F32)).reshape(all_tok, width)
    expert_own = weight_sums[0] + weight_yl.astype(F32)
    out = (middle.reshape(moe.shape) + moe.astype(F32)).astype(BF)
    start = tokens.reshape(all_tok, width).astype(F32)
    inv_one = lax.rsqrt(jnp.mean(start * start, axis=-1, keepdims=True) + EPS)
    u = d_hidden * gain_attn
    d_input = (
        d_middle
        + inv_one * u
        - start * (inv_one**3 * jnp.mean(u * start, axis=-1, keepdims=True))
    )

    return (
        out[:, None],
        d_input.reshape(tokens.shape),
        own_heads[:, :, :heads].reshape(rows, -1),
        own_heads[:, :, heads : heads + DH].reshape(rows, -1),
        own_heads[:, :, heads + DH :].reshape(rows, -1),
        own_out,
        own_small[:, :experts],
        own_small[:, experts],
        own_small[:, experts + 1],
        own_small[:1, experts + 2],
        expert_own[:, 0],
        expert_own[:, 1],
        expert_own[:, 2],
    )


def solution(mesh):
    mesh = Mesh(mesh.devices.reshape(4, 2, 2, 4, 2), ALL)
    weight = P(ALL, None)
    gain = P(ALL)
    rows = P(None, FSDP, CTX, None)
    expert = P(FSDP, CTX, None)
    return jax.shard_map(
        body,
        mesh=mesh,
        in_specs=(rows, P(None, FSDP, None), rows)
        + (weight,) * 5
        + (gain,) * 3
        + (expert,) * 3
        + (rows,),
        out_specs=(rows, rows) + (weight,) * 5 + (gain,) * 3 + (expert,) * 3,
        check_vma=False,
    )
```

```python
import functools

import jax
import jax.numpy as jnp
from jax import lax
from jax.experimental import pallas as pl
from jax.experimental.pallas import tpu as pltpu
from jax.sharding import Mesh
from jax.sharding import PartitionSpec as P

BF = jnp.bfloat16
F32 = jnp.float32
H = 16
KV = 8
DH = 64
TOPK = 8
WINDOW = 1024
EPS = 1e-06
THETA = 10000.0
COST = pl.CostEstimate(flops=10**7, bytes_accessed=10**5, transcendentals=0)


def dot(a, b, ca, cb):
    return lax.dot_general(a, b, (((ca,), (cb,)), ((), ())), preferred_element_type=F32)


def lanes_of(v):
    return lax.broadcasted_iota(jnp.int32, v.shape, v.ndim - 1)


def head_sums(v):
    low = lanes_of(v) < DH
    first = jnp.sum(jnp.where(low, v, 0.0), axis=1, keepdims=True)
    second = jnp.sum(jnp.where(low, 0.0, v), axis=1, keepdims=True)
    return jnp.where(low, first, second)


def trade(v):
    return jnp.where(
        lanes_of(v) % DH < DH // 2, pltpu.roll(v, 128 - DH // 2, 1), pltpu.roll(v, DH // 2, 1)
    )


def both_halves(v, second):
    low = lanes_of(v) < DH
    other = pltpu.roll(v, DH, 1)
    return jnp.where(low, other, v) if second else jnp.where(low, v, other)


def stack_heads(v):
    low = lanes_of(v) < DH
    zero = jnp.zeros_like(v)
    return jnp.concatenate([jnp.where(low, v, zero), jnp.where(low, zero, v)], axis=0)


def key_span(start, block, length):
    reach = WINDOW // 2 - 1
    low = max(0, start - reach) // 128 * 128
    high = min(length, -(-(start + block + reach) // 128) * 128)
    return low, high


def masked_probs(q_two, keys, seg_col, seg_row, start, low):
    block = q_two.shape[0] // 2
    scores = dot(q_two, keys, 1, 1)
    shape = (block, keys.shape[0])
    gap = (
        lax.broadcasted_iota(jnp.int32, shape, 0)
        - lax.broadcasted_iota(jnp.int32, shape, 1)
        + (start - low)
    )
    allowed = (seg_col == seg_row) & (jnp.abs(gap) < WINDOW // 2)
    bias = jnp.where(allowed, 0.0, -1e30)
    scores = scores + jnp.concatenate([bias, bias], axis=0)
    raised = jnp.exp(scores - jnp.max(scores, axis=1, keepdims=True))
    return raised * (1.0 / jnp.sum(raised, axis=1, keepdims=True))


def attend_kernel(
    order_ref,
    *refs,
):
    pieces, refs = refs[:-13], refs[-13:]
    gain_ref, w_ref, head_gain_ref, cos_ref, sin_ref, seg_col_ref, seg_row_ref = refs[:7]
    mixed_ref, hidden_ref, q_ref, kv_ref, keys_ref, values_ref = refs[7:]
    tok, width = pieces[0].shape[1:]
    length = hidden_ref.shape[0]
    pieces = [(ref, i) for ref in pieces for i in range(ref.shape[0])]
    for r, (ref, i) in enumerate(pieces):
        x = ref[i].astype(F32)
        x = x * lax.rsqrt(jnp.mean(x * x, axis=1, keepdims=True) + EPS) * gain_ref[...]
        rows = pl.ds(pl.multiple_of(order_ref[r] * tok, tok), tok)
        hidden_ref[rows] = x.astype(BF)
    raw = dot(hidden_ref[...], w_ref[...], 1, 0)
    for half in range(2):
        u = raw[:, half * 128 : half * 128 + 128]
        gain = head_gain_ref[:, half * 128 : half * 128 + 128]
        n = u * lax.rsqrt(head_sums(u * u) * (1.0 / DH) + EPS) * gain
        turned = n * cos_ref[...] + trade(n) * sin_ref[...]
        if half == 0:
            q_ref[...] = turned.astype(BF)
        else:
            kv = jnp.where(lanes_of(u) < DH, turned, u)
            kv_ref[...] = kv.astype(BF)
            keys_ref[...] = both_halves(kv, False).astype(BF)
            values_ref[...] = both_halves(kv, True).astype(BF)
    block = 256
    for start in range(0, length, block):
        low, high = key_span(start, block, length)
        q_two = stack_heads(q_ref[start : start + block].astype(F32) * DH**-0.5).astype(BF)
        probs = masked_probs(
            q_two,
            keys_ref[low:high],
            seg_col_ref[start : start + block],
            seg_row_ref[:, low:high],
            start,
            low,
        )
        result = dot(probs.astype(BF), values_ref[low:high], 1, 0)
        first = lanes_of(result[:block]) < DH
        mixed_ref[start : start + block] = jnp.where(first, result[:block], result[block:]).astype(
            BF
        )


def attend_back_kernel(order_ref, *refs, again):
    hidden_ref, q_ref, kv_ref, d_mixed_ref, gain_ref, w_ref, head_gain_ref = refs[:7]
    cos_ref, sin_ref, seg_col_ref, seg_row_ref = refs[7:11]
    refs = refs[15:] if again else refs[11:]
    outs, refs = refs[:4], refs[4:]
    grad_w_ref, grad_gain_ref, grad_heads_ref = refs[:3]
    keys_ref, values_ref, d_q_ref, d_k_ref, d_v_ref, d_raw_ref = refs[3:]
    length = hidden_ref.shape[0]
    kv = kv_ref[...].astype(F32)
    keys_ref[...] = both_halves(kv, False).astype(BF)
    values_ref[...] = both_halves(kv, True).astype(BF)
    d_k_ref[...] = jnp.zeros_like(d_k_ref)
    d_v_ref[...] = jnp.zeros_like(d_v_ref)
    block = 256
    for start in range(0, length, block):
        low, high = key_span(start, block, length)
        q_two = stack_heads(q_ref[start : start + block].astype(F32) * DH**-0.5).astype(BF)
        m_two = stack_heads(d_mixed_ref[start : start + block].astype(F32)).astype(BF)
        probs = masked_probs(
            q_two,
            keys_ref[low:high],
            seg_col_ref[start : start + block],
            seg_row_ref[:, low:high],
            start,
            low,
        )
        d_probs = dot(m_two, values_ref[low:high], 1, 1)
        inner = jnp.sum(probs * d_probs, axis=1, keepdims=True)
        d_scores = (probs * (d_probs - inner)).astype(BF)
        result = dot(d_scores, keys_ref[low:high], 1, 0)
        first = lanes_of(result[:block]) < DH
        d_q_ref[start : start + block] = jnp.where(first, result[:block], result[block:]) * (
            DH**-0.5
        )
        d_k_ref[low:high] += dot(d_scores, q_two, 0, 0)
        d_v_ref[low:high] += dot(probs.astype(BF), m_two, 0, 0)
    raw = dot(hidden_ref[...], w_ref[...], 1, 0)
    d_k = d_k_ref[...]
    d_k = d_k + pltpu.roll(d_k, DH, 1)
    d_v = d_v_ref[...]
    d_v = d_v + pltpu.roll(d_v, DH, 1)
    for half in range(2):
        lanes = slice(half * 128, half * 128 + 128)
        u = raw[:, lanes]
        gain = head_gain_ref[:, lanes]
        d = d_q_ref[...] if half == 0 else d_k
        d = d * cos_ref[...] + trade(d * sin_ref[...])
        r = lax.rsqrt(head_sums(u * u) * (1.0 / DH) + EPS)
        grad_heads_ref[:, lanes] = jnp.sum(d * u * r, axis=0, keepdims=True)
        d = d * gain
        d = d * r - u * (r * r * r * (head_sums(d * u) * (1.0 / DH)))
        if half == 1:
            d = jnp.where(lanes_of(d) < DH, d, d_v)
        d_raw_ref[:, lanes] = d.astype(BF)
    grad_w_ref[...] = dot(hidden_ref[...], d_raw_ref[...], 0, 0)
    total = jnp.zeros(grad_gain_ref.shape, F32)
    tok = length // 8
    for step in range(4):
        rows = pl.ds(pl.multiple_of(order_ref[2 * step] // 2 * (2 * tok), 2 * tok), 2 * tok)
        d_hidden = dot(d_raw_ref[rows], w_ref[...], 1, 1)
        own = order_ref[0] % 2
        outs[step][0, own] = d_hidden[:tok].astype(BF)
        outs[step][0, 1 - own] = d_hidden[tok:].astype(BF)
        total = total + jnp.sum(d_hidden * hidden_ref[rows].astype(F32), axis=0, keepdims=True)
    grad_gain_ref[...] = total / gain_ref[...]


def whole(a):
    return pl.BlockSpec(a.shape, lambda i: (0,) * len(a.shape), pipeline_mode=pl.Buffered(1))


def attend_forward(order, pieces, gain, w_heads, head_gain, cosine, sine, seg_col, seg_row):
    length = cosine.shape[0]
    width = w_heads.shape[0]
    shape = jax.ShapeDtypeStruct
    outs = [
        shape((length, 128), BF),
        shape((length, width), BF),
        shape((length, 128), BF),
        shape((length, 128), BF),
    ]
    args = list(pieces) + [gain, w_heads, head_gain, cosine, sine, seg_col, seg_row]
    return pl.pallas_call(
        attend_kernel,
        out_shape=outs,
        grid=(1,),
        in_specs=[pl.BlockSpec(memory_space=pltpu.SMEM)] + [whole(a) for a in args],
        out_specs=[whole(o) for o in outs],
        scratch_shapes=[pltpu.VMEM((length, 128), BF), pltpu.VMEM((length, 128), BF)],
        compiler_params=pltpu.CompilerParams(vmem_limit_bytes=40 * 1024 * 1024),
        cost_estimate=COST,
    )(order, *args)


def attend_backward(micro, held, order, *args):
    length, width = args[0].shape
    shape = jax.ShapeDtypeStruct
    outs = [shape((2, 2, length // 8, width), BF)] * 4 + [
        shape((width, 256), F32),
        shape((1, width), F32),
        shape((1, 256), F32),
    ]
    part = pl.BlockSpec(
        (1, 2, length // 8, width), lambda i: (micro, 0, 0, 0), pipeline_mode=pl.Buffered(1)
    )
    return pl.pallas_call(
        functools.partial(attend_back_kernel, again=len(held) > 0),
        out_shape=outs,
        grid=(1,),
        in_specs=[pl.BlockSpec(memory_space=pltpu.SMEM)]
        + [whole(a) for a in args]
        + [pl.BlockSpec(memory_space=pl.ANY)] * len(held),
        out_specs=[part] * 4 + [whole(o) for o in outs[4:]],
        input_output_aliases={1 + len(args) + n: n for n in range(len(held))},
        scratch_shapes=[pltpu.VMEM((length, 128), BF)] * 2
        + [pltpu.VMEM((length, 128), F32)] * 3
        + [pltpu.VMEM((length, 256), BF)],
        compiler_params=pltpu.CompilerParams(vmem_limit_bytes=40 * 1024 * 1024),
        cost_estimate=COST,
    )(order, *args, *held)


def halves(v):
    high = v.astype(BF)
    return high, (v - high.astype(F32)).astype(BF)


def expert_kernel(scalar_ref, *refs, again):
    x_own_ref, x_other_ref, g_ref, router_ref = refs[:4]
    pieces, refs = refs[4:12], refs[12:]
    if again:
        refs = refs[1:]
    out_ref, back_own_ref, back_other_ref = refs[:3]
    kept_refs, refs = refs[3:8], refs[8:]
    xe_ref, de_ref, act_ref, da_ref, db_ref, *refs = refs
    pick_ref, weight_ref, dgate_ref, eo_ref, dr_ref, w_ref, in_sem, out_sem = refs
    half, tok, width = x_own_ref.shape
    sources = 2 * half
    core = scalar_ref[1]
    depth = w_ref.shape[2] // 8

    loads = []
    for r, ref in enumerate(pieces):
        rows = pl.ds(pl.multiple_of(scalar_ref[2 + r] * depth, depth), depth)
        loads.append(pltpu.make_async_copy(ref.at[0], w_ref.at[:, :, rows], in_sem.at[r]))
        loads[-1].start()
    local, slots, hidden = act_ref.shape
    cap = slots // sources
    first = scalar_ref[0]
    lane = lax.broadcasted_iota(jnp.int32, (tok, 128), 1)
    spot = lax.broadcasted_iota(jnp.int32, (tok, local * cap), 1)
    row_expert = lax.broadcasted_iota(jnp.int32, (local * cap, 128), 0) // cap
    slot_lane = lax.broadcasted_iota(jnp.int32, (local * cap, 128), 1)
    own_lane = slot_lane == first + row_expert

    def fetch(i, carry, x_ref, offset, column):
        s = i + offset
        x = x_ref[i]
        from_g = 2 * i + column
        held = g_ref[from_g, :, width:].astype(F32)
        chosen = held >= 0.0
        logits = jnp.where(chosen, dot(x, router_ref[...], 1, 0), -1e30)
        top = jnp.max(logits, axis=1, keepdims=True)
        raised = jnp.where(chosen, jnp.exp(logits - top), 0.0)
        gates = raised / jnp.sum(raised, axis=1, keepdims=True)
        pick = jnp.zeros((tok, local * cap), F32)
        for e in range(local):
            mine = jnp.max(jnp.where(lane == first + e, held, -1.0), axis=1, keepdims=True)
            goal = jnp.where(mine >= 0.0, mine + e * cap, -1.0).astype(jnp.int32)
            pick = jnp.where(spot == goal, 1.0, pick)
        pick = pick.astype(BF)
        pick_ref[s] = pick
        rows = pl.ds(pl.multiple_of(s * cap, 16), cap)
        x_slots = dot(pick, x, 0, 0).astype(BF)
        g_slots = dot(pick, g_ref[from_g, :, :width], 0, 0).astype(BF)
        high, low = halves(gates)
        weight = dot(pick, high, 0, 0) + dot(pick, low, 0, 0)
        weight = jnp.sum(jnp.where(own_lane, weight, 0.0), axis=1, keepdims=True)
        for e in range(local):
            part = slice(e * cap, (e + 1) * cap)
            xe_ref[e, rows] = x_slots[part]
            de_ref[e, rows] = g_slots[part]
            weight_ref[e, rows] = weight[part]
        return carry

    for x_ref, offset, column in ((x_own_ref, 0, core), (x_other_ref, half, 1 - core)):
        step = functools.partial(fetch, x_ref=x_ref, offset=offset, column=column)
        lax.fori_loop(0, half, step, 0, unroll=4)
    for load in loads:
        load.wait()
    chunk = 384

    def work(i, carry):
        e = i // (slots // chunk)
        rows = pl.ds(pl.multiple_of((i % (slots // chunk)) * chunk, chunk), chunk)
        w_gate = w_ref[e, 0]
        w_up = w_ref[e, 1]
        w_down = w_ref[e, 2]
        x = xe_ref[e, rows]
        a = dot(x, w_gate, 1, 0)
        b = dot(x, w_up, 1, 0)
        sig = 1.0 / (1.0 + jnp.exp(-a))
        silu = a * sig
        active = (silu * b).astype(BF)
        act_ref[e, rows] = active
        slope = b * (sig * (1.0 + a * (1.0 - sig)))
        weight = weight_ref[e, rows]
        g = de_ref[e, rows].astype(F32)
        result = dot(active, w_down, 1, 1).astype(BF).astype(F32)
        dgate_ref[e, rows] = jnp.sum(result * g, axis=1, keepdims=True)
        eo_ref[e, rows] = (weight * result).astype(BF)
        d_expert = (weight * g).astype(BF)
        de_ref[e, rows] = d_expert
        d_active = dot(d_expert, w_down, 1, 0)
        da = (d_active * slope).astype(BF)
        db = (d_active * silu).astype(BF)
        da_ref[e, rows] = da
        db_ref[e, rows] = db
        dr_ref[e, rows] = (dot(da, w_gate, 1, 1) + dot(db, w_up, 1, 1)).astype(BF)
        return carry

    lax.fori_loop(0, local * (slots // chunk), work, 0)
    stores = [
        pltpu.make_async_copy(ref, kept, out_sem.at[n])
        for n, (ref, kept) in enumerate(
            zip((xe_ref, de_ref, act_ref, da_ref, db_ref), kept_refs)
        )
    ]
    for store in stores:
        store.start()

    def give(i, carry, back_ref, offset, column):
        s = i + offset
        rows = pl.ds(pl.multiple_of(s * cap, 16), cap)
        pick = pick_ref[s]
        eo = jnp.concatenate([eo_ref[e, rows] for e in range(local)], axis=0)
        dr = jnp.concatenate([dr_ref[e, rows] for e in range(local)], axis=0)
        dgate = jnp.concatenate([dgate_ref[e, rows] for e in range(local)], axis=0)
        high, low = halves(dgate)
        spread = jnp.where(own_lane, high.astype(F32), 0.0) + jnp.where(
            slot_lane == first + row_expert + 64, low.astype(F32), 0.0
        )
        out_ref[2 * i + column, 0] = dot(pick, eo, 1, 0).astype(BF)
        back_ref[i, :, :width] = dot(pick, dr, 1, 0).astype(BF)
        back_ref[i, :, width:] = dot(pick, spread.astype(BF), 1, 0).astype(BF)
        return carry

    for back_ref, offset, column in ((back_own_ref, 0, core), (back_other_ref, half, 1 - core)):
        step = functools.partial(give, back_ref=back_ref, offset=offset, column=column)
        lax.fori_loop(0, half, step, 0, unroll=4)
    for store in stores:
        store.wait()


def run_experts(scalars, x_own, x_other, g_all, micro, router, pieces, cap, moe=None):
    half, tok, width = x_own.shape
    sources = 2 * half
    _, local, _, _, hidden = pieces[0].shape
    slots = sources * cap
    wide = g_all.shape[2]
    shape = jax.ShapeDtypeStruct
    outs = [
        shape((sources, 2, tok, width), BF),
        shape((half, tok, wide), BF),
        shape((half, tok, wide), BF),
        shape((local, slots, width), BF),
        shape((local, slots, width), BF),
        shape((local, slots, hidden), BF),
        shape((local, slots, hidden), BF),
        shape((local, slots, hidden), BF),
    ]
    g_spec = pl.BlockSpec(
        (sources, tok, wide), lambda i: (0, micro, 0), pipeline_mode=pl.Buffered(1)
    )
    args = list(pieces)
    any_place = pl.BlockSpec(memory_space=pl.ANY)
    held = [] if moe is None else [moe]
    moe_spec = pl.BlockSpec(
        (sources, 1, tok, width), lambda i: (0, micro, 0, 0), pipeline_mode=pl.Buffered(1)
    )
    return pl.pallas_call(
        functools.partial(expert_kernel, again=moe is not None),
        out_shape=outs,
        grid=(1,),
        in_specs=[pl.BlockSpec(memory_space=pltpu.SMEM), whole(x_own), whole(x_other), g_spec]
        + [whole(router)]
        + [any_place] * (len(args) + len(held)),
        out_specs=[moe_spec] + [whole(o) for o in outs[1:3]] + [any_place] * 5,
        input_output_aliases={5 + len(args): 0} if held else {},
        scratch_shapes=[pltpu.VMEM(o.shape, o.dtype) for o in outs[3:]]
        + [
            pltpu.VMEM((sources, tok, local * cap), BF),
            pltpu.VMEM((local, slots, 1), F32),
            pltpu.VMEM((local, slots, 1), F32),
            pltpu.VMEM((local, slots, width), BF),
            pltpu.VMEM((local, slots, width), BF),
            pltpu.VMEM((local, 3, width, hidden), BF),
            pltpu.SemaphoreType.DMA((8,)),
            pltpu.SemaphoreType.DMA((5,)),
        ],
        compiler_params=pltpu.CompilerParams(vmem_limit_bytes=60 * 1024 * 1024),
        cost_estimate=COST,
    )(scalars, x_own, x_other, g_all, router, *args, *held)


def expert_grad_kernel(order_ref, *refs):
    kept, outs, total_ref = refs[:10], refs[10:14], refs[14]
    left = (kept[0:2], kept[0:2], kept[2:4])
    right = (kept[6:8], kept[8:10], kept[4:6])
    step = pl.program_id(0)
    depth = outs[0].shape[3]
    for kind in range(3):

        @pl.when(step % 3 == kind)
        def _(kind=kind):
            total = dot(left[kind][0][0], right[kind][0][0], 0, 0)
            total_ref[...] = total + dot(left[kind][1][0], right[kind][1][0], 0, 0)

    for r in range(8):
        rows = pl.ds(pl.multiple_of(order_ref[r] * depth, depth), depth)
        outs[r // 2][r % 2, 0, 0] = total_ref[rows].astype(BF)


def expert_grads(order, kept):
    local, slots, width = kept[0][0].shape
    hidden = kept[0][2].shape[2]
    args = [kept[m][i] for i in range(5) for m in range(2)]
    depth = width // 8
    shape = jax.ShapeDtypeStruct
    return pl.pallas_call(
        expert_grad_kernel,
        out_shape=[shape((2, local, 3, depth, hidden), BF)] * 4,
        grid=(3 * local,),
        in_specs=[pl.BlockSpec(memory_space=pltpu.SMEM)]
        + [pl.BlockSpec((1,) + a.shape[1:], lambda i: (i // 3, 0, 0)) for a in args],
        out_specs=[
            pl.BlockSpec((2, 1, 1, depth, hidden), lambda i: (0, i // 3, i % 3, 0, 0))
        ]
        * 4,
        scratch_shapes=[pltpu.VMEM((width, hidden), F32)],
        compiler_params=pltpu.CompilerParams(vmem_limit_bytes=48 * 1024 * 1024),
        cost_estimate=COST,
    )(order, *args)


CTX = ("z", "yl")
GROUP = ("yh", "x")
FSDP = ("yh", "x", "core")
ALL = CTX + FSDP
UP = [(i, (i + 1) % 4) for i in range(4)]
DOWN = [(i, (i - 1) % 4) for i in range(4)]
TWO = [(i, (i + 2) % 4) for i in range(4)]
FLIP = [(0, 1), (1, 0)]


def mm(a, b):
    return jnp.dot(a, b, preferred_element_type=F32)


def mm_t(a, b):
    return lax.dot_general(a, b, (((1,), (1,)), ((), ())), preferred_element_type=F32)


def t_mm(a, b):
    return lax.dot_general(a, b, (((0,), (0,)), ((), ())), preferred_element_type=F32)


def ein(spec, a, b):
    return jnp.einsum(spec, a, b, preferred_element_type=F32)


def swap(parts, axis):
    return lax.all_to_all(parts, axis, split_axis=0, concat_axis=0, tiled=True)


def flip(block, axis):
    return lax.ppermute(block, axis, FLIP)


def by_z(parts):
    return [lax.ppermute(parts[k], "z", perm) for k, perm in ((1, UP), (2, TWO), (3, DOWN))]


def along_z(both):
    before, far, after = by_z([both] * 4)
    return [both, after, far, before]


class Exchange:
    def __init__(self):
        self.last = None

    def __call__(self, parts, axis):
        if self.last is not None:
            parts = after_all(parts, self.last)
        self.last = swap(parts, axis)
        return self.last

    def copies(self, block, axis, count):
        return self(jnp.broadcast_to(block[None], (count,) + block.shape), axis)


def add(a, b):
    return (a.astype(F32) + b.astype(F32)).astype(BF)


def add_part(parts, i, more):
    pieces = [parts[:1], parts[1:]]
    pieces[i] = add(pieces[i], more)
    return jnp.concatenate(pieces, axis=0)


def relay(far):
    return [lax.ppermute(far[:1], "z", UP), lax.ppermute(far[1:], "z", DOWN)]


def ring_sums(parts, far):
    return [
        lax.ppermute(add_part(parts[1], 0, far[0]), "z", UP),
        lax.ppermute(add_part(parts[3], 1, far[1]), "z", DOWN),
    ]


def pair_sums(parts, moved):
    return [sum(part[i].astype(F32) for part in [parts[0]] + moved) for i in range(2)]


def sum_parts(parts):
    return jnp.sum(parts.astype(F32), axis=0)


def after_all(value, *others):
    return lax.optimization_barrier((value,) + others)[0]


def rope_tables(positions):
    half = DH // 2
    inverse = THETA ** (-(jnp.arange(half, dtype=F32) * 2.0) / DH)
    angles = positions.astype(F32)[:, None] * inverse[None, :]
    return (jnp.cos(angles), jnp.sin(angles))


def rms_scale(values, gain):
    return values * lax.rsqrt(jnp.mean(values * values, axis=-1, keepdims=True) + EPS) * gain


def body(
    tokens,
    segments,
    routes,
    w_query,
    w_key,
    w_value,
    w_out,
    w_router,
    attn_gain,
    mlp_gain,
    qk_gain,
    w_gate,
    w_up,
    w_down,
    cotangent,
):
    micro = tokens.shape[0]
    tok = tokens.shape[2]
    width = tokens.shape[3]
    length = segments.shape[2]
    rows = w_query.shape[0]
    n_ctx, n_fsdp = 8, 16
    n_all = n_ctx * n_fsdp
    z, yl, yh, x, core = (lax.axis_index(name) for name in ALL)
    shard = (yh * 4 + x) * 2 + core
    local = w_gate.shape[0]
    experts = local * n_fsdp
    cap = (3 * tok * TOPK + 2 * experts - 1) // (2 * experts)
    all_tok = micro * tok
    ratio = H // KV
    heads = ratio * DH
    span = heads + 2 * DH

    exchange = Exchange()
    small = jnp.concatenate(
        [
            w_router,
            attn_gain[:, None],
            mlp_gain[:, None],
            jnp.pad(qk_gain[:, None], ((0, rows - 1), (0, 0))),
        ],
        axis=1,
    )
    small = jnp.pad(small, ((0, 0), (0, 128 - small.shape[1])))
    pieces = jnp.concatenate(
        [
            w_query.reshape(rows, n_ctx, heads),
            w_key.reshape(rows, n_ctx, DH),
            w_value.reshape(rows, n_ctx, DH),
            jnp.broadcast_to(small[:, None], (rows, n_ctx, 128)),
        ],
        axis=2,
    ).transpose(1, 0, 2)
    pieces = jnp.broadcast_to(pieces[:, None], (n_ctx, n_fsdp) + pieces.shape[1:])
    both_0, both_1 = (
        jnp.concatenate([tokens[m], flip(tokens[m], "yl")], axis=0) for m in range(micro)
    )
    own_w = jnp.stack([w_gate, w_up, w_down], axis=1)[None]
    own_before = lax.ppermute(own_w, "z", UP)
    own_after = lax.ppermute(own_w, "z", DOWN)
    both_0 = after_all(both_0, own_before, own_after)
    head_all = exchange(pieces.reshape((n_all,) + pieces.shape[2:]), ALL).reshape(width, -1)
    other_w = flip(own_w, "yl")
    seq_rows = [along_z(both_0)]
    seq_rows.append(along_z(after_all(both_1, *seq_rows[0][1:])))
    head_all = after_all(head_all, *seq_rows[0][1:], other_w)
    w_heads = head_all[:, :span]
    small_all = head_all[:, span:]
    router = small_all[:, :experts]
    small_wide = small_all.astype(F32)
    gain_attn = small_wide[:, experts]
    gain_mlp = small_wide[:, experts + 1]
    gain_heads = small_wide[:, experts + 2].reshape(-1, rows)[:, 0]
    gain_row = gain_attn[None]
    head_row = jnp.concatenate(
        [gain_heads[:DH]] * ratio + [gain_heads[DH:], jnp.ones((DH,), F32)]
    )[None]
    router_pad = jnp.pad(router, ((0, 0), (0, 128 - experts)))

    out_own = exchange.copies(after_all(w_out, *seq_rows[0][1:]), CTX + GROUP, n_all // 2)

    expert_ids = jnp.arange(experts, dtype=jnp.int32)
    cot = cotangent.reshape(all_tok, width)
    chosen = jnp.any(routes.reshape(all_tok, TOPK)[:, :, None] == expert_ids, axis=1)
    before = jnp.arange(tok, dtype=jnp.int32)
    lower = (before[:, None] >= before[None, :]).astype(BF)
    counts = ein("ut,mte->mue", lower, chosen.reshape(micro, tok, experts).astype(BF))
    held = jnp.where(chosen, counts.reshape(all_tok, experts) - 1.0, -1.0)
    held = jnp.pad(held, ((0, 0), (0, 128 - experts)), constant_values=-1.0).astype(BF)
    pack = after_all(jnp.concatenate([cot, held], axis=1), both_0, both_1)
    g_all = lax.all_gather(pack, FSDP, axis=0)

    cosine, sine = rope_tables(jnp.arange(length, dtype=jnp.int32))
    cosine = jnp.tile(cosine, (1, 4))
    sine = jnp.tile(jnp.concatenate([-sine, sine], axis=1), (1, 2))
    rel = jnp.arange(n_ctx, dtype=jnp.int32)
    order = ((z + rel // 2) % 4) * 2 + (yl + rel % 2) % 2
    scalars = jnp.concatenate([jnp.stack([shard * local, core]), order]).astype(jnp.int32)

    def to_owner(v):
        return exchange(v.reshape(n_ctx, tok, -1), CTX)

    def attention_args(m):
        seg = segments[m, 0]
        return gain_row, w_heads, head_row, cosine, sine, seg[:, None], seg[None, :]

    mixed_0, *saved_0 = attend_forward(order, seq_rows[0], *attention_args(0))
    seq_rows[1], mixed_0 = lax.optimization_barrier((seq_rows[1], mixed_0))
    late_w = after_all(other_w, *seq_rows[1][1:])
    other_before = lax.ppermute(late_w, "z", UP)
    other_after = lax.ppermute(late_w, "z", DOWN)
    own_far = lax.ppermute(after_all(own_before, other_before), "z", UP)
    other_far = lax.ppermute(other_after, "z", DOWN)
    mixed_1, *saved_1 = attend_forward(order, seq_rows[1], *attention_args(1))
    saved = [saved_0, saved_1]
    out_own, mixed_0, mixed_1 = lax.optimization_barrier((out_own, mixed_0, mixed_1))
    out_other = flip(out_own, "core")
    mixed = jnp.stack([mixed_0, mixed_1]).reshape(micro, n_ctx, tok, heads).transpose(1, 0, 2, 3)
    mixed = exchange(mixed.reshape(n_ctx, all_tok, heads), CTX)
    mixed, other_before, other_after = lax.optimization_barrier(
        (mixed, other_before, other_after)
    )
    mixed = mixed.transpose(1, 0, 2).reshape(all_tok, width)
    out_full = jnp.where(
        core == 0,
        jnp.stack([out_own, out_other], axis=1),
        jnp.stack([out_other, out_own], axis=1),
    ).reshape(width, width)
    middle = tokens.reshape(all_tok, width).astype(F32) + mm(mixed, out_full)
    inv_two = lax.rsqrt(jnp.mean(middle * middle, axis=-1, keepdims=True) + EPS)
    hidden_two = (middle * inv_two * gain_mlp).astype(BF)
    x_0 = exchange.copies(hidden_two[:tok], GROUP, n_ctx)
    weights = [own_w, other_w, own_after, other_after, own_far, other_far, own_before, other_before]
    x_0, weights = lax.optimization_barrier((x_0, weights))
    x_1 = exchange.copies(hidden_two[tok:], GROUP, n_ctx)
    logits = jnp.where(chosen, mm(hidden_two, router), -1e30)
    gates_all = jnp.where(chosen, jax.nn.softmax(logits, axis=-1), 0.0)

    def experts_of(m, x_own, *moe):
        return run_experts(
            scalars,
            x_own,
            flip(x_own, "core"),
            g_all,
            m,
            router_pad,
            weights,
            cap,
            *moe,
        )

    def back_sum(own, other):
        return add(own, flip(other, "core"))

    def middle_back(back):
        tail = back[:, width:]
        d_gates = tail[:, :experts] + tail[:, 64 : 64 + experts]
        d_select = gates_all * (d_gates - jnp.sum(gates_all * d_gates, axis=-1, keepdims=True))
        d_logits = d_select.astype(BF)
        d_two = back[:, :width] + mm_t(d_logits, router)
        u = d_two * gain_mlp
        d_middle = (
            cot.astype(F32)
            + inv_two * u
            - middle * (inv_two**3 * jnp.mean(u * middle, axis=-1, keepdims=True))
        )
        d_branch = d_middle.astype(BF)
        d_mixed = mm_t(d_branch, out_full).astype(BF)
        d_mixed = d_mixed.reshape(all_tok, n_ctx, heads).transpose(1, 0, 2)
        return d_middle, d_mixed, (d_branch, d_logits, d_two)

    def weight_grads(d_branch, d_logits, d_two):
        grad_mlp = jnp.sum(d_two * middle * inv_two, axis=0)
        return t_mm(mixed, d_branch), t_mm(hidden_two, d_logits), grad_mlp

    def pack_grads(grad_heads, grad_router, grad_attn, grad_mlp, grad_qk):
        grad_qk = jnp.pad(grad_qk[:, None], ((0, 0), (0, rows - 1))).reshape(-1)
        grad_small = jnp.concatenate(
            [grad_router, grad_attn[:, None], grad_mlp[:, None], grad_qk[:, None]], axis=1
        )
        grad_small = jnp.pad(grad_small, ((0, 0), (0, 128 - grad_small.shape[1])))
        grad_pack = jnp.concatenate([grad_heads, grad_small], axis=1).astype(BF)
        return grad_pack.reshape(n_all, rows, -1)

    def attention_back(m, d_mixed, held):
        *d_hidden, grad_heads, grad_attn, grad_qk = attend_backward(
            m, held, order, *saved[m], d_mixed.reshape(length, heads), *attention_args(m)
        )
        grad_qk = jnp.concatenate(
            [grad_qk[0, :DH] + grad_qk[0, DH : 2 * DH], grad_qk[0, 2 * DH : 3 * DH]]
        )
        return d_hidden, (grad_heads, grad_attn[0], grad_qk)

    moe, back_own, back_other, *kept_0 = experts_of(0, x_0)
    x_1, back_own, back_other = lax.optimization_barrier((x_1, back_own, back_other))
    back_0 = back_sum(back_own, back_other)
    x_1 = after_all(x_1, back_0)
    back_0 = exchange(back_0, GROUP)
    moe, back_own, back_other, *kept_1 = experts_of(1, x_1, moe)
    back_0, back_own, back_other, moe = lax.optimization_barrier(
        (back_0, back_own, back_other, moe)
    )
    moe = lax.psum_scatter(moe, FSDP, scatter_dimension=0, tiled=True)[0]
    back_1 = back_sum(back_own, back_other)
    kept_1[0], back_1 = lax.optimization_barrier((kept_1[0], back_1))
    back_1 = exchange(back_1, GROUP)
    parts = expert_grads(order, (kept_0, kept_1))
    far = relay(parts[2])
    back_1, parts = lax.optimization_barrier((back_1, parts))
    d_middle, d_mixed, d_rows = middle_back(
        jnp.concatenate([sum_parts(back_0), sum_parts(back_1)], axis=0)
    )
    d_mixed, far = lax.optimization_barrier((d_mixed, far))
    d_mixed = exchange(d_mixed, CTX)
    d_mixed, far = lax.optimization_barrier((d_mixed, far))
    moved = ring_sums(parts, far)
    d_mixed = d_mixed.reshape(n_ctx, micro, tok, heads)
    d_hidden, head_grads_0 = attention_back(0, d_mixed[:, 0], [])
    d_hidden, d_mixed, d_rows = lax.optimization_barrier((d_hidden, d_mixed, d_rows))
    grad_out, grad_router, grad_mlp = weight_grads(*d_rows)
    grad_out = grad_out.astype(BF).reshape(n_all // 2, 2, rows, width)
    grad_own = lax.dynamic_index_in_dim(grad_out, core, axis=1, keepdims=False)
    grad_other = lax.dynamic_index_in_dim(grad_out, 1 - core, axis=1, keepdims=False)
    grad_out = back_sum(grad_own, grad_other)
    d_mixed, grad_out = lax.optimization_barrier((d_mixed, grad_out))
    grad_out = exchange(grad_out, CTX + GROUP)
    d_hidden, head_grads_1 = attention_back(1, d_mixed[:, 1], d_hidden)
    d_hidden, moved = lax.optimization_barrier((d_hidden, moved))
    hidden_moved = by_z(d_hidden)
    grad_heads, grad_attn, grad_qk = jax.tree.map(jnp.add, head_grads_0, head_grads_1)
    grad_pack = pack_grads(grad_heads, grad_router, grad_attn, grad_mlp, grad_qk)
    grad_pack, grad_out = lax.optimization_barrier((grad_pack, grad_out))
    grad_pack = exchange(grad_pack, ALL)
    weight_sums = pair_sums(parts, moved)
    weight_yl = flip(weight_sums[1].astype(BF), "yl")
    hidden_sums = [
        sum(part[:, i].astype(F32) for part in [d_hidden[0]] + hidden_moved) for i in range(2)
    ]
    hidden_yl = flip(hidden_sums[1].astype(BF), "yl")
    grad_pack, hidden_yl, weight_yl = lax.optimization_barrier((grad_pack, hidden_yl, weight_yl))

    grad_pack = grad_pack.astype(F32)
    own_heads = jnp.sum(grad_pack[:, :, :span].reshape(n_ctx, n_fsdp, rows, -1), axis=1)
    own_heads = own_heads.transpose(1, 0, 2)
    own_small = jnp.sum(grad_pack[:, :, span:], axis=0)
    own_out = sum_parts(grad_out)
    moe = after_all(moe, grad_pack)
    d_hidden = (hidden_sums[0] + hidden_yl.astype(F32)).reshape(all_tok, width)
    expert_own = weight_sums[0] + weight_yl.astype(F32)
    out = (middle.reshape(moe.shape) + moe.astype(F32)).astype(BF)
    start = tokens.reshape(all_tok, width).astype(F32)
    inv_one = lax.rsqrt(jnp.mean(start * start, axis=-1, keepdims=True) + EPS)
    u = d_hidden * gain_attn
    d_input = (
        d_middle
        + inv_one * u
        - start * (inv_one**3 * jnp.mean(u * start, axis=-1, keepdims=True))
    )

    return (
        out[:, None],
        d_input.reshape(tokens.shape),
        own_heads[:, :, :heads].reshape(rows, -1),
        own_heads[:, :, heads : heads + DH].reshape(rows, -1),
        own_heads[:, :, heads + DH :].reshape(rows, -1),
        own_out,
        own_small[:, :experts],
        own_small[:, experts],
        own_small[:, experts + 1],
        own_small[:1, experts + 2],
        expert_own[:, 0],
        expert_own[:, 1],
        expert_own[:, 2],
    )


def solution(mesh):
    mesh = Mesh(mesh.devices.reshape(4, 2, 2, 4, 2), ALL)
    weight = P(ALL, None)
    gain = P(ALL)
    rows = P(None, FSDP, CTX, None)
    expert = P(FSDP, CTX, None)
    return jax.shard_map(
        body,
        mesh=mesh,
        in_specs=(rows, P(None, FSDP, None), rows)
        + (weight,) * 5
        + (gain,) * 3
        + (expert,) * 3
        + (rows,),
        out_specs=(rows, rows) + (weight,) * 5 + (gain,) * 3 + (expert,) * 3,
        check_vma=False,
    )
```

```python
import functools

import jax
import jax.numpy as jnp
from jax import lax
from jax.experimental import pallas as pl
from jax.experimental.pallas import tpu as pltpu
from jax.sharding import Mesh
from jax.sharding import PartitionSpec as P

BF = jnp.bfloat16
F32 = jnp.float32
H = 16
KV = 8
DH = 64
TOPK = 8
WINDOW = 1024
EPS = 1e-06
THETA = 10000.0
COST = pl.CostEstimate(flops=10**7, bytes_accessed=10**5, transcendentals=0)


def dot(a, b, ca, cb):
    return lax.dot_general(a, b, (((ca,), (cb,)), ((), ())), preferred_element_type=F32)


def lanes_of(v):
    return lax.broadcasted_iota(jnp.int32, v.shape, v.ndim - 1)


def head_sums(v):
    low = lanes_of(v) < DH
    first = jnp.sum(jnp.where(low, v, 0.0), axis=1, keepdims=True)
    second = jnp.sum(jnp.where(low, 0.0, v), axis=1, keepdims=True)
    return jnp.where(low, first, second)


def trade(v):
    return jnp.where(
        lanes_of(v) % DH < DH // 2, pltpu.roll(v, 128 - DH // 2, 1), pltpu.roll(v, DH // 2, 1)
    )


def both_halves(v, second):
    low = lanes_of(v) < DH
    other = pltpu.roll(v, DH, 1)
    return jnp.where(low, other, v) if second else jnp.where(low, v, other)


def stack_heads(v):
    low = lanes_of(v) < DH
    zero = jnp.zeros_like(v)
    return jnp.concatenate([jnp.where(low, v, zero), jnp.where(low, zero, v)], axis=0)


def key_span(start, block, length):
    reach = WINDOW // 2 - 1
    low = max(0, start - reach) // 128 * 128
    high = min(length, -(-(start + block + reach) // 128) * 128)
    return low, high


def masked_probs(q_two, keys, seg_col, seg_row, start, low):
    block = q_two.shape[0] // 2
    scores = dot(q_two, keys, 1, 1)
    shape = (block, keys.shape[0])
    gap = (
        lax.broadcasted_iota(jnp.int32, shape, 0)
        - lax.broadcasted_iota(jnp.int32, shape, 1)
        + (start - low)
    )
    allowed = (seg_col == seg_row) & (jnp.abs(gap) < WINDOW // 2)
    bias = jnp.where(allowed, 0.0, -1e30)
    scores = scores + jnp.concatenate([bias, bias], axis=0)
    raised = jnp.exp(scores - jnp.max(scores, axis=1, keepdims=True))
    return raised * (1.0 / jnp.sum(raised, axis=1, keepdims=True))


def attend_kernel(
    order_ref,
    *refs,
):
    pieces, refs = refs[:-13], refs[-13:]
    gain_ref, w_ref, head_gain_ref, cos_ref, sin_ref, seg_col_ref, seg_row_ref = refs[:7]
    mixed_ref, hidden_ref, q_ref, kv_ref, keys_ref, values_ref = refs[7:]
    tok, width = pieces[0].shape[1:]
    length = hidden_ref.shape[0]
    pieces = [(ref, i) for ref in pieces for i in range(ref.shape[0])]
    for r, (ref, i) in enumerate(pieces):
        x = ref[i].astype(F32)
        x = x * lax.rsqrt(jnp.mean(x * x, axis=1, keepdims=True) + EPS) * gain_ref[...]
        rows = pl.ds(pl.multiple_of(order_ref[r] * tok, tok), tok)
        hidden_ref[rows] = x.astype(BF)
    raw = dot(hidden_ref[...], w_ref[...], 1, 0)
    for half in range(2):
        u = raw[:, half * 128 : half * 128 + 128]
        gain = head_gain_ref[:, half * 128 : half * 128 + 128]
        n = u * lax.rsqrt(head_sums(u * u) * (1.0 / DH) + EPS) * gain
        turned = n * cos_ref[...] + trade(n) * sin_ref[...]
        if half == 0:
            q_ref[...] = turned.astype(BF)
        else:
            kv = jnp.where(lanes_of(u) < DH, turned, u)
            kv_ref[...] = kv.astype(BF)
            keys_ref[...] = both_halves(kv, False).astype(BF)
            values_ref[...] = both_halves(kv, True).astype(BF)
    block = 256
    for start in range(0, length, block):
        low, high = key_span(start, block, length)
        q_two = stack_heads(q_ref[start : start + block].astype(F32) * DH**-0.5).astype(BF)
        probs = masked_probs(
            q_two,
            keys_ref[low:high],
            seg_col_ref[start : start + block],
            seg_row_ref[:, low:high],
            start,
            low,
        )
        result = dot(probs.astype(BF), values_ref[low:high], 1, 0)
        first = lanes_of(result[:block]) < DH
        mixed_ref[start : start + block] = jnp.where(first, result[:block], result[block:]).astype(
            BF
        )


def attend_back_kernel(order_ref, *refs, again):
    hidden_ref, q_ref, kv_ref, d_mixed_ref, gain_ref, w_ref, head_gain_ref = refs[:7]
    cos_ref, sin_ref, seg_col_ref, seg_row_ref = refs[7:11]
    refs = refs[15:] if again else refs[11:]
    outs, refs = refs[:4], refs[4:]
    grad_w_ref, grad_gain_ref, grad_heads_ref = refs[:3]
    keys_ref, values_ref, d_q_ref, d_k_ref, d_v_ref, d_raw_ref = refs[3:]
    length = hidden_ref.shape[0]
    kv = kv_ref[...].astype(F32)
    keys_ref[...] = both_halves(kv, False).astype(BF)
    values_ref[...] = both_halves(kv, True).astype(BF)
    d_k_ref[...] = jnp.zeros_like(d_k_ref)
    d_v_ref[...] = jnp.zeros_like(d_v_ref)
    block = 256
    for start in range(0, length, block):
        low, high = key_span(start, block, length)
        q_two = stack_heads(q_ref[start : start + block].astype(F32) * DH**-0.5).astype(BF)
        m_two = stack_heads(d_mixed_ref[start : start + block].astype(F32)).astype(BF)
        probs = masked_probs(
            q_two,
            keys_ref[low:high],
            seg_col_ref[start : start + block],
            seg_row_ref[:, low:high],
            start,
            low,
        )
        d_probs = dot(m_two, values_ref[low:high], 1, 1)
        inner = jnp.sum(probs * d_probs, axis=1, keepdims=True)
        d_scores = (probs * (d_probs - inner)).astype(BF)
        result = dot(d_scores, keys_ref[low:high], 1, 0)
        first = lanes_of(result[:block]) < DH
        d_q_ref[start : start + block] = jnp.where(first, result[:block], result[block:]) * (
            DH**-0.5
        )
        d_k_ref[low:high] += dot(d_scores, q_two, 0, 0)
        d_v_ref[low:high] += dot(probs.astype(BF), m_two, 0, 0)
    raw = dot(hidden_ref[...], w_ref[...], 1, 0)
    d_k = d_k_ref[...]
    d_k = d_k + pltpu.roll(d_k, DH, 1)
    d_v = d_v_ref[...]
    d_v = d_v + pltpu.roll(d_v, DH, 1)
    for half in range(2):
        lanes = slice(half * 128, half * 128 + 128)
        u = raw[:, lanes]
        gain = head_gain_ref[:, lanes]
        d = d_q_ref[...] if half == 0 else d_k
        d = d * cos_ref[...] + trade(d * sin_ref[...])
        r = lax.rsqrt(head_sums(u * u) * (1.0 / DH) + EPS)
        grad_heads_ref[:, lanes] = jnp.sum(d * u * r, axis=0, keepdims=True)
        d = d * gain
        d = d * r - u * (r * r * r * (head_sums(d * u) * (1.0 / DH)))
        if half == 1:
            d = jnp.where(lanes_of(d) < DH, d, d_v)
        d_raw_ref[:, lanes] = d.astype(BF)
    grad_w_ref[...] = dot(hidden_ref[...], d_raw_ref[...], 0, 0)
    total = jnp.zeros(grad_gain_ref.shape, F32)
    tok = length // 8
    for step in range(4):
        rows = pl.ds(pl.multiple_of(order_ref[2 * step] // 2 * (2 * tok), 2 * tok), 2 * tok)
        d_hidden = dot(d_raw_ref[rows], w_ref[...], 1, 1)
        own = order_ref[0] % 2
        outs[step][0, own] = d_hidden[:tok].astype(BF)
        outs[step][0, 1 - own] = d_hidden[tok:].astype(BF)
        total = total + jnp.sum(d_hidden * hidden_ref[rows].astype(F32), axis=0, keepdims=True)
    grad_gain_ref[...] = total / gain_ref[...]


def whole(a):
    return pl.BlockSpec(a.shape, lambda i: (0,) * len(a.shape), pipeline_mode=pl.Buffered(1))


def attend_forward(order, pieces, gain, w_heads, head_gain, cosine, sine, seg_col, seg_row):
    length = cosine.shape[0]
    width = w_heads.shape[0]
    shape = jax.ShapeDtypeStruct
    outs = [
        shape((length, 128), BF),
        shape((length, width), BF),
        shape((length, 128), BF),
        shape((length, 128), BF),
    ]
    args = list(pieces) + [gain, w_heads, head_gain, cosine, sine, seg_col, seg_row]
    return pl.pallas_call(
        attend_kernel,
        out_shape=outs,
        grid=(1,),
        in_specs=[pl.BlockSpec(memory_space=pltpu.SMEM)] + [whole(a) for a in args],
        out_specs=[whole(o) for o in outs],
        scratch_shapes=[pltpu.VMEM((length, 128), BF), pltpu.VMEM((length, 128), BF)],
        compiler_params=pltpu.CompilerParams(vmem_limit_bytes=40 * 1024 * 1024),
        cost_estimate=COST,
    )(order, *args)


def attend_backward(micro, held, order, *args):
    length, width = args[0].shape
    shape = jax.ShapeDtypeStruct
    outs = [shape((2, 2, length // 8, width), BF)] * 4 + [
        shape((width, 256), F32),
        shape((1, width), F32),
        shape((1, 256), F32),
    ]
    part = pl.BlockSpec(
        (1, 2, length // 8, width), lambda i: (micro, 0, 0, 0), pipeline_mode=pl.Buffered(1)
    )
    return pl.pallas_call(
        functools.partial(attend_back_kernel, again=len(held) > 0),
        out_shape=outs,
        grid=(1,),
        in_specs=[pl.BlockSpec(memory_space=pltpu.SMEM)]
        + [whole(a) for a in args]
        + [pl.BlockSpec(memory_space=pl.ANY)] * len(held),
        out_specs=[part] * 4 + [whole(o) for o in outs[4:]],
        input_output_aliases={1 + len(args) + n: n for n in range(len(held))},
        scratch_shapes=[pltpu.VMEM((length, 128), BF)] * 2
        + [pltpu.VMEM((length, 128), F32)] * 3
        + [pltpu.VMEM((length, 256), BF)],
        compiler_params=pltpu.CompilerParams(vmem_limit_bytes=40 * 1024 * 1024),
        cost_estimate=COST,
    )(order, *args, *held)


def halves(v):
    high = v.astype(BF)
    return high, (v - high.astype(F32)).astype(BF)


def expert_kernel(scalar_ref, *refs, again):
    x_own_ref, x_other_ref, g_ref, router_ref = refs[:4]
    pieces, refs = refs[4:12], refs[12:]
    if again:
        refs = refs[1:]
    out_ref, back_own_ref, back_other_ref = refs[:3]
    kept_refs, refs = refs[3:8], refs[8:]
    xe_ref, de_ref, act_ref, da_ref, db_ref, *refs = refs
    pick_ref, weight_ref, dgate_ref, eo_ref, dr_ref, w_ref, in_sem, out_sem = refs
    half, tok, width = x_own_ref.shape
    sources = 2 * half
    core = scalar_ref[1]
    depth = w_ref.shape[2] // 8

    loads = []
    for r, ref in enumerate(pieces):
        rows = pl.ds(pl.multiple_of(scalar_ref[2 + r] * depth, depth), depth)
        loads.append(pltpu.make_async_copy(ref.at[0], w_ref.at[:, :, rows], in_sem.at[r]))
        loads[-1].start()
    local, slots, hidden = act_ref.shape
    cap = slots // sources
    first = scalar_ref[0]
    lane = lax.broadcasted_iota(jnp.int32, (tok, 128), 1)
    spot = lax.broadcasted_iota(jnp.int32, (tok, local * cap), 1)
    row_expert = lax.broadcasted_iota(jnp.int32, (local * cap, 128), 0) // cap
    slot_lane = lax.broadcasted_iota(jnp.int32, (local * cap, 128), 1)
    own_lane = slot_lane == first + row_expert

    def fetch(i, carry, x_ref, offset, column):
        s = i + offset
        x = x_ref[i]
        from_g = 2 * i + column
        held = g_ref[from_g, :, width:].astype(F32)
        chosen = held >= 0.0
        logits = jnp.where(chosen, dot(x, router_ref[...], 1, 0), -1e30)
        top = jnp.max(logits, axis=1, keepdims=True)
        raised = jnp.where(chosen, jnp.exp(logits - top), 0.0)
        gates = raised / jnp.sum(raised, axis=1, keepdims=True)
        pick = jnp.zeros((tok, local * cap), F32)
        for e in range(local):
            mine = jnp.max(jnp.where(lane == first + e, held, -1.0), axis=1, keepdims=True)
            goal = jnp.where(mine >= 0.0, mine + e * cap, -1.0).astype(jnp.int32)
            pick = jnp.where(spot == goal, 1.0, pick)
        pick = pick.astype(BF)
        pick_ref[s] = pick
        rows = pl.ds(pl.multiple_of(s * cap, 16), cap)
        x_slots = dot(pick, x, 0, 0).astype(BF)
        g_slots = dot(pick, g_ref[from_g, :, :width], 0, 0).astype(BF)
        high, low = halves(gates)
        weight = dot(pick, high, 0, 0) + dot(pick, low, 0, 0)
        weight = jnp.sum(jnp.where(own_lane, weight, 0.0), axis=1, keepdims=True)
        for e in range(local):
            part = slice(e * cap, (e + 1) * cap)
            xe_ref[e, rows] = x_slots[part]
            de_ref[e, rows] = g_slots[part]
            weight_ref[e, rows] = weight[part]
        return carry

    for x_ref, offset, column in ((x_own_ref, 0, core), (x_other_ref, half, 1 - core)):
        step = functools.partial(fetch, x_ref=x_ref, offset=offset, column=column)
        lax.fori_loop(0, half, step, 0, unroll=4)
    for load in loads:
        load.wait()
    chunk = 384

    def work(i, carry):
        e = i // (slots // chunk)
        rows = pl.ds(pl.multiple_of((i % (slots // chunk)) * chunk, chunk), chunk)
        w_gate = w_ref[e, 0]
        w_up = w_ref[e, 1]
        w_down = w_ref[e, 2]
        x = xe_ref[e, rows]
        a = dot(x, w_gate, 1, 0)
        b = dot(x, w_up, 1, 0)
        sig = 1.0 / (1.0 + jnp.exp(-a))
        silu = a * sig
        active = (silu * b).astype(BF)
        act_ref[e, rows] = active
        slope = b * (sig * (1.0 + a * (1.0 - sig)))
        weight = weight_ref[e, rows]
        g = de_ref[e, rows].astype(F32)
        result = dot(active, w_down, 1, 1).astype(BF).astype(F32)
        dgate_ref[e, rows] = jnp.sum(result * g, axis=1, keepdims=True)
        eo_ref[e, rows] = (weight * result).astype(BF)
        d_expert = (weight * g).astype(BF)
        de_ref[e, rows] = d_expert
        d_active = dot(d_expert, w_down, 1, 0)
        da = (d_active * slope).astype(BF)
        db = (d_active * silu).astype(BF)
        da_ref[e, rows] = da
        db_ref[e, rows] = db
        dr_ref[e, rows] = (dot(da, w_gate, 1, 1) + dot(db, w_up, 1, 1)).astype(BF)
        return carry

    lax.fori_loop(0, local * (slots // chunk), work, 0)
    stores = [
        pltpu.make_async_copy(ref, kept, out_sem.at[n])
        for n, (ref, kept) in enumerate(
            zip((xe_ref, de_ref, act_ref, da_ref, db_ref), kept_refs)
        )
    ]
    for store in stores:
        store.start()

    def give(i, carry, back_ref, offset, column):
        s = i + offset
        rows = pl.ds(pl.multiple_of(s * cap, 16), cap)
        pick = pick_ref[s]
        eo = jnp.concatenate([eo_ref[e, rows] for e in range(local)], axis=0)
        dr = jnp.concatenate([dr_ref[e, rows] for e in range(local)], axis=0)
        dgate = jnp.concatenate([dgate_ref[e, rows] for e in range(local)], axis=0)
        high, low = halves(dgate)
        spread = jnp.where(own_lane, high.astype(F32), 0.0) + jnp.where(
            slot_lane == first + row_expert + 64, low.astype(F32), 0.0
        )
        out_ref[2 * i + column, 0] = dot(pick, eo, 1, 0).astype(BF)
        back_ref[i, :, :width] = dot(pick, dr, 1, 0).astype(BF)
        back_ref[i, :, width:] = dot(pick, spread.astype(BF), 1, 0).astype(BF)
        return carry

    for back_ref, offset, column in ((back_own_ref, 0, core), (back_other_ref, half, 1 - core)):
        step = functools.partial(give, back_ref=back_ref, offset=offset, column=column)
        lax.fori_loop(0, half, step, 0, unroll=4)
    for store in stores:
        store.wait()


def run_experts(scalars, x_own, x_other, g_all, micro, router, pieces, cap, moe=None):
    half, tok, width = x_own.shape
    sources = 2 * half
    _, local, _, _, hidden = pieces[0].shape
    slots = sources * cap
    wide = g_all.shape[2]
    shape = jax.ShapeDtypeStruct
    outs = [
        shape((sources, 2, tok, width), BF),
        shape((half, tok, wide), BF),
        shape((half, tok, wide), BF),
        shape((local, slots, width), BF),
        shape((local, slots, width), BF),
        shape((local, slots, hidden), BF),
        shape((local, slots, hidden), BF),
        shape((local, slots, hidden), BF),
    ]
    g_spec = pl.BlockSpec(
        (sources, tok, wide), lambda i: (0, micro, 0), pipeline_mode=pl.Buffered(1)
    )
    args = list(pieces)
    any_place = pl.BlockSpec(memory_space=pl.ANY)
    held = [] if moe is None else [moe]
    moe_spec = pl.BlockSpec(
        (sources, 1, tok, width), lambda i: (0, micro, 0, 0), pipeline_mode=pl.Buffered(1)
    )
    return pl.pallas_call(
        functools.partial(expert_kernel, again=moe is not None),
        out_shape=outs,
        grid=(1,),
        in_specs=[pl.BlockSpec(memory_space=pltpu.SMEM), whole(x_own), whole(x_other), g_spec]
        + [whole(router)]
        + [any_place] * (len(args) + len(held)),
        out_specs=[moe_spec] + [whole(o) for o in outs[1:3]] + [any_place] * 5,
        input_output_aliases={5 + len(args): 0} if held else {},
        scratch_shapes=[pltpu.VMEM(o.shape, o.dtype) for o in outs[3:]]
        + [
            pltpu.VMEM((sources, tok, local * cap), BF),
            pltpu.VMEM((local, slots, 1), F32),
            pltpu.VMEM((local, slots, 1), F32),
            pltpu.VMEM((local, slots, width), BF),
            pltpu.VMEM((local, slots, width), BF),
            pltpu.VMEM((local, 3, width, hidden), BF),
            pltpu.SemaphoreType.DMA((8,)),
            pltpu.SemaphoreType.DMA((5,)),
        ],
        compiler_params=pltpu.CompilerParams(vmem_limit_bytes=60 * 1024 * 1024),
        cost_estimate=COST,
    )(scalars, x_own, x_other, g_all, router, *args, *held)


def expert_grad_kernel(order_ref, *refs):
    kept, outs, total_ref = refs[:10], refs[10:14], refs[14]
    left = (kept[0:2], kept[0:2], kept[2:4])
    right = (kept[6:8], kept[8:10], kept[4:6])
    step = pl.program_id(0)
    depth = outs[0].shape[3]
    for kind in range(3):

        @pl.when(step % 3 == kind)
        def _(kind=kind):
            total = dot(left[kind][0][0], right[kind][0][0], 0, 0)
            total_ref[...] = total + dot(left[kind][1][0], right[kind][1][0], 0, 0)

    for r in range(8):
        rows = pl.ds(pl.multiple_of(order_ref[r] * depth, depth), depth)
        outs[r // 2][r % 2, 0, 0] = total_ref[rows].astype(BF)


def expert_grads(order, kept):
    local, slots, width = kept[0][0].shape
    hidden = kept[0][2].shape[2]
    args = [kept[m][i] for i in range(5) for m in range(2)]
    depth = width // 8
    shape = jax.ShapeDtypeStruct
    return pl.pallas_call(
        expert_grad_kernel,
        out_shape=[shape((2, local, 3, depth, hidden), BF)] * 4,
        grid=(3 * local,),
        in_specs=[pl.BlockSpec(memory_space=pltpu.SMEM)]
        + [pl.BlockSpec((1,) + a.shape[1:], lambda i: (i // 3, 0, 0)) for a in args],
        out_specs=[
            pl.BlockSpec((2, 1, 1, depth, hidden), lambda i: (0, i // 3, i % 3, 0, 0))
        ]
        * 4,
        scratch_shapes=[pltpu.VMEM((width, hidden), F32)],
        compiler_params=pltpu.CompilerParams(vmem_limit_bytes=48 * 1024 * 1024),
        cost_estimate=COST,
    )(order, *args)


CTX = ("z", "yl")
GROUP = ("yh", "x")
FSDP = ("yh", "x", "core")
ALL = CTX + FSDP
UP = [(i, (i + 1) % 4) for i in range(4)]
DOWN = [(i, (i - 1) % 4) for i in range(4)]
TWO = [(i, (i + 2) % 4) for i in range(4)]
FLIP = [(0, 1), (1, 0)]


def mm(a, b):
    return jnp.dot(a, b, preferred_element_type=F32)


def mm_t(a, b):
    return lax.dot_general(a, b, (((1,), (1,)), ((), ())), preferred_element_type=F32)


def t_mm(a, b):
    return lax.dot_general(a, b, (((0,), (0,)), ((), ())), preferred_element_type=F32)


def ein(spec, a, b):
    return jnp.einsum(spec, a, b, preferred_element_type=F32)


def swap(parts, axis):
    return lax.all_to_all(parts, axis, split_axis=0, concat_axis=0, tiled=True)


def flip(block, axis):
    return lax.ppermute(block, axis, FLIP)


def by_z(parts):
    return [lax.ppermute(parts[k], "z", perm) for k, perm in ((1, UP), (2, TWO), (3, DOWN))]


def along_z(both):
    before, far, after = by_z([both] * 4)
    return [both, after, far, before]


class Exchange:
    def __init__(self):
        self.last = None

    def __call__(self, parts, axis):
        if self.last is not None:
            parts = after_all(parts, self.last)
        self.last = swap(parts, axis)
        return self.last

    def copies(self, block, axis, count):
        return self(jnp.broadcast_to(block[None], (count,) + block.shape), axis)


def add(a, b):
    return (a.astype(F32) + b.astype(F32)).astype(BF)


def add_part(parts, i, more):
    pieces = [parts[:1], parts[1:]]
    pieces[i] = add(pieces[i], more)
    return jnp.concatenate(pieces, axis=0)


def relay(far):
    return [lax.ppermute(far[:1], "z", UP), lax.ppermute(far[1:], "z", DOWN)]


def ring_sums(parts, far):
    return [
        lax.ppermute(add_part(parts[1], 0, far[0]), "z", UP),
        lax.ppermute(add_part(parts[3], 1, far[1]), "z", DOWN),
    ]


def pair_sums(parts, moved):
    return [sum(part[i].astype(F32) for part in [parts[0]] + moved) for i in range(2)]


def sum_parts(parts):
    return jnp.sum(parts.astype(F32), axis=0)


def after_all(value, *others):
    return lax.optimization_barrier((value,) + others)[0]


def rope_tables(positions):
    half = DH // 2
    inverse = THETA ** (-(jnp.arange(half, dtype=F32) * 2.0) / DH)
    angles = positions.astype(F32)[:, None] * inverse[None, :]
    return (jnp.cos(angles), jnp.sin(angles))


def rms_scale(values, gain):
    return values * lax.rsqrt(jnp.mean(values * values, axis=-1, keepdims=True) + EPS) * gain


def body(
    tokens,
    segments,
    routes,
    w_query,
    w_key,
    w_value,
    w_out,
    w_router,
    attn_gain,
    mlp_gain,
    qk_gain,
    w_gate,
    w_up,
    w_down,
    cotangent,
):
    micro = tokens.shape[0]
    tok = tokens.shape[2]
    width = tokens.shape[3]
    length = segments.shape[2]
    rows = w_query.shape[0]
    n_ctx, n_fsdp = 8, 16
    n_all = n_ctx * n_fsdp
    z, yl, yh, x, core = (lax.axis_index(name) for name in ALL)
    shard = (yh * 4 + x) * 2 + core
    local = w_gate.shape[0]
    experts = local * n_fsdp
    cap = (3 * tok * TOPK + 2 * experts - 1) // (2 * experts)
    all_tok = micro * tok
    ratio = H // KV
    heads = ratio * DH
    span = heads + 2 * DH

    exchange = Exchange()
    small = jnp.concatenate(
        [
            w_router,
            attn_gain[:, None],
            mlp_gain[:, None],
            jnp.pad(qk_gain[:, None], ((0, rows - 1), (0, 0))),
        ],
        axis=1,
    )
    small = jnp.pad(small, ((0, 0), (0, 128 - small.shape[1])))
    pieces = jnp.concatenate(
        [
            w_query.reshape(rows, n_ctx, heads),
            w_key.reshape(rows, n_ctx, DH),
            w_value.reshape(rows, n_ctx, DH),
            jnp.broadcast_to(small[:, None], (rows, n_ctx, 128)),
        ],
        axis=2,
    ).transpose(1, 0, 2)
    pieces = jnp.broadcast_to(pieces[:, None], (n_ctx, n_fsdp) + pieces.shape[1:])
    both_0, both_1 = (
        jnp.concatenate([tokens[m], flip(tokens[m], "yl")], axis=0) for m in range(micro)
    )
    own_w = jnp.stack([w_gate, w_up, w_down], axis=1)[None]
    own_before = lax.ppermute(own_w, "z", UP)
    own_after = lax.ppermute(own_w, "z", DOWN)
    both_0 = after_all(both_0, own_before, own_after)
    head_all = exchange(pieces.reshape((n_all,) + pieces.shape[2:]), ALL).reshape(width, -1)
    other_w = flip(own_w, "yl")
    seq_rows = [along_z(both_0)]
    seq_rows.append(along_z(after_all(both_1, *seq_rows[0][1:])))
    head_all = after_all(head_all, *seq_rows[0][1:], other_w)
    w_heads = head_all[:, :span]
    small_all = head_all[:, span:]
    router = small_all[:, :experts]
    small_wide = small_all.astype(F32)
    gain_attn = small_wide[:, experts]
    gain_mlp = small_wide[:, experts + 1]
    gain_heads = small_wide[:, experts + 2].reshape(-1, rows)[:, 0]
    gain_row = gain_attn[None]
    head_row = jnp.concatenate(
        [gain_heads[:DH]] * ratio + [gain_heads[DH:], jnp.ones((DH,), F32)]
    )[None]
    router_pad = jnp.pad(router, ((0, 0), (0, 128 - experts)))

    out_own = exchange.copies(w_out, CTX + GROUP, n_all // 2)

    expert_ids = jnp.arange(experts, dtype=jnp.int32)
    cot = cotangent.reshape(all_tok, width)
    chosen = jnp.any(routes.reshape(all_tok, TOPK)[:, :, None] == expert_ids, axis=1)
    before = jnp.arange(tok, dtype=jnp.int32)
    lower = (before[:, None] >= before[None, :]).astype(BF)
    counts = ein("ut,mte->mue", lower, chosen.reshape(micro, tok, experts).astype(BF))
    held = jnp.where(chosen, counts.reshape(all_tok, experts) - 1.0, -1.0)
    held = jnp.pad(held, ((0, 0), (0, 128 - experts)), constant_values=-1.0).astype(BF)
    pack = after_all(jnp.concatenate([cot, held], axis=1), *seq_rows[0][1:])
    g_all = lax.all_gather(pack, FSDP, axis=0)

    cosine, sine = rope_tables(jnp.arange(length, dtype=jnp.int32))
    cosine = jnp.tile(cosine, (1, 4))
    sine = jnp.tile(jnp.concatenate([-sine, sine], axis=1), (1, 2))
    rel = jnp.arange(n_ctx, dtype=jnp.int32)
    order = ((z + rel // 2) % 4) * 2 + (yl + rel % 2) % 2
    scalars = jnp.concatenate([jnp.stack([shard * local, core]), order]).astype(jnp.int32)

    def to_owner(v):
        return exchange(v.reshape(n_ctx, tok, -1), CTX)

    def attention_args(m):
        seg = segments[m, 0]
        return gain_row, w_heads, head_row, cosine, sine, seg[:, None], seg[None, :]

    mixed_0, *saved_0 = attend_forward(order, seq_rows[0], *attention_args(0))
    seq_rows[1], mixed_0 = lax.optimization_barrier((seq_rows[1], mixed_0))
    late_w = after_all(other_w, *seq_rows[1][1:])
    other_before = lax.ppermute(late_w, "z", UP)
    other_after = lax.ppermute(late_w, "z", DOWN)
    own_far = lax.ppermute(after_all(own_before, other_before), "z", UP)
    other_far = lax.ppermute(other_after, "z", DOWN)
    mixed_1, *saved_1 = attend_forward(order, seq_rows[1], *attention_args(1))
    saved = [saved_0, saved_1]
    out_own, mixed_0, mixed_1 = lax.optimization_barrier((out_own, mixed_0, mixed_1))
    out_other = flip(out_own, "core")
    mixed = jnp.stack([mixed_0, mixed_1]).reshape(micro, n_ctx, tok, heads).transpose(1, 0, 2, 3)
    mixed = exchange(mixed.reshape(n_ctx, all_tok, heads), CTX)
    mixed, other_before, other_after = lax.optimization_barrier(
        (mixed, other_before, other_after)
    )
    mixed = mixed.transpose(1, 0, 2).reshape(all_tok, width)
    out_full = jnp.where(
        core == 0,
        jnp.stack([out_own, out_other], axis=1),
        jnp.stack([out_other, out_own], axis=1),
    ).reshape(width, width)
    middle = tokens.reshape(all_tok, width).astype(F32) + mm(mixed, out_full)
    inv_two = lax.rsqrt(jnp.mean(middle * middle, axis=-1, keepdims=True) + EPS)
    hidden_two = (middle * inv_two * gain_mlp).astype(BF)
    x_0 = exchange.copies(hidden_two[:tok], GROUP, n_ctx)
    weights = [own_w, other_w, own_after, other_after, own_far, other_far, own_before, other_before]
    x_0, weights = lax.optimization_barrier((x_0, weights))
    x_1 = exchange.copies(hidden_two[tok:], GROUP, n_ctx)
    logits = jnp.where(chosen, mm(hidden_two, router), -1e30)
    gates_all = jnp.where(chosen, jax.nn.softmax(logits, axis=-1), 0.0)

    def experts_of(m, x_own, *moe):
        return run_experts(
            scalars,
            x_own,
            flip(x_own, "core"),
            g_all,
            m,
            router_pad,
            weights,
            cap,
            *moe,
        )

    def back_sum(own, other):
        return add(own, flip(other, "core"))

    def middle_back(back):
        tail = back[:, width:]
        d_gates = tail[:, :experts] + tail[:, 64 : 64 + experts]
        d_select = gates_all * (d_gates - jnp.sum(gates_all * d_gates, axis=-1, keepdims=True))
        d_logits = d_select.astype(BF)
        d_two = back[:, :width] + mm_t(d_logits, router)
        u = d_two * gain_mlp
        d_middle = (
            cot.astype(F32)
            + inv_two * u
            - middle * (inv_two**3 * jnp.mean(u * middle, axis=-1, keepdims=True))
        )
        d_branch = d_middle.astype(BF)
        d_mixed = mm_t(d_branch, out_full).astype(BF)
        d_mixed = d_mixed.reshape(all_tok, n_ctx, heads).transpose(1, 0, 2)
        return d_middle, d_mixed, (d_branch, d_logits, d_two)

    def weight_grads(d_branch, d_logits, d_two):
        grad_mlp = jnp.sum(d_two * middle * inv_two, axis=0)
        return t_mm(mixed, d_branch), t_mm(hidden_two, d_logits), grad_mlp

    def pack_grads(grad_heads, grad_router, grad_attn, grad_mlp, grad_qk):
        grad_qk = jnp.pad(grad_qk[:, None], ((0, 0), (0, rows - 1))).reshape(-1)
        grad_small = jnp.concatenate(
            [grad_router, grad_attn[:, None], grad_mlp[:, None], grad_qk[:, None]], axis=1
        )
        grad_small = jnp.pad(grad_small, ((0, 0), (0, 128 - grad_small.shape[1])))
        grad_pack = jnp.concatenate([grad_heads, grad_small], axis=1).astype(BF)
        return grad_pack.reshape(n_all, rows, -1)

    def attention_back(m, d_mixed, held):
        *d_hidden, grad_heads, grad_attn, grad_qk = attend_backward(
            m, held, order, *saved[m], d_mixed.reshape(length, heads), *attention_args(m)
        )
        grad_qk = jnp.concatenate(
            [grad_qk[0, :DH] + grad_qk[0, DH : 2 * DH], grad_qk[0, 2 * DH : 3 * DH]]
        )
        return d_hidden, (grad_heads, grad_attn[0], grad_qk)

    moe, back_own, back_other, *kept_0 = experts_of(0, x_0)
    x_1, back_own, back_other = lax.optimization_barrier((x_1, back_own, back_other))
    back_0 = back_sum(back_own, back_other)
    x_1 = after_all(x_1, back_0)
    back_0 = exchange(back_0, GROUP)
    moe, back_own, back_other, *kept_1 = experts_of(1, x_1, moe)
    back_0, back_own, back_other, moe = lax.optimization_barrier(
        (back_0, back_own, back_other, moe)
    )
    moe = lax.psum_scatter(moe, FSDP, scatter_dimension=0, tiled=True)[0]
    back_1 = back_sum(back_own, back_other)
    kept_1[0], back_1 = lax.optimization_barrier((kept_1[0], back_1))
    back_1 = exchange(back_1, GROUP)
    parts = expert_grads(order, (kept_0, kept_1))
    far = relay(parts[2])
    back_1, parts = lax.optimization_barrier((back_1, parts))
    d_middle, d_mixed, d_rows = middle_back(
        jnp.concatenate([sum_parts(back_0), sum_parts(back_1)], axis=0)
    )
    d_mixed, far = lax.optimization_barrier((d_mixed, far))
    d_mixed = exchange(d_mixed, CTX)
    d_mixed, far = lax.optimization_barrier((d_mixed, far))
    moved = ring_sums(parts, far)
    d_mixed = d_mixed.reshape(n_ctx, micro, tok, heads)
    d_hidden, head_grads_0 = attention_back(0, d_mixed[:, 0], [])
    d_hidden, head_grads_1 = attention_back(1, d_mixed[:, 1], d_hidden)
    d_hidden, moved, d_rows = lax.optimization_barrier((d_hidden, moved, d_rows))
    hidden_moved = by_z(d_hidden)
    grad_out, grad_router, grad_mlp = weight_grads(*d_rows)
    grad_heads, grad_attn, grad_qk = jax.tree.map(jnp.add, head_grads_0, head_grads_1)
    grad_pack = pack_grads(grad_heads, grad_router, grad_attn, grad_mlp, grad_qk)
    grad_pack = exchange(grad_pack, ALL)
    grad_out = grad_out.astype(BF).reshape(n_all // 2, 2, rows, width)
    grad_own = lax.dynamic_index_in_dim(grad_out, core, axis=1, keepdims=False)
    grad_other = lax.dynamic_index_in_dim(grad_out, 1 - core, axis=1, keepdims=False)
    grad_out = back_sum(grad_own, grad_other)
    weight_sums = pair_sums(parts, moved)
    weight_yl = flip(weight_sums[1].astype(BF), "yl")
    grad_pack, grad_out, weight_yl = lax.optimization_barrier((grad_pack, grad_out, weight_yl))
    exchange.last = grad_pack
    grad_out = exchange(grad_out, CTX + GROUP)
    hidden_sums = [
        sum(part[:, i].astype(F32) for part in [d_hidden[0]] + hidden_moved) for i in range(2)
    ]
    hidden_yl = flip(hidden_sums[1].astype(BF), "yl")
    grad_out, hidden_yl = lax.optimization_barrier((grad_out, hidden_yl))

    grad_pack = grad_pack.astype(F32)
    own_heads = jnp.sum(grad_pack[:, :, :span].reshape(n_ctx, n_fsdp, rows, -1), axis=1)
    own_heads = own_heads.transpose(1, 0, 2)
    own_small = jnp.sum(grad_pack[:, :, span:], axis=0)
    own_out = sum_parts(grad_out)
    moe = after_all(moe, grad_pack)
    d_hidden = (hidden_sums[0] + hidden_yl.astype(F32)).reshape(all_tok, width)
    expert_own = weight_sums[0] + weight_yl.astype(F32)
    out = (middle.reshape(moe.shape) + moe.astype(F32)).astype(BF)
    start = tokens.reshape(all_tok, width).astype(F32)
    inv_one = lax.rsqrt(jnp.mean(start * start, axis=-1, keepdims=True) + EPS)
    u = d_hidden * gain_attn
    d_input = (
        d_middle
        + inv_one * u
        - start * (inv_one**3 * jnp.mean(u * start, axis=-1, keepdims=True))
    )

    return (
        out[:, None],
        d_input.reshape(tokens.shape),
        own_heads[:, :, :heads].reshape(rows, -1),
        own_heads[:, :, heads : heads + DH].reshape(rows, -1),
        own_heads[:, :, heads + DH :].reshape(rows, -1),
        own_out,
        own_small[:, :experts],
        own_small[:, experts],
        own_small[:, experts + 1],
        own_small[:1, experts + 2],
        expert_own[:, 0],
        expert_own[:, 1],
        expert_own[:, 2],
    )


def solution(mesh):
    mesh = Mesh(mesh.devices.reshape(4, 2, 2, 4, 2), ALL)
    weight = P(ALL, None)
    gain = P(ALL)
    rows = P(None, FSDP, CTX, None)
    expert = P(FSDP, CTX, None)
    return jax.shard_map(
        body,
        mesh=mesh,
        in_specs=(rows, P(None, FSDP, None), rows)
        + (weight,) * 5
        + (gain,) * 3
        + (expert,) * 3
        + (rows,),
        out_specs=(rows, rows) + (weight,) * 5 + (gain,) * 3 + (expert,) * 3,
        check_vma=False,
    )
```
